128 devices in a mesh: rows: 32 (over y_lo, x, z), cols: 4 (over y_hi, core).
Axes of the slice: x: 4, y: 4 (y_hi: 2, y_lo: 2; y = y_hi * 2 + y_lo), z: 4, core: 2. Of those that a mesh axis runs over, the one named last changes fastest.
Arguments:
- features: bfloat16 [256, 64, 2048], P('rows', 'cols'), may hold values from -6 to 12
- image_rows: int32 [256], P('rows'), may hold values from 0 to 3, never falling along the last dimension, each value on 1 to 96 neighbouring positions
- seg_labels: int32 [256, 64], P('rows', 'cols'), may hold values from 0 to 12
- edge_labels: int32 [256, 64], P('rows', 'cols'), may hold values from 0 to 1
- part_labels: int32 [256, 64], P('rows', 'cols'), may hold values from 0 to 2
- task_weights: int32 [3], replicated, may hold values from 1 to 8
- block_params: float32 [4472832], P(('rows', 'cols'))
- block_moment: float32 [4472832], P(('rows', 'cols')), may hold values from -0.03 to 0.03
- head_params: float32 [1392640], P(('rows', 'cols'))
- head_moment: float32 [1392640], P(('rows', 'cols')), may hold values from -0.03 to 0.03
- rate_params: float32 [2048, 6912], P('cols', 'rows'), may hold values from -0.046875 to 0.046875
- rate_moment: float32 [2048, 6912], P('cols', 'rows'), may hold values from -0.03 to 0.03
Outputs:
- loss_value: float32 [], replicated
- pooled: float32 [4, 2048], replicated
- feature_grad: float32 [256, 64, 2048], P('rows', 'cols')
- block_moment_next: float32 [4472832], P(('rows', 'cols'))
- head_moment_next: float32 [1392640], P(('rows', 'cols'))
- rate_moment_next: float32 [2048, 6912], P('cols', 'rows')
The draws below stay inside these ranges and needn't reach their ends.
Inputs may be any that keep to these rules, and one draw needn't show every extreme that they name: `image_rows`: image numbers never fall along the rows; each of the 4 images covers 1 to 96 consecutive rows, and one covers exactly 96.
All inputs are finite; a program needn't handle non-finite values.
Results may differ from the reference program's by a relative error of at most 0.018.
Values may be sent and summed in bfloat16 or wider, within the bound.
A program may use at most 320 MiB of HBM per device.

```python
import math
from functools import partial
import jax
import jax.numpy as jnp
import numpy as np
from jax import lax

CIN = 2048
MID = 512
ASPP = 256
SEG = 13
PART = 3
HEADS = 17
WIDTH = 64
NR = 256
IMGS = 4
TALL = 96
BLOCK_PARAMS = 4472832
HEAD_PARAMS = 1392640


def shape_noise(noise, profile):
    centers = []
    spreads = []
    for number, center, spread in profile:
        centers.append(jnp.full((number,), center, jnp.float32))
        spreads.append(jnp.full((number,), spread, jnp.float32))
    used = sum((item[0] for item in profile))
    rest = noise.shape[0] - used
    centers.append(jnp.zeros((rest,), jnp.float32))
    spreads.append(jnp.full((rest,), 0.01, jnp.float32))
    return jnp.concatenate(centers) + jnp.concatenate(spreads) * noise


def block_profile():
    profile = [(CIN * MID, 0.0, CIN ** (-0.5)), (9 * MID * MID, 0.0, (9 * MID) ** (-0.5)), (MID * CIN, 0.0, MID ** (-0.5))]
    for layer in range(2):
        profile.append((MID, 1.0, 0.2))
        profile.append((MID, 0.0, 0.3))
    profile.append((CIN, 1.0, 0.2))
    profile.append((CIN, 0.0, 0.3))
    return profile


def head_profile():
    profile = [(CIN * ASPP, 0.0, CIN ** (-0.5)), (CIN * ASPP, 0.0, 3.0 * CIN ** (-0.5)), (ASPP, 0.0, 0.3), (5 * ASPP * ASPP, 0.0, (5 * ASPP) ** (-0.5))]
    for branch in range(5):
        profile.append((ASPP, 1.0, 0.2))
        profile.append((ASPP, 0.0, 0.3))
    profile.append((ASPP * HEADS, 0.0, 2.5 * ASPP ** (-0.5)))
    profile.append((HEADS, 0.0, 0.5))
    return profile


def draw_features(key, part):
    key = jax.random.fold_in(key, 37)
    noise_key, row_key, channel_key = jax.random.split(key, 3)
    noise = jnp.clip(jax.random.normal(noise_key, (NR, WIDTH, CIN), jnp.float32), -6.0, 6.0)
    ramp = 0.5 + jnp.arange(NR, dtype=jnp.float32) / NR
    row_factor = jax.random.uniform(row_key, (NR,), jnp.float32, 0.0, 1.0) * ramp
    channel_offset = jax.random.uniform(channel_key, (CIN,), jnp.float32, 0.0, 4.0)
    values = noise + row_factor[:, None, None] * channel_offset[None, None, :]
    return values.astype(jnp.bfloat16)


def draw_block_params(key, part):
    key = jax.random.fold_in(key, 11)
    noise = jax.random.normal(key, (BLOCK_PARAMS,), jnp.float32)
    return shape_noise(noise, block_profile())


def draw_head_params(key, part):
    key = jax.random.fold_in(key, 23)
    noise = jax.random.normal(key, (HEAD_PARAMS,), jnp.float32)
    return shape_noise(noise, head_profile())


def set_ends(values, rng, low, largest):
    longest = values.shape.index(max(values.shape))
    spots = []
    for shift in (0, 1):
        where = [jax.random.randint(jax.random.fold_in(rng, axis), (), 0, length) for axis, length in enumerate(values.shape)]
        where[longest] = (where[longest] + shift) % values.shape[longest]
        spots.append(tuple(where))
    return values.at[spots[0]].set(low).at[spots[1]].set(largest)


def levels(stream_key, shape, cuts, least, high):
    loudness = 1.0
    for axis_at, blocks in cuts:
        heights = jax.random.uniform(jax.random.fold_in(jax.random.fold_in(stream_key, 6), axis_at), (blocks,), jnp.float32, least / len(cuts), high / len(cuts))
        loudness = loudness * jnp.repeat(jnp.exp(heights), shape[axis_at] // blocks).reshape((-1,) + (1,) * (len(shape) - 1 - axis_at))
    return loudness


def length_profile(amount, total, bound, lean):
    portions = [(1 << 20) // math.isqrt(rank ** lean) + 1 for rank in range(2, amount + 1)]
    spare, given = total - bound - (amount - 1), [1] * (amount - 1)
    while spare > 0:
        movable = [i for i in range(amount - 1) if given[i] < bound]
        whole, remaining = sum([portions[i] for i in movable]), spare
        for i in movable:
            extra = min(bound - given[i], max(1, remaining * portions[i] // whole), spare)
            given[i] = given[i] + extra
            spare = spare - extra
    return np.array([bound] + given)


def uneven(own_key, count, total, most, slope):
    if count == 2:
        one = jax.random.randint(own_key, (), max(1, total - most), min(most, total - 1) + 1)
        return jnp.stack([one, total - one])
    sizes = jnp.asarray(length_profile(count, total, most, slope), jnp.int32)
    twos = (count - 1) // 2
    giver, receiver = sizes[1:1 + 2 * twos:2], sizes[2:2 + 2 * twos:2]
    room = jnp.minimum(giver - 1, most - receiver)
    passed = jax.random.randint(jax.random.fold_in(own_key, 1), (twos,), 0, 1 << 20) % (room + 1)
    sizes = sizes.at[1:1 + 2 * twos:2].set(giver - passed).at[2:2 + 2 * twos:2].set(receiver + passed)
    return sizes[jax.random.permutation(jax.random.fold_in(own_key, 2), count)]


def bell_draw(stream_key, shape, width, reach, cuts=(), kind=jnp.bfloat16):
    level = levels(stream_key, shape, cuts, -0.22, 0.18) if cuts else 1.0
    values = jax.random.normal(stream_key, shape, jnp.float32) * width * level
    return jnp.minimum(jnp.maximum(values, -reach), reach).astype(kind)


def setup_inputs(seed: int = 0) -> dict:
    key_list = jax.random.split(jax.random.key(seed), 13)
    return {
        "features": draw_features(jax.random.fold_in(key_list[12], 71), 0),
        "image_rows": jnp.searchsorted(jnp.cumsum(uneven(key_list[1], IMGS, NR, TALL, 0)), jnp.arange(NR), side="right").astype(jnp.int32),
        "seg_labels": set_ends(jax.random.randint(key_list[2], (NR, WIDTH), 0, SEG), jax.random.fold_in(key_list[2], 1), 0, SEG - 1).astype(jnp.int32),
        "edge_labels": set_ends(jax.random.randint(key_list[3], (NR, WIDTH), 0, 2), jax.random.fold_in(key_list[3], 1), 0, 1).astype(jnp.int32),
        "part_labels": set_ends(jax.random.randint(key_list[4], (NR, WIDTH), 0, PART), jax.random.fold_in(key_list[4], 1), 0, PART - 1).astype(jnp.int32),
        "task_weights": jax.random.randint(key_list[5], (3,), 1, 9).astype(jnp.int32),
        "block_params": draw_block_params(jax.random.fold_in(key_list[12], 71), 0),
        "block_moment": bell_draw(key_list[7], (BLOCK_PARAMS,), 0.005, 0.03, ((0, 128),), jnp.float32),
        "head_params": draw_head_params(jax.random.fold_in(key_list[12], 71), 0),
        "head_moment": bell_draw(key_list[9], (HEAD_PARAMS,), 0.005, 0.03, ((0, 128),), jnp.float32),
        "rate_params": bell_draw(key_list[10], (CIN, 27 * ASPP), (9 * CIN) ** -0.5, 0.046875, ((0, 4), (1, 32)), jnp.float32),
        "rate_moment": bell_draw(key_list[11], (CIN, 27 * ASPP), 0.005, 0.03, ((0, 4), (1, 32)), jnp.float32),
    }


EPSILON = 1e-05
MOMENTUM_KEEP = 0.5
rate_list = (6, 12, 18)
block_dilation = 4

@jax.custom_vjp
def low(v):
    return lax.optimization_barrier(v.astype(jnp.bfloat16)).astype(jnp.float32)

@jax.custom_vjp
def low_back(v):
    return v

def low_keep(v):
    return (low(v), None)

def low_pass(kept, grad):
    return (grad,)

def back_keep(v):
    return (v, None)

def back_low(kept, grad):
    return (low(grad),)
low.defvjp(low_keep, low_pass)
low_back.defvjp(back_keep, back_low)

def product(left, right):
    return jnp.dot(left, right, precision=lax.Precision.HIGHEST, preferred_element_type=jnp.float32)

def block_layout():
    return [(CIN, MID), (9, MID, MID), (MID, CIN), (2, 2, MID), (2, CIN)]

def head_layout():
    return [(CIN, ASPP), (CIN, ASPP), (ASPP,), (5 * ASPP, ASPP), (5, 2, ASPP), (ASPP, HEADS), (HEADS,)]

def unpack(vector, layout):
    pieces = []
    cursor = 0
    for extent in layout:
        number = math.prod(extent)
        pieces.append(vector[cursor:cursor + number].reshape(extent))
        cursor = cursor + number
    return pieces

def batch_norm(values, gain_row, shift_row):
    average = lax.optimization_barrier(jnp.mean(values, axis=0))
    variance = lax.optimization_barrier(jnp.mean(values * values, axis=0)) - average * average
    return (values - average) * lax.rsqrt(variance + EPSILON) * gain_row + shift_row

def row_keep(image_ids, offset):
    height = image_ids.shape[0]
    margin = abs(offset)
    padded = jnp.pad(image_ids, (margin, margin), constant_values=-1)
    shifted = padded[margin + offset:margin + offset + height]
    return (shifted == image_ids).astype(jnp.float32)

def dilated(field_in, kernel, image_ids, dilation):
    height, columns, channels = field_in.shape
    padded = jnp.pad(field_in, ((dilation, dilation), (dilation, dilation), (0, 0)))
    running = jnp.zeros((height, columns, kernel.shape[2]), jnp.float32)
    for row_tap in range(3):
        keep_rows = row_keep(image_ids, (row_tap - 1) * dilation)
        for col_tap in range(3):
            top_row = dilation + (row_tap - 1) * dilation
            left_col = dilation + (col_tap - 1) * dilation
            region = padded[top_row:top_row + height, left_col:left_col + columns].reshape(height * columns, channels)
            partial_out = product(region, kernel[3 * row_tap + col_tap]).reshape(height, columns, -1)
            running = running + partial_out * keep_rows[:, None, None]
    return running.reshape(height * columns, -1)

def spatial_conv(field_in, kernel, image_ids, dilation):
    return jax.checkpoint(partial(dilated, dilation=dilation))(field_in, kernel, image_ids)

def cross_entropy(scores, labels):
    classes = jnp.arange(scores.shape[1], dtype=jnp.int32)
    picked = lax.optimization_barrier(jnp.sum(jnp.where(labels[:, None] == classes[None, :], scores, 0.0), axis=1))
    return jnp.mean(jax.nn.logsumexp(scores, axis=1) - picked)

def forward(feature_in, block_vec, head_vec, rate_vec, image_ids, seg_labels, edge_labels, part_labels, task_weights):
    rows_all, columns, channels = feature_in.shape
    pixels = rows_all * columns
    w_reduce, w_spatial, w_expand, mid_norm, out_norm = unpack(low(block_vec), block_layout())
    w_point, w_pool, pool_bias, w_project, head_norm, w_heads, heads_bias = unpack(low(head_vec), head_layout())
    w_rates = low(rate_vec).reshape(CIN, 3, 9, ASPP).transpose(1, 2, 0, 3)
    inputs = feature_in.reshape(pixels, channels)
    first_pre = low_back(product(inputs, w_reduce))
    first_act = low(jax.nn.silu(batch_norm(first_pre, mid_norm[0, 0], mid_norm[0, 1])))
    second_pre = low_back(spatial_conv(first_act.reshape(rows_all, columns, MID), w_spatial, image_ids, block_dilation))
    second_act = low(jax.nn.silu(batch_norm(second_pre, mid_norm[1, 0], mid_norm[1, 1])))
    third_pre = low_back(product(second_act, w_expand))
    block_out = low(jax.nn.silu(batch_norm(third_pre, out_norm[0], out_norm[1]) + inputs))
    grid = block_out.reshape(rows_all, columns, channels)
    branch_list = [low_back(product(block_out, w_point))]
    for branch in range(3):
        branch_list.append(low_back(spatial_conv(grid, w_rates[branch], image_ids, rate_list[branch])))
    branch_acts = [jax.nn.silu(batch_norm(branch_list[branch], head_norm[branch, 0], head_norm[branch, 1])) for branch in range(4)]
    images = max(rows_all // 64, 2)
    member = (image_ids[None, :] == jnp.arange(images, dtype=jnp.int32)[:, None]).astype(jnp.float32)
    image_area = lax.optimization_barrier(jnp.sum(member, axis=1)) * columns
    pooled = product(member, lax.optimization_barrier(jnp.sum(grid, axis=1))) / image_area[:, None]
    pool_act = jax.nn.silu(product(low(pooled), w_pool) + pool_bias)
    pool_rows = product(member.T, pool_act)
    pool_map = jnp.broadcast_to(pool_rows[:, None, :], (rows_all, columns, ASPP)).reshape(pixels, ASPP)
    joined = low(jnp.concatenate(branch_acts + [pool_map], axis=1))
    projected = low_back(product(joined, w_project))
    feature_map = low(jax.nn.silu(batch_norm(projected, head_norm[4, 0], head_norm[4, 1])))
    logits = low_back(product(feature_map, w_heads) + heads_bias)
    weight_vals = task_weights.astype(jnp.float32)
    shares = weight_vals / jnp.sum(weight_vals)
    seg_loss = cross_entropy(logits[:, :SEG], seg_labels.reshape(pixels))
    edge_logit = logits[:, SEG]
    edge_target = edge_labels.reshape(pixels).astype(jnp.float32)
    edge_loss = jnp.mean(jax.nn.softplus(edge_logit) - edge_target * edge_logit)
    part_loss = cross_entropy(logits[:, SEG + 1:], part_labels.reshape(pixels))
    return (shares[0] * seg_loss + shares[1] * edge_loss + shares[2] * part_loss, pooled)

def reference(features, image_rows, seg_labels, edge_labels, part_labels, task_weights, block_params, block_moment, head_params, head_moment, rate_params, rate_moment):

    def objective(feature_in, block_vec, head_vec, rate_vec):
        return forward(feature_in, block_vec, head_vec, rate_vec, image_rows, seg_labels, edge_labels, part_labels, task_weights)
    loss_value, pullback, pooled = jax.vjp(objective, features.astype(jnp.float32), block_params, head_params, rate_params, has_aux=True)
    feature_grad, block_grad, head_grad, rate_grad = pullback(jnp.ones_like(loss_value))
    block_moment_next = MOMENTUM_KEEP * block_moment + block_grad
    head_moment_next = MOMENTUM_KEEP * head_moment + head_grad
    rate_moment_next = MOMENTUM_KEEP * rate_moment + rate_grad
    return (loss_value, pooled, feature_grad, block_moment_next, head_moment_next, rate_moment_next)
```

```python
import functools
import math

import jax
import jax.numpy as jnp
from jax import lax
from jax.experimental import pallas as pl
from jax.experimental.pallas import tpu as pltpu
from jax.sharding import PartitionSpec as P

MESH = pl.DeviceIdType.MESH
ANY = pl.BlockSpec(memory_space=pl.ANY)
VMEM = pl.BlockSpec(memory_space=pltpu.VMEM)
BLOCK_ROWS = 273
HEAD_ROWS = 85
PAYLOAD = 384

CIN = 2048
MID = 512
ASPP = 256
SEG = 13
PART = 3
HEADS = 17


EPSILON = 1e-05
MOMENTUM_KEEP = 0.5
rate_list = (6, 12, 18)
block_dilation = 4
widest_margin = 18


def device_of(row, col):
    return {"rows": row, "cols": col}


def split_place():
    row, col = lax.axis_index("rows"), lax.axis_index("cols")
    return {
        "y": (row // 16) + 2 * (col // 2),
        "x": lax.rem(row // 4, 4),
        "z": lax.rem(row, 4),
        "core": lax.rem(col, 2),
    }


def device_at(place):
    row = lax.rem(place["y"], 2) * 16 + place["x"] * 4 + place["z"]
    return device_of(row, (place["y"] // 2) * 2 + place["core"])


def moved(place, axis, step, extent=4):
    other = dict(place)
    other[axis] = lax.rem(place[axis] + step + extent, extent)
    return other


def meet(sources, targets):
    barrier = pltpu.get_barrier_semaphore()
    for device in sources:
        pl.semaphore_signal(barrier, inc=1, device_id=device, device_id_type=MESH)
    pl.semaphore_wait(barrier, targets)


def remote(source, target, send_sem, recv_sem, device):
    return pltpu.make_async_remote_copy(
        src_ref=source,
        dst_ref=target,
        send_sem=send_sem,
        recv_sem=recv_sem,
        device_id=device,
        device_id_type=MESH,
    )


def total_kernel(x_ref, o_ref, near, far, near_send, near_recv, far_send, far_recv):
    row, col = lax.axis_index("rows"), lax.axis_index("cols")
    near_me = (row // 16) * 4 + col
    far_me = lax.rem(row, 16)

    def near_device(index):
        return device_of((index // 4) * 16 + far_me, lax.rem(index, 4))

    def far_device(index):
        return device_of((row // 16) * 16 + index, col)

    near_others = [lax.rem(near_me + step, 8) for step in range(1, 8)]
    far_others = [lax.rem(far_me + step, 16) for step in range(1, 16)]
    meet(
        [near_device(i) for i in near_others] + [far_device(i) for i in far_others],
        len(near_others) + len(far_others),
    )

    def stage(source, buffer, me, others, device, send_sem, recv_sem):
        for step, index in enumerate(others):
            remote(source, buffer.at[me], send_sem.at[step], recv_sem.at[me], device(index)).start()
        buffer[me] = source[...]
        for step, index in enumerate(others):
            copy = remote(source, buffer.at[index], send_sem.at[step], recv_sem.at[index], device(index))
            copy.wait_send()
            copy.wait_recv()
        total = buffer[0]
        for index in range(1, buffer.shape[0]):
            total = total + buffer[index]
        o_ref[...] = total

    stage(x_ref, near, near_me, near_others, near_device, near_send, near_recv)
    stage(o_ref, far, far_me, far_others, far_device, far_send, far_recv)


def all_sum(packed, collective):
    shape = packed.shape
    return pl.pallas_call(
        total_kernel,
        out_shape=jax.ShapeDtypeStruct(shape, jnp.float32),
        in_specs=[VMEM],
        out_specs=VMEM,
        scratch_shapes=[
            pltpu.VMEM((8,) + shape, jnp.float32),
            pltpu.VMEM((16,) + shape, jnp.float32),
            pltpu.SemaphoreType.DMA((7,)),
            pltpu.SemaphoreType.DMA((8,)),
            pltpu.SemaphoreType.DMA((15,)),
            pltpu.SemaphoreType.DMA((16,)),
        ],
        compiler_params=pltpu.CompilerParams(
            collective_id=collective, has_side_effects=True, vmem_limit_bytes=32 * 1024 * 1024
        ),
    )(packed)


def sums_over_all(pieces, collective):
    flat = jnp.concatenate([piece.reshape(-1) for piece in pieces])
    rows = -(-flat.shape[0] // 1024) * 8
    packed = jnp.pad(flat, (0, rows * 128 - flat.shape[0])).reshape(rows, 128)
    flat = all_sum(packed, collective).reshape(-1)
    results = []
    cursor = 0
    for piece in pieces:
        results.append(flat[cursor : cursor + piece.size].reshape(piece.shape))
        cursor += piece.size
    return results


GATHER_ORDERS = (("z", "x", "y"), ("x", "y", "z"), ("y", "z", "x"))


def axis_view(place, fixed):
    index = [slice(None)] * 4
    if "y" in fixed:
        index[0], index[3] = lax.rem(place["y"], 2), place["y"] // 2
    if "x" in fixed:
        index[1] = place["x"]
    if "z" in fixed:
        index[2] = place["z"]
    return tuple(index)


def params_kernel(x_ref, o_ref, local_sem, sends, recvs, core_send, core_recv):
    me = split_place()
    partners = [moved(me, axis, step) for axis in "xyz" for step in (1, 2, 3)]
    twin = moved(me, "core", 1, 2)
    meet([device_at(place) for place in partners + [twin]], 10)

    def rows_of(third):
        return pl.ds(third * 128, 128)

    def block(place, third, free):
        fixed = [axis for axis in "xyz" if axis not in free]
        return o_ref.at[axis_view(place, fixed) + (place["core"], rows_of(third))]

    own = pltpu.make_async_copy(x_ref, o_ref.at[axis_view(me, "xyz") + (me["core"],)], local_sem)
    own.start()

    def copy(third, phase, step, place, source):
        order = GATHER_ORDERS[third]
        free = order[:phase]
        target = moved(me, order[phase], step)
        if phase == 0:
            outgoing = x_ref.at[rows_of(third)]
        else:
            outgoing = block(place, third, free)
        return remote(
            outgoing,
            block(source, third, free),
            sends.at[third, phase, step - 1],
            recvs.at[third, phase, step - 1],
            device_at(target),
        )

    for phase in range(3):
        for third in range(3):
            if phase > 0:
                axis = GATHER_ORDERS[third][phase - 1]
                for step in (1, 2, 3):
                    copy(third, phase - 1, step, me, moved(me, axis, 4 - step)).wait_recv()
                if phase == 1 and third == 0:
                    own.wait()
            for step in (1, 2, 3):
                copy(third, phase, step, me, me).start()
    core_copies = []
    for third in range(3):
        order = GATHER_ORDERS[third]
        for step in (0, 1, 2, 3):
            if step:
                copy(third, 2, step, me, moved(me, order[2], 4 - step)).wait_recv()
            view = block(moved(me, order[2], 4 - step), third, order[:2])
            core_copy = remote(
                view, view, core_send.at[third, step], core_recv.at[third, step], device_at(twin)
            )
            core_copy.start()
            core_copies.append(core_copy)
    for phase in range(3):
        for third in range(3):
            for step in (1, 2, 3):
                copy(third, phase, step, me, me).wait_send()
    for third in range(3):
        order = GATHER_ORDERS[third]
        for step in (0, 1, 2, 3):
            core_copies[third * 4 + step].wait_send()
            view = block(moved(moved(me, order[2], 4 - step), "core", 1, 2), third, order[:2])
            remote(
                view, view, core_send.at[third, step], core_recv.at[third, step], device_at(twin)
            ).wait_recv()


def gather_params(payload, collective):
    gathered = pl.pallas_call(
        params_kernel,
        out_shape=jax.ShapeDtypeStruct((2, 4, 4, 2, 2, PAYLOAD, 128), jnp.bfloat16),
        in_specs=[ANY],
        out_specs=ANY,
        scratch_shapes=[
            pltpu.SemaphoreType.DMA,
            pltpu.SemaphoreType.DMA((3, 3, 3)),
            pltpu.SemaphoreType.DMA((3, 3, 3)),
            pltpu.SemaphoreType.DMA((3, 4)),
            pltpu.SemaphoreType.DMA((3, 4)),
        ],
        compiler_params=pltpu.CompilerParams(collective_id=collective, has_side_effects=True),
    )(payload)
    return gathered.reshape(128, PAYLOAD, 128)


def scatter_kernel(
    p_ref, o_ref, held, twin_part, parts, sums, local_sem, core_sems, sends, recvs
):
    me = split_place()
    partners = [moved(me, axis, step) for axis in "xyz" for step in (1, 2, 3)]
    twin = moved(me, "core", 1, 2)
    meet([device_at(place) for place in partners + [twin]], 10)
    core_copy = remote(
        p_ref.at[:, :, :, :, 1 - me["core"]], twin_part, core_sems.at[0], core_sems.at[1], device_at(twin)
    )
    core_copy.start()
    own = pltpu.make_async_copy(p_ref.at[:, :, :, :, me["core"]], held, local_sem)
    own.start()
    own.wait()
    core_copy.wait()

    def add_block(step, carry):
        low_y, x, z, high_y = step // 32, lax.rem(step // 8, 4), lax.rem(step // 2, 4), lax.rem(step, 2)
        total = held[low_y, x, z, high_y].astype(jnp.float32) + twin_part[
            low_y, x, z, high_y
        ].astype(jnp.float32)
        held[low_y, x, z, high_y] = total.astype(jnp.bfloat16)
        return carry

    lax.fori_loop(0, 64, add_block, 0)

    def view_of(third, phase, place):
        order = GATHER_ORDERS[third]
        axis = order[2 - phase]
        if phase == 0:
            return held.at[axis_view(place, [axis]) + (pl.ds(third * 128, 128),)]
        left = order[: 3 - phase]
        index = []
        for name, key in (("y", 0), ("x", 1), ("z", 2), ("y", 3)):
            if name not in left:
                continue
            if name != axis:
                index.append(slice(None))
            elif name == "y":
                index.append(lax.rem(place["y"], 2) if key == 0 else place["y"] // 2)
            else:
                index.append(place[name])
        return sums[third][phase - 1].at[tuple(index)]

    def copy(third, phase, step):
        axis = GATHER_ORDERS[third][2 - phase]
        target = moved(me, axis, step)
        return remote(
            view_of(third, phase, target),
            parts[third][phase].at[step - 1],
            sends.at[third, phase, step - 1],
            recvs.at[third, phase, step - 1],
            device_at(target),
        )

    for phase in range(4):
        for third in range(3):
            if phase > 0:
                total = view_of(third, phase - 1, me)[...].astype(jnp.float32)
                for step in (1, 2, 3):
                    copy(third, phase - 1, step).wait_recv()
                    total = total + parts[third][phase - 1][step - 1].astype(jnp.float32)
                if phase == 3:
                    o_ref[pl.ds(third * 128, 128), :] = total
                else:
                    sums[third][phase - 1][...] = total.astype(jnp.bfloat16)
            if phase < 3:
                for step in (1, 2, 3):
                    copy(third, phase, step).start()
    for phase in range(3):
        for third in range(3):
            for step in (1, 2, 3):
                copy(third, phase, step).wait_send()


def scatter_entry(p_ref, o_ref, held, twin_part, *rest):
    parts = [rest[3 * third : 3 * third + 3] for third in range(3)]
    sums = [rest[9 + 2 * third : 11 + 2 * third] for third in range(3)]
    scatter_kernel(p_ref, o_ref, held, twin_part, parts, sums, *rest[15:])


def scatter_params(packed, collective):
    lengths = {"y": (2, 2), "x": (4,), "z": (4,)}

    def shape_left(left):
        shape = ()
        for name, number in (("y", 2), ("x", 4), ("z", 4), ("y", 2)):
            if name in left:
                shape += (number,)
        return shape + (128, 128)

    parts = []
    sums = []
    for order in GATHER_ORDERS:
        for phase in range(3):
            parts.append(pltpu.VMEM((3,) + shape_left(order[: 2 - phase]), jnp.bfloat16))
        for phase in range(2):
            sums.append(pltpu.VMEM(shape_left(order[: 2 - phase]), jnp.bfloat16))
    half = (2, 4, 4, 2, PAYLOAD, 128)
    return pl.pallas_call(
        scatter_entry,
        out_shape=jax.ShapeDtypeStruct((PAYLOAD, 128), jnp.float32),
        in_specs=[ANY],
        out_specs=VMEM,
        scratch_shapes=[pltpu.VMEM(half, jnp.bfloat16), pltpu.VMEM(half, jnp.bfloat16)]
        + parts
        + sums
        + [
            pltpu.SemaphoreType.DMA,
            pltpu.SemaphoreType.DMA((2,)),
            pltpu.SemaphoreType.DMA((3, 3, 3)),
            pltpu.SemaphoreType.DMA((3, 3, 3)),
        ],
        compiler_params=pltpu.CompilerParams(
            collective_id=collective, has_side_effects=True, vmem_limit_bytes=56 * 1024 * 1024
        ),
    )(packed.reshape(2, 4, 4, 2, 2, PAYLOAD, 128))


def neighbour(row, col, offset):
    return lax.rem(row + offset[0] + 32, 32), lax.rem(col + offset[1] + 4, 4)


def exchange_kernel(count, transfers, *refs):
    ins, outs = refs[:count], refs[count:-3]
    sends, recvs, locals_ = refs[-3:]
    row, col = lax.axis_index("rows"), lax.axis_index("cols")
    offsets = sorted({item[4] for item in transfers if item[4] != (0, 0)})
    meet(
        [device_of(*neighbour(row, col, (-o[0], -o[1]))) for o in offsets],
        len(offsets),
    )

    def copy(number, receiving):
        source_index, source, out_index, target, offset = transfers[number]
        there = neighbour(row, col, offset)
        origin = neighbour(row, col, (-offset[0], -offset[1])) if receiving else (row, col)
        outgoing = ins[source_index].at[source(row, col)]
        incoming = outs[out_index].at[target(*origin)]
        if offset == (0, 0):
            return pltpu.make_async_copy(outgoing, incoming, locals_.at[number])
        return remote(outgoing, incoming, sends.at[number], recvs.at[number], device_of(*there))

    for number, item in enumerate(transfers):
        copy(number, False).start()
    for number, item in enumerate(transfers):
        if item[4] == (0, 0):
            copy(number, False).wait()
        else:
            copy(number, True).wait_send()
            copy(number, True).wait_recv()


def exchange(arrays, shapes, transfers, collective):
    number = len(transfers)
    return pl.pallas_call(
        functools.partial(exchange_kernel, len(arrays), transfers),
        out_shape=[jax.ShapeDtypeStruct(shape, jnp.bfloat16) for shape in shapes],
        in_specs=[VMEM] * len(arrays),
        out_specs=[VMEM] * len(shapes),
        scratch_shapes=[pltpu.SemaphoreType.DMA((number,)) for _ in range(3)],
        compiler_params=pltpu.CompilerParams(
            collective_id=collective, has_side_effects=True, vmem_limit_bytes=48 * 1024 * 1024
        ),
    )(*arrays)


def every(row, col):
    return (slice(None),)


def halo_window(act, collective):
    height, across, _ = act.shape
    half = height // 2
    transfers = []
    for row_step in (-1, 0, 1):
        for col_step in (-1, 0, 1):
            rows = {-1: slice(0, half), 0: slice(0, height), 1: slice(half, height)}[row_step]
            top = {-1: half + height, 0: half, 1: 0}[row_step]
            left = {-1: 2 * across, 0: across, 1: 0}[col_step]
            size = rows.stop - rows.start
            transfers.append(
                (
                    0,
                    lambda row, col, rows=rows: (pl.ds(rows.start, rows.stop - rows.start),),
                    0,
                    lambda row, col, top=top, size=size, left=left: (
                        pl.ds(top, size),
                        pl.ds(left, across),
                    ),
                    (row_step, col_step),
                )
            )
    (window,) = exchange([act], [(2 * height, 3 * across, act.shape[2])], transfers, collective)
    inside = jnp.arange(3 * across) + (lax.axis_index("cols") - 1) * across
    keep = ((inside >= 0) & (inside < 4 * across)).astype(window.dtype)
    return window * keep[None, :, None]


def columns_to_channels(own, collective):
    height, across, channels = own.shape
    part = channels // 4
    transfers = [
        (
            0,
            lambda row, col, step=step: (
                slice(None),
                slice(None),
                pl.ds(pl.multiple_of(lax.rem(col + step, 4) * part, part), part),
            ),
            0,
            lambda row, col: (
                slice(None),
                pl.ds(pl.multiple_of(col * across, across), across),
            ),
            (0, step),
        )
        for step in range(4)
    ]
    return exchange([own], [(height, 4 * across, part)], transfers, collective)[0]


def channels_to_columns(slab, collective):
    height, width, channels = slab.shape
    across = width // 4
    transfers = [
        (
            0,
            lambda row, col, step=step: (
                slice(None),
                pl.ds(pl.multiple_of(lax.rem(col + step, 4) * across, across), across),
            ),
            0,
            lambda row, col: (col,),
            (0, step),
        )
        for step in range(4)
    ]
    return exchange([slab], [(4, height, across, channels)], transfers, collective)[0]


def channels_to_columns_back(slab, collective):
    height, width, part = slab.shape
    across = width // 4
    transfers = [
        (
            0,
            lambda row, col, step=step: (
                slice(None),
                pl.ds(pl.multiple_of(lax.rem(col + step, 4) * across, across), across),
            ),
            0,
            lambda row, col: (
                slice(None),
                slice(None),
                pl.ds(pl.multiple_of(col * part, part), part),
            ),
            (0, step),
        )
        for step in range(4)
    ]
    return exchange([slab], [(height, across, 4 * part)], transfers, collective)[0]


def columns_together(own, collective):
    height, across, channels = own.shape
    transfers = [
        (
            0,
            every,
            0,
            lambda row, col: (
                slice(None),
                pl.ds(pl.multiple_of(col * across, across), across),
            ),
            (0, step),
        )
        for step in range(4)
    ]
    return exchange([own], [(height, 4 * across, channels)], transfers, collective)[0]


def shifted_rows(arrays, pick, collective):
    height, across, channels = arrays[0].shape
    transfers = []
    for branch, rate in enumerate(rate_list):
        for direction in range(2):
            for hop in range(4):
                if direction == 0:
                    first, last = max(0, height * hop - rate), min(height, height * hop - rate + height)
                    top = first + rate - height * hop
                else:
                    first, last = max(0, rate - height * hop), min(height, rate - height * hop + height)
                    top = first - rate + height * hop
                if first >= last:
                    continue
                transfers.append(
                    (
                        pick(branch, direction),
                        lambda row, col, first=first, last=last: (pl.ds(first, last - first),),
                        2 * branch + direction,
                        lambda row, col, top=top, size=last - first: (pl.ds(top, size),),
                        (hop if direction == 0 else -hop, 0),
                    )
                )
    return exchange(arrays, [(height, across, channels)] * 6, transfers, collective)


def silu_slope(values):
    sigmoid_part = jax.nn.sigmoid(values)
    return sigmoid_part * (1.0 + values * (1.0 - sigmoid_part))


def block_layout():
    return [(CIN, MID), (9, MID, MID), (MID, CIN), (2, 2, MID), (2, CIN)]


def head_layout():
    return [
        (CIN, ASPP),
        (CIN, ASPP),
        (ASPP,),
        (5 * ASPP, ASPP),
        (5, 2, ASPP),
        (ASPP, HEADS),
        (HEADS,),
    ]


def unpack(vector, layout):
    pieces = []
    cursor = 0
    for extent in layout:
        number = math.prod(extent)
        pieces.append(vector[cursor : cursor + number].reshape(extent))
        cursor = cursor + number
    return pieces


def pack_flat(pieces, length):
    joined = jnp.concatenate([item.reshape(-1) for item in pieces])
    return jnp.pad(joined, (0, length - joined.shape[0]))


def row_masks(all_ids, first_row, height, margin, dilation):
    padded = jnp.pad(all_ids, (margin, margin), constant_values=-1)
    window = lax.dynamic_slice_in_dim(padded, first_row, height + 2 * margin)
    own_ids = window[margin : margin + height]
    mask_list = []
    for row_tap in range(3):
        offset = margin + (row_tap - 1) * dilation
        mask_list.append((window[offset : offset + height] == own_ids).astype(jnp.bfloat16))
    return mask_list


def conv_forward(window, kernel, mask_list, margin, dilation, height, across):
    running = None
    for row_tap in range(3):
        for col_tap in range(3):
            top_row = margin + (row_tap - 1) * dilation
            left_col = across + (col_tap - 1) * dilation
            masked = (
                window[top_row : top_row + height, left_col : left_col + across]
                * mask_list[row_tap][:, None, None]
            )
            partial_out = jnp.dot(
                masked.reshape(height * across, -1),
                kernel[3 * row_tap + col_tap],
                preferred_element_type=jnp.float32,
            )
            running = partial_out if running is None else running + partial_out
    return running


def conv_weight_grad(window, grad_out, mask_list, margin, dilation, height, across):
    tap_grads = []
    for row_tap in range(3):
        for col_tap in range(3):
            top_row = margin + (row_tap - 1) * dilation
            left_col = across + (col_tap - 1) * dilation
            masked = (
                window[top_row : top_row + height, left_col : left_col + across]
                * mask_list[row_tap][:, None, None]
            )
            tap_grads.append(
                jnp.einsum(
                    "pc,po->co",
                    masked.reshape(height * across, -1),
                    grad_out,
                    preferred_element_type=jnp.float32,
                )
            )
    return jnp.stack(tap_grads)


def conv_input_grad(grad_window, kernel, mask_list, margin, dilation, height, across):
    running = None
    for row_tap in range(3):
        for col_tap in range(3):
            top_row = margin - (row_tap - 1) * dilation
            left_col = across - (col_tap - 1) * dilation
            region = (
                grad_window[top_row : top_row + height, left_col : left_col + across]
                * mask_list[2 - row_tap][:, None, None]
            )
            partial_out = jnp.einsum(
                "po,co->pc",
                region.reshape(height * across, -1),
                kernel[3 * row_tap + col_tap],
                preferred_element_type=jnp.float32,
            )
            running = partial_out if running is None else running + partial_out
    return running


def moments(values):
    return (jnp.sum(values, axis=0), jnp.sum(values * values, axis=0))


def normalize(values, totals, number, gain_row, shift_row):
    average = totals[0] / number
    variance = totals[1] / number - average * average
    scale_row = lax.rsqrt(variance + EPSILON)
    centered = (values - average) * scale_row
    return (centered, centered * gain_row + shift_row, scale_row)


def norm_back(grad_norm, centered, scale_row, gain_row, totals, number):
    return gain_row * scale_row * (grad_norm - totals[0] / number - centered * totals[1] / number)


def per_device(
    features,
    image_rows,
    seg_labels,
    edge_labels,
    part_labels,
    task_weights,
    block_params,
    block_moment,
    head_params,
    head_moment,
    rate_params,
    rate_moment,
):
    height, across, channels = features.shape
    pixels = height * across
    columns = across * lax.axis_size("cols")
    rows_all = height * lax.axis_size("rows")
    total_pixels = rows_all * columns
    images = max(rows_all // 64, 2)
    highest = lax.Precision.HIGHEST
    payload = jnp.concatenate(
        [
            block_params.astype(jnp.bfloat16).reshape(BLOCK_ROWS, 128),
            head_params.astype(jnp.bfloat16).reshape(HEAD_ROWS, 128),
            jnp.pad(
                image_rows.astype(jnp.bfloat16).reshape(1, height),
                ((0, PAYLOAD - BLOCK_ROWS - HEAD_ROWS - 1), (0, 128 - height)),
            ),
        ],
        axis=0,
    )
    rate_slab = lax.all_gather(rate_params.astype(jnp.bfloat16), "rows", axis=1, tiled=True)
    everything = gather_params(payload, 1)
    block_all = everything[:, :BLOCK_ROWS].reshape(-1)
    head_all = everything[:, BLOCK_ROWS : BLOCK_ROWS + HEAD_ROWS].reshape(-1)
    all_ids = everything.reshape(32, 4, PAYLOAD, 128)[:, 0, BLOCK_ROWS + HEAD_ROWS, :height]
    all_ids = all_ids.reshape(-1).astype(jnp.int32)
    slab = rate_slab.shape[0]
    w_rates = rate_slab.reshape(slab, 3, 9, ASPP)
    first_row = lax.axis_index("rows") * height
    w_reduce, w_spatial, w_expand, mid_norm, out_norm = unpack(block_all, block_layout())
    w_point, w_pool, pool_bias, w_project, head_norm, w_heads, heads_bias = unpack(
        head_all, head_layout()
    )
    mid_norm = mid_norm.astype(jnp.float32)
    out_norm = out_norm.astype(jnp.float32)
    head_norm = head_norm.astype(jnp.float32)
    pool_bias = pool_bias.astype(jnp.float32)
    heads_bias = heads_bias.astype(jnp.float32)
    inputs = features.reshape(pixels, channels)
    block_masks = row_masks(all_ids, first_row, height, block_dilation, block_dilation)
    rate_masks = [
        row_masks(all_ids, first_row, height, widest_margin, dilation) for dilation in rate_list
    ]
    image_range = jnp.arange(images, dtype=jnp.int32)
    member = (image_rows[None, :] == image_range[:, None]).astype(jnp.float32)
    image_area = (
        jnp.sum((all_ids[None, :] == image_range[:, None]).astype(jnp.float32), axis=1) * columns
    )
    first_pre = jnp.dot(inputs, w_reduce, preferred_element_type=jnp.float32)
    first_cent, first_norm, first_scale = normalize(
        first_pre, sums_over_all(moments(first_pre), 2), total_pixels, mid_norm[0, 0], mid_norm[0, 1]
    )
    first_act = jax.nn.silu(first_norm).astype(jnp.bfloat16)
    block_window = halo_window(first_act.reshape(height, across, MID), 3)
    second_pre = conv_forward(
        block_window, w_spatial, block_masks, block_dilation, block_dilation, height, across
    )
    second_cent, second_norm, second_scale = normalize(
        second_pre, sums_over_all(moments(second_pre), 4), total_pixels, mid_norm[1, 0], mid_norm[1, 1]
    )
    second_act = jax.nn.silu(second_norm).astype(jnp.bfloat16)
    third_pre = jnp.dot(second_act, w_expand, preferred_element_type=jnp.float32)
    third_cent, third_norm, third_scale = normalize(
        third_pre, sums_over_all(moments(third_pre), 5), total_pixels, out_norm[0], out_norm[1]
    )
    residual = third_norm + inputs.astype(jnp.float32)
    block_out = jax.nn.silu(residual).astype(jnp.bfloat16)
    grid = block_out.reshape(height, across, channels)
    width = 4 * across
    slab_map = columns_to_channels(grid, 6)
    slab_padded = jnp.pad(slab_map, ((0, 0), (widest_margin, widest_margin), (0, 0)))
    tap_sums = []
    for branch, rate in enumerate(rate_list):
        running = None
        for col_tap in range(3):
            start = widest_margin + (col_tap - 1) * rate
            moved_map = slab_padded[:, start : start + width].reshape(height * width, slab)
            part = jnp.dot(
                moved_map,
                w_rates[:, branch, col_tap::3].reshape(slab, 3 * ASPP),
                preferred_element_type=jnp.float32,
            )
            running = part if running is None else running + part
        tap_sums.append(running.astype(jnp.bfloat16))
    tap_map = jnp.concatenate(tap_sums, axis=1).reshape(height, width, 9 * ASPP)
    tap_parts = channels_to_columns(tap_map, 7)
    tap_own = jnp.sum(tap_parts.astype(jnp.float32), axis=0).reshape(height, across, 3, 3, ASPP)
    moved_taps = shifted_rows(
        [tap_own[:, :, branch, tap].astype(jnp.bfloat16) for branch in range(3) for tap in (0, 2)],
        lambda branch, direction: 2 * branch + direction,
        8,
    )
    rate_parts = []
    for branch in range(3):
        masks = [mask.astype(jnp.float32)[:, None, None] for mask in rate_masks[branch]]
        total = (
            tap_own[:, :, branch, 1]
            + moved_taps[2 * branch].astype(jnp.float32) * masks[0]
            + moved_taps[2 * branch + 1].astype(jnp.float32) * masks[2]
        )
        rate_parts.append(total.reshape(pixels, ASPP))
    branch_list = [jnp.dot(block_out, w_point, preferred_element_type=jnp.float32)] + rate_parts
    branch_pre = jnp.stack(branch_list)
    pool_local = jnp.dot(member, jnp.sum(grid, axis=1, dtype=jnp.float32), precision=highest)
    branch_sums, branch_squares, pool_total = sums_over_all(
        (jnp.sum(branch_pre, axis=1), jnp.sum(branch_pre * branch_pre, axis=1), pool_local), 9
    )
    branch_gain = head_norm[:4, 0][:, None, :]
    branch_cent, branch_norm, branch_scale = normalize(
        branch_pre,
        (branch_sums[:, None, :], branch_squares[:, None, :]),
        total_pixels,
        branch_gain,
        head_norm[:4, 1][:, None, :],
    )
    branch_act = jax.nn.silu(branch_norm)
    pooled = pool_total / image_area[:, None]
    pooled_low = pooled.astype(jnp.bfloat16)
    pool_pre = jnp.dot(pooled_low, w_pool, preferred_element_type=jnp.float32) + pool_bias
    pool_act = jax.nn.silu(pool_pre)
    pool_rows = jnp.dot(member.T, pool_act, precision=highest)
    pool_map = jnp.broadcast_to(pool_rows[:, None, :], (height, across, ASPP)).reshape(pixels, ASPP)
    joined = jnp.concatenate(
        [branch_act[0], branch_act[1], branch_act[2], branch_act[3], pool_map], axis=1
    ).astype(jnp.bfloat16)
    projected = jnp.dot(joined, w_project, preferred_element_type=jnp.float32)
    proj_cent, proj_norm, proj_scale = normalize(
        projected, sums_over_all(moments(projected), 10), total_pixels, head_norm[4, 0], head_norm[4, 1]
    )
    feature_map = jax.nn.silu(proj_norm).astype(jnp.bfloat16)
    logits = jnp.dot(feature_map, w_heads, preferred_element_type=jnp.float32) + heads_bias
    weight_vals = task_weights.astype(jnp.float32)
    shares = weight_vals / jnp.sum(weight_vals)
    seg_scores = logits[:, :SEG]
    seg_hot = (
        seg_labels.reshape(pixels)[:, None] == jnp.arange(SEG, dtype=jnp.int32)[None, :]
    ).astype(jnp.float32)
    seg_lse = jax.nn.logsumexp(seg_scores, axis=1)
    seg_terms = seg_lse - jnp.sum(seg_scores * seg_hot, axis=1)
    seg_grad = jnp.exp(seg_scores - seg_lse[:, None]) - seg_hot
    edge_logit = logits[:, SEG]
    edge_target = edge_labels.reshape(pixels).astype(jnp.float32)
    edge_terms = jax.nn.softplus(edge_logit) - edge_target * edge_logit
    edge_grad = jax.nn.sigmoid(edge_logit) - edge_target
    part_scores = logits[:, SEG + 1 :]
    part_hot = (
        part_labels.reshape(pixels)[:, None] == jnp.arange(PART, dtype=jnp.int32)[None, :]
    ).astype(jnp.float32)
    part_lse = jax.nn.logsumexp(part_scores, axis=1)
    part_terms = part_lse - jnp.sum(part_scores * part_hot, axis=1)
    part_grad = jnp.exp(part_scores - part_lse[:, None]) - part_hot
    loss_local = (
        shares[0] * jnp.sum(seg_terms)
        + shares[1] * jnp.sum(edge_terms)
        + shares[2] * jnp.sum(part_terms)
    ) / total_pixels
    logit_grad = (
        jnp.concatenate(
            [seg_grad * shares[0], edge_grad[:, None] * shares[1], part_grad * shares[2]], axis=1
        )
        / total_pixels
    ).astype(jnp.bfloat16)
    grad_heads = jnp.einsum(
        "pc,pk->ck", feature_map, logit_grad, preferred_element_type=jnp.float32
    )
    grad_heads_bias = jnp.sum(logit_grad, axis=0, dtype=jnp.float32)
    feature_grad_map = jnp.einsum(
        "pk,ck->pc", logit_grad, w_heads, preferred_element_type=jnp.float32
    )
    proj_grad_norm = feature_grad_map * silu_slope(proj_norm)
    proj_shift_grad = jnp.sum(proj_grad_norm, axis=0)
    proj_gain_grad = jnp.sum(proj_grad_norm * proj_cent, axis=0)
    loss_total, proj_shift_all, proj_gain_all = sums_over_all(
        (loss_local, proj_shift_grad, proj_gain_grad), 11
    )
    projected_grad = norm_back(
        proj_grad_norm,
        proj_cent,
        proj_scale,
        head_norm[4, 0],
        (proj_shift_all, proj_gain_all),
        total_pixels,
    ).astype(jnp.bfloat16)
    grad_project = jnp.einsum(
        "pc,po->co", joined, projected_grad, preferred_element_type=jnp.float32
    )
    joined_grad = jnp.einsum(
        "po,co->pc", projected_grad, w_project, preferred_element_type=jnp.float32
    )
    branch_in_grad = joined_grad[:, : 4 * ASPP].reshape(pixels, 4, ASPP).transpose(1, 0, 2)
    pool_map_grad = joined_grad[:, 4 * ASPP :]
    pool_act_local = jnp.dot(
        member, jnp.sum(pool_map_grad.reshape(height, across, ASPP), axis=1), precision=highest
    )
    branch_grad_norm = branch_in_grad * silu_slope(branch_norm)
    branch_shift_grad = jnp.sum(branch_grad_norm, axis=1)
    branch_gain_grad = jnp.sum(branch_grad_norm * branch_cent, axis=1)
    branch_shift_all, branch_gain_all, pool_act_grad = sums_over_all(
        (branch_shift_grad, branch_gain_grad, pool_act_local), 12
    )
    branch_grad = norm_back(
        branch_grad_norm,
        branch_cent,
        branch_scale,
        branch_gain,
        (branch_shift_all[:, None, :], branch_gain_all[:, None, :]),
        total_pixels,
    ).astype(jnp.bfloat16)
    pool_slope = silu_slope(pool_pre)
    pool_pre_local = pool_act_local * pool_slope
    grad_pool = jnp.dot(pooled_low.astype(jnp.float32).T, pool_pre_local, precision=highest)
    grad_pool_bias = jnp.sum(pool_pre_local, axis=0)
    pooled_grad = (
        jnp.dot(pool_act_grad * pool_slope, w_pool.astype(jnp.float32).T, precision=highest)
        / image_area[:, None]
    )
    pool_back_rows = jnp.dot(member.T, pooled_grad, precision=highest)
    grad_point = jnp.einsum(
        "pc,po->co", block_out, branch_grad[0], preferred_element_type=jnp.float32
    )
    out_grad = jnp.einsum("po,co->pc", branch_grad[0], w_point, preferred_element_type=jnp.float32)
    rate_grad_maps = [branch_grad[branch + 1].reshape(height, across, ASPP) for branch in range(3)]
    moved_grads = shifted_rows(rate_grad_maps, lambda branch, direction: branch, 13)
    stacked = []
    for branch in range(3):
        masks = [mask[:, None, None] for mask in rate_masks[branch]]
        stacked.append(moved_grads[2 * branch + 1] * masks[2])
        stacked.append(rate_grad_maps[branch])
        stacked.append(moved_grads[2 * branch] * masks[0])
    wide_grads = columns_together(jnp.concatenate(stacked, axis=2), 14)
    wide_padded = jnp.pad(wide_grads, ((0, 0), (widest_margin, widest_margin), (0, 0)))
    tap_list = []
    for branch, rate in enumerate(rate_list):
        for row_tap in range(3):
            first_channel = (3 * branch + row_tap) * ASPP
            for col_tap in range(3):
                start = widest_margin - (col_tap - 1) * rate
                tap_list.append(
                    wide_padded[:, start : start + width, first_channel : first_channel + ASPP]
                )
    tap_grads = jnp.concatenate(tap_list, axis=2).reshape(height * width, 27 * ASPP)
    rate_flat = jnp.einsum(
        "pc,pn->cn",
        slab_map.reshape(height * width, slab),
        tap_grads,
        preferred_element_type=jnp.float32,
    ).astype(jnp.bfloat16)
    rate_share = lax.psum_scatter(rate_flat, "rows", scatter_dimension=1, tiled=True).astype(
        jnp.float32
    )
    slab_grad = jnp.einsum(
        "pn,cn->pc", tap_grads, rate_slab, preferred_element_type=jnp.float32
    ).astype(jnp.bfloat16)
    own_parts = channels_to_columns_back(slab_grad.reshape(height, width, slab), 15)
    out_grad = out_grad + own_parts.reshape(pixels, channels).astype(jnp.float32)
    out_grad = out_grad + jnp.broadcast_to(
        pool_back_rows[:, None, :], (height, across, channels)
    ).reshape(pixels, channels)
    norm_grads = jnp.concatenate(
        [
            jnp.stack([branch_gain_grad, branch_shift_grad], axis=1),
            jnp.stack([proj_gain_grad, proj_shift_grad])[None],
        ],
        axis=0,
    )
    head_grad = pack_flat(
        [
            grad_point,
            grad_pool,
            grad_pool_bias,
            grad_project,
            norm_grads,
            grad_heads,
            grad_heads_bias,
        ],
        head_all.shape[0],
    )
    residual_grad = out_grad * silu_slope(residual)
    third_shift_grad = jnp.sum(residual_grad, axis=0)
    third_gain_grad = jnp.sum(residual_grad * third_cent, axis=0)
    third_grad = norm_back(
        residual_grad,
        third_cent,
        third_scale,
        out_norm[0],
        sums_over_all((third_shift_grad, third_gain_grad), 16),
        total_pixels,
    ).astype(jnp.bfloat16)
    grad_expand = jnp.einsum(
        "pc,po->co", second_act, third_grad, preferred_element_type=jnp.float32
    )
    second_act_grad = jnp.einsum(
        "po,co->pc", third_grad, w_expand, preferred_element_type=jnp.float32
    )
    second_grad_norm = second_act_grad * silu_slope(second_norm)
    second_shift_grad = jnp.sum(second_grad_norm, axis=0)
    second_gain_grad = jnp.sum(second_grad_norm * second_cent, axis=0)
    second_grad = norm_back(
        second_grad_norm,
        second_cent,
        second_scale,
        mid_norm[1, 0],
        sums_over_all((second_shift_grad, second_gain_grad), 17),
        total_pixels,
    ).astype(jnp.bfloat16)
    grad_spatial = conv_weight_grad(
        block_window, second_grad, block_masks, block_dilation, block_dilation, height, across
    )
    block_grad_window = halo_window(second_grad.reshape(height, across, MID), 18)
    first_act_grad = conv_input_grad(
        block_grad_window, w_spatial, block_masks, block_dilation, block_dilation, height, across
    )
    first_grad_norm = first_act_grad * silu_slope(first_norm)
    first_shift_grad = jnp.sum(first_grad_norm, axis=0)
    first_gain_grad = jnp.sum(first_grad_norm * first_cent, axis=0)
    first_grad = norm_back(
        first_grad_norm,
        first_cent,
        first_scale,
        mid_norm[0, 0],
        sums_over_all((first_shift_grad, first_gain_grad), 19),
        total_pixels,
    ).astype(jnp.bfloat16)
    grad_reduce = jnp.einsum("pc,po->co", inputs, first_grad, preferred_element_type=jnp.float32)
    input_grad = residual_grad + jnp.einsum(
        "po,co->pc", first_grad, w_reduce, preferred_element_type=jnp.float32
    )
    mid_grads = jnp.stack(
        [
            jnp.stack([first_gain_grad, first_shift_grad]),
            jnp.stack([second_gain_grad, second_shift_grad]),
        ]
    )
    out_grads = jnp.stack([third_gain_grad, third_shift_grad])
    block_grad = pack_flat(
        [grad_reduce, grad_spatial, grad_expand, mid_grads, out_grads], block_all.shape[0]
    )
    packed = jnp.concatenate(
        [
            block_grad.astype(jnp.bfloat16).reshape(128, BLOCK_ROWS, 128),
            head_grad.astype(jnp.bfloat16).reshape(128, HEAD_ROWS, 128),
            jnp.zeros((128, PAYLOAD - BLOCK_ROWS - HEAD_ROWS, 128), jnp.bfloat16),
        ],
        axis=1,
    )
    shares_all = scatter_params(packed, 20)
    block_share = shares_all[:BLOCK_ROWS].reshape(-1)
    head_share = shares_all[BLOCK_ROWS : BLOCK_ROWS + HEAD_ROWS].reshape(-1)
    block_moment_next = MOMENTUM_KEEP * block_moment + block_share
    head_moment_next = MOMENTUM_KEEP * head_moment + head_share
    rate_moment_next = MOMENTUM_KEEP * rate_moment + rate_share
    return (
        loss_total,
        pooled,
        input_grad.reshape(height, across, channels),
        block_moment_next,
        head_moment_next,
        rate_moment_next,
    )


def solution(mesh):
    return jax.shard_map(
        per_device,
        mesh=mesh,
        in_specs=(
            P("rows", "cols", None),
            P("rows"),
            P("rows", "cols"),
            P("rows", "cols"),
            P("rows", "cols"),
            P(),
            P(("rows", "cols")),
            P(("rows", "cols")),
            P(("rows", "cols")),
            P(("rows", "cols")),
            P("cols", "rows"),
            P("cols", "rows"),
        ),
        out_specs=(
            P(),
            P(),
            P("rows", "cols", None),
            P(("rows", "cols")),
            P(("rows", "cols")),
            P("cols", "rows"),
        ),
        check_vma=False,
    )
```

```python
import functools
import math

import jax
import jax.numpy as jnp
from jax import lax
from jax.experimental import pallas as pl
from jax.experimental.pallas import tpu as pltpu
from jax.sharding import PartitionSpec as P

MESH = pl.DeviceIdType.MESH
ANY = pl.BlockSpec(memory_space=pl.ANY)
VMEM = pl.BlockSpec(memory_space=pltpu.VMEM)
SMEM = pl.BlockSpec(memory_space=pltpu.SMEM)
BLOCK_ROWS = 273
HEAD_ROWS = 85
PAYLOAD = 384

CIN = 2048
MID = 512
ASPP = 256
SEG = 13
PART = 3
HEADS = 17


EPSILON = 1e-05
MOMENTUM_KEEP = 0.5
rate_list = (6, 12, 18)
block_dilation = 4
widest_margin = 18


def device_of(row, col):
    return {"rows": row, "cols": col}


def split_place():
    row, col = lax.axis_index("rows"), lax.axis_index("cols")
    return {
        "y": (row // 16) + 2 * (col // 2),
        "x": lax.rem(row // 4, 4),
        "z": lax.rem(row, 4),
        "core": lax.rem(col, 2),
    }


def device_at(place):
    row = lax.rem(place["y"], 2) * 16 + place["x"] * 4 + place["z"]
    return device_of(row, (place["y"] // 2) * 2 + place["core"])


def moved(place, axis, step, extent=4):
    other = dict(place)
    other[axis] = lax.rem(place[axis] + step + extent, extent)
    return other


def meet(sources, targets):
    barrier = pltpu.get_barrier_semaphore()
    for device in sources:
        pl.semaphore_signal(barrier, inc=1, device_id=device, device_id_type=MESH)
    pl.semaphore_wait(barrier, targets)


def remote(source, target, send_sem, recv_sem, device):
    return pltpu.make_async_remote_copy(
        src_ref=source,
        dst_ref=target,
        send_sem=send_sem,
        recv_sem=recv_sem,
        device_id=device,
        device_id_type=MESH,
    )


GATHER_ORDERS = (("z", "x", "y"), ("x", "y", "z"), ("y", "z", "x"))


def axis_view(place, fixed):
    index = [slice(None)] * 4
    if "y" in fixed:
        index[0], index[3] = lax.rem(place["y"], 2), place["y"] // 2
    if "x" in fixed:
        index[1] = place["x"]
    if "z" in fixed:
        index[2] = place["z"]
    return tuple(index)


def scatter_kernel(p_ref, o_ref, held, *rest):
    relays = rest[0:3]
    parts = [rest[3 + 3 * third : 6 + 3 * third] for third in range(3)]
    sums = [rest[12 + 2 * third : 14 + 2 * third] for third in range(3)]
    links = Links(rest[-2], rest[-1])
    first, own_first = links.take(45), links.take(3)
    me = split_place()
    everywhere = (slice(None),) * 4
    own_copies = []
    for third in range(3):
        rows = pl.ds(third * 128, 128)
        own_copies.append(
            pltpu.make_async_copy(
                p_ref.at[everywhere + (rows,)],
                held.at[everywhere + (rows,)],
                links.sends.at[own_first + third],
            )
        )
        own_copies[third].start()
    partners = [moved(me, axis, step) for axis in "xyz" for step in (1, 2, 3)]
    meet([device_at(place) for place in partners], 9)

    def view_of(third, phase, place, part=None):
        order = GATHER_ORDERS[third]
        axis = order[2 - phase]
        start, size = (0, 128) if part is None else (64 * part, 64)
        if phase == 0:
            return held.at[axis_view(place, [axis]) + (pl.ds(third * 128 + start, size),)]
        index = []
        for name, key in (("y", 0), ("x", 1), ("z", 2), ("y", 3)):
            if name not in order[: 3 - phase]:
                continue
            if name != axis:
                index.append(slice(None))
            elif name == "y":
                index.append(lax.rem(place["y"], 2) if key == 0 else place["y"] // 2)
            else:
                index.append(place[name])
        return sums[third][phase - 1].at[tuple(index) + (pl.ds(start, size),)]

    def link(third, phase, kind, step, outgoing, incoming):
        number = first + 15 * third + 5 * phase + (3 + step // 2 if kind else step - 1)
        return remote(
            outgoing,
            incoming,
            links.sends.at[number],
            links.recvs.at[number],
            device_at(moved(me, GATHER_ORDERS[third][2 - phase], step)),
        )

    def steps(phase):
        return (1, 2, 3) if phase else (1, 3)

    def relay(third, step):
        axis = GATHER_ORDERS[third][2]
        outgoing = view_of(third, 0, moved(me, axis, 2), step // 2)
        return link(third, 0, 1, step, outgoing, relays[third].at[step // 2])

    def copy(third, phase, step):
        axis = GATHER_ORDERS[third][2 - phase]
        outgoing = view_of(third, phase, moved(me, axis, step))
        slot = steps(phase).index(step)
        return link(third, phase, 0, step, outgoing, parts[third][phase].at[slot])

    for third in range(3):
        own_copies[third].wait()
        for step in (1, 3):
            relay(third, step).start()
    for third in range(3):
        axis = GATHER_ORDERS[third][2]
        for step in (1, 3):
            relay(third, step).wait_recv()
            view = view_of(third, 0, moved(me, axis, step), step // 2)
            view[...] = view[...] + relays[third][step // 2]
            copy(third, 0, step).start()
    for phase in range(1, 4):
        for third in range(3):
            total = view_of(third, phase - 1, me)[...].astype(jnp.float32)
            for slot, step in enumerate(steps(phase - 1)):
                copy(third, phase - 1, step).wait_recv()
                total = total + parts[third][phase - 1][slot].astype(jnp.float32)
            if phase == 3:
                o_ref[128 * third : 128 * third + 128] = total
            else:
                sums[third][phase - 1][...] = total.astype(jnp.bfloat16)
                for step in steps(phase):
                    copy(third, phase, step).start()
    for third in range(3):
        for step in (1, 3):
            relay(third, step).wait_send()
        for phase in range(3):
            for step in steps(phase):
                copy(third, phase, step).wait_send()


def scatter_params(packed, collective):
    def shape_left(left, rows):
        shape = ()
        for name, number in (("y", 2), ("x", 4), ("z", 4), ("y", 2)):
            if name in left:
                shape += (number,)
        return shape + (rows, 128)

    relays = []
    parts = []
    sums = []
    for order in GATHER_ORDERS:
        relays.append(pltpu.VMEM((2,) + shape_left(order[:2], 64), jnp.bfloat16))
        for phase in range(3):
            number = 3 if phase else 2
            parts.append(pltpu.VMEM((number,) + shape_left(order[: 2 - phase], 128), jnp.bfloat16))
        for phase in range(2):
            sums.append(pltpu.VMEM(shape_left(order[: 2 - phase], 128), jnp.bfloat16))
    half = (2, 4, 4, 2, PAYLOAD, 128)
    return pl.pallas_call(
        scatter_kernel,
        out_shape=jax.ShapeDtypeStruct((PAYLOAD, 128), jnp.float32),
        in_specs=[ANY],
        out_specs=VMEM,
        scratch_shapes=[pltpu.VMEM(half, jnp.bfloat16)]
        + relays
        + parts
        + sums
        + [pltpu.SemaphoreType.DMA((51,)), pltpu.SemaphoreType.DMA((51,))],
        compiler_params=pltpu.CompilerParams(
            collective_id=collective, has_side_effects=True, vmem_limit_bytes=56 * MEGABYTE
        ),
    )(packed)


def neighbour(row, col, offset):
    return lax.rem(row + offset[0] + 32, 32), lax.rem(col + offset[1] + 4, 4)


MEGABYTE = 1024 * 1024
OFFSETS = (-4, 4, -6, 6, -12, 12, -18, 18)
ID_ROW = 368
RATE_ROWS = 224


class Links:
    def __init__(self, sends, recvs):
        self.sends, self.recvs = sends, recvs
        self.cursor = 0

    def take(self, number):
        first = self.cursor
        self.cursor = first + number
        return first


class Total:
    def __init__(self, links, value, near, far):
        self.links, self.value, self.near, self.far = links, value, near, far
        self.first = links.take(24)
        self.row, self.col = lax.axis_index("rows"), lax.axis_index("cols")
        self.near_me = (self.row // 16) * 4 + self.col
        self.far_me = lax.rem(self.row, 16)

    def near_device(self, index):
        return device_of((index // 4) * 16 + self.far_me, lax.rem(index, 4))

    def far_device(self, index):
        return device_of((self.row // 16) * 16 + index, self.col)

    def copy(self, far, step, slot):
        buffer, me, size = (self.far, self.far_me, 16) if far else (self.near, self.near_me, 8)
        base = self.first + (8 if far else 0)
        target = lax.rem(me + step, size)
        return remote(
            self.value,
            buffer.at[slot],
            self.links.sends.at[base + step],
            self.links.recvs.at[base + slot],
            self.far_device(target) if far else self.near_device(target),
        )

    def send(self, far):
        buffer, me, size = (self.far, self.far_me, 16) if far else (self.near, self.near_me, 8)
        for step in range(1, size):
            self.copy(far, step, me).start()
        buffer[me] = self.value[...]

    def collect(self, far):
        buffer, me, size = (self.far, self.far_me, 16) if far else (self.near, self.near_me, 8)
        for step in range(1, size):
            self.copy(far, step, lax.rem(me + step, size)).wait_recv()
        for step in range(1, size):
            self.copy(far, step, me).wait_send()
        total = buffer[0]
        for index in range(1, size):
            total = total + buffer[index]
        self.value[...] = total

    def start(self, value):
        self.value[...] = value
        self.send(False)

    def middle(self):
        self.collect(False)
        self.send(True)

    def finish(self):
        self.collect(True)
        return self.value[...]


def total_scratch(rows, columns):
    return [
        pltpu.VMEM((rows, columns), jnp.float32),
        pltpu.VMEM((8, rows, columns), jnp.float32),
        pltpu.VMEM((16, rows, columns), jnp.float32),
    ]


def total_peers():
    row, col = lax.axis_index("rows"), lax.axis_index("cols")
    near_me, far_me = (row // 16) * 4 + col, lax.rem(row, 16)
    peers = []
    for step in range(1, 8):
        index = lax.rem(near_me + step, 8)
        peers.append(device_of((index // 4) * 16 + far_me, lax.rem(index, 4)))
    for step in range(1, 16):
        peers.append(device_of((row // 16) * 16 + lax.rem(far_me + step, 16), col))
    return peers


def halo_peers():
    row, col = lax.axis_index("rows"), lax.axis_index("cols")
    return [
        device_of(*neighbour(row, col, (row_step, col_step)))
        for row_step in (-1, 0, 1)
        for col_step in (-1, 0, 1)
        if (row_step, col_step) != (0, 0)
    ]


class Halo:
    def __init__(self, links, source, window):
        self.links, self.source, self.window = links, source, window
        self.first = links.take(9)

    def copies(self, own_side):
        row, col = lax.axis_index("rows"), lax.axis_index("cols")
        listed = []
        for row_step in (-1, 0, 1):
            for col_step in (-1, 0, 1):
                if (row_step, col_step) == (0, 0):
                    continue
                low, size, top = {-1: (0, 4, 12), 0: (0, 8, 4), 1: (4, 4, 0)}[row_step]
                left = {-1: 32, 0: 16, 1: 0}[col_step]
                number = self.first + 3 * (row_step + 1) + col_step + 1
                listed.append(
                    remote(
                        self.source.at[pl.ds(low, size)],
                        self.window.at[pl.ds(top, size), pl.ds(left, 16)],
                        self.links.sends.at[number],
                        self.links.recvs.at[number],
                        device_of(*neighbour(row, col, (row_step, col_step))),
                    )
                )
        return listed

    def start(self):
        for copy in self.copies(True):
            copy.start()
        self.window[4:12, 16:32] = self.source[...]

    def finish(self):
        for copy in self.copies(False):
            copy.wait_recv()
        for copy in self.copies(False):
            copy.wait_send()


def widen_window(window, wide):
    col = lax.axis_index("cols")
    left = jnp.where(col > 0, 1.0, 0.0)
    right = jnp.where(col < 3, 1.0, 0.0)
    wide[:, 0:16] = window[:, 0:16].astype(jnp.float32) * left
    wide[:, 16:32] = window[:, 16:32].astype(jnp.float32)
    wide[:, 32:48] = window[:, 32:48].astype(jnp.float32) * right


def pixel_mask(mask):
    return jnp.broadcast_to(mask[:, None, :], (8, 16, 128)).reshape(128, 128)


def across_lanes(mask, width):
    return jnp.concatenate([mask] * (width // 128), axis=1)


class Gather:
    def __init__(self, links, source, target):
        self.links, self.source, self.target = links, source, target
        self.first = links.take(45)
        self.core_first = links.take(12)
        self.me = split_place()
        self.twin = moved(self.me, "core", 1, 2)

    def block(self, place, third, free, part=None):
        fixed = [axis for axis in "xyz" if axis not in free]
        rows = pl.ds(third * 128, 128) if part is None else pl.ds(third * 128 + 64 * part, 64)
        return self.target.at[axis_view(place, fixed) + (place["core"], rows)]

    def link(self, third, phase, kind, step, outgoing, incoming):
        number = self.first + 15 * third + 5 * phase + (3 + step // 2 if kind else step - 1)
        return remote(
            outgoing,
            incoming,
            self.links.sends.at[number],
            self.links.recvs.at[number],
            device_at(moved(self.me, GATHER_ORDERS[third][phase], step)),
        )

    def copy(self, third, phase, step, sender):
        free = GATHER_ORDERS[third][:phase]
        if phase == 0:
            outgoing = self.source.at[pl.ds(third * 128, 128)]
        else:
            outgoing = self.block(self.me, third, free)
        return self.link(third, phase, 0, step, outgoing, self.block(sender, third, free))

    def relay(self, third, phase, step, sender):
        order = GATHER_ORDERS[third]
        view = self.block(moved(sender, order[phase], 4 - step), third, order[:phase], step // 2)
        return self.link(third, phase, 1, step, view, view)

    def core_copy(self, third, distance, sender):
        order = GATHER_ORDERS[third]
        view = self.block(moved(sender, order[2], distance), third, order[:2])
        number = self.core_first + 4 * third + distance
        return remote(
            view, view, self.links.sends.at[number], self.links.recvs.at[number], device_at(self.twin)
        )

    def behind(self, third, phase, step):
        return moved(self.me, GATHER_ORDERS[third][phase], 4 - step)

    def steps(self, phase):
        return (1, 3) if phase == 2 else (1, 2, 3)

    def run(self):
        me = self.me
        for phase in range(3):
            for third in range(3):
                if phase > 0:
                    for step in (1, 2, 3):
                        self.copy(third, phase - 1, step, self.behind(third, phase - 1, step)).wait_recv()
                for step in self.steps(phase):
                    self.copy(third, phase, step, me).start()
                if phase == 0:
                    self.block(me, third, ())[...] = self.source[pl.ds(third * 128, 128)]
                if phase == 2:
                    self.core_copy(third, 0, me).start()
        for third in range(3):
            for step in (1, 3):
                self.copy(third, 2, step, self.behind(third, 2, step)).wait_recv()
                self.relay(third, 2, step, me).start()
                self.core_copy(third, 4 - step, me).start()
        for third in range(3):
            for step in (1, 3):
                self.relay(third, 2, step, self.behind(third, 2, step)).wait_recv()
            self.core_copy(third, 2, me).start()
        for third in range(3):
            for distance in range(4):
                self.core_copy(third, distance, self.twin).wait_recv()

    def close(self):
        for third in range(3):
            for phase in range(3):
                for step in self.steps(phase):
                    self.copy(third, phase, step, self.me).wait_send()
            for step in (1, 3):
                self.relay(third, 2, step, self.me).wait_send()
            for distance in range(4):
                self.core_copy(third, distance, self.me).wait_send()


RATE_ORDERS = (("x", "z"), ("z", "x"))


class RateGather:
    def __init__(self, links, source, target):
        self.links, self.source, self.target = links, source, target
        self.first = links.take(82)
        self.me = split_place()
        self.low_y = lax.rem(self.me["y"], 2)
        self.other = dict(self.me)
        self.other["y"] = self.me["y"] + 1 - 2 * self.low_y
        self.half = RATE_ROWS // 2

    def own(self):
        return pltpu.make_async_copy(
            self.source,
            self.target.at[self.low_y, self.me["x"], self.me["z"]],
            self.links.recvs.at[self.first + 81],
        )

    def pair(self, sender):
        return remote(
            self.source,
            self.target.at[lax.rem(sender["y"], 2), self.me["x"], self.me["z"]],
            self.links.sends.at[self.first + 80],
            self.links.recvs.at[self.first + 80],
            device_at(self.other),
        )

    def axis(self, half, unit):
        return RATE_ORDERS[half][0 if unit < 2 else 1]

    def piece(self, half, unit, place, part=None):
        near = RATE_ORDERS[half][0]
        low_y = lax.rem(self.low_y + (unit if unit < 2 else (unit - 2) // 4), 2)
        places = {"x": place["x"], "z": place["z"]}
        if unit >= 2:
            places[near] = lax.rem(places[near] + (unit - 2) % 4, 4)
        start, size = {None: (0, 112), 0: (0, 64), 1: (64, 48)}[part]
        return self.target.at[low_y, places["x"], places["z"], pl.ds(half * self.half + start, size)]

    def link(self, half, unit, kind, step, view):
        number = self.first + 8 * unit + 4 * half + 2 * kind + step // 2
        return remote(
            view,
            view,
            self.links.sends.at[number],
            self.links.recvs.at[number],
            device_at(moved(self.me, self.axis(half, unit), step)),
        )

    def copy(self, half, unit, step, sender):
        return self.link(half, unit, 0, step, self.piece(half, unit, sender))

    def relay(self, half, unit, step, sender):
        first = moved(sender, self.axis(half, unit), 4 - step)
        return self.link(half, unit, 1, step, self.piece(half, unit, first, step // 2))

    def behind(self, half, unit, step):
        return moved(self.me, self.axis(half, unit), 4 - step)

    def each(self):
        return [(half, step) for half in range(2) for step in (1, 3)]

    def begin(self):
        self.own().start()
        self.pair(self.me).start()

    def send(self, *units):
        for unit in units:
            if unit == 0:
                self.own().wait()
            if unit == 1:
                self.pair(self.other).wait_recv()
            for half, step in self.each():
                self.copy(half, unit, step, self.me).start()

    def forward(self, *units):
        for unit in units:
            for half, step in self.each():
                self.copy(half, unit, step, self.behind(half, unit, step)).wait_recv()
                self.relay(half, unit, step, self.me).start()

    def receive(self, *units):
        for unit in units:
            for half, step in self.each():
                self.relay(half, unit, step, self.behind(half, unit, step)).wait_recv()

    def close(self):
        self.pair(self.me).wait_send()
        for unit in range(10):
            for half, step in self.each():
                self.copy(half, unit, step, self.me).wait_send()
                self.relay(half, unit, step, self.me).wait_send()


def assemble(gathered, first_row_group, staging, wide, stride):
    parts = len(wide)
    count, offset = (BLOCK_ROWS, 0) if parts == 4 else (HEAD_ROWS, BLOCK_ROWS)

    def step(group, carry):
        low_y, x, z = first_row_group // 16, group // 4, lax.rem(group, 4)
        for column in range(4):
            area = staging[column]
            if parts == 4:
                area[0:288] = gathered[low_y, x, z, column // 2, column % 2, 0:288].astype(jnp.float32)
            else:
                area[0:96] = gathered[low_y, x, z, column // 2, column % 2, 272:368].astype(jnp.float32)
            skip = offset - (0 if parts == 4 else 272)
            for part in range(parts):
                begin = (part - column * count) % parts
                number = (count - begin + parts - 1) // parts
                row = (column * count + begin - part) // parts
                group_rows = 4 * count // parts
                target = group_rows * (group + stride) + row
                wide[part][pl.ds(target, number), :] = area[
                    pl.ds(skip + begin, number, stride=parts), :
                ]
        return carry

    lax.fori_loop(0, 16, step, 0)


def wide_rows(wide, first, number):
    return jnp.concatenate([part[pl.ds(first, number), :] for part in wide], axis=1)


def block_forward_kernel(
    x_ref,
    block_ref,
    head_ref,
    image_ref,
    rate_params_ref,
    reduce_ref,
    spatial_ref,
    expand_ref,
    point_ref,
    pool_ref,
    project_ref,
    misc_ref,
    norms_ref,
    masks_ref,
    first_ref,
    second_ref,
    third_ref,
    act_ref,
    window_ref,
    out_ref,
    slab_ref,
    rates_ref,
    gathered,
    s0,
    s1,
    s2,
    s3,
    w0,
    w1,
    w2,
    w3,
    h0,
    h1,
    ids,
    wide,
    act_map,
    payload_wide,
    payload_ref,
    rate_ref,
    *rest,
):
    staging, matrix, head = (s0, s1, s2, s3), (w0, w1, w2, w3), (h0, h1)
    links = Links(rest[-2], rest[-1])
    totals = [Total(links, *rest[3 * number : 3 * number + 3]) for number in range(3)]
    payload_wide[0:BLOCK_ROWS, :] = block_ref[...]
    payload_wide[BLOCK_ROWS : BLOCK_ROWS + HEAD_ROWS, :] = head_ref[...]
    payload_wide[BLOCK_ROWS + HEAD_ROWS : PAYLOAD, :] = jnp.zeros(
        (PAYLOAD - BLOCK_ROWS - HEAD_ROWS, 128), jnp.float32
    )
    for step in range(8):
        payload_wide[ID_ROW + step : ID_ROW + step + 1, :] = jnp.full(
            (1, 128), image_ref[step].astype(jnp.float32)
        )
    payload_ref[...] = payload_wide[...].astype(jnp.bfloat16)
    rate_ref[...] = jnp.concatenate(
        [rate_params_ref[...], jnp.zeros((RATE_ROWS - 216, 512), jnp.float32)], axis=0
    ).astype(jnp.bfloat16)
    gather = Gather(links, payload_ref, gathered)
    rates = RateGather(links, rate_ref, rates_ref)
    halo = Halo(links, act_map, window_ref)
    slab_first = links.take(3)
    row, col = lax.axis_index("rows"), lax.axis_index("cols")
    peers = total_peers() + halo_peers()
    meet(peers, len(peers))
    rates.begin()
    gather.run()
    rates.send(0, 2, 1)

    for step in range(-3, 4):
        other = lax.rem(row + step + 32, 32)
        rows_there = gathered[
            other // 16, lax.rem(other // 4, 4), lax.rem(other, 4), 0, 0, ID_ROW : ID_ROW + 16
        ].astype(jnp.float32)[0:8]
        inside = jnp.logical_and(row + step >= 0, row + step < 32)
        ids[8 * (step + 3) : 8 * (step + 3) + 8, :] = jnp.where(inside, rows_there, -1.0)
    own_ids = ids[24:32, :]
    for number, offset in enumerate(OFFSETS):
        masks_ref[number] = jnp.where(ids[24 + offset : 32 + offset, :] == own_ids, 1.0, 0.0)
    masks_ref[len(OFFSETS)] = own_ids

    assemble(gathered, 0, staging, matrix, 0)
    for step in range(8):
        reduce_ref[256 * step : 256 * step + 256] = wide_rows(matrix, 256 * step, 256).astype(jnp.bfloat16)
    first = jnp.dot(x_ref[...], reduce_ref[...], preferred_element_type=jnp.float32)
    totals[0].start(
        jnp.concatenate(
            [jnp.sum(first, axis=0, keepdims=True), jnp.sum(first * first, axis=0, keepdims=True)], axis=0
        )
    )
    for step in range(5):
        spatial_ref[464 * step : 464 * step + 464] = wide_rows(matrix, 2048 + 464 * step, 464).astype(
            jnp.bfloat16
        )
    totals[0].middle()
    assemble(gathered, 16, staging, matrix, 0)
    for step in range(13):
        spatial_ref[2320 + 176 * step : 2320 + 176 * step + 176] = wide_rows(
            matrix, 176 * step, 176
        ).astype(jnp.bfloat16)
    for part in range(4):
        expand_ref[:, 512 * part : 512 * part + 512] = jnp.concatenate(
            [array[pl.ds(2288 + part, 512, stride=4), :] for array in matrix], axis=1
        ).astype(jnp.bfloat16)
    norms_ref[...] = wide_rows(matrix, 4336, 16)

    def normal(total, values, gain, shift, kept):
        average = total[0:1] / 16384.0
        variance = total[1:2] / 16384.0 - average * average
        scale = lax.rsqrt(variance + EPSILON)
        centered = (values - average) * scale
        kept[0:128] = centered
        kept[128:136] = jnp.broadcast_to(scale, (8, scale.shape[1]))
        return centered * gain + shift

    def silu(values):
        return values * jax.nn.sigmoid(values)

    def stats(values):
        return jnp.concatenate(
            [jnp.sum(values, axis=0, keepdims=True), jnp.sum(values * values, axis=0, keepdims=True)], axis=0
        )

    normed = normal(totals[0].finish(), first, norms_ref[0:1], norms_ref[1:2], first_ref)
    act_map[...] = silu(normed).astype(jnp.bfloat16).reshape(8, 16, MID)
    halo.start()
    rates.forward(0, 2, 1)
    rates.receive(0)
    rates.send(3)
    halo.finish()
    widen_window(window_ref, wide)
    second = None
    for row_tap in range(3):
        part = None
        for col_tap in range(3):
            tap = 3 * row_tap + col_tap
            region = wide[4 * row_tap : 4 * row_tap + 8, 12 + 4 * col_tap : 28 + 4 * col_tap]
            product = jnp.dot(
                region.reshape(128, MID).astype(jnp.bfloat16),
                spatial_ref[512 * tap : 512 * tap + 512],
                preferred_element_type=jnp.float32,
            )
            part = product if part is None else part + product
        if row_tap != 1:
            part = part * across_lanes(pixel_mask(masks_ref[row_tap // 2]), MID)
        second = part if second is None else second + part
    totals[1].start(stats(second))
    assemble(gathered, 0, staging, head, 0)
    assemble(gathered, 16, staging, head, 16)
    totals[1].middle()
    for step in range(8):
        point_ref[256 * step : 256 * step + 256] = wide_rows(head, 256 * step, 256).astype(jnp.bfloat16)
        pool_ref[256 * step : 256 * step + 256] = wide_rows(head, 2048 + 256 * step, 256).astype(jnp.bfloat16)
    for step in range(5):
        project_ref[256 * step : 256 * step + 256] = wide_rows(head, 4097 + 256 * step, 256).astype(
            jnp.bfloat16
        )
    misc_ref[0:8] = wide_rows(head, 4096, 8)
    misc_ref[8:72] = wide_rows(head, 5376, 64)
    normed = normal(totals[1].finish(), second, norms_ref[2:3], norms_ref[3:4], second_ref)
    rates.forward(3)
    rates.receive(1)
    rates.send(4, 5)
    act_ref[...] = silu(normed).astype(jnp.bfloat16)
    third = jnp.dot(act_ref[...], expand_ref[...], preferred_element_type=jnp.float32)
    totals[2].start(stats(third))
    totals[2].middle()
    out_gain = jnp.concatenate([norms_ref[4 + part : 5 + part] for part in range(4)], axis=1)
    out_shift = jnp.concatenate([norms_ref[8 + part : 9 + part] for part in range(4)], axis=1)
    normed = normal(totals[2].finish(), third, out_gain, out_shift, third_ref)
    block_out = silu(normed + x_ref[...].astype(jnp.float32)).astype(jnp.bfloat16)
    out_ref[...] = block_out.reshape(8, 16, CIN)

    def slab_copy(step, sender):
        return remote(
            out_ref.at[:, :, pl.ds(pl.multiple_of(lax.rem(col + step, 4) * 512, 512), 512)],
            slab_ref.at[:, pl.ds(pl.multiple_of(sender * 16, 16), 16)],
            links.sends.at[slab_first + step - 1],
            links.recvs.at[slab_first + step - 1],
            device_of(row, lax.rem(col + step, 4)),
        )

    for step in (1, 2, 3):
        slab_copy(step, col).start()
    rates.forward(4, 5)
    rates.send(6, 7, 8, 9)
    slab_ref[:, pl.ds(pl.multiple_of(col * 16, 16), 16)] = out_ref[
        :, :, pl.ds(pl.multiple_of(col * 512, 512), 512)
    ]
    for step in (1, 2, 3):
        copy = slab_copy(step, lax.rem(col + 4 - step, 4))
        copy.wait_recv()
        copy.wait_send()
    rates.forward(6, 7, 8, 9)
    rates.receive(2, 3, 4, 5, 6, 7, 8, 9)
    rates.close()
    gather.close()


def block_forward(arrays, collective):
    bf16, f32 = jnp.bfloat16, jnp.float32
    outs = [
        ((CIN, MID), bf16),
        ((9 * MID, MID), bf16),
        ((MID, CIN), bf16),
        ((CIN, ASPP), bf16),
        ((CIN, ASPP), bf16),
        ((5 * ASPP, ASPP), bf16),
        ((72, ASPP), f32),
        ((16, MID), f32),
        ((9, 8, 128), f32),
        ((136, MID), f32),
        ((136, MID), f32),
        ((136, CIN), f32),
        ((128, MID), bf16),
        ((16, 48, MID), bf16),
        ((8, 16, CIN), bf16),
        ((8, 64, CIN // 4), bf16),
        ((2, 4, 4, RATE_ROWS, CIN // 4), bf16),
    ]
    scratch = [pltpu.VMEM((2, 4, 4, 2, 2, PAYLOAD, 128), bf16)]
    scratch += [pltpu.VMEM((288, 128), f32)] * 4
    scratch += [pltpu.VMEM((4368, 128), f32)] * 4
    scratch += [pltpu.VMEM((5440, 128), f32)] * 2
    scratch += [
        pltpu.VMEM((56, 128), f32),
        pltpu.VMEM((16, 48, MID), f32),
        pltpu.VMEM((8, 16, MID), bf16),
        pltpu.VMEM((PAYLOAD, 128), f32),
        pltpu.VMEM((PAYLOAD, 128), bf16),
        pltpu.VMEM((RATE_ROWS, 512), bf16),
    ]
    for rows, columns in ((2, MID), (2, MID), (2, CIN)):
        scratch += total_scratch(rows, columns)
    scratch += [pltpu.SemaphoreType.DMA((240,)), pltpu.SemaphoreType.DMA((240,))]
    return pl.pallas_call(
        block_forward_kernel,
        out_shape=[jax.ShapeDtypeStruct(shape, dtype) for shape, dtype in outs],
        in_specs=[VMEM, VMEM, VMEM, SMEM, VMEM],
        out_specs=[VMEM] * 16 + [ANY],
        scratch_shapes=scratch,
        compiler_params=pltpu.CompilerParams(
            collective_id=collective, has_side_effects=True, vmem_limit_bytes=60 * MEGABYTE
        ),
    )(*arrays)


class RatePieces:
    def __init__(self, links, units):
        self.links = links
        self.first = links.take(6 * units + 4)
        self.extra = self.first + 6 * units
        self.me = split_place()
        self.low_y = lax.rem(self.me["y"], 2)
        self.other = dict(self.me)
        self.other["y"] = self.me["y"] + 1 - 2 * self.low_y

    def rows(self, half):
        return pl.ds(half * (RATE_ROWS // 2), RATE_ROWS // 2)

    def piece(self, array, half, low_y, first_axis, second_axis):
        places = {RATE_ORDERS[half][0]: first_axis, RATE_ORDERS[half][1]: second_axis}
        return array.at[low_y, places["x"], places["z"], self.rows(half)]

    def remote(self, unit, half, step, outgoing, incoming, axis):
        number = self.first + 6 * unit + 3 * half + step - 1
        return remote(
            outgoing,
            incoming,
            self.links.sends.at[number],
            self.links.recvs.at[number],
            device_at(moved(self.me, axis, step)),
        )

    def each(self):
        return [(half, step) for half in range(2) for step in (1, 2, 3)]


class RateFirst(RatePieces):
    def __init__(self, links, pieces, parts, sums, low_y):
        super().__init__(links, 4)
        self.pieces, self.parts, self.sums, self.from_y = pieces, parts, sums, low_y

    def copy(self, unit, half, step):
        far = RATE_ORDERS[half][1]
        target = moved(self.me, far, step)
        outgoing = self.piece(self.pieces, half, self.from_y, unit, target[far])
        return self.remote(unit, half, step, outgoing, self.parts.at[half, unit, step - 1], far)

    def send(self, unit):
        for half, step in self.each():
            self.copy(unit, half, step).start()

    def collect(self, unit, own=None):
        for half in range(2):
            total = None
            if own is None:
                mine = self.piece(self.pieces, half, self.from_y, unit, self.me[RATE_ORDERS[half][1]])[...]
            else:
                mine = own[half, unit]
            total = mine.astype(jnp.float32)
            for step in (1, 2, 3):
                self.copy(unit, half, step).wait_recv()
                total = total + self.parts[half, unit, step - 1].astype(jnp.float32)
            self.sums[half, unit] = total.astype(jnp.bfloat16)
        for half, step in self.each():
            self.copy(unit, half, step).wait_send()


class RateScatter(RatePieces):
    def __init__(self, links, sums, parts, pair_sums, pair_parts, target):
        super().__init__(links, 2)
        self.sums, self.parts, self.target = sums, parts, target
        self.pair_sums, self.pair_parts = pair_sums, pair_parts

    def copy(self, low_y, half, step):
        near = RATE_ORDERS[half][0]
        target = moved(self.me, near, step)
        outgoing = self.sums[low_y].at[half, target[near]]
        return self.remote(low_y, half, step, outgoing, self.parts.at[half, low_y, step - 1], near)

    def pair(self):
        return remote(
            self.pair_sums.at[1 - self.low_y],
            self.pair_parts,
            self.links.sends.at[self.extra],
            self.links.recvs.at[self.extra],
            device_at(self.other),
        )

    def send(self, low_y):
        for half, step in self.each():
            self.copy(low_y, half, step).start()

    def collect(self, low_y):
        for half in range(2):
            total = self.sums[low_y][half, self.me[RATE_ORDERS[half][0]]].astype(jnp.float32)
            for step in (1, 2, 3):
                self.copy(low_y, half, step).wait_recv()
                total = total + self.parts[half, low_y, step - 1].astype(jnp.float32)
            self.pair_sums[low_y, half] = total.astype(jnp.bfloat16)

    def finish(self):
        self.pair().wait_recv()
        for half in range(2):
            rows = slice(half * (RATE_ROWS // 2), (half + 1) * (RATE_ROWS // 2))
            self.target[rows] = self.pair_sums[self.low_y, half].astype(jnp.float32) + self.pair_parts[
                half
            ].astype(jnp.float32)
        for low_y in range(2):
            for half, step in self.each():
                self.copy(low_y, half, step).wait_send()
        self.pair().wait_send()


def disassemble(packed, first_row_group, staging, wide, stride):
    parts = len(wide)
    core = lax.rem(lax.axis_index("cols"), 2)
    count = BLOCK_ROWS if parts == 4 else HEAD_ROWS
    low_y = first_row_group // 16

    def step(group, carry):
        x, z = group // 4, lax.rem(group, 4)
        for column in range(4):
            area = staging[column]
            here = (lax.rem(column + core, 2), low_y, x, z, column // 2)
            if parts == 4:
                skip = 0
                area[272:288] = packed[here + (slice(272, 288),)].astype(jnp.float32)
            else:
                skip = 1
                area[80:112] = jnp.zeros((32, 128), jnp.float32)
            for part in range(parts):
                begin = (part - column * count) % parts
                number = (count - begin + parts - 1) // parts
                row = (column * count + begin - part) // parts
                origin = (4 * count // parts) * (group + stride) + row
                area[pl.ds(skip + begin, number, stride=parts), :] = wide[part][
                    pl.ds(origin, number), :
                ]
            if parts == 4:
                packed[here + (slice(0, 288),)] = area[0:288].astype(jnp.bfloat16)
            else:
                packed[here + (slice(272, 384),)] = area[0:112].astype(jnp.bfloat16)
        return carry

    lax.fori_loop(0, 16, step, 0)


def deal(wide, first, values):
    number = values.shape[0]
    for part, array in enumerate(wide):
        array[first : first + number, :] = values[:, 128 * part : 128 * part + 128]


def against_rows(left, right):
    return lax.dot_general(left, right, (((1,), (1,)), ((), ())), preferred_element_type=jnp.float32)


def over_pixels(left, right):
    return lax.dot_general(left, right, (((0,), (0,)), ((), ())), preferred_element_type=jnp.float32)


def block_backward_kernel(
    x_ref,
    grad_ref,
    norms_ref,
    masks_ref,
    first_ref,
    second_ref,
    third_ref,
    act_ref,
    window_ref,
    reduce_hbm,
    spatial_hbm,
    expand_hbm,
    point_ref,
    pool_ref,
    project_ref,
    misc_ref,
    pieces_ref,
    out_ref,
    held_ref,
    share_ref,
    s0,
    s1,
    s2,
    s3,
    w0,
    w1,
    w2,
    w3,
    wide,
    act_map,
    window,
    packed,
    twin_part,
    reduce_ref,
    spatial_ref,
    expand_ref,
    free_sem,
    *rest,
):
    staging, matrix, head = (s0, s1, s2, s3), (w0, w1, w2, w3), (w0, w1)
    links = Links(rest[-2], rest[-1])
    totals = [Total(links, *rest[3 * number : 3 * number + 3]) for number in range(3)]
    own, first_parts, first_sums_here, second_parts, pair_sums, pair_parts = rest[9:15]
    rates = [
        RateFirst(links, pieces_ref, first_parts.at[low_y], first_sums_here.at[low_y], low_y)
        for low_y in range(2)
    ]
    scatter = RateScatter(
        links,
        (first_sums_here.at[0], first_sums_here.at[1]),
        second_parts,
        pair_sums,
        pair_parts,
        share_ref,
    )
    me = scatter.me
    twin = device_at(moved(me, "core", 1, 2))
    halo = Halo(links, act_map, window)
    load_first, own_first, twin_first, out_first = (links.take(number) for number in (3, 4, 2, 2))
    loads = [
        pltpu.make_async_copy(source, target, links.recvs.at[load_first + number])
        for number, (source, target) in enumerate(
            ((expand_hbm, expand_ref), (spatial_hbm, spatial_ref), (reduce_hbm, reduce_ref))
        )
    ]
    own_copies = []
    for low_y in range(2):
        for half in range(2):
            places = {RATE_ORDERS[half][0]: slice(None), RATE_ORDERS[half][1]: me[RATE_ORDERS[half][1]]}
            own_copies.append(
                pltpu.make_async_copy(
                    pieces_ref.at[low_y, places["x"], places["z"], scatter.rows(half)],
                    own.at[low_y, half],
                    links.recvs.at[own_first + 2 * low_y + half],
                )
            )
    for copy in loads + own_copies:
        copy.start()

    def twin_copy(low_y):
        return remote(
            packed.at[1, low_y],
            twin_part,
            links.sends.at[twin_first + low_y],
            links.recvs.at[twin_first + low_y],
            twin,
        )

    def out_copy(low_y):
        return pltpu.make_async_copy(
            packed.at[0, low_y], held_ref.at[low_y], links.sends.at[out_first + low_y]
        )

    def join_twin(low_y):
        twin_copy(low_y).wait_recv()

        def add_block(index, carry):
            place = (index // 8, lax.rem(index // 2, 4), lax.rem(index, 2))
            packed[(0, low_y) + place] = packed[(0, low_y) + place] + twin_part[place]
            return carry

        lax.fori_loop(0, 32, add_block, 0)
        out_copy(low_y).start()

    peers = total_peers() + halo_peers()
    meet(peers, len(peers))

    def slope(values):
        part = jax.nn.sigmoid(values)
        return part * (1.0 + values * (1.0 - part))

    def local_sums(grad, kept):
        return jnp.concatenate(
            [
                jnp.sum(grad, axis=0, keepdims=True),
                jnp.sum(grad * kept[0:128], axis=0, keepdims=True),
            ],
            axis=0,
        )

    def through_norm(total, grad, kept, gain):
        return (
            gain
            * kept[128:129]
            * (grad - total[0:1] / 16384.0 - kept[0:128] * (total[1:2] / 16384.0))
        ).astype(jnp.bfloat16)

    rates[0].send(0)
    out_gain = jnp.concatenate([norms_ref[4 + part : 5 + part] for part in range(4)], axis=1)
    out_shift = jnp.concatenate([norms_ref[8 + part : 9 + part] for part in range(4)], axis=1)
    residual = third_ref[0:128] * out_gain + out_shift + x_ref[...].astype(jnp.float32)
    out_ref[...] = grad_ref[...] * slope(residual)
    third_sums = local_sums(out_ref[...], third_ref)
    totals[0].start(third_sums)
    for step in range(4):
        deal(head, 512 * step, point_ref[512 * step : 512 * step + 512].astype(jnp.float32))
    deal(head, 2048, pool_ref[0:672].astype(jnp.float32))
    disassemble(packed, 0, staging, head, 0)
    totals[0].middle()
    for step in range(4):
        deal(head, 344 * step, pool_ref[672 + 344 * step : 1016 + 344 * step].astype(jnp.float32))
    deal(head, 1376, misc_ref[0:1])
    for step in range(5):
        deal(head, 1377 + 256 * step, project_ref[256 * step : 256 * step + 256].astype(jnp.float32))
    deal(head, 2657, misc_ref[1:64])
    disassemble(packed, 16, staging, head, 0)
    third_grad = through_norm(totals[0].finish(), out_ref[...], third_ref, out_gain)
    rates[0].send(1)
    loads[0].wait()
    second_gain, second_shift = norms_ref[2:3], norms_ref[3:4]
    second_norm = second_ref[0:128] * second_gain + second_shift
    second_back = against_rows(third_grad, expand_ref[...]) * slope(second_norm)
    second_sums = local_sums(second_back, second_ref)
    totals[1].start(second_sums)
    for part in range(4):
        product = over_pixels(act_ref[...], third_grad[:, 512 * part : 512 * part + 512])
        for number, array in enumerate(matrix):
            array[pl.ds(2288 + part, 512, stride=4), :] = product[:, 128 * number : 128 * number + 128]
    totals[1].middle()
    widen_window(window_ref, wide)
    second_grad = through_norm(totals[1].finish(), second_back, second_ref, second_gain)
    act_map[...] = second_grad.reshape(8, 16, MID)
    halo.start()
    rates[0].send(2)
    rates[0].send(3)

    def spatial_grad(tap):
        row_tap, col_tap = tap // 3, tap % 3
        region = wide[4 * row_tap : 4 * row_tap + 8, 12 + 4 * col_tap : 28 + 4 * col_tap].reshape(128, MID)
        if row_tap != 1:
            region = region * across_lanes(pixel_mask(masks_ref[row_tap // 2]), MID)
        return over_pixels(region.astype(jnp.bfloat16), second_grad)

    middle_tap = spatial_grad(4)
    deal(matrix, 0, middle_tap[272:512])
    for tap in range(5, 9):
        deal(matrix, 240 + 512 * (tap - 5), spatial_grad(tap))
    halo.finish()
    widen_window(window, wide)
    loads[1].wait()
    first_back = None
    for row_tap in range(3):
        part = None
        for col_tap in range(3):
            tap = 3 * row_tap + col_tap
            region = wide[
                8 - 4 * row_tap : 16 - 4 * row_tap, 20 - 4 * col_tap : 36 - 4 * col_tap
            ]
            product = against_rows(
                region.reshape(128, MID).astype(jnp.bfloat16), spatial_ref[512 * tap : 512 * tap + 512]
            )
            part = product if part is None else part + product
        if row_tap != 1:
            part = part * across_lanes(pixel_mask(masks_ref[1 - row_tap // 2]), MID)
        first_back = part if first_back is None else first_back + part
    first_gain, first_shift = norms_ref[0:1], norms_ref[1:2]
    first_back = first_back * slope(first_ref[0:128] * first_gain + first_shift)
    first_sums = local_sums(first_back, first_ref)
    totals[2].start(first_sums)
    deal(matrix, 4336, first_sums[1:2])
    deal(matrix, 4337, first_sums[0:1])
    deal(matrix, 4338, second_sums[1:2])
    deal(matrix, 4339, second_sums[0:1])
    for part in range(4):
        deal(matrix, 4340 + part, third_sums[1:2, 512 * part : 512 * part + 512])
        deal(matrix, 4344 + part, third_sums[0:1, 512 * part : 512 * part + 512])
    deal(matrix, 4348, jnp.zeros((20, MID), jnp.float32))
    disassemble(packed, 16, staging, matrix, 0)
    twin_copy(1).start()
    totals[2].middle()
    widen_window(window_ref, wide)
    for copy in own_copies:
        copy.wait()
    for unit in range(3):
        rates[0].collect(unit, own.at[0])
    deal(matrix, 4096, middle_tap[0:272])
    for tap in range(4):
        deal(matrix, 2048 + 512 * tap, spatial_grad(tap))
    first_total = totals[2].finish()
    for unit in range(4):
        rates[1].send(unit)
    rates[0].collect(3, own.at[0])
    scatter.send(0)
    join_twin(1)
    pl.semaphore_signal(free_sem, inc=1, device_id=twin, device_id_type=MESH)
    loads[2].wait()
    first_grad = through_norm(first_total, first_back, first_ref, first_gain)
    for part in range(4):
        rows = slice(512 * part, 512 * part + 512)
        deal(matrix, 512 * part, over_pixels(x_ref[:, rows], first_grad))
        out_ref[:, rows] = out_ref[:, rows] + against_rows(first_grad, reduce_ref[rows])
    disassemble(packed, 0, staging, matrix, 0)
    pl.semaphore_wait(free_sem, 1)
    twin_copy(0).start()
    for unit in range(4):
        rates[1].collect(unit, own.at[1])
    scatter.send(1)
    scatter.collect(0)
    join_twin(0)
    scatter.collect(1)
    scatter.pair().start()
    scatter.finish()
    for low_y in range(2):
        twin_copy(low_y).wait_send()
        out_copy(low_y).wait()


def block_backward(arrays, collective):
    bf16, f32 = jnp.bfloat16, jnp.float32
    half = RATE_ROWS // 2
    scratch = [pltpu.VMEM((384, 128), f32)] * 4
    scratch += [pltpu.VMEM((4368, 128), f32)] * 4
    scratch += [
        pltpu.VMEM((16, 48, MID), f32),
        pltpu.VMEM((8, 16, MID), bf16),
        pltpu.VMEM((16, 48, MID), bf16),
        pltpu.VMEM((2, 2, 4, 4, 2, PAYLOAD, 128), bf16),
        pltpu.VMEM((4, 4, 2, PAYLOAD, 128), bf16),
        pltpu.VMEM((CIN, MID), bf16),
        pltpu.VMEM((9 * MID, MID), bf16),
        pltpu.VMEM((MID, CIN), bf16),
        pltpu.SemaphoreType.REGULAR,
    ]
    for rows, columns in ((2, CIN), (2, MID), (2, MID)):
        scratch += total_scratch(rows, columns)
    scratch += [
        pltpu.VMEM((2, 2, 4, half, 512), bf16),
        pltpu.VMEM((2, 2, 4, 3, half, 512), bf16),
        pltpu.VMEM((2, 2, 4, half, 512), bf16),
        pltpu.VMEM((2, 2, 3, half, 512), bf16),
        pltpu.VMEM((2, 2, half, 512), bf16),
        pltpu.VMEM((2, half, 512), bf16),
    ]
    scratch += [pltpu.SemaphoreType.DMA((176,)), pltpu.SemaphoreType.DMA((176,))]
    outs = [
        ((128, CIN), f32),
        ((2, 4, 4, 2, PAYLOAD, 128), bf16),
        ((RATE_ROWS, 512), f32),
    ]
    return pl.pallas_call(
        block_backward_kernel,
        out_shape=[jax.ShapeDtypeStruct(shape, dtype) for shape, dtype in outs],
        in_specs=[VMEM] * 9 + [ANY] * 3 + [VMEM] * (len(arrays) - 13) + [ANY],
        out_specs=[VMEM, ANY, VMEM],
        scratch_shapes=scratch,
        compiler_params=pltpu.CompilerParams(
            collective_id=collective, has_side_effects=True, vmem_limit_bytes=62 * MEGABYTE
        ),
    )(*arrays)


def row_peers():
    row, col = lax.axis_index("rows"), lax.axis_index("cols")
    return [device_of(lax.rem(row + step + 32, 32), col) for step in (-3, -2, -1, 1, 2, 3)]


def row_moves():
    listed = []
    for branch, rate in enumerate(rate_list):
        for direction in range(2):
            for hop in range(4):
                lead = 8 * hop - rate if direction == 0 else rate - 8 * hop
                first, last = max(0, lead), min(8, lead + 8)
                if first < last:
                    sign = 1 if direction == 0 else -1
                    listed.append((branch, direction, sign * hop, first, first - lead, last - first))
    return listed


class RowShift:
    def __init__(self, links, sources, target):
        self.links, self.sources, self.target = links, sources, target
        self.moves = row_moves()
        self.first = links.take(len(self.moves))

    def copies(self, branch):
        row, col = lax.axis_index("rows"), lax.axis_index("cols")
        for number, (owner, direction, hop, first, top, size) in enumerate(self.moves):
            if owner == branch and hop:
                yield remote(
                    self.sources[branch][direction].at[pl.ds(first, size)],
                    self.target.at[branch, direction, pl.ds(top, size)],
                    self.links.sends.at[self.first + number],
                    self.links.recvs.at[self.first + number],
                    device_of(lax.rem(row + hop + 32, 32), col),
                )

    def start(self, branch):
        for copy in self.copies(branch):
            copy.start()
        for owner, direction, hop, first, top, size in self.moves:
            if owner == branch and hop == 0:
                self.target[branch, direction, top : top + size] = self.sources[branch][direction][
                    first : first + size
                ]

    def finish(self, branch):
        for copy in self.copies(branch):
            copy.wait_recv()
            copy.wait_send()


MARGIN = 24


def silu_value(values):
    return values * jax.nn.sigmoid(values)


def silu_grad(values):
    part = jax.nn.sigmoid(values)
    return part * (1.0 + values * (1.0 - part))


def two_sums(first, second):
    return jnp.concatenate(
        [jnp.sum(first, axis=0, keepdims=True), jnp.sum(second, axis=0, keepdims=True)], axis=0
    )


def centered_values(total, values):
    average = total[0:1] / 16384.0
    variance = total[1:2] / 16384.0 - average * average
    scale = lax.rsqrt(variance + EPSILON)
    return (values - average) * scale, scale


def norm_grad(total, grad, centered, scale, gain):
    return (
        gain * scale * (grad - total[0:1] / 16384.0 - centered * (total[1:2] / 16384.0))
    ).astype(jnp.bfloat16)


def pyramid_kernel(
    grid_ref,
    slab_ref,
    pieces_ref,
    point_ref,
    pool_ref,
    project_ref,
    misc_ref,
    heads_ref,
    bias_ref,
    masks_ref,
    seg_ref,
    edge_ref,
    part_ref,
    weights_ref,
    loss_out,
    pooled_out,
    grad_out,
    point_out,
    pool_out,
    project_out,
    heads_out,
    norms_out,
    pieces_out,
    kernels,
    padded,
    moved_maps,
    taps,
    core_part,
    high_out,
    high_part,
    tap_own,
    rows_out,
    rows_in,
    grads_own,
    grads_in,
    stack,
    grad_taps,
    back_out,
    back_in,
    *rest,
):
    bf16, f32 = jnp.bfloat16, jnp.float32
    links = Links(rest[-2], rest[-1])
    totals = [Total(links, *rest[3 * number : 3 * number + 3]) for number in range(5)]
    row, col = lax.axis_index("rows"), lax.axis_index("cols")
    core, high = lax.rem(col, 2), col // 2
    twin = device_of(row, col + 1 - 2 * core)
    far_twin = device_of(row, col + 2 - 4 * high)
    pieces_sem = links.take(1)
    tap_core, tap_high = links.take(6), links.take(3)
    stack_high, stack_core = links.take(3), links.take(6)
    back = links.take(3)
    forward_shift = RowShift(
        links, [[rows_out.at[branch, direction] for direction in range(2)] for branch in range(3)], rows_in
    )
    backward_shift = RowShift(
        links, [[grads_own.at[branch] for _ in range(2)] for branch in range(3)], grads_in
    )
    load = pltpu.make_async_copy(pieces_ref, pieces_out, links.recvs.at[pieces_sem])
    load.start()
    peers = total_peers() + row_peers()
    meet(peers, len(peers))

    members_low = [jnp.where(masks_ref[8] == float(image), 1.0, 0.0) for image in range(4)]
    row_sums = jnp.sum(grid_ref[...].astype(f32), axis=1)
    pieces = []
    for image in range(4):
        chosen = members_low[image]
        pieces.append(
            jnp.concatenate(
                [
                    jnp.sum(row_sums * across_lanes(chosen, CIN), axis=0, keepdims=True),
                    jnp.sum(chosen, axis=0, keepdims=True),
                ],
                axis=1,
            )
        )
    totals[4].start(jnp.concatenate(pieces, axis=0))

    def columns_of(place):
        return pl.ds(pl.multiple_of(place * 16, 16), 16)

    padded[:, 0:MARGIN] = jnp.zeros((8, MARGIN, 512), f32)
    padded[:, MARGIN + 64 :] = jnp.zeros((8, MARGIN, 512), f32)
    padded[:, MARGIN : MARGIN + 64] = slab_ref[...].astype(f32)
    for branch, rate in enumerate(rate_list):
        for side in range(2):
            start = MARGIN + (2 * side - 1) * rate
            moved_maps[2 * branch + side] = (
                padded[:, start : start + 64].reshape(512, 512).astype(bf16)
            )
    slab = slab_ref[...].reshape(512, 512)
    load.wait()

    def join(pair, carry):
        both = jnp.concatenate(
            [pieces_out[2 * pair, 0:216].astype(f32), pieces_out[2 * pair + 1, 0:216].astype(f32)], axis=0
        )
        kernels[pl.ds(pl.multiple_of(432 * pair, 16), 432)] = both.astype(bf16)
        return carry

    lax.fori_loop(0, 16, join, 0)

    def tap_core_copy(branch, place):
        return remote(
            taps.at[pl.ds(3 * branch, 3), :, columns_of(2 * place + 1 - core)],
            core_part.at[branch, place],
            links.sends.at[tap_core + 2 * branch + place],
            links.recvs.at[tap_core + 2 * branch + place],
            twin,
        )

    def tap_high_copy(branch):
        return remote(
            high_out.at[branch],
            high_part.at[branch],
            links.sends.at[tap_high + branch],
            links.recvs.at[tap_high + branch],
            far_twin,
        )

    def tap_meet(branch):
        for place in range(2):
            tap_core_copy(branch, place).wait_recv()
        away = taps[pl.ds(3 * branch, 3), :, columns_of(2 * (1 - high) + core)].astype(f32)
        high_out[branch] = (away + core_part[branch, 1 - high].astype(f32)).astype(bf16)
        tap_high_copy(branch).start()
        here = taps[pl.ds(3 * branch, 3), :, columns_of(col)].astype(f32)
        tap_own[branch] = here + core_part[branch, high].astype(f32)

    def tap_finish(branch):
        tap_high_copy(branch).wait_recv()
        tap_own[branch] = tap_own[branch] + high_part[branch].astype(f32)
        for direction in range(2):
            rows_out[branch, direction] = tap_own[branch, 2 * direction].astype(bf16)
        forward_shift.start(branch)

    for branch in range(3):
        result = None
        for col_tap in range(3):
            left = slab if col_tap == 1 else moved_maps[2 * branch + col_tap // 2]
            right = jnp.concatenate(
                [
                    kernels[(9 * branch + 3 * tap + col_tap) * 256 : (9 * branch + 3 * tap + col_tap + 1) * 256]
                    for tap in range(3)
                ],
                axis=0,
            )
            product = against_rows(left, right)
            result = product if result is None else result + product
        for tap in range(3):
            taps[3 * branch + tap] = result[:, 256 * tap : 256 * tap + 256].astype(bf16).reshape(8, 64, 256)
        for place in range(2):
            tap_core_copy(branch, place).start()
        if branch == 0:
            totals[4].middle()
        else:
            tap_meet(branch - 1)
    tap_meet(2)
    grid = grid_ref[...].reshape(128, CIN)
    branches = [jnp.dot(grid, point_ref[...], preferred_element_type=f32)]
    pooled_sums = totals[4].finish()
    area = jnp.concatenate([pooled_sums[:, CIN : CIN + 128]] * 16, axis=1) * 16.0
    pooled = pooled_sums[:, 0:CIN] / area
    pooled_out[...] = pooled
    pooled_low = jnp.concatenate([pooled, jnp.zeros((4, CIN), f32)], axis=0).astype(bf16)
    pool_pre = jnp.dot(pooled_low, pool_ref[...], preferred_element_type=f32)[0:4] + misc_ref[0:1]
    pool_act = silu_value(pool_pre)
    members = [across_lanes(pixel_mask(members_low[image]), ASPP) for image in range(4)]
    pool_map = members[0] * pool_act[0:1]
    for image in range(1, 4):
        pool_map = pool_map + members[image] * pool_act[image : image + 1]
    for branch in range(3):
        tap_finish(branch)
    for branch in range(3):
        forward_shift.finish(branch)
        value = tap_own[branch, 1].reshape(128, 256)
        for direction in range(2):
            mask = across_lanes(pixel_mask(masks_ref[2 + 2 * branch + direction]), ASPP)
            value = value + rows_in[branch, direction].astype(f32).reshape(128, 256) * mask
        branches.append(value)
    before = jnp.concatenate(branches, axis=1)
    totals[0].start(two_sums(before, before * before))
    totals[0].middle()
    gains = jnp.concatenate([misc_ref[9 + 2 * branch : 10 + 2 * branch] for branch in range(4)], axis=1)
    shifts = jnp.concatenate([misc_ref[10 + 2 * branch : 11 + 2 * branch] for branch in range(4)], axis=1)
    centered, scale = centered_values(totals[0].finish(), before)
    normed = centered * gains + shifts
    joined = jnp.concatenate([silu_value(normed).astype(bf16), pool_map.astype(bf16)], axis=1)
    projected = jnp.dot(joined, project_ref[...], preferred_element_type=f32)
    totals[1].start(two_sums(projected, projected * projected))
    totals[1].middle()
    last_gain, last_shift = misc_ref[17:18], misc_ref[18:19]
    proj_centered, proj_scale = centered_values(totals[1].finish(), projected)
    proj_normed = proj_centered * last_gain + last_shift
    feature_map = silu_value(proj_normed).astype(bf16)
    logits = jnp.dot(feature_map, heads_ref[...], preferred_element_type=f32) + bias_ref[0:1]
    lane = lax.broadcasted_iota(jnp.int32, (128, 128), 1)

    def per_pixel(labels_ref):
        spread = jnp.broadcast_to(labels_ref[...].astype(f32)[:, None, :], (8, 16, 16))
        here = lax.broadcasted_iota(jnp.int32, (8, 16, 16), 1) == lax.broadcasted_iota(
            jnp.int32, (8, 16, 16), 2
        )
        return jnp.sum(jnp.where(here, spread, 0.0), axis=2, keepdims=True).reshape(128, 1)

    lane_value = lane.astype(f32)
    hot = (
        jnp.where(lane_value == per_pixel(seg_ref), 1.0, 0.0)
        + jnp.where(lane == SEG, per_pixel(edge_ref), 0.0)
        + jnp.where(lane_value == per_pixel(part_ref) + (SEG + 1.0), 1.0, 0.0)
    )

    def cross_entropy(inside):
        highest = jnp.max(jnp.where(inside, logits, -3.0e38), axis=1, keepdims=True)
        powers = jnp.where(inside, jnp.exp(jnp.where(inside, logits - highest, 0.0)), 0.0)
        total = jnp.sum(powers, axis=1, keepdims=True)
        picked = jnp.sum(jnp.where(inside, logits * hot, 0.0), axis=1, keepdims=True)
        return highest + jnp.log(total) - picked, powers / total

    seg_inside, part_inside = lane < SEG, jnp.logical_and(lane > SEG, lane < HEADS)
    seg_terms, seg_soft = cross_entropy(seg_inside)
    part_terms, part_soft = cross_entropy(part_inside)
    edge_inside = lane == SEG
    edge_all = (
        jnp.maximum(logits, 0.0) + jnp.log1p(jnp.exp(-jnp.abs(logits))) - hot * logits
    )
    edge_soft = jax.nn.sigmoid(logits)
    weights = [weights_ref[task].astype(f32) for task in range(3)]
    weight_total = weights[0] + weights[1] + weights[2]
    row_lane = lax.broadcasted_iota(jnp.int32, (1, 128), 1)
    shares = jnp.where(
        row_lane < SEG, weights[0], jnp.where(row_lane == SEG, weights[1], weights[2])
    ) / jnp.full((1, 128), weight_total)
    shares = jnp.where(row_lane < HEADS, shares, 0.0)
    terms = jnp.where(lane == 0, seg_terms, 0.0) + jnp.where(edge_inside, edge_all, 0.0)
    terms = (terms + jnp.where(lane == SEG + 1, part_terms, 0.0)) * shares
    loss_local = jnp.sum(jnp.sum(terms, axis=0, keepdims=True), axis=1, keepdims=True) / 16384.0
    soft = seg_soft + part_soft + jnp.where(edge_inside, edge_soft, 0.0)
    logit_grad = ((soft - hot) * shares / 16384.0).astype(bf16)
    feature_back = against_rows(logit_grad, heads_ref[...]) * silu_grad(proj_normed)
    proj_sums = two_sums(feature_back, feature_back * proj_centered)
    totals[2].start(
        jnp.concatenate([proj_sums, jnp.broadcast_to(loss_local, (1, ASPP))], axis=0)
    )
    heads_out[0:256] = over_pixels(feature_map, logit_grad)
    heads_out[256:264] = jnp.broadcast_to(
        jnp.sum(logit_grad.astype(f32), axis=0, keepdims=True), (8, 128)
    )
    totals[2].middle()
    total = totals[2].finish()
    loss_out[...] = jnp.broadcast_to(total[2:3, 0:128], (8, 128))
    projected_grad = norm_grad(total, feature_back, proj_centered, proj_scale, last_gain)
    joined_grad = against_rows(projected_grad, project_ref[...])
    pool_map_grad = joined_grad[:, 4 * ASPP :]
    pool_local = jnp.concatenate(
        [jnp.sum(pool_map_grad * members[image], axis=0, keepdims=True) for image in range(4)], axis=0
    )
    branch_back = joined_grad[:, : 4 * ASPP] * silu_grad(normed)
    branch_sums = two_sums(branch_back, branch_back * centered)
    pool_row = jnp.concatenate([pool_local[image : image + 1] for image in range(4)], axis=1)
    totals[3].start(jnp.concatenate([branch_sums, pool_row], axis=0))
    project_out[...] = over_pixels(joined, projected_grad).astype(bf16)
    totals[3].middle()
    pool_slope = silu_grad(pool_pre)
    pool_pre_local = pool_local * pool_slope
    norms_out[0:1] = jnp.sum(pool_pre_local, axis=0, keepdims=True)
    for branch in range(4):
        lanes = slice(256 * branch, 256 * branch + 256)
        norms_out[1 + 2 * branch : 2 + 2 * branch] = branch_sums[1:2, lanes]
        norms_out[2 + 2 * branch : 3 + 2 * branch] = branch_sums[0:1, lanes]
    norms_out[9:10] = proj_sums[1:2]
    norms_out[10:11] = proj_sums[0:1]
    norms_out[11:16] = jnp.zeros((5, ASPP), f32)
    padding = jnp.zeros((4, ASPP), f32)
    pool_out[...] = over_pixels(
        pooled_low, jnp.concatenate([pool_pre_local, padding], axis=0).astype(bf16)
    ).astype(bf16)
    total = totals[3].finish()
    branch_grad = norm_grad(total, branch_back, centered, scale, gains)
    for branch in range(3):
        grads_own[branch] = branch_grad[:, 256 * branch + 256 : 256 * branch + 512].reshape(8, 16, 256)
        backward_shift.start(branch)

    def stack_high_copy(branch, sender):
        view = stack.at[branch, :, :, columns_of(sender)]
        return remote(
            view, view, links.sends.at[stack_high + branch], links.recvs.at[stack_high + branch], far_twin
        )

    def stack_core_copy(branch, place, sender_core):
        view = stack.at[branch, :, :, columns_of(2 * place + sender_core)]
        number = stack_core + 2 * branch + place
        return remote(view, view, links.sends.at[number], links.recvs.at[number], twin)

    pool_grad = jnp.concatenate(
        [total[2:3, 256 * image : 256 * image + 256] for image in range(4)], axis=0
    )
    pooled_grad = against_rows(
        jnp.concatenate([pool_grad * pool_slope, padding], axis=0).astype(bf16), pool_ref[...]
    )[0:4] / area
    for branch in range(3):
        backward_shift.finish(branch)
        for tap, direction in ((0, 1), (2, 0)):
            mask = across_lanes(pixel_mask(masks_ref[2 + 2 * branch + direction]), ASPP)
            shifted = grads_in[branch, direction].astype(f32).reshape(128, 256) * mask
            stack[branch, tap, :, columns_of(col)] = shifted.astype(bf16).reshape(8, 16, 256)
        stack[branch, 1, :, columns_of(col)] = grads_own[branch]
        stack_high_copy(branch, col).start()
    point_grad = branch_grad[:, 0:256]
    point_out[...] = over_pixels(grid, point_grad).astype(bf16)
    grad_out[...] = against_rows(point_grad, point_ref[...])
    for image in range(4):
        grad_out[...] = grad_out[...] + across_lanes(
            pixel_mask(members_low[image]), CIN
        ) * pooled_grad[image : image + 1]
    for branch in range(3):
        stack_high_copy(branch, col + 2 - 4 * high).wait_recv()
        for place in range(2):
            stack_core_copy(branch, place, core).start()
    slab_grad = None
    for branch, rate in enumerate(rate_list):
        for place in range(2):
            stack_core_copy(branch, place, 1 - core).wait_recv()
        for tap in range(3):
            padded[:, MARGIN : MARGIN + 64, 0:256] = stack[branch, tap].astype(f32)
            for col_tap in range(3):
                start = MARGIN - (col_tap - 1) * rate
                lanes = slice(256 * (3 * tap + col_tap), 256 * (3 * tap + col_tap) + 256)
                grad_taps[:, lanes] = (
                    padded[:, start : start + 64, 0:256].reshape(512, 256).astype(bf16)
                )
        rows = slice(2304 * branch, 2304 * branch + 2304)
        product = jnp.dot(grad_taps[...], kernels[rows], preferred_element_type=f32)
        slab_grad = product if slab_grad is None else slab_grad + product
        kernels[rows] = over_pixels(grad_taps[...], slab).astype(bf16)
    back_out[...] = slab_grad.astype(bf16).reshape(8, 64, 512)

    def back_copy(step, sender):
        return remote(
            back_out.at[:, columns_of(lax.rem(col + step, 4))],
            back_in.at[:, :, pl.ds(pl.multiple_of(sender * 512, 512), 512)],
            links.sends.at[back + step - 1],
            links.recvs.at[back + step - 1],
            device_of(row, lax.rem(col + step, 4)),
        )

    for step in (1, 2, 3):
        back_copy(step, col).start()
    back_in[:, :, pl.ds(pl.multiple_of(col * 512, 512), 512)] = back_out[:, columns_of(col)]

    def split(pair, carry):
        both = kernels[pl.ds(pl.multiple_of(432 * pair, 16), 432)].astype(f32)
        zeros = jnp.zeros((8, 512), f32)
        pieces_out[2 * pair] = jnp.concatenate([both[0:216], zeros], axis=0).astype(bf16)
        pieces_out[2 * pair + 1] = jnp.concatenate([both[216:432], zeros], axis=0).astype(bf16)
        return carry

    lax.fori_loop(0, 16, split, 0)
    for step in (1, 2, 3):
        copy = back_copy(step, lax.rem(col + 4 - step, 4))
        copy.wait_recv()
        copy.wait_send()
    grad_out[...] = grad_out[...] + back_in[...].reshape(128, CIN).astype(f32)
    for branch in range(3):
        for place in range(2):
            tap_core_copy(branch, place).wait_send()
            stack_core_copy(branch, place, core).wait_send()
        tap_high_copy(branch).wait_send()
        stack_high_copy(branch, col).wait_send()


def pyramid(arrays, collective):
    bf16, f32 = jnp.bfloat16, jnp.float32
    outs = [
        ((8, 128), f32),
        ((4, CIN), f32),
        ((128, CIN), f32),
        ((CIN, ASPP), bf16),
        ((CIN, ASPP), bf16),
        ((5 * ASPP, ASPP), bf16),
        ((264, 128), f32),
        ((16, ASPP), f32),
        ((32, RATE_ROWS, 512), bf16),
    ]
    scratch = [
        pltpu.VMEM((27 * ASPP, 512), bf16),
        pltpu.VMEM((8, 64 + 2 * MARGIN, 512), f32),
        pltpu.VMEM((6, 512, 512), bf16),
        pltpu.VMEM((9, 8, 64, ASPP), bf16),
        pltpu.VMEM((3, 2, 3, 8, 16, ASPP), bf16),
        pltpu.VMEM((3, 3, 8, 16, ASPP), bf16),
        pltpu.VMEM((3, 3, 8, 16, ASPP), bf16),
        pltpu.VMEM((3, 3, 8, 16, ASPP), f32),
        pltpu.VMEM((3, 2, 8, 16, ASPP), bf16),
        pltpu.VMEM((3, 2, 8, 16, ASPP), bf16),
        pltpu.VMEM((3, 8, 16, ASPP), bf16),
        pltpu.VMEM((3, 2, 8, 16, ASPP), bf16),
        pltpu.VMEM((3, 3, 8, 64, ASPP), bf16),
        pltpu.VMEM((512, 9 * ASPP), bf16),
        pltpu.VMEM((8, 64, 512), bf16),
        pltpu.VMEM((8, 16, CIN), bf16),
    ]
    for rows, columns in ((2, 4 * ASPP), (2, ASPP), (3, ASPP), (3, 4 * ASPP), (4, CIN + 128)):
        scratch += total_scratch(rows, columns)
    scratch += [pltpu.SemaphoreType.DMA((184,)), pltpu.SemaphoreType.DMA((184,))]
    in_specs = [VMEM] * len(arrays)
    in_specs[2] = ANY
    in_specs[-1] = SMEM
    return pl.pallas_call(
        pyramid_kernel,
        out_shape=[jax.ShapeDtypeStruct(shape, dtype) for shape, dtype in outs],
        in_specs=in_specs,
        out_specs=[VMEM] * len(outs),
        scratch_shapes=scratch,
        compiler_params=pltpu.CompilerParams(
            collective_id=collective, has_side_effects=True, vmem_limit_bytes=62 * MEGABYTE
        ),
    )(*arrays)


def per_device(
    features,
    image_rows,
    seg_labels,
    edge_labels,
    part_labels,
    task_weights,
    block_params,
    block_moment,
    head_params,
    head_moment,
    rate_params,
    rate_moment,
):
    height, across, channels = features.shape
    pixels = height * across
    inputs = features.reshape(pixels, channels)
    (
        w_reduce,
        w_spatial,
        w_expand,
        w_point,
        w_pool,
        w_project,
        misc,
        norms,
        masks,
        first_kept,
        second_kept,
        third_kept,
        second_act,
        block_window,
        grid,
        slab_map,
        rates_all,
    ) = block_forward(
        (
            inputs,
            block_params.reshape(BLOCK_ROWS, 128),
            head_params.reshape(HEAD_ROWS, 128),
            image_rows,
            rate_params.T,
        ),
        1,
    )
    w_heads = jnp.pad(
        misc[19:36].reshape(ASPP, HEADS).astype(jnp.bfloat16), ((0, 0), (0, 128 - HEADS))
    )
    heads_bias = jnp.broadcast_to(misc[36:37, :128], (8, 128))
    heads_bias = heads_bias * (jnp.arange(128) < HEADS).astype(jnp.float32)
    (
        loss_rows,
        pooled,
        out_grad,
        grad_point,
        grad_pool,
        grad_project,
        grad_heads,
        norm_grads,
        rate_pieces,
    ) = pyramid(
        (
            grid,
            slab_map,
            rates_all.reshape(32, RATE_ROWS, channels // 4),
            w_point,
            w_pool,
            w_project,
            misc,
            w_heads,
            heads_bias,
            masks,
            seg_labels,
            edge_labels,
            part_labels,
            task_weights,
        ),
        2,
    )
    loss_total = loss_rows[0, 0]
    heads_flat = jnp.concatenate([grad_heads[:ASPP, :HEADS].reshape(-1), grad_heads[ASPP, :HEADS]])
    heads_flat = jnp.pad(heads_flat, (0, 53 * ASPP - heads_flat.shape[0])).reshape(53, ASPP)
    misc_grads = jnp.concatenate(
        [norm_grads[:11], heads_flat], axis=0
    )
    input_grad, packed, rate_sum = block_backward(
        (
            inputs,
            out_grad,
            norms,
            masks,
            first_kept,
            second_kept,
            third_kept,
            second_act,
            block_window,
            w_reduce,
            w_spatial,
            w_expand,
            grad_point,
            grad_pool,
            grad_project,
            misc_grads,
            rate_pieces.reshape(2, 4, 4, RATE_ROWS, channels // 4),
        ),
        16,
    )
    rate_share = rate_sum[: rate_params.shape[1]].T
    shares_all = scatter_params(packed, 20)
    block_share = shares_all[:BLOCK_ROWS].reshape(-1)
    head_share = shares_all[BLOCK_ROWS : BLOCK_ROWS + HEAD_ROWS].reshape(-1)
    block_moment_next = MOMENTUM_KEEP * block_moment + block_share
    head_moment_next = MOMENTUM_KEEP * head_moment + head_share
    rate_moment_next = MOMENTUM_KEEP * rate_moment + rate_share
    return (
        loss_total,
        pooled,
        input_grad.reshape(height, across, channels),
        block_moment_next,
        head_moment_next,
        rate_moment_next,
    )


def solution(mesh):
    return jax.shard_map(
        per_device,
        mesh=mesh,
        in_specs=(
            P("rows", "cols", None),
            P("rows"),
            P("rows", "cols"),
            P("rows", "cols"),
            P("rows", "cols"),
            P(),
            P(("rows", "cols")),
            P(("rows", "cols")),
            P(("rows", "cols")),
            P(("rows", "cols")),
            P("cols", "rows"),
            P("cols", "rows"),
        ),
        out_specs=(
            P(),
            P(),
            P("rows", "cols", None),
            P(("rows", "cols")),
            P(("rows", "cols")),
            P("cols", "rows"),
        ),
        check_vma=False,
    )
```

```python
import functools
import math

import jax
import jax.numpy as jnp
from jax import lax
from jax.experimental import pallas as pl
from jax.experimental.pallas import tpu as pltpu
from jax.sharding import PartitionSpec as P

MESH = pl.DeviceIdType.MESH
ANY = pl.BlockSpec(memory_space=pl.ANY)
VMEM = pl.BlockSpec(memory_space=pltpu.VMEM)
SMEM = pl.BlockSpec(memory_space=pltpu.SMEM)
BLOCK_ROWS = 273
HEAD_ROWS = 85
PAYLOAD = 384

CIN = 2048
MID = 512
ASPP = 256
SEG = 13
PART = 3
HEADS = 17


EPSILON = 1e-05
MOMENTUM_KEEP = 0.5
rate_list = (6, 12, 18)
block_dilation = 4
widest_margin = 18


def device_of(row, col):
    return {"rows": row, "cols": col}


def split_place():
    row, col = lax.axis_index("rows"), lax.axis_index("cols")
    return {
        "y": (row // 16) + 2 * (col // 2),
        "x": lax.rem(row // 4, 4),
        "z": lax.rem(row, 4),
        "core": lax.rem(col, 2),
    }


def device_at(place):
    row = lax.rem(place["y"], 2) * 16 + place["x"] * 4 + place["z"]
    return device_of(row, (place["y"] // 2) * 2 + place["core"])


def moved(place, axis, step, extent=4):
    other = dict(place)
    other[axis] = lax.rem(place[axis] + step + extent, extent)
    return other


def meet(sources, targets):
    barrier = pltpu.get_barrier_semaphore()
    for device in sources:
        pl.semaphore_signal(barrier, inc=1, device_id=device, device_id_type=MESH)
    pl.semaphore_wait(barrier, targets)


def remote(source, target, send_sem, recv_sem, device):
    return pltpu.make_async_remote_copy(
        src_ref=source,
        dst_ref=target,
        send_sem=send_sem,
        recv_sem=recv_sem,
        device_id=device,
        device_id_type=MESH,
    )


GATHER_ORDERS = (("z", "x", "y"), ("x", "y", "z"), ("y", "z", "x"))


def axis_view(place, fixed):
    index = [slice(None)] * 4
    if "y" in fixed:
        index[0], index[3] = lax.rem(place["y"], 2), place["y"] // 2
    if "x" in fixed:
        index[1] = place["x"]
    if "z" in fixed:
        index[2] = place["z"]
    return tuple(index)


def scatter_kernel(p_ref, late_ref, pair_ref, o_ref, share_ref, held, rate_parts, rate_sums, rate_pair, *rest):
    relays = rest[0:3]
    parts = [rest[3 + 3 * third : 6 + 3 * third] for third in range(3)]
    sums = [rest[12 + 2 * third : 14 + 2 * third] for third in range(3)]
    links = Links(rest[-2], rest[-1])
    first, own_first = links.take(45), links.take(3)
    rates = RateScatter(links, late_ref, rate_parts)
    me = rates.me
    everywhere = (slice(None),) * 4
    own_copies = []
    for third in range(3):
        rows = pl.ds(third * 128, 128)
        own_copies.append(
            pltpu.make_async_copy(
                p_ref.at[everywhere + (rows,)],
                held.at[everywhere + (rows,)],
                links.sends.at[own_first + third],
            )
        )
        own_copies[third].start()
    partners = [moved(me, axis, step) for axis in "xyz" for step in (1, 2, 3)]
    meet([device_at(place) for place in partners], 9)
    rates.send()

    def view_of(third, phase, place, part=None):
        order = GATHER_ORDERS[third]
        axis = order[2 - phase]
        start, size = (0, 128) if part is None else (64 * part, 64)
        if phase == 0:
            return held.at[axis_view(place, [axis]) + (pl.ds(third * 128 + start, size),)]
        index = []
        for name, key in (("y", 0), ("x", 1), ("z", 2), ("y", 3)):
            if name not in order[: 3 - phase]:
                continue
            if name != axis:
                index.append(slice(None))
            elif name == "y":
                index.append(lax.rem(place["y"], 2) if key == 0 else place["y"] // 2)
            else:
                index.append(place[name])
        return sums[third][phase - 1].at[tuple(index) + (pl.ds(start, size),)]

    def link(third, phase, kind, step, outgoing, incoming):
        number = first + 15 * third + 5 * phase + (3 + step // 2 if kind else step - 1)
        return remote(
            outgoing,
            incoming,
            links.sends.at[number],
            links.recvs.at[number],
            device_at(moved(me, GATHER_ORDERS[third][2 - phase], step)),
        )

    def steps(phase):
        return (1, 2, 3) if phase else (1, 3)

    def relay(third, step):
        axis = GATHER_ORDERS[third][2]
        outgoing = view_of(third, 0, moved(me, axis, 2), step // 2)
        return link(third, 0, 1, step, outgoing, relays[third].at[step // 2])

    def copy(third, phase, step):
        axis = GATHER_ORDERS[third][2 - phase]
        outgoing = view_of(third, phase, moved(me, axis, step))
        slot = steps(phase).index(step)
        return link(third, phase, 0, step, outgoing, parts[third][phase].at[slot])

    for third in range(3):
        own_copies[third].wait()
        for step in (1, 3):
            relay(third, step).start()
    for third in range(3):
        axis = GATHER_ORDERS[third][2]
        for step in (1, 3):
            relay(third, step).wait_recv()
            view = view_of(third, 0, moved(me, axis, step), step // 2)
            view[...] = view[...] + relays[third][step // 2]
            copy(third, 0, step).start()
    rate_sums[0] = pair_ref[...]
    rates.collect(rate_sums.at[1])
    rate_exchange = rates.pair(rate_sums.at[1 - rates.low_y], rate_pair)
    rate_exchange.start()
    for phase in range(1, 4):
        for third in range(3):
            total = view_of(third, phase - 1, me)[...].astype(jnp.float32)
            for slot, step in enumerate(steps(phase - 1)):
                copy(third, phase - 1, step).wait_recv()
                total = total + parts[third][phase - 1][slot].astype(jnp.float32)
            if phase == 3:
                o_ref[128 * third : 128 * third + 128] = total
            else:
                sums[third][phase - 1][...] = total.astype(jnp.bfloat16)
                for step in steps(phase):
                    copy(third, phase, step).start()
    rate_exchange.wait()
    for half in range(2):
        rows = slice(half * (RATE_ROWS // 2), (half + 1) * (RATE_ROWS // 2))
        share_ref[rows] = rate_sums[rates.low_y, half].astype(jnp.float32) + rate_pair[half].astype(
            jnp.float32
        )
    for third in range(3):
        for step in (1, 3):
            relay(third, step).wait_send()
        for phase in range(3):
            for step in steps(phase):
                copy(third, phase, step).wait_send()


def scatter_params(arrays, collective):
    def shape_left(left, rows):
        shape = ()
        for name, number in (("y", 2), ("x", 4), ("z", 4), ("y", 2)):
            if name in left:
                shape += (number,)
        return shape + (rows, 128)

    relays = []
    parts = []
    sums = []
    for order in GATHER_ORDERS:
        relays.append(pltpu.VMEM((2,) + shape_left(order[:2], 64), jnp.bfloat16))
        for phase in range(3):
            number = 3 if phase else 2
            parts.append(pltpu.VMEM((number,) + shape_left(order[: 2 - phase], 128), jnp.bfloat16))
        for phase in range(2):
            sums.append(pltpu.VMEM(shape_left(order[: 2 - phase], 128), jnp.bfloat16))
    held = pltpu.VMEM((2, 4, 4, 2, PAYLOAD, 128), jnp.bfloat16)
    half = (2, RATE_ROWS // 2, 512)
    rates = [pltpu.VMEM(shape, jnp.bfloat16) for shape in ((2, 3) + half[1:], (2,) + half, half)]
    return pl.pallas_call(
        scatter_kernel,
        out_shape=[
            jax.ShapeDtypeStruct((PAYLOAD, 128), jnp.float32),
            jax.ShapeDtypeStruct((RATE_ROWS, 512), jnp.float32),
        ],
        in_specs=[ANY, VMEM, VMEM],
        out_specs=[VMEM, VMEM],
        scratch_shapes=[held]
        + rates
        + relays
        + parts
        + sums
        + [pltpu.SemaphoreType.DMA((64,)), pltpu.SemaphoreType.DMA((64,))],
        compiler_params=pltpu.CompilerParams(
            collective_id=collective, has_side_effects=True, vmem_limit_bytes=56 * MEGABYTE
        ),
    )(*arrays)


def neighbour(row, col, offset):
    return lax.rem(row + offset[0] + 32, 32), lax.rem(col + offset[1] + 4, 4)


MEGABYTE = 1024 * 1024
OFFSETS = (-4, 4, -6, 6, -12, 12, -18, 18)
ID_ROW = 368
RATE_ROWS = 224


class Links:
    def __init__(self, sends, recvs):
        self.sends, self.recvs = sends, recvs
        self.cursor = 0

    def take(self, number):
        first = self.cursor
        self.cursor = first + number
        return first


class Total:
    def __init__(self, links, value, near, far):
        self.links, self.value, self.near, self.far = links, value, near, far
        self.first = links.take(24)
        self.row, self.col = lax.axis_index("rows"), lax.axis_index("cols")
        self.near_me = (self.row // 16) * 4 + self.col
        self.far_me = lax.rem(self.row, 16)

    def near_device(self, index):
        return device_of((index // 4) * 16 + self.far_me, lax.rem(index, 4))

    def far_device(self, index):
        return device_of((self.row // 16) * 16 + index, self.col)

    def copy(self, far, step, slot):
        buffer, me, size = (self.far, self.far_me, 16) if far else (self.near, self.near_me, 8)
        base = self.first + (8 if far else 0)
        target = lax.rem(me + step, size)
        return remote(
            self.value,
            buffer.at[slot],
            self.links.sends.at[base + step],
            self.links.recvs.at[base + slot],
            self.far_device(target) if far else self.near_device(target),
        )

    def send(self, far):
        buffer, me, size = (self.far, self.far_me, 16) if far else (self.near, self.near_me, 8)
        for step in range(1, size):
            self.copy(far, step, me).start()
        buffer[me] = self.value[...]

    def collect(self, far):
        buffer, me, size = (self.far, self.far_me, 16) if far else (self.near, self.near_me, 8)
        for step in range(1, size):
            self.copy(far, step, lax.rem(me + step, size)).wait_recv()
        for step in range(1, size):
            self.copy(far, step, me).wait_send()
        total = buffer[0]
        for index in range(1, size):
            total = total + buffer[index]
        self.value[...] = total

    def start(self, value):
        self.value[...] = value
        self.send(False)

    def middle(self):
        self.collect(False)
        self.send(True)

    def finish(self):
        self.collect(True)
        return self.value[...]


def total_scratch(rows, columns):
    return [
        pltpu.VMEM((rows, columns), jnp.float32),
        pltpu.VMEM((8, rows, columns), jnp.float32),
        pltpu.VMEM((16, rows, columns), jnp.float32),
    ]


def total_peers():
    row, col = lax.axis_index("rows"), lax.axis_index("cols")
    near_me, far_me = (row // 16) * 4 + col, lax.rem(row, 16)
    peers = []
    for step in range(1, 8):
        index = lax.rem(near_me + step, 8)
        peers.append(device_of((index // 4) * 16 + far_me, lax.rem(index, 4)))
    for step in range(1, 16):
        peers.append(device_of((row // 16) * 16 + lax.rem(far_me + step, 16), col))
    return peers


def halo_peers():
    row, col = lax.axis_index("rows"), lax.axis_index("cols")
    return [
        device_of(*neighbour(row, col, (row_step, col_step)))
        for row_step in (-1, 0, 1)
        for col_step in (-1, 0, 1)
        if (row_step, col_step) != (0, 0)
    ]


class Halo:
    def __init__(self, links, source, window):
        self.links, self.source, self.window = links, source, window
        self.first = links.take(9)

    def copies(self, own_side):
        row, col = lax.axis_index("rows"), lax.axis_index("cols")
        listed = []
        for row_step in (-1, 0, 1):
            for col_step in (-1, 0, 1):
                if (row_step, col_step) == (0, 0):
                    continue
                low, size, top = {-1: (0, 4, 12), 0: (0, 8, 4), 1: (4, 4, 0)}[row_step]
                left = {-1: 32, 0: 16, 1: 0}[col_step]
                number = self.first + 3 * (row_step + 1) + col_step + 1
                listed.append(
                    remote(
                        self.source.at[pl.ds(low, size)],
                        self.window.at[pl.ds(top, size), pl.ds(left, 16)],
                        self.links.sends.at[number],
                        self.links.recvs.at[number],
                        device_of(*neighbour(row, col, (row_step, col_step))),
                    )
                )
        return listed

    def start(self):
        for copy in self.copies(True):
            copy.start()
        self.window[4:12, 16:32] = self.source[...]

    def finish(self):
        for copy in self.copies(False):
            copy.wait_recv()
        for copy in self.copies(False):
            copy.wait_send()


def widen_window(window, wide):
    col = lax.axis_index("cols")
    left = jnp.where(col > 0, 1.0, 0.0)
    right = jnp.where(col < 3, 1.0, 0.0)
    wide[:, 0:16] = window[:, 0:16].astype(jnp.float32) * left
    wide[:, 16:32] = window[:, 16:32].astype(jnp.float32)
    wide[:, 32:48] = window[:, 32:48].astype(jnp.float32) * right


def pixel_mask(mask):
    return jnp.broadcast_to(mask[:, None, :], (8, 16, 128)).reshape(128, 128)


def across_lanes(mask, width):
    return jnp.concatenate([mask] * (width // 128), axis=1)


class Gather:
    def __init__(self, links, source, target):
        self.links, self.source, self.target = links, source, target
        self.first = links.take(45)
        self.core_first = links.take(12)
        self.me = split_place()
        self.twin = moved(self.me, "core", 1, 2)

    def block(self, place, third, free, part=None):
        fixed = [axis for axis in "xyz" if axis not in free]
        rows = pl.ds(third * 128, 128) if part is None else pl.ds(third * 128 + 64 * part, 64)
        return self.target.at[axis_view(place, fixed) + (place["core"], rows)]

    def link(self, third, phase, kind, step, outgoing, incoming):
        number = self.first + 15 * third + 5 * phase + (3 + step // 2 if kind else step - 1)
        return remote(
            outgoing,
            incoming,
            self.links.sends.at[number],
            self.links.recvs.at[number],
            device_at(moved(self.me, GATHER_ORDERS[third][phase], step)),
        )

    def copy(self, third, phase, step, sender):
        free = GATHER_ORDERS[third][:phase]
        if phase == 0:
            outgoing = self.source.at[pl.ds(third * 128, 128)]
        else:
            outgoing = self.block(self.me, third, free)
        return self.link(third, phase, 0, step, outgoing, self.block(sender, third, free))

    def relay(self, third, phase, step, sender):
        order = GATHER_ORDERS[third]
        view = self.block(moved(sender, order[phase], 4 - step), third, order[:phase], step // 2)
        return self.link(third, phase, 1, step, view, view)

    def core_copy(self, third, distance, sender):
        order = GATHER_ORDERS[third]
        view = self.block(moved(sender, order[2], distance), third, order[:2])
        number = self.core_first + 4 * third + distance
        return remote(
            view, view, self.links.sends.at[number], self.links.recvs.at[number], device_at(self.twin)
        )

    def behind(self, third, phase, step):
        return moved(self.me, GATHER_ORDERS[third][phase], 4 - step)

    def steps(self, phase):
        return (1, 3) if phase == 2 else (1, 2, 3)

    def run(self, early, late):
        me = self.me
        for phase in range(3):
            for third in range(3):
                if phase > 0:
                    for step in (1, 2, 3):
                        self.copy(third, phase - 1, step, self.behind(third, phase - 1, step)).wait_recv()
                for step in self.steps(phase):
                    self.copy(third, phase, step, me).start()
                if phase == 0:
                    self.block(me, third, ())[...] = self.source[pl.ds(third * 128, 128)]
                if phase == 2:
                    self.core_copy(third, 0, me).start()
            if phase == 0:
                early()
        for third in range(3):
            for step in (1, 3):
                self.copy(third, 2, step, self.behind(third, 2, step)).wait_recv()
                self.relay(third, 2, step, me).start()
                self.core_copy(third, 4 - step, me).start()
        for third in range(3):
            for step in (1, 3):
                self.relay(third, 2, step, self.behind(third, 2, step)).wait_recv()
            self.core_copy(third, 2, me).start()
        late()
        for third in range(3):
            for distance in range(4):
                self.core_copy(third, distance, self.twin).wait_recv()

    def close(self):
        for third in range(3):
            for phase in range(3):
                for step in self.steps(phase):
                    self.copy(third, phase, step, self.me).wait_send()
            for step in (1, 3):
                self.relay(third, 2, step, self.me).wait_send()
            for distance in range(4):
                self.core_copy(third, distance, self.me).wait_send()


RATE_ORDERS = (("x", "z"), ("z", "x"))


class RateGather:
    def __init__(self, links, source, target):
        self.links, self.source, self.target = links, source, target
        self.first = links.take(82)
        self.me = split_place()
        self.low_y = lax.rem(self.me["y"], 2)
        self.other = dict(self.me)
        self.other["y"] = self.me["y"] + 1 - 2 * self.low_y
        self.half = RATE_ROWS // 2

    def own(self):
        return pltpu.make_async_copy(
            self.source,
            self.target.at[self.low_y, self.me["x"], self.me["z"]],
            self.links.recvs.at[self.first + 81],
        )

    def pair(self, sender):
        return remote(
            self.source,
            self.target.at[lax.rem(sender["y"], 2), self.me["x"], self.me["z"]],
            self.links.sends.at[self.first + 80],
            self.links.recvs.at[self.first + 80],
            device_at(self.other),
        )

    def axis(self, half, unit):
        return RATE_ORDERS[half][0 if unit < 2 else 1]

    def piece(self, half, unit, place, part=None):
        near = RATE_ORDERS[half][0]
        low_y = lax.rem(self.low_y + (unit if unit < 2 else (unit - 2) // 4), 2)
        places = {"x": place["x"], "z": place["z"]}
        if unit >= 2:
            places[near] = lax.rem(places[near] + (unit - 2) % 4, 4)
        start, size = {None: (0, 112), 0: (0, 64), 1: (64, 48)}[part]
        return self.target.at[low_y, places["x"], places["z"], pl.ds(half * self.half + start, size)]

    def link(self, half, unit, kind, step, view):
        number = self.first + 8 * unit + 4 * half + 2 * kind + step // 2
        return remote(
            view,
            view,
            self.links.sends.at[number],
            self.links.recvs.at[number],
            device_at(moved(self.me, self.axis(half, unit), step)),
        )

    def copy(self, half, unit, step, sender):
        return self.link(half, unit, 0, step, self.piece(half, unit, sender))

    def relay(self, half, unit, step, sender):
        first = moved(sender, self.axis(half, unit), 4 - step)
        return self.link(half, unit, 1, step, self.piece(half, unit, first, step // 2))

    def behind(self, half, unit, step):
        return moved(self.me, self.axis(half, unit), 4 - step)

    def each(self):
        return [(half, step) for half in range(2) for step in (1, 3)]

    def begin(self):
        self.own().start()
        self.pair(self.me).start()

    def send(self, *units):
        for unit in units:
            if unit == 0:
                self.own().wait()
            if unit == 1:
                self.pair(self.other).wait_recv()
            for half, step in self.each():
                self.copy(half, unit, step, self.me).start()

    def forward(self, *units):
        for unit in units:
            for half, step in self.each():
                self.copy(half, unit, step, self.behind(half, unit, step)).wait_recv()
                self.relay(half, unit, step, self.me).start()

    def receive(self, *units):
        for unit in units:
            for half, step in self.each():
                self.relay(half, unit, step, self.behind(half, unit, step)).wait_recv()

    def close(self):
        self.pair(self.me).wait_send()
        for unit in range(10):
            for half, step in self.each():
                self.copy(half, unit, step, self.me).wait_send()
                self.relay(half, unit, step, self.me).wait_send()


def assemble(gathered, first_row_group, staging, wide, stride):
    parts = len(wide)
    count, offset = (BLOCK_ROWS, 0) if parts == 4 else (HEAD_ROWS, BLOCK_ROWS)

    def step(group, carry):
        low_y, x, z = first_row_group // 16, group // 4, lax.rem(group, 4)
        for column in range(4):
            area = staging[column]
            if parts == 4:
                area[0:288] = gathered[low_y, x, z, column // 2, column % 2, 0:288].astype(jnp.float32)
            else:
                area[0:96] = gathered[low_y, x, z, column // 2, column % 2, 272:368].astype(jnp.float32)
            skip = offset - (0 if parts == 4 else 272)
            for part in range(parts):
                begin = (part - column * count) % parts
                number = (count - begin + parts - 1) // parts
                row = (column * count + begin - part) // parts
                group_rows = 4 * count // parts
                target = group_rows * (group + stride) + row
                wide[part][pl.ds(target, number), :] = area[
                    pl.ds(skip + begin, number, stride=parts), :
                ]
        return carry

    lax.fori_loop(0, 16, step, 0)


def wide_rows(wide, first, number):
    return jnp.concatenate([part[pl.ds(first, number), :] for part in wide], axis=1)


def block_forward_kernel(
    x_ref,
    block_ref,
    head_ref,
    image_ref,
    rate_params_ref,
    reduce_hbm,
    spatial_hbm,
    expand_hbm,
    point_hbm,
    pool_hbm,
    project_hbm,
    misc_ref,
    norms_ref,
    masks_ref,
    first_ref,
    second_ref,
    third_ref,
    act_ref,
    window_ref,
    out_ref,
    slab_ref,
    rates_ref,
    gathered,
    s0,
    s1,
    s2,
    s3,
    w0,
    w1,
    w2,
    w3,
    h0,
    h1,
    ids,
    wide,
    act_map,
    payload_wide,
    payload_ref,
    rate_ref,
    reduce_ref,
    spatial_ref,
    expand_ref,
    point_ref,
    pool_ref,
    project_ref,
    *rest,
):
    staging, matrix, head = (s0, s1, s2, s3), (w0, w1, w2, w3), (h0, h1)
    links = Links(rest[-2], rest[-1])
    totals = [Total(links, *rest[3 * number : 3 * number + 3]) for number in range(3)]
    payload_wide[0:BLOCK_ROWS, :] = block_ref[...]
    payload_wide[BLOCK_ROWS : BLOCK_ROWS + HEAD_ROWS, :] = head_ref[...]
    payload_wide[BLOCK_ROWS + HEAD_ROWS : PAYLOAD, :] = jnp.zeros(
        (PAYLOAD - BLOCK_ROWS - HEAD_ROWS, 128), jnp.float32
    )
    for step in range(8):
        payload_wide[ID_ROW + step : ID_ROW + step + 1, :] = jnp.full(
            (1, 128), image_ref[step].astype(jnp.float32)
        )
    payload_ref[...] = payload_wide[...].astype(jnp.bfloat16)
    rate_ref[...] = jnp.concatenate(
        [rate_params_ref[...], jnp.zeros((RATE_ROWS - 216, 512), jnp.float32)], axis=0
    ).astype(jnp.bfloat16)
    gather = Gather(links, payload_ref, gathered)
    rates = RateGather(links, rate_ref, rates_ref)
    halo = Halo(links, act_map, window_ref)
    slab_first = links.take(3)
    out_first = links.take(6)
    stores = [
        pltpu.make_async_copy(source, target, links.sends.at[out_first + number])
        for number, (source, target) in enumerate(
            (
                (reduce_ref, reduce_hbm),
                (spatial_ref, spatial_hbm),
                (expand_ref, expand_hbm),
                (point_ref, point_hbm),
                (pool_ref, pool_hbm),
                (project_ref, project_hbm),
            )
        )
    ]
    row, col = lax.axis_index("rows"), lax.axis_index("cols")
    peers = total_peers() + halo_peers()
    meet(peers, len(peers))

    def rates_early():
        rates.begin()
        rates.send(0)

    def rates_late():
        rates.forward(0)
        rates.send(2, 1)

    gather.run(rates_early, rates_late)

    for step in range(-3, 4):
        other = lax.rem(row + step + 32, 32)
        rows_there = gathered[
            other // 16, lax.rem(other // 4, 4), lax.rem(other, 4), 0, 0, ID_ROW : ID_ROW + 16
        ].astype(jnp.float32)[0:8]
        inside = jnp.logical_and(row + step >= 0, row + step < 32)
        ids[8 * (step + 3) : 8 * (step + 3) + 8, :] = jnp.where(inside, rows_there, -1.0)
    own_ids = ids[24:32, :]
    for number, offset in enumerate(OFFSETS):
        masks_ref[number] = jnp.where(ids[24 + offset : 32 + offset, :] == own_ids, 1.0, 0.0)
    masks_ref[len(OFFSETS)] = own_ids

    assemble(gathered, 0, staging, matrix, 0)
    for step in range(8):
        reduce_ref[256 * step : 256 * step + 256] = wide_rows(matrix, 256 * step, 256).astype(jnp.bfloat16)
    first = jnp.dot(x_ref[...], reduce_ref[...], preferred_element_type=jnp.float32)
    totals[0].start(
        jnp.concatenate(
            [jnp.sum(first, axis=0, keepdims=True), jnp.sum(first * first, axis=0, keepdims=True)], axis=0
        )
    )
    for step in range(5):
        spatial_ref[464 * step : 464 * step + 464] = wide_rows(matrix, 2048 + 464 * step, 464).astype(
            jnp.bfloat16
        )
    totals[0].middle()
    assemble(gathered, 16, staging, matrix, 0)
    for step in range(13):
        spatial_ref[2320 + 176 * step : 2320 + 176 * step + 176] = wide_rows(
            matrix, 176 * step, 176
        ).astype(jnp.bfloat16)
    for part in range(4):
        expand_ref[:, 512 * part : 512 * part + 512] = jnp.concatenate(
            [array[pl.ds(2288 + part, 512, stride=4), :] for array in matrix], axis=1
        ).astype(jnp.bfloat16)
    norms_ref[...] = wide_rows(matrix, 4336, 16)
    for store in stores[0:3]:
        store.start()

    def normal(total, values, gain, shift, kept):
        average = total[0:1] / 16384.0
        variance = total[1:2] / 16384.0 - average * average
        scale = lax.rsqrt(variance + EPSILON)
        centered = (values - average) * scale
        kept[0:128] = centered
        kept[128:136] = jnp.broadcast_to(scale, (8, scale.shape[1]))
        return centered * gain + shift

    def silu(values):
        return values * jax.nn.sigmoid(values)

    def stats(values):
        return jnp.concatenate(
            [jnp.sum(values, axis=0, keepdims=True), jnp.sum(values * values, axis=0, keepdims=True)], axis=0
        )

    normed = normal(totals[0].finish(), first, norms_ref[0:1], norms_ref[1:2], first_ref)
    act_map[...] = silu(normed).astype(jnp.bfloat16).reshape(8, 16, MID)
    halo.start()
    rates.forward(2, 1)
    rates.receive(0)
    rates.send(3, 4)
    halo.finish()
    widen_window(window_ref, wide)
    second = None
    for row_tap in range(3):
        part = None
        for col_tap in range(3):
            tap = 3 * row_tap + col_tap
            region = wide[4 * row_tap : 4 * row_tap + 8, 12 + 4 * col_tap : 28 + 4 * col_tap]
            product = jnp.dot(
                region.reshape(128, MID).astype(jnp.bfloat16),
                spatial_ref[512 * tap : 512 * tap + 512],
                preferred_element_type=jnp.float32,
            )
            part = product if part is None else part + product
        if row_tap != 1:
            part = part * across_lanes(pixel_mask(masks_ref[row_tap // 2]), MID)
        second = part if second is None else second + part
    totals[1].start(stats(second))
    assemble(gathered, 0, staging, head, 0)
    assemble(gathered, 16, staging, head, 16)
    totals[1].middle()
    for step in range(8):
        point_ref[256 * step : 256 * step + 256] = wide_rows(head, 256 * step, 256).astype(jnp.bfloat16)
        pool_ref[256 * step : 256 * step + 256] = wide_rows(head, 2048 + 256 * step, 256).astype(jnp.bfloat16)
    for step in range(5):
        project_ref[256 * step : 256 * step + 256] = wide_rows(head, 4097 + 256 * step, 256).astype(
            jnp.bfloat16
        )
    for store in stores[3:6]:
        store.start()
    misc_ref[0:8] = wide_rows(head, 4096, 8)
    misc_ref[8:72] = wide_rows(head, 5376, 64)
    normed = normal(totals[1].finish(), second, norms_ref[2:3], norms_ref[3:4], second_ref)
    rates.forward(3, 4)
    rates.receive(1)
    rates.send(5, 6)
    act_ref[...] = silu(normed).astype(jnp.bfloat16)
    third = jnp.dot(act_ref[...], expand_ref[...], preferred_element_type=jnp.float32)
    totals[2].start(stats(third))
    totals[2].middle()
    out_gain = jnp.concatenate([norms_ref[4 + part : 5 + part] for part in range(4)], axis=1)
    out_shift = jnp.concatenate([norms_ref[8 + part : 9 + part] for part in range(4)], axis=1)
    normed = normal(totals[2].finish(), third, out_gain, out_shift, third_ref)
    block_out = silu(normed + x_ref[...].astype(jnp.float32)).astype(jnp.bfloat16)
    out_ref[...] = block_out.reshape(8, 16, CIN)

    def slab_copy(step, sender):
        return remote(
            out_ref.at[:, :, pl.ds(pl.multiple_of(lax.rem(col + step, 4) * 512, 512), 512)],
            slab_ref.at[:, pl.ds(pl.multiple_of(sender * 16, 16), 16)],
            links.sends.at[slab_first + step - 1],
            links.recvs.at[slab_first + step - 1],
            device_of(row, lax.rem(col + step, 4)),
        )

    for step in (1, 2, 3):
        slab_copy(step, col).start()
    rates.forward(5, 6)
    rates.send(7, 8, 9)
    slab_ref[:, pl.ds(pl.multiple_of(col * 16, 16), 16)] = out_ref[
        :, :, pl.ds(pl.multiple_of(col * 512, 512), 512)
    ]
    for step in (1, 2, 3):
        copy = slab_copy(step, lax.rem(col + 4 - step, 4))
        copy.wait_recv()
        copy.wait_send()
    rates.forward(7, 8, 9)
    rates.receive(2, 3, 4, 5, 6, 7, 8, 9)
    rates.close()
    gather.close()
    for store in stores:
        store.wait()


def block_forward(arrays, collective):
    bf16, f32 = jnp.bfloat16, jnp.float32
    outs = [
        ((CIN, MID), bf16),
        ((9 * MID, MID), bf16),
        ((MID, CIN), bf16),
        ((CIN, ASPP), bf16),
        ((CIN, ASPP), bf16),
        ((5 * ASPP, ASPP), bf16),
        ((72, ASPP), f32),
        ((16, MID), f32),
        ((9, 8, 128), f32),
        ((136, MID), f32),
        ((136, MID), f32),
        ((136, CIN), f32),
        ((128, MID), bf16),
        ((16, 48, MID), bf16),
        ((8, 16, CIN), bf16),
        ((8, 64, CIN // 4), bf16),
        ((2, 4, 4, RATE_ROWS, CIN // 4), bf16),
    ]
    scratch = [pltpu.VMEM((2, 4, 4, 2, 2, PAYLOAD, 128), bf16)]
    scratch += [pltpu.VMEM((288, 128), f32)] * 4
    scratch += [pltpu.VMEM((4368, 128), f32)] * 4
    scratch += [pltpu.VMEM((5440, 128), f32)] * 2
    scratch += [
        pltpu.VMEM((56, 128), f32),
        pltpu.VMEM((16, 48, MID), f32),
        pltpu.VMEM((8, 16, MID), bf16),
        pltpu.VMEM((PAYLOAD, 128), f32),
        pltpu.VMEM((PAYLOAD, 128), bf16),
        pltpu.VMEM((RATE_ROWS, 512), bf16),
    ]
    scratch += [pltpu.VMEM(shape, dtype) for shape, dtype in outs[:6]]
    for rows, columns in ((2, MID), (2, MID), (2, CIN)):
        scratch += total_scratch(rows, columns)
    scratch += [pltpu.SemaphoreType.DMA((248,)), pltpu.SemaphoreType.DMA((248,))]
    return pl.pallas_call(
        block_forward_kernel,
        out_shape=[jax.ShapeDtypeStruct(shape, dtype) for shape, dtype in outs],
        in_specs=[VMEM, VMEM, VMEM, SMEM, VMEM],
        out_specs=[ANY] * 6 + [VMEM] * 10 + [ANY],
        scratch_shapes=scratch,
        compiler_params=pltpu.CompilerParams(
            collective_id=collective, has_side_effects=True, vmem_limit_bytes=60 * MEGABYTE
        ),
    )(*arrays)


class RatePieces:
    def __init__(self, links, units):
        self.links = links
        self.first = links.take(8 * units + 4)
        self.extra = self.first + 8 * units
        self.me = split_place()
        self.low_y = lax.rem(self.me["y"], 2)
        self.other = dict(self.me)
        self.other["y"] = self.me["y"] + 1 - 2 * self.low_y

    def rows(self, half):
        return pl.ds(half * (RATE_ROWS // 2), RATE_ROWS // 2)

    def piece(self, array, half, low_y, first_axis, second_axis):
        places = {RATE_ORDERS[half][0]: first_axis, RATE_ORDERS[half][1]: second_axis}
        return array.at[low_y, places["x"], places["z"], self.rows(half)]

    def remote(self, unit, half, slot, outgoing, incoming, axis, step):
        number = self.first + 8 * unit + 4 * half + slot
        return remote(
            outgoing,
            incoming,
            self.links.sends.at[number],
            self.links.recvs.at[number],
            device_at(moved(self.me, axis, step)),
        )

    def each(self):
        return [(half, step) for half in range(2) for step in (1, 2, 3)]


class RateFirst(RatePieces):
    def __init__(self, links, pieces, own, relays, parts, low_y):
        super().__init__(links, 4)
        self.pieces, self.own, self.relays, self.parts, self.from_y = pieces, own, relays, parts, low_y
        loads = links.take(6)
        self.loads = []
        for half in range(2):
            near, far = RATE_ORDERS[half]
            for slot, step in enumerate((0, 1, 3)):
                places = {near: slice(None), far: moved(self.me, far, step)[far]}
                self.loads.append(
                    pltpu.make_async_copy(
                        pieces.at[low_y, places["x"], places["z"], self.rows(half)],
                        own.at[half, slot],
                        links.recvs.at[loads + 3 * half + slot],
                    )
                )

    def part(self, step):
        return pl.ds(0, 64) if step == 1 else pl.ds(64, 48)

    def relay(self, unit, half, step):
        far = RATE_ORDERS[half][1]
        places = {RATE_ORDERS[half][0]: unit, far: moved(self.me, far, 2)[far]}
        rows = self.part(step)
        start = half * (RATE_ROWS // 2) + rows.start
        return self.remote(
            unit,
            half,
            step // 2 + 2,
            self.pieces.at[self.from_y, places["x"], places["z"], pl.ds(start, rows.size)],
            self.relays.at[half, unit, rows],
            far,
            step,
        )

    def copy(self, unit, half, step):
        far = RATE_ORDERS[half][1]
        slot = step // 2
        return self.remote(
            unit, half, slot, self.own.at[half, 1 + slot, unit], self.parts.at[half, unit, slot], far, step
        )

    def each(self):
        return [(half, step) for half in range(2) for step in (1, 3)]

    def send(self, *units):
        for unit in units:
            for half, step in self.each():
                self.relay(unit, half, step).start()

    def forward(self, *units):
        for unit in units:
            for half, step in self.each():
                self.relay(unit, half, step).wait_recv()
                rows = self.part(step)
                place = (half, 1 + step // 2, unit, rows)
                self.own[place] = self.own[place] + self.relays[half, unit, rows]
                self.copy(unit, half, step).start()

    def collect(self, *units):
        for unit in units:
            for half in range(2):
                total = self.own[half, 0, unit].astype(jnp.float32)
                for step in (1, 3):
                    self.copy(unit, half, step).wait_recv()
                    total = total + self.parts[half, unit, step // 2].astype(jnp.float32)
                self.own[half, 0, unit] = total.astype(jnp.bfloat16)
            for half, step in self.each():
                self.relay(unit, half, step).wait_send()
                self.copy(unit, half, step).wait_send()


class RateScatter(RatePieces):
    def __init__(self, links, sums, parts):
        super().__init__(links, 1)
        self.sums, self.parts = sums, parts

    def copy(self, half, step):
        near = RATE_ORDERS[half][0]
        outgoing = self.sums.at[half, moved(self.me, near, step)[near]]
        return self.remote(0, half, step - 1, outgoing, self.parts.at[half, step - 1], near, step)

    def pair(self, outgoing, incoming):
        return remote(
            outgoing,
            incoming,
            self.links.sends.at[self.extra],
            self.links.recvs.at[self.extra],
            device_at(self.other),
        )

    def send(self):
        for half, step in self.each():
            self.copy(half, step).start()

    def collect(self, target):
        for half in range(2):
            total = self.sums[half, self.me[RATE_ORDERS[half][0]]].astype(jnp.float32)
            for step in (1, 2, 3):
                self.copy(half, step).wait_recv()
                total = total + self.parts[half, step - 1].astype(jnp.float32)
            target[half] = total.astype(jnp.bfloat16)
        for half, step in self.each():
            self.copy(half, step).wait_send()


def disassemble(packed, first_row_group, staging, wide, stride):
    parts = len(wide)
    core = lax.rem(lax.axis_index("cols"), 2)
    count = BLOCK_ROWS if parts == 4 else HEAD_ROWS
    low_y = first_row_group // 16

    def step(group, carry):
        x, z = group // 4, lax.rem(group, 4)
        for column in range(4):
            area = staging[column]
            here = (lax.rem(column + core, 2), low_y, x, z, column // 2)
            if parts == 4:
                skip = 0
                area[272:288] = packed[here + (slice(272, 288),)].astype(jnp.float32)
            else:
                skip = 1
                area[80:112] = jnp.zeros((32, 128), jnp.float32)
            for part in range(parts):
                begin = (part - column * count) % parts
                number = (count - begin + parts - 1) // parts
                row = (column * count + begin - part) // parts
                origin = (4 * count // parts) * (group + stride) + row
                area[pl.ds(skip + begin, number, stride=parts), :] = wide[part][
                    pl.ds(origin, number), :
                ]
            if parts == 4:
                packed[here + (slice(0, 288),)] = area[0:288].astype(jnp.bfloat16)
            else:
                packed[here + (slice(272, 384),)] = area[0:112].astype(jnp.bfloat16)
        return carry

    lax.fori_loop(0, 16, step, 0)


def deal(wide, first, values):
    number = values.shape[0]
    for part, array in enumerate(wide):
        array[first : first + number, :] = values[:, 128 * part : 128 * part + 128]


def against_rows(left, right):
    return lax.dot_general(left, right, (((1,), (1,)), ((), ())), preferred_element_type=jnp.float32)


def over_pixels(left, right):
    return lax.dot_general(left, right, (((0,), (0,)), ((), ())), preferred_element_type=jnp.float32)


def block_backward_kernel(
    x_ref,
    grad_ref,
    norms_ref,
    masks_ref,
    first_ref,
    second_ref,
    third_ref,
    act_ref,
    window_ref,
    reduce_hbm,
    spatial_hbm,
    expand_hbm,
    point_ref,
    pool_ref,
    project_ref,
    misc_ref,
    pieces_ref,
    out_ref,
    held_ref,
    late_ref,
    pair_ref,
    s0,
    s1,
    s2,
    s3,
    w0,
    w1,
    w2,
    w3,
    wide,
    act_map,
    window,
    packed,
    twin_part,
    reduce_ref,
    spatial_ref,
    expand_ref,
    free_sem,
    *rest,
):
    staging, matrix, head = (s0, s1, s2, s3), (w0, w1, w2, w3), (w0, w1)
    links = Links(rest[-2], rest[-1])
    totals = [Total(links, *rest[3 * number : 3 * number + 3]) for number in range(3)]
    own, relays, first_parts, second_parts = rest[9:13]
    rates = [
        RateFirst(links, pieces_ref, own.at[low_y], relays.at[low_y], first_parts.at[low_y], low_y)
        for low_y in range(2)
    ]
    scatter = RateScatter(links, own.at[0, :, 0], second_parts)
    me = scatter.me
    twin = device_at(moved(me, "core", 1, 2))
    halo = Halo(links, act_map, window)
    load_first, twin_first, out_first = (links.take(number) for number in (3, 2, 2))
    loads = [
        pltpu.make_async_copy(source, target, links.recvs.at[load_first + number])
        for number, (source, target) in enumerate(
            ((expand_hbm, expand_ref), (spatial_hbm, spatial_ref), (reduce_hbm, reduce_ref))
        )
    ]
    for copy in loads + rates[0].loads + rates[1].loads:
        copy.start()

    def twin_copy(low_y):
        return remote(
            packed.at[1, low_y],
            twin_part,
            links.sends.at[twin_first + low_y],
            links.recvs.at[twin_first + low_y],
            twin,
        )

    def out_copy(low_y):
        return pltpu.make_async_copy(
            packed.at[0, low_y], held_ref.at[low_y], links.sends.at[out_first + low_y]
        )

    def join_twin(low_y):
        twin_copy(low_y).wait_recv()

        def add_block(index, carry):
            place = (index // 8, lax.rem(index // 2, 4), lax.rem(index, 2))
            packed[(0, low_y) + place] = packed[(0, low_y) + place] + twin_part[place]
            return carry

        lax.fori_loop(0, 32, add_block, 0)
        out_copy(low_y).start()

    peers = total_peers() + halo_peers()
    meet(peers, len(peers))

    def slope(values):
        part = jax.nn.sigmoid(values)
        return part * (1.0 + values * (1.0 - part))

    def local_sums(grad, kept):
        return jnp.concatenate(
            [
                jnp.sum(grad, axis=0, keepdims=True),
                jnp.sum(grad * kept[0:128], axis=0, keepdims=True),
            ],
            axis=0,
        )

    def through_norm(total, grad, kept, gain):
        return (
            gain
            * kept[128:129]
            * (grad - total[0:1] / 16384.0 - kept[0:128] * (total[1:2] / 16384.0))
        ).astype(jnp.bfloat16)

    rates[0].send(0, 1, 2, 3)
    out_gain = jnp.concatenate([norms_ref[4 + part : 5 + part] for part in range(4)], axis=1)
    out_shift = jnp.concatenate([norms_ref[8 + part : 9 + part] for part in range(4)], axis=1)
    residual = third_ref[0:128] * out_gain + out_shift + x_ref[...].astype(jnp.float32)
    out_ref[...] = grad_ref[...] * slope(residual)
    third_sums = local_sums(out_ref[...], third_ref)
    totals[0].start(third_sums)
    for step in range(4):
        deal(head, 512 * step, point_ref[512 * step : 512 * step + 512].astype(jnp.float32))
    deal(head, 2048, pool_ref[0:672].astype(jnp.float32))
    disassemble(packed, 0, staging, head, 0)
    totals[0].middle()
    for step in range(4):
        deal(head, 344 * step, pool_ref[672 + 344 * step : 1016 + 344 * step].astype(jnp.float32))
    deal(head, 1376, misc_ref[0:1])
    for step in range(5):
        deal(head, 1377 + 256 * step, project_ref[256 * step : 256 * step + 256].astype(jnp.float32))
    deal(head, 2657, misc_ref[1:64])
    disassemble(packed, 16, staging, head, 0)
    third_grad = through_norm(totals[0].finish(), out_ref[...], third_ref, out_gain)
    for copy in rates[0].loads + rates[1].loads:
        copy.wait()
    rates[0].forward(0, 1)
    loads[0].wait()
    second_gain, second_shift = norms_ref[2:3], norms_ref[3:4]
    second_norm = second_ref[0:128] * second_gain + second_shift
    second_back = against_rows(third_grad, expand_ref[...]) * slope(second_norm)
    second_sums = local_sums(second_back, second_ref)
    totals[1].start(second_sums)
    for part in range(4):
        product = over_pixels(act_ref[...], third_grad[:, 512 * part : 512 * part + 512])
        for number, array in enumerate(matrix):
            array[pl.ds(2288 + part, 512, stride=4), :] = product[:, 128 * number : 128 * number + 128]
    totals[1].middle()
    widen_window(window_ref, wide)
    second_grad = through_norm(totals[1].finish(), second_back, second_ref, second_gain)
    act_map[...] = second_grad.reshape(8, 16, MID)
    halo.start()
    rates[0].forward(2, 3)
    rates[1].send(0, 1, 2, 3)

    def spatial_grad(tap):
        row_tap, col_tap = tap // 3, tap % 3
        region = wide[4 * row_tap : 4 * row_tap + 8, 12 + 4 * col_tap : 28 + 4 * col_tap].reshape(128, MID)
        if row_tap != 1:
            region = region * across_lanes(pixel_mask(masks_ref[row_tap // 2]), MID)
        return over_pixels(region.astype(jnp.bfloat16), second_grad)

    middle_tap = spatial_grad(4)
    deal(matrix, 0, middle_tap[272:512])
    for tap in range(5, 9):
        deal(matrix, 240 + 512 * (tap - 5), spatial_grad(tap))
    halo.finish()
    rates[0].collect(0, 1, 2, 3)
    scatter.send()
    widen_window(window, wide)
    loads[1].wait()
    first_back = None
    for row_tap in range(3):
        part = None
        for col_tap in range(3):
            tap = 3 * row_tap + col_tap
            region = wide[
                8 - 4 * row_tap : 16 - 4 * row_tap, 20 - 4 * col_tap : 36 - 4 * col_tap
            ]
            product = against_rows(
                region.reshape(128, MID).astype(jnp.bfloat16), spatial_ref[512 * tap : 512 * tap + 512]
            )
            part = product if part is None else part + product
        if row_tap != 1:
            part = part * across_lanes(pixel_mask(masks_ref[1 - row_tap // 2]), MID)
        first_back = part if first_back is None else first_back + part
    first_gain, first_shift = norms_ref[0:1], norms_ref[1:2]
    first_back = first_back * slope(first_ref[0:128] * first_gain + first_shift)
    first_sums = local_sums(first_back, first_ref)
    totals[2].start(first_sums)
    deal(matrix, 4336, first_sums[1:2])
    deal(matrix, 4337, first_sums[0:1])
    deal(matrix, 4338, second_sums[1:2])
    deal(matrix, 4339, second_sums[0:1])
    for part in range(4):
        deal(matrix, 4340 + part, third_sums[1:2, 512 * part : 512 * part + 512])
        deal(matrix, 4344 + part, third_sums[0:1, 512 * part : 512 * part + 512])
    deal(matrix, 4348, jnp.zeros((20, MID), jnp.float32))
    disassemble(packed, 16, staging, matrix, 0)
    twin_copy(1).start()
    totals[2].middle()
    widen_window(window_ref, wide)
    deal(matrix, 4096, middle_tap[0:272])
    for tap in range(4):
        deal(matrix, 2048 + 512 * tap, spatial_grad(tap))
    first_total = totals[2].finish()
    rates[1].forward(0, 1, 2, 3)
    join_twin(1)
    pl.semaphore_signal(free_sem, inc=1, device_id=twin, device_id_type=MESH)
    loads[2].wait()
    first_grad = through_norm(first_total, first_back, first_ref, first_gain)
    for part in range(4):
        rows = slice(512 * part, 512 * part + 512)
        deal(matrix, 512 * part, over_pixels(x_ref[:, rows], first_grad))
        out_ref[:, rows] = out_ref[:, rows] + against_rows(first_grad, reduce_ref[rows])
    disassemble(packed, 0, staging, matrix, 0)
    pl.semaphore_wait(free_sem, 1)
    twin_copy(0).start()
    rates[1].collect(0, 1, 2, 3)
    late_ref[...] = own[1, :, 0]
    scatter.collect(pair_ref)
    join_twin(0)
    for low_y in range(2):
        twin_copy(low_y).wait_send()
        out_copy(low_y).wait()


def block_backward(arrays, collective):
    bf16, f32 = jnp.bfloat16, jnp.float32
    half = RATE_ROWS // 2
    scratch = [pltpu.VMEM((384, 128), f32)] * 4
    scratch += [pltpu.VMEM((4368, 128), f32)] * 4
    scratch += [
        pltpu.VMEM((16, 48, MID), f32),
        pltpu.VMEM((8, 16, MID), bf16),
        pltpu.VMEM((16, 48, MID), bf16),
        pltpu.VMEM((2, 2, 4, 4, 2, PAYLOAD, 128), bf16),
        pltpu.VMEM((4, 4, 2, PAYLOAD, 128), bf16),
        pltpu.VMEM((CIN, MID), bf16),
        pltpu.VMEM((9 * MID, MID), bf16),
        pltpu.VMEM((MID, CIN), bf16),
        pltpu.SemaphoreType.REGULAR,
    ]
    for rows, columns in ((2, CIN), (2, MID), (2, MID)):
        scratch += total_scratch(rows, columns)
    scratch += [
        pltpu.VMEM((2, 2, 3, 4, half, 512), bf16),
        pltpu.VMEM((2, 2, 4, half, 512), bf16),
        pltpu.VMEM((2, 2, 4, 2, half, 512), bf16),
        pltpu.VMEM((2, 3, half, 512), bf16),
    ]
    scratch += [pltpu.SemaphoreType.DMA((232,)), pltpu.SemaphoreType.DMA((232,))]
    outs = [
        ((128, CIN), f32),
        ((2, 4, 4, 2, PAYLOAD, 128), bf16),
        ((2, 4, half, 512), bf16),
        ((2, half, 512), bf16),
    ]
    return pl.pallas_call(
        block_backward_kernel,
        out_shape=[jax.ShapeDtypeStruct(shape, dtype) for shape, dtype in outs],
        in_specs=[VMEM] * 9 + [ANY] * 3 + [VMEM] * (len(arrays) - 13) + [ANY],
        out_specs=[VMEM, ANY, VMEM, VMEM],
        scratch_shapes=scratch,
        compiler_params=pltpu.CompilerParams(
            collective_id=collective, has_side_effects=True, vmem_limit_bytes=62 * MEGABYTE
        ),
    )(*arrays)


def row_peers():
    row, col = lax.axis_index("rows"), lax.axis_index("cols")
    return [device_of(lax.rem(row + step + 32, 32), col) for step in (-3, -2, -1, 1, 2, 3)]


def row_moves():
    listed = []
    for branch, rate in enumerate(rate_list):
        for direction in range(2):
            for hop in range(4):
                lead = 8 * hop - rate if direction == 0 else rate - 8 * hop
                first, last = max(0, lead), min(8, lead + 8)
                if first < last:
                    sign = 1 if direction == 0 else -1
                    listed.append((branch, direction, sign * hop, first, first - lead, last - first))
    return listed


class RowShift:
    def __init__(self, links, sources, target):
        self.links, self.sources, self.target = links, sources, target
        self.moves = row_moves()
        self.first = links.take(len(self.moves))

    def copies(self, branch):
        row, col = lax.axis_index("rows"), lax.axis_index("cols")
        for number, (owner, direction, hop, first, top, size) in enumerate(self.moves):
            if owner == branch and hop:
                yield remote(
                    self.sources[branch][direction].at[pl.ds(first, size)],
                    self.target.at[branch, direction, pl.ds(top, size)],
                    self.links.sends.at[self.first + number],
                    self.links.recvs.at[self.first + number],
                    device_of(lax.rem(row + hop + 32, 32), col),
                )

    def start(self, branch):
        for copy in self.copies(branch):
            copy.start()
        for owner, direction, hop, first, top, size in self.moves:
            if owner == branch and hop == 0:
                self.target[branch, direction, top : top + size] = self.sources[branch][direction][
                    first : first + size
                ]

    def finish(self, branch):
        for copy in self.copies(branch):
            copy.wait_recv()
            copy.wait_send()


MARGIN = 24


def silu_value(values):
    return values * jax.nn.sigmoid(values)


def silu_grad(values):
    part = jax.nn.sigmoid(values)
    return part * (1.0 + values * (1.0 - part))


def two_sums(first, second):
    return jnp.concatenate(
        [jnp.sum(first, axis=0, keepdims=True), jnp.sum(second, axis=0, keepdims=True)], axis=0
    )


def centered_values(total, values):
    average = total[0:1] / 16384.0
    variance = total[1:2] / 16384.0 - average * average
    scale = lax.rsqrt(variance + EPSILON)
    return (values - average) * scale, scale


def norm_grad(total, grad, centered, scale, gain):
    return (
        gain * scale * (grad - total[0:1] / 16384.0 - centered * (total[1:2] / 16384.0))
    ).astype(jnp.bfloat16)


def pyramid_kernel(
    grid_ref,
    slab_ref,
    pieces_ref,
    point_hbm,
    pool_hbm,
    project_hbm,
    misc_ref,
    masks_ref,
    seg_ref,
    edge_ref,
    part_ref,
    weights_ref,
    loss_out,
    pooled_out,
    grad_out,
    point_out,
    pool_out,
    project_out,
    norms_out,
    pieces_hbm,
    kernels,
    padded,
    moved_maps,
    taps,
    core_part,
    high_out,
    high_part,
    tap_own,
    rows_out,
    rows_in,
    grads_own,
    grads_in,
    stack,
    grad_taps,
    back_out,
    back_in,
    pieces_out,
    point_ref,
    pool_ref,
    project_ref,
    heads_ref,
    *rest,
):
    bf16, f32 = jnp.bfloat16, jnp.float32
    links = Links(rest[-2], rest[-1])
    totals = [Total(links, *rest[3 * number : 3 * number + 3]) for number in range(5)]
    row, col = lax.axis_index("rows"), lax.axis_index("cols")
    core, high = lax.rem(col, 2), col // 2
    twin = device_of(row, col + 1 - 2 * core)
    far_twin = device_of(row, col + 2 - 4 * high)
    pieces_sem = links.take(4)
    tap_core, tap_high = links.take(6), links.take(3)
    stack_high, stack_core = links.take(3), links.take(6)
    back = links.take(3)
    forward_shift = RowShift(
        links, [[rows_out.at[branch, direction] for direction in range(2)] for branch in range(3)], rows_in
    )
    backward_shift = RowShift(
        links, [[grads_own.at[branch] for _ in range(2)] for branch in range(3)], grads_in
    )
    loads = [
        pltpu.make_async_copy(source, target, links.recvs.at[pieces_sem + number])
        for number, (source, target) in enumerate(
            (
                (pieces_ref, pieces_out),
                (point_hbm, point_ref),
                (pool_hbm, pool_ref),
                (project_hbm, project_ref),
            )
        )
    ]
    stores = [
        pltpu.make_async_copy(
            pieces_out.at[pl.ds(16 * part, 16)],
            pieces_hbm.at[pl.ds(16 * part, 16)],
            links.sends.at[pieces_sem + part],
        )
        for part in range(2)
    ]
    for load in loads:
        load.start()
    peers = total_peers() + row_peers()
    meet(peers, len(peers))

    members_low = [jnp.where(masks_ref[8] == float(image), 1.0, 0.0) for image in range(4)]
    row_sums = jnp.sum(grid_ref[...].astype(f32), axis=1)
    pieces = []
    for image in range(4):
        chosen = members_low[image]
        pieces.append(
            jnp.concatenate(
                [
                    jnp.sum(row_sums * across_lanes(chosen, CIN), axis=0, keepdims=True),
                    jnp.sum(chosen, axis=0, keepdims=True),
                ],
                axis=1,
            )
        )
    totals[4].start(jnp.concatenate(pieces, axis=0))

    def columns_of(place):
        return pl.ds(pl.multiple_of(place * 16, 16), 16)

    padded[:, 0:MARGIN] = jnp.zeros((8, MARGIN, 512), f32)
    padded[:, MARGIN + 64 :] = jnp.zeros((8, MARGIN, 512), f32)
    padded[:, MARGIN : MARGIN + 64] = slab_ref[...].astype(f32)
    for branch, rate in enumerate(rate_list):
        for side in range(2):
            start = MARGIN + (2 * side - 1) * rate
            moved_maps[2 * branch + side] = (
                padded[:, start : start + 64].reshape(512, 512).astype(bf16)
            )
    slab = slab_ref[...].reshape(512, 512)
    for load in loads:
        load.wait()

    def join(pair, carry):
        both = jnp.concatenate(
            [pieces_out[2 * pair, 0:216].astype(f32), pieces_out[2 * pair + 1, 0:216].astype(f32)], axis=0
        )
        kernels[pl.ds(pl.multiple_of(432 * pair, 16), 432)] = both.astype(bf16)
        return carry

    lax.fori_loop(0, 16, join, 0)

    def tap_core_copy(branch, place):
        return remote(
            taps.at[pl.ds(3 * branch, 3), :, columns_of(2 * place + 1 - core)],
            core_part.at[branch, place],
            links.sends.at[tap_core + 2 * branch + place],
            links.recvs.at[tap_core + 2 * branch + place],
            twin,
        )

    def tap_high_copy(branch):
        return remote(
            high_out.at[branch],
            high_part.at[branch],
            links.sends.at[tap_high + branch],
            links.recvs.at[tap_high + branch],
            far_twin,
        )

    def tap_meet(branch):
        for place in range(2):
            tap_core_copy(branch, place).wait_recv()
        away = taps[pl.ds(3 * branch, 3), :, columns_of(2 * (1 - high) + core)].astype(f32)
        high_out[branch] = (away + core_part[branch, 1 - high].astype(f32)).astype(bf16)
        tap_high_copy(branch).start()
        here = taps[pl.ds(3 * branch, 3), :, columns_of(col)].astype(f32)
        tap_own[branch] = here + core_part[branch, high].astype(f32)

    def tap_finish(branch):
        tap_high_copy(branch).wait_recv()
        tap_own[branch] = tap_own[branch] + high_part[branch].astype(f32)
        for direction in range(2):
            rows_out[branch, direction] = tap_own[branch, 2 * direction].astype(bf16)
        forward_shift.start(branch)

    for branch in range(3):
        result = None
        for col_tap in range(3):
            left = slab if col_tap == 1 else moved_maps[2 * branch + col_tap // 2]
            right = jnp.concatenate(
                [
                    kernels[(9 * branch + 3 * tap + col_tap) * 256 : (9 * branch + 3 * tap + col_tap + 1) * 256]
                    for tap in range(3)
                ],
                axis=0,
            )
            product = against_rows(left, right)
            result = product if result is None else result + product
        for tap in range(3):
            taps[3 * branch + tap] = result[:, 256 * tap : 256 * tap + 256].astype(bf16).reshape(8, 64, 256)
        for place in range(2):
            tap_core_copy(branch, place).start()
        if branch == 0:
            totals[4].middle()
        else:
            tap_meet(branch - 1)
    tap_meet(2)
    grid = grid_ref[...].reshape(128, CIN)
    branches = [jnp.dot(grid, point_ref[...], preferred_element_type=f32)]
    number = lax.broadcasted_iota(jnp.int32, (256, 256), 0) * HEADS
    lane_256 = lax.broadcasted_iota(jnp.int32, (256, 256), 1)
    number_32 = lax.broadcasted_iota(jnp.int32, (256, 32), 0) * HEADS
    lane_32 = lax.broadcasted_iota(jnp.int32, (256, 32), 1)
    lane_128 = lax.broadcasted_iota(jnp.int32, (256, 128), 1)

    def rows_of_head(head):
        return jnp.where(lane_32 == (number_32 + head) // 256, 1.0, 0.0).astype(bf16)

    def lanes_of_head(head):
        return lane_256 == lax.rem(number + head, 256)

    flat_heads = misc_ref[19:51].astype(bf16)
    heads = jnp.zeros((256, 128), f32)
    for head in range(HEADS):
        spread = jnp.dot(rows_of_head(head), flat_heads, preferred_element_type=f32)
        column = jnp.sum(jnp.where(lanes_of_head(head), spread, 0.0), axis=1, keepdims=True)
        heads = heads + jnp.where(lane_128 == head, column, 0.0)
    heads_ref[...] = heads.astype(bf16)
    bias = jnp.where(
        lax.broadcasted_iota(jnp.int32, (1, 128), 1) < HEADS, misc_ref[36:37, 0:128], 0.0
    )
    pooled_sums = totals[4].finish()
    area = jnp.concatenate([pooled_sums[:, CIN : CIN + 128]] * 16, axis=1) * 16.0
    pooled = pooled_sums[:, 0:CIN] / area
    pooled_out[...] = pooled
    pooled_low = jnp.concatenate([pooled, jnp.zeros((4, CIN), f32)], axis=0).astype(bf16)
    pool_pre = jnp.dot(pooled_low, pool_ref[...], preferred_element_type=f32)[0:4] + misc_ref[0:1]
    pool_act = silu_value(pool_pre)
    members = [across_lanes(pixel_mask(members_low[image]), ASPP) for image in range(4)]
    pool_map = members[0] * pool_act[0:1]
    for image in range(1, 4):
        pool_map = pool_map + members[image] * pool_act[image : image + 1]
    for branch in range(3):
        tap_finish(branch)
    for branch in range(3):
        forward_shift.finish(branch)
        value = tap_own[branch, 1].reshape(128, 256)
        for direction in range(2):
            mask = across_lanes(pixel_mask(masks_ref[2 + 2 * branch + direction]), ASPP)
            value = value + rows_in[branch, direction].astype(f32).reshape(128, 256) * mask
        branches.append(value)
    before = jnp.concatenate(branches, axis=1)
    totals[0].start(two_sums(before, before * before))
    totals[0].middle()
    gains = jnp.concatenate([misc_ref[9 + 2 * branch : 10 + 2 * branch] for branch in range(4)], axis=1)
    shifts = jnp.concatenate([misc_ref[10 + 2 * branch : 11 + 2 * branch] for branch in range(4)], axis=1)
    centered, scale = centered_values(totals[0].finish(), before)
    normed = centered * gains + shifts
    joined = jnp.concatenate([silu_value(normed).astype(bf16), pool_map.astype(bf16)], axis=1)
    projected = jnp.dot(joined, project_ref[...], preferred_element_type=f32)
    totals[1].start(two_sums(projected, projected * projected))
    totals[1].middle()
    last_gain, last_shift = misc_ref[17:18], misc_ref[18:19]
    proj_centered, proj_scale = centered_values(totals[1].finish(), projected)
    proj_normed = proj_centered * last_gain + last_shift
    feature_map = silu_value(proj_normed).astype(bf16)
    logits = jnp.dot(feature_map, heads_ref[...], preferred_element_type=f32) + bias
    lane = lax.broadcasted_iota(jnp.int32, (128, 128), 1)

    def per_pixel(labels_ref):
        spread = jnp.broadcast_to(labels_ref[...].astype(f32)[:, None, :], (8, 16, 16))
        here = lax.broadcasted_iota(jnp.int32, (8, 16, 16), 1) == lax.broadcasted_iota(
            jnp.int32, (8, 16, 16), 2
        )
        return jnp.sum(jnp.where(here, spread, 0.0), axis=2, keepdims=True).reshape(128, 1)

    lane_value = lane.astype(f32)
    hot = (
        jnp.where(lane_value == per_pixel(seg_ref), 1.0, 0.0)
        + jnp.where(lane == SEG, per_pixel(edge_ref), 0.0)
        + jnp.where(lane_value == per_pixel(part_ref) + (SEG + 1.0), 1.0, 0.0)
    )

    def cross_entropy(inside):
        highest = jnp.max(jnp.where(inside, logits, -3.0e38), axis=1, keepdims=True)
        powers = jnp.where(inside, jnp.exp(jnp.where(inside, logits - highest, 0.0)), 0.0)
        total = jnp.sum(powers, axis=1, keepdims=True)
        picked = jnp.sum(jnp.where(inside, logits * hot, 0.0), axis=1, keepdims=True)
        return highest + jnp.log(total) - picked, powers / total

    seg_inside, part_inside = lane < SEG, jnp.logical_and(lane > SEG, lane < HEADS)
    seg_terms, seg_soft = cross_entropy(seg_inside)
    part_terms, part_soft = cross_entropy(part_inside)
    edge_inside = lane == SEG
    edge_all = (
        jnp.maximum(logits, 0.0) + jnp.log1p(jnp.exp(-jnp.abs(logits))) - hot * logits
    )
    edge_soft = jax.nn.sigmoid(logits)
    weights = [weights_ref[task].astype(f32) for task in range(3)]
    weight_total = weights[0] + weights[1] + weights[2]
    row_lane = lax.broadcasted_iota(jnp.int32, (1, 128), 1)
    shares = jnp.where(
        row_lane < SEG, weights[0], jnp.where(row_lane == SEG, weights[1], weights[2])
    ) / jnp.full((1, 128), weight_total)
    shares = jnp.where(row_lane < HEADS, shares, 0.0)
    terms = jnp.where(lane == 0, seg_terms, 0.0) + jnp.where(edge_inside, edge_all, 0.0)
    terms = (terms + jnp.where(lane == SEG + 1, part_terms, 0.0)) * shares
    loss_local = jnp.sum(jnp.sum(terms, axis=0, keepdims=True), axis=1, keepdims=True) / 16384.0
    soft = seg_soft + part_soft + jnp.where(edge_inside, edge_soft, 0.0)
    logit_grad = ((soft - hot) * shares / 16384.0).astype(bf16)
    feature_back = against_rows(logit_grad, heads_ref[...]) * silu_grad(proj_normed)
    proj_sums = two_sums(feature_back, feature_back * proj_centered)
    totals[2].start(
        jnp.concatenate([proj_sums, jnp.broadcast_to(loss_local, (1, ASPP))], axis=0)
    )
    heads_grad = over_pixels(feature_map, logit_grad)
    norms_out[11:64] = jnp.zeros((53, ASPP), f32)
    flat_grad = None
    for head in range(HEADS):
        column = jnp.broadcast_to(heads_grad[:, head : head + 1], (256, 256))
        spread = jnp.where(lanes_of_head(head), column, 0.0).astype(bf16)
        part = over_pixels(rows_of_head(head), spread)
        flat_grad = part if flat_grad is None else flat_grad + part
    norms_out[11:28] = flat_grad[0:17]
    norms_out[28:29, 0:128] = jnp.sum(logit_grad.astype(f32), axis=0, keepdims=True)
    totals[2].middle()
    total = totals[2].finish()
    loss_out[...] = total[2:3, 0:1]
    projected_grad = norm_grad(total, feature_back, proj_centered, proj_scale, last_gain)
    joined_grad = against_rows(projected_grad, project_ref[...])
    pool_map_grad = joined_grad[:, 4 * ASPP :]
    pool_local = jnp.concatenate(
        [jnp.sum(pool_map_grad * members[image], axis=0, keepdims=True) for image in range(4)], axis=0
    )
    branch_back = joined_grad[:, : 4 * ASPP] * silu_grad(normed)
    branch_sums = two_sums(branch_back, branch_back * centered)
    pool_row = jnp.concatenate([pool_local[image : image + 1] for image in range(4)], axis=1)
    totals[3].start(jnp.concatenate([branch_sums, pool_row], axis=0))
    project_out[...] = over_pixels(joined, projected_grad).astype(bf16)
    totals[3].middle()
    pool_slope = silu_grad(pool_pre)
    pool_pre_local = pool_local * pool_slope
    norms_out[0:1] = jnp.sum(pool_pre_local, axis=0, keepdims=True)
    for branch in range(4):
        lanes = slice(256 * branch, 256 * branch + 256)
        norms_out[1 + 2 * branch : 2 + 2 * branch] = branch_sums[1:2, lanes]
        norms_out[2 + 2 * branch : 3 + 2 * branch] = branch_sums[0:1, lanes]
    norms_out[9:10] = proj_sums[1:2]
    norms_out[10:11] = proj_sums[0:1]
    padding = jnp.zeros((4, ASPP), f32)
    pool_out[...] = over_pixels(
        pooled_low, jnp.concatenate([pool_pre_local, padding], axis=0).astype(bf16)
    ).astype(bf16)
    total = totals[3].finish()
    branch_grad = norm_grad(total, branch_back, centered, scale, gains)
    for branch in range(3):
        grads_own[branch] = branch_grad[:, 256 * branch + 256 : 256 * branch + 512].reshape(8, 16, 256)
        backward_shift.start(branch)

    def stack_high_copy(branch, sender):
        view = stack.at[branch, :, :, columns_of(sender)]
        return remote(
            view, view, links.sends.at[stack_high + branch], links.recvs.at[stack_high + branch], far_twin
        )

    def stack_core_copy(branch, place, sender_core):
        view = stack.at[branch, :, :, columns_of(2 * place + sender_core)]
        number = stack_core + 2 * branch + place
        return remote(view, view, links.sends.at[number], links.recvs.at[number], twin)

    pool_grad = jnp.concatenate(
        [total[2:3, 256 * image : 256 * image + 256] for image in range(4)], axis=0
    )
    pooled_grad = against_rows(
        jnp.concatenate([pool_grad * pool_slope, padding], axis=0).astype(bf16), pool_ref[...]
    )[0:4] / area
    for branch in range(3):
        backward_shift.finish(branch)
        for tap, direction in ((0, 1), (2, 0)):
            mask = across_lanes(pixel_mask(masks_ref[2 + 2 * branch + direction]), ASPP)
            shifted = grads_in[branch, direction].astype(f32).reshape(128, 256) * mask
            stack[branch, tap, :, columns_of(col)] = shifted.astype(bf16).reshape(8, 16, 256)
        stack[branch, 1, :, columns_of(col)] = grads_own[branch]
        stack_high_copy(branch, col).start()
    point_grad = branch_grad[:, 0:256]
    point_out[...] = over_pixels(grid, point_grad).astype(bf16)
    grad_out[...] = against_rows(point_grad, point_ref[...])
    for image in range(4):
        grad_out[...] = grad_out[...] + across_lanes(
            pixel_mask(members_low[image]), CIN
        ) * pooled_grad[image : image + 1]
    for branch in range(3):
        stack_high_copy(branch, col + 2 - 4 * high).wait_recv()
        for place in range(2):
            stack_core_copy(branch, place, core).start()
    def split(pair, carry):
        both = kernels[pl.ds(pl.multiple_of(432 * pair, 16), 432)].astype(f32)
        zeros = jnp.zeros((8, 512), f32)
        pieces_out[2 * pair] = jnp.concatenate([both[0:216], zeros], axis=0).astype(bf16)
        pieces_out[2 * pair + 1] = jnp.concatenate([both[216:432], zeros], axis=0).astype(bf16)
        return carry

    slab_grad = None
    for branch, rate in enumerate(rate_list):
        for place in range(2):
            stack_core_copy(branch, place, 1 - core).wait_recv()
        for tap in range(3):
            padded[:, MARGIN : MARGIN + 64, 0:256] = stack[branch, tap].astype(f32)
            for col_tap in range(3):
                start = MARGIN - (col_tap - 1) * rate
                lanes = slice(256 * (3 * tap + col_tap), 256 * (3 * tap + col_tap) + 256)
                grad_taps[:, lanes] = (
                    padded[:, start : start + 64, 0:256].reshape(512, 256).astype(bf16)
                )
        rows = slice(2304 * branch, 2304 * branch + 2304)
        product = jnp.dot(grad_taps[...], kernels[rows], preferred_element_type=f32)
        slab_grad = product if slab_grad is None else slab_grad + product
        kernels[rows] = over_pixels(grad_taps[...], slab).astype(bf16)
        if branch == 1:
            lax.fori_loop(0, 8, split, 0)
            stores[0].start()
    back_out[...] = slab_grad.astype(bf16).reshape(8, 64, 512)

    def back_copy(step, sender):
        return remote(
            back_out.at[:, columns_of(lax.rem(col + step, 4))],
            back_in.at[:, :, pl.ds(pl.multiple_of(sender * 512, 512), 512)],
            links.sends.at[back + step - 1],
            links.recvs.at[back + step - 1],
            device_of(row, lax.rem(col + step, 4)),
        )

    for step in (1, 2, 3):
        back_copy(step, col).start()
    back_in[:, :, pl.ds(pl.multiple_of(col * 512, 512), 512)] = back_out[:, columns_of(col)]

    lax.fori_loop(8, 16, split, 0)
    stores[1].start()
    for step in (1, 2, 3):
        copy = back_copy(step, lax.rem(col + 4 - step, 4))
        copy.wait_recv()
        copy.wait_send()
    grad_out[...] = grad_out[...] + back_in[...].reshape(128, CIN).astype(f32)
    for branch in range(3):
        for place in range(2):
            tap_core_copy(branch, place).wait_send()
            stack_core_copy(branch, place, core).wait_send()
        tap_high_copy(branch).wait_send()
        stack_high_copy(branch, col).wait_send()
    for store in stores:
        store.wait()


def pyramid(arrays, collective):
    bf16, f32 = jnp.bfloat16, jnp.float32
    outs = [
        ((1, 1), f32),
        ((4, CIN), f32),
        ((128, CIN), f32),
        ((CIN, ASPP), bf16),
        ((CIN, ASPP), bf16),
        ((5 * ASPP, ASPP), bf16),
        ((64, ASPP), f32),
        ((32, RATE_ROWS, 512), bf16),
    ]
    scratch = [
        pltpu.VMEM((27 * ASPP, 512), bf16),
        pltpu.VMEM((8, 64 + 2 * MARGIN, 512), f32),
        pltpu.VMEM((6, 512, 512), bf16),
        pltpu.VMEM((9, 8, 64, ASPP), bf16),
        pltpu.VMEM((3, 2, 3, 8, 16, ASPP), bf16),
        pltpu.VMEM((3, 3, 8, 16, ASPP), bf16),
        pltpu.VMEM((3, 3, 8, 16, ASPP), bf16),
        pltpu.VMEM((3, 3, 8, 16, ASPP), f32),
        pltpu.VMEM((3, 2, 8, 16, ASPP), bf16),
        pltpu.VMEM((3, 2, 8, 16, ASPP), bf16),
        pltpu.VMEM((3, 8, 16, ASPP), bf16),
        pltpu.VMEM((3, 2, 8, 16, ASPP), bf16),
        pltpu.VMEM((3, 3, 8, 64, ASPP), bf16),
        pltpu.VMEM((512, 9 * ASPP), bf16),
        pltpu.VMEM((8, 64, 512), bf16),
        pltpu.VMEM((8, 16, CIN), bf16),
        pltpu.VMEM((32, RATE_ROWS, 512), bf16),
        pltpu.VMEM((CIN, ASPP), bf16),
        pltpu.VMEM((CIN, ASPP), bf16),
        pltpu.VMEM((5 * ASPP, ASPP), bf16),
        pltpu.VMEM((ASPP, 128), bf16),
    ]
    for rows, columns in ((2, 4 * ASPP), (2, ASPP), (3, ASPP), (3, 4 * ASPP), (4, CIN + 128)):
        scratch += total_scratch(rows, columns)
    scratch += [pltpu.SemaphoreType.DMA((184,)), pltpu.SemaphoreType.DMA((184,))]
    in_specs = [VMEM] * len(arrays)
    in_specs[2:6] = [ANY] * 4
    in_specs[-1] = SMEM
    return pl.pallas_call(
        pyramid_kernel,
        out_shape=[jax.ShapeDtypeStruct(shape, dtype) for shape, dtype in outs],
        in_specs=in_specs,
        out_specs=[VMEM] * (len(outs) - 1) + [ANY],
        scratch_shapes=scratch,
        compiler_params=pltpu.CompilerParams(
            collective_id=collective, has_side_effects=True, vmem_limit_bytes=62 * MEGABYTE
        ),
    )(*arrays)


def per_device(
    features,
    image_rows,
    seg_labels,
    edge_labels,
    part_labels,
    task_weights,
    block_params,
    block_moment,
    head_params,
    head_moment,
    rate_params,
    rate_moment,
):
    height, across, channels = features.shape
    pixels = height * across
    inputs = features.reshape(pixels, channels)
    (
        w_reduce,
        w_spatial,
        w_expand,
        w_point,
        w_pool,
        w_project,
        misc,
        norms,
        masks,
        first_kept,
        second_kept,
        third_kept,
        second_act,
        block_window,
        grid,
        slab_map,
        rates_all,
    ) = block_forward(
        (
            inputs,
            block_params.reshape(BLOCK_ROWS, 128),
            head_params.reshape(HEAD_ROWS, 128),
            image_rows,
            rate_params.T,
        ),
        1,
    )
    (
        loss_rows,
        pooled,
        out_grad,
        grad_point,
        grad_pool,
        grad_project,
        misc_grads,
        rate_pieces,
    ) = pyramid(
        (
            grid,
            slab_map,
            rates_all.reshape(32, RATE_ROWS, channels // 4),
            w_point,
            w_pool,
            w_project,
            misc,
            masks,
            seg_labels,
            edge_labels,
            part_labels,
            task_weights,
        ),
        2,
    )
    loss_total = loss_rows.reshape(())
    input_grad, *flat_sums = block_backward(
        (
            inputs,
            out_grad,
            norms,
            masks,
            first_kept,
            second_kept,
            third_kept,
            second_act,
            block_window,
            w_reduce,
            w_spatial,
            w_expand,
            grad_point,
            grad_pool,
            grad_project,
            misc_grads,
            rate_pieces.reshape(2, 4, 4, RATE_ROWS, channels // 4),
        ),
        16,
    )
    shares_all, rate_sum = scatter_params(flat_sums, 20)
    rate_share = rate_sum[: rate_params.shape[1]].T
    block_share = shares_all[:BLOCK_ROWS].reshape(-1)
    head_share = shares_all[BLOCK_ROWS : BLOCK_ROWS + HEAD_ROWS].reshape(-1)
    block_moment_next = MOMENTUM_KEEP * block_moment + block_share
    head_moment_next = MOMENTUM_KEEP * head_moment + head_share
    rate_moment_next = MOMENTUM_KEEP * rate_moment + rate_share
    return (
        loss_total,
        pooled,
        input_grad.reshape(height, across, channels),
        block_moment_next,
        head_moment_next,
        rate_moment_next,
    )


def solution(mesh):
    return jax.shard_map(
        per_device,
        mesh=mesh,
        in_specs=(
            P("rows", "cols", None),
            P("rows"),
            P("rows", "cols"),
            P("rows", "cols"),
            P("rows", "cols"),
            P(),
            P(("rows", "cols")),
            P(("rows", "cols")),
            P(("rows", "cols")),
            P(("rows", "cols")),
            P("cols", "rows"),
            P("cols", "rows"),
        ),
        out_specs=(
            P(),
            P(),
            P("rows", "cols", None),
            P(("rows", "cols")),
            P(("rows", "cols")),
            P("cols", "rows"),
        ),
        check_vma=False,
    )
```

```python
import functools
import math

import jax
import jax.numpy as jnp
from jax import lax
from jax.experimental import pallas as pl
from jax.experimental.pallas import tpu as pltpu
from jax.sharding import PartitionSpec as P

MESH = pl.DeviceIdType.MESH
ANY = pl.BlockSpec(memory_space=pl.ANY)
VMEM = pl.BlockSpec(memory_space=pltpu.VMEM)
SMEM = pl.BlockSpec(memory_space=pltpu.SMEM)
BLOCK_ROWS = 273
HEAD_ROWS = 85
PAYLOAD = 384

CIN = 2048
MID = 512
ASPP = 256
SEG = 13
PART = 3
HEADS = 17


EPSILON = 1e-05
MOMENTUM_KEEP = 0.5
rate_list = (6, 12, 18)
block_dilation = 4
widest_margin = 18


def device_of(row, col):
    return {"rows": row, "cols": col}


def split_place():
    row, col = lax.axis_index("rows"), lax.axis_index("cols")
    return {
        "y": (row // 16) + 2 * (col // 2),
        "x": lax.rem(row // 4, 4),
        "z": lax.rem(row, 4),
        "core": lax.rem(col, 2),
    }


def device_at(place):
    row = lax.rem(place["y"], 2) * 16 + place["x"] * 4 + place["z"]
    return device_of(row, (place["y"] // 2) * 2 + place["core"])


def moved(place, axis, step, extent=4):
    other = dict(place)
    other[axis] = lax.rem(place[axis] + step + extent, extent)
    return other


def greet(peers):
    barrier = pltpu.get_barrier_semaphore()
    for device in peers:
        pl.semaphore_signal(barrier, inc=1, device_id=device, device_id_type=MESH)


def meet(peers):
    pl.semaphore_wait(pltpu.get_barrier_semaphore(), len(peers))


def remote(source, target, send_sem, recv_sem, device):
    return pltpu.make_async_remote_copy(
        src_ref=source,
        dst_ref=target,
        send_sem=send_sem,
        recv_sem=recv_sem,
        device_id=device,
        device_id_type=MESH,
    )


GATHER_ORDERS = (("z", "x", "y"), ("x", "y", "z"), ("y", "z", "x"))


def axis_view(place, fixed):
    index = [slice(None)] * 4
    if "y" in fixed:
        index[0], index[3] = lax.rem(place["y"], 2), place["y"] // 2
    if "x" in fixed:
        index[1] = place["x"]
    if "z" in fixed:
        index[2] = place["z"]
    return tuple(index)


def scatter_kernel(p_ref, late_ref, pair_ref, o_ref, share_ref, held, rate_parts, rate_sums, rate_pair, *rest):
    relays = rest[0:3]
    parts = [rest[3 + 3 * third : 6 + 3 * third] for third in range(3)]
    sums = [rest[12 + 2 * third : 14 + 2 * third] for third in range(3)]
    links = Links(rest[-2], rest[-1])
    first, own_first = links.take(45), links.take(3)
    rates = RateScatter(links, late_ref, rate_parts)
    me = rates.me
    everywhere = (slice(None),) * 4
    own_copies = []
    for third in range(3):
        rows = pl.ds(third * 128, 128)
        own_copies.append(
            pltpu.make_async_copy(
                p_ref.at[everywhere + (rows,)],
                held.at[everywhere + (rows,)],
                links.sends.at[own_first + third],
            )
        )
        own_copies[third].start()
    partners = [moved(me, axis, step) for axis in "xyz" for step in (1, 2, 3)]
    peers = [device_at(place) for place in partners]
    greet(peers)
    meet(peers)
    rates.send()

    def view_of(third, phase, place, part=None):
        order = GATHER_ORDERS[third]
        axis = order[2 - phase]
        start, size = (0, 128) if part is None else (64 * part, 64)
        if phase == 0:
            return held.at[axis_view(place, [axis]) + (pl.ds(third * 128 + start, size),)]
        index = []
        for name, key in (("y", 0), ("x", 1), ("z", 2), ("y", 3)):
            if name not in order[: 3 - phase]:
                continue
            if name != axis:
                index.append(slice(None))
            elif name == "y":
                index.append(lax.rem(place["y"], 2) if key == 0 else place["y"] // 2)
            else:
                index.append(place[name])
        return sums[third][phase - 1].at[tuple(index) + (pl.ds(start, size),)]

    def link(third, phase, kind, step, outgoing, incoming):
        number = first + 15 * third + 5 * phase + (3 + step // 2 if kind else step - 1)
        return remote(
            outgoing,
            incoming,
            links.sends.at[number],
            links.recvs.at[number],
            device_at(moved(me, GATHER_ORDERS[third][2 - phase], step)),
        )

    def steps(phase):
        return (1, 2, 3) if phase else (1, 3)

    def relay(third, step):
        axis = GATHER_ORDERS[third][2]
        outgoing = view_of(third, 0, moved(me, axis, 2), step // 2)
        return link(third, 0, 1, step, outgoing, relays[third].at[step // 2])

    def copy(third, phase, step):
        axis = GATHER_ORDERS[third][2 - phase]
        outgoing = view_of(third, phase, moved(me, axis, step))
        slot = steps(phase).index(step)
        return link(third, phase, 0, step, outgoing, parts[third][phase].at[slot])

    for third in range(3):
        own_copies[third].wait()
        for step in (1, 3):
            relay(third, step).start()
    for third in range(3):
        axis = GATHER_ORDERS[third][2]
        for step in (1, 3):
            relay(third, step).wait_recv()
            view = view_of(third, 0, moved(me, axis, step), step // 2)
            view[...] = view[...] + relays[third][step // 2]
            copy(third, 0, step).start()
    rate_sums[0] = pair_ref[...]
    rates.collect(rate_sums.at[1])
    rate_exchange = rates.pair(rate_sums.at[1 - rates.low_y], rate_pair)
    rate_exchange.start()
    for phase in range(1, 4):
        for third in range(3):
            total = view_of(third, phase - 1, me)[...].astype(jnp.float32)
            for slot, step in enumerate(steps(phase - 1)):
                copy(third, phase - 1, step).wait_recv()
                total = total + parts[third][phase - 1][slot].astype(jnp.float32)
            if phase == 3:
                o_ref[128 * third : 128 * third + 128] = total
            else:
                sums[third][phase - 1][...] = total.astype(jnp.bfloat16)
                for step in steps(phase):
                    copy(third, phase, step).start()
    rate_exchange.wait()
    for half in range(2):
        rows = slice(half * (RATE_ROWS // 2), (half + 1) * (RATE_ROWS // 2))
        share_ref[rows] = rate_sums[rates.low_y, half].astype(jnp.float32) + rate_pair[half].astype(
            jnp.float32
        )
    for third in range(3):
        for step in (1, 3):
            relay(third, step).wait_send()
        for phase in range(3):
            for step in steps(phase):
                copy(third, phase, step).wait_send()


def scatter_params(arrays, collective):
    def shape_left(left, rows):
        shape = ()
        for name, number in (("y", 2), ("x", 4), ("z", 4), ("y", 2)):
            if name in left:
                shape += (number,)
        return shape + (rows, 128)

    relays = []
    parts = []
    sums = []
    for order in GATHER_ORDERS:
        relays.append(pltpu.VMEM((2,) + shape_left(order[:2], 64), jnp.bfloat16))
        for phase in range(3):
            number = 3 if phase else 2
            parts.append(pltpu.VMEM((number,) + shape_left(order[: 2 - phase], 128), jnp.bfloat16))
        for phase in range(2):
            sums.append(pltpu.VMEM(shape_left(order[: 2 - phase], 128), jnp.bfloat16))
    held = pltpu.VMEM((2, 4, 4, 2, PAYLOAD, 128), jnp.bfloat16)
    half = (2, RATE_ROWS // 2, 512)
    rates = [pltpu.VMEM(shape, jnp.bfloat16) for shape in ((2, 3) + half[1:], (2,) + half, half)]
    return pl.pallas_call(
        scatter_kernel,
        out_shape=[
            jax.ShapeDtypeStruct((PAYLOAD, 128), jnp.float32),
            jax.ShapeDtypeStruct((RATE_ROWS, 512), jnp.float32),
        ],
        in_specs=[ANY, VMEM, VMEM],
        out_specs=[VMEM, VMEM],
        scratch_shapes=[held]
        + rates
        + relays
        + parts
        + sums
        + [pltpu.SemaphoreType.DMA((64,)), pltpu.SemaphoreType.DMA((64,))],
        compiler_params=pltpu.CompilerParams(
            collective_id=collective, has_side_effects=True, vmem_limit_bytes=56 * MEGABYTE
        ),
    )(*arrays)


def neighbour(row, col, offset):
    return lax.rem(row + offset[0] + 32, 32), lax.rem(col + offset[1] + 4, 4)


MEGABYTE = 1024 * 1024
OFFSETS = (-4, 4, -6, 6, -12, 12, -18, 18)
ID_ROW = 368
RATE_ROWS = 224


class Links:
    def __init__(self, sends, recvs):
        self.sends, self.recvs = sends, recvs
        self.cursor = 0

    def take(self, number):
        first = self.cursor
        self.cursor = first + number
        return first


class Total:
    def __init__(self, links, near_value, far_value, near, far):
        self.links = links
        self.values, self.buffers = (near_value, far_value), (near, far)
        self.first = links.take(2)
        self.row, self.col = lax.axis_index("rows"), lax.axis_index("cols")
        self.me = ((self.row // 16) * 4 + self.col, lax.rem(self.row, 16))

    def device(self, far, index):
        if far:
            return device_of((self.row // 16) * 16 + index, self.col)
        return device_of((index // 4) * 16 + self.me[1], lax.rem(index, 4))

    def link(self, far, outgoing, incoming, index):
        return remote(
            outgoing,
            incoming,
            self.links.sends.at[self.first + far],
            self.links.recvs.at[self.first + far],
            self.device(far, index),
        )

    def send(self, far, value):
        buffer, me, size = self.buffers[far], self.me[far], self.buffers[far].shape[0]
        self.values[far][...] = value
        for step in range(1, size):
            self.link(far, self.values[far], buffer.at[me], lax.rem(me + step, size)).start()
        buffer[me] = value

    def others(self, far):
        buffer, me, size = self.buffers[far], self.me[far], self.buffers[far].shape[0]
        view = buffer.at[pl.ds(0, size - 1)]
        return self.link(far, view, view, lax.rem(me + 1, size))

    def collect(self, far):
        self.others(far).wait_recv()
        total = self.buffers[far][0]
        for index in range(1, self.buffers[far].shape[0]):
            total = total + self.buffers[far][index]
        return total

    def start(self, value):
        self.send(0, value)

    def middle(self):
        self.send(1, self.collect(0))

    def finish(self):
        return self.collect(1)

    def close(self):
        for far in range(2):
            self.others(far).wait_send()


def total_scratch(rows, columns):
    return [
        pltpu.VMEM((rows, columns), jnp.float32),
        pltpu.VMEM((rows, columns), jnp.float32),
        pltpu.VMEM((8, rows, columns), jnp.float32),
        pltpu.VMEM((16, rows, columns), jnp.float32),
    ]


def total_peers():
    row, col = lax.axis_index("rows"), lax.axis_index("cols")
    near_me, far_me = (row // 16) * 4 + col, lax.rem(row, 16)
    peers = []
    for step in range(1, 8):
        index = lax.rem(near_me + step, 8)
        peers.append(device_of((index // 4) * 16 + far_me, lax.rem(index, 4)))
    for step in range(1, 16):
        peers.append(device_of((row // 16) * 16 + lax.rem(far_me + step, 16), col))
    return peers


def halo_peers():
    row, col = lax.axis_index("rows"), lax.axis_index("cols")
    return [
        device_of(*neighbour(row, col, (row_step, col_step)))
        for row_step in (-1, 0, 1)
        for col_step in (-1, 0, 1)
        if (row_step, col_step) != (0, 0)
    ]


class Halo:
    def __init__(self, links, source, window):
        self.links, self.source, self.window = links, source, window
        self.first = links.take(9)

    def copies(self, own_side):
        row, col = lax.axis_index("rows"), lax.axis_index("cols")
        listed = []
        for row_step in (-1, 0, 1):
            for col_step in (-1, 0, 1):
                if (row_step, col_step) == (0, 0):
                    continue
                low, size, top = {-1: (0, 4, 12), 0: (0, 8, 4), 1: (4, 4, 0)}[row_step]
                left = {-1: 32, 0: 16, 1: 0}[col_step]
                number = self.first + 3 * (row_step + 1) + col_step + 1
                listed.append(
                    remote(
                        self.source.at[pl.ds(low, size)],
                        self.window.at[pl.ds(top, size), pl.ds(left, 16)],
                        self.links.sends.at[number],
                        self.links.recvs.at[number],
                        device_of(*neighbour(row, col, (row_step, col_step))),
                    )
                )
        return listed

    def start(self):
        for copy in self.copies(True):
            copy.start()
        self.window[4:12, 16:32] = self.source[...]

    def finish(self):
        for copy in self.copies(False):
            copy.wait_recv()
        for copy in self.copies(False):
            copy.wait_send()


def widen_window(window, wide):
    col = lax.axis_index("cols")
    left = jnp.where(col > 0, 1.0, 0.0)
    right = jnp.where(col < 3, 1.0, 0.0)
    wide[:, 0:16] = window[:, 0:16].astype(jnp.float32) * left
    wide[:, 16:32] = window[:, 16:32].astype(jnp.float32)
    wide[:, 32:48] = window[:, 32:48].astype(jnp.float32) * right


def pixel_mask(mask):
    return jnp.broadcast_to(mask[:, None, :], (8, 16, 128)).reshape(128, 128)


def across_lanes(mask, width):
    return jnp.concatenate([mask] * (width // 128), axis=1)


class Gather:
    def __init__(self, links, source, target):
        self.links, self.source, self.target = links, source, target
        self.first = links.take(45)
        self.core_first = links.take(12)
        self.me = split_place()
        self.twin = moved(self.me, "core", 1, 2)

    def block(self, place, third, free, part=None):
        fixed = [axis for axis in "xyz" if axis not in free]
        rows = pl.ds(third * 128, 128) if part is None else pl.ds(third * 128 + 64 * part, 64)
        return self.target.at[axis_view(place, fixed) + (place["core"], rows)]

    def link(self, third, phase, kind, step, outgoing, incoming):
        number = self.first + 15 * third + 5 * phase + (3 + step // 2 if kind else step - 1)
        return remote(
            outgoing,
            incoming,
            self.links.sends.at[number],
            self.links.recvs.at[number],
            device_at(moved(self.me, GATHER_ORDERS[third][phase], step)),
        )

    def copy(self, third, phase, step, sender):
        free = GATHER_ORDERS[third][:phase]
        if phase == 0:
            outgoing = self.source.at[pl.ds(third * 128, 128)]
        else:
            outgoing = self.block(self.me, third, free)
        return self.link(third, phase, 0, step, outgoing, self.block(sender, third, free))

    def relay(self, third, phase, step, sender):
        order = GATHER_ORDERS[third]
        view = self.block(moved(sender, order[phase], 4 - step), third, order[:phase], step // 2)
        return self.link(third, phase, 1, step, view, view)

    def core_copy(self, third, distance, sender):
        order = GATHER_ORDERS[third]
        view = self.block(moved(sender, order[2], distance), third, order[:2])
        number = self.core_first + 4 * third + distance
        return remote(
            view, view, self.links.sends.at[number], self.links.recvs.at[number], device_at(self.twin)
        )

    def behind(self, third, phase, step):
        return moved(self.me, GATHER_ORDERS[third][phase], 4 - step)

    def steps(self, phase):
        return (1, 3) if phase == 2 else (1, 2, 3)

    def run(self, early, late):
        me = self.me
        for phase in range(3):
            for third in range(3):
                if phase > 0:
                    for step in (1, 2, 3):
                        self.copy(third, phase - 1, step, self.behind(third, phase - 1, step)).wait_recv()
                for step in self.steps(phase):
                    self.copy(third, phase, step, me).start()
                if phase == 0:
                    self.block(me, third, ())[...] = self.source[pl.ds(third * 128, 128)]
                if phase == 2:
                    self.core_copy(third, 0, me).start()
            if phase == 0:
                early()
        for third in range(3):
            for step in (1, 3):
                self.copy(third, 2, step, self.behind(third, 2, step)).wait_recv()
                self.relay(third, 2, step, me).start()
                self.core_copy(third, 4 - step, me).start()
        for third in range(3):
            for step in (1, 3):
                self.relay(third, 2, step, self.behind(third, 2, step)).wait_recv()
            self.core_copy(third, 2, me).start()
        late()
        for third in range(3):
            for distance in range(4):
                self.core_copy(third, distance, self.twin).wait_recv()

    def close(self):
        for third in range(3):
            for phase in range(3):
                for step in self.steps(phase):
                    self.copy(third, phase, step, self.me).wait_send()
            for step in (1, 3):
                self.relay(third, 2, step, self.me).wait_send()
            for distance in range(4):
                self.core_copy(third, distance, self.me).wait_send()


RATE_ORDERS = (("x", "z"), ("z", "x"))


class RateGather:
    def __init__(self, links, source, target):
        self.links, self.source, self.target = links, source, target
        self.first = links.take(82)
        self.me = split_place()
        self.low_y = lax.rem(self.me["y"], 2)
        self.other = dict(self.me)
        self.other["y"] = self.me["y"] + 1 - 2 * self.low_y
        self.half = RATE_ROWS // 2

    def own(self):
        return pltpu.make_async_copy(
            self.source,
            self.target.at[self.low_y, self.me["x"], self.me["z"]],
            self.links.recvs.at[self.first + 81],
        )

    def pair(self, sender):
        return remote(
            self.source,
            self.target.at[lax.rem(sender["y"], 2), self.me["x"], self.me["z"]],
            self.links.sends.at[self.first + 80],
            self.links.recvs.at[self.first + 80],
            device_at(self.other),
        )

    def axis(self, half, unit):
        return RATE_ORDERS[half][0 if unit < 2 else 1]

    def piece(self, half, unit, place, part=None):
        near = RATE_ORDERS[half][0]
        low_y = lax.rem(self.low_y + (unit if unit < 2 else (unit - 2) // 4), 2)
        places = {"x": place["x"], "z": place["z"]}
        if unit >= 2:
            places[near] = lax.rem(places[near] + (unit - 2) % 4, 4)
        start, size = {None: (0, 112), 0: (0, 64), 1: (64, 48)}[part]
        return self.target.at[low_y, places["x"], places["z"], pl.ds(half * self.half + start, size)]

    def link(self, half, unit, kind, step, view):
        number = self.first + 8 * unit + 4 * half + 2 * kind + step // 2
        return remote(
            view,
            view,
            self.links.sends.at[number],
            self.links.recvs.at[number],
            device_at(moved(self.me, self.axis(half, unit), step)),
        )

    def copy(self, half, unit, step, sender):
        return self.link(half, unit, 0, step, self.piece(half, unit, sender))

    def relay(self, half, unit, step, sender):
        first = moved(sender, self.axis(half, unit), 4 - step)
        return self.link(half, unit, 1, step, self.piece(half, unit, first, step // 2))

    def behind(self, half, unit, step):
        return moved(self.me, self.axis(half, unit), 4 - step)

    def each(self):
        return [(half, step) for half in range(2) for step in (1, 3)]

    def begin(self):
        self.own().start()
        self.pair(self.me).start()

    def send(self, *units):
        for unit in units:
            if unit == 0:
                self.own().wait()
            if unit == 1:
                self.pair(self.other).wait_recv()
            for half, step in self.each():
                self.copy(half, unit, step, self.me).start()

    def forward(self, *units):
        for unit in units:
            for half, step in self.each():
                self.copy(half, unit, step, self.behind(half, unit, step)).wait_recv()
                self.relay(half, unit, step, self.me).start()

    def receive(self, *units):
        for unit in units:
            for half, step in self.each():
                self.relay(half, unit, step, self.behind(half, unit, step)).wait_recv()

    def close(self):
        self.pair(self.me).wait_send()
        for unit in range(10):
            for half, step in self.each():
                self.copy(half, unit, step, self.me).wait_send()
                self.relay(half, unit, step, self.me).wait_send()


def assemble(gathered, first_row_group, staging, wide, stride):
    parts = len(wide)
    count, offset = (BLOCK_ROWS, 0) if parts == 4 else (HEAD_ROWS, BLOCK_ROWS)

    def step(group, carry):
        low_y, x, z = first_row_group // 16, group // 4, lax.rem(group, 4)
        for column in range(4):
            area = staging[column]
            if parts == 4:
                area[0:288] = gathered[low_y, x, z, column // 2, column % 2, 0:288].astype(jnp.float32)
            else:
                area[0:96] = gathered[low_y, x, z, column // 2, column % 2, 272:368].astype(jnp.float32)
            skip = offset - (0 if parts == 4 else 272)
            for part in range(parts):
                begin = (part - column * count) % parts
                number = (count - begin + parts - 1) // parts
                row = (column * count + begin - part) // parts
                group_rows = 4 * count // parts
                target = group_rows * (group + stride) + row
                wide[part][pl.ds(target, number), :] = area[
                    pl.ds(skip + begin, number, stride=parts), :
                ]
        return carry

    lax.fori_loop(0, 16, step, 0)


def wide_rows(wide, first, number):
    return jnp.concatenate([part[pl.ds(first, number), :] for part in wide], axis=1)


def block_forward_kernel(
    x_ref,
    block_ref,
    head_ref,
    image_ref,
    rate_params_ref,
    reduce_hbm,
    spatial_hbm,
    expand_hbm,
    point_hbm,
    pool_hbm,
    project_hbm,
    misc_ref,
    norms_ref,
    masks_ref,
    first_ref,
    second_ref,
    third_ref,
    act_ref,
    window_ref,
    out_ref,
    slab_ref,
    rates_ref,
    gathered,
    s0,
    s1,
    s2,
    s3,
    w0,
    w1,
    w2,
    w3,
    h0,
    h1,
    ids,
    wide,
    act_map,
    payload_wide,
    payload_ref,
    rate_ref,
    reduce_ref,
    spatial_ref,
    expand_ref,
    point_ref,
    pool_ref,
    project_ref,
    *rest,
):
    staging, matrix, head = (s0, s1, s2, s3), (w0, w1, w2, w3), (h0, h1)
    links = Links(rest[-2], rest[-1])
    totals = [Total(links, *rest[4 * number : 4 * number + 4]) for number in range(3)]
    peers = total_peers() + halo_peers()
    greet(peers)
    payload_wide[0:BLOCK_ROWS, :] = block_ref[...]
    payload_wide[BLOCK_ROWS : BLOCK_ROWS + HEAD_ROWS, :] = head_ref[...]
    payload_wide[BLOCK_ROWS + HEAD_ROWS : PAYLOAD, :] = jnp.zeros(
        (PAYLOAD - BLOCK_ROWS - HEAD_ROWS, 128), jnp.float32
    )
    for step in range(8):
        payload_wide[ID_ROW + step : ID_ROW + step + 1, :] = jnp.full(
            (1, 128), image_ref[step].astype(jnp.float32)
        )
    payload_ref[...] = payload_wide[...].astype(jnp.bfloat16)
    rate_ref[...] = jnp.concatenate(
        [rate_params_ref[...], jnp.zeros((RATE_ROWS - 216, 512), jnp.float32)], axis=0
    ).astype(jnp.bfloat16)
    gather = Gather(links, payload_ref, gathered)
    rates = RateGather(links, rate_ref, rates_ref)
    halo = Halo(links, act_map, window_ref)
    slab_first = links.take(3)
    out_first = links.take(6)
    stores = [
        pltpu.make_async_copy(source, target, links.sends.at[out_first + number])
        for number, (source, target) in enumerate(
            (
                (reduce_ref, reduce_hbm),
                (spatial_ref, spatial_hbm),
                (expand_ref, expand_hbm),
                (point_ref, point_hbm),
                (pool_ref, pool_hbm),
                (project_ref, project_hbm),
            )
        )
    ]
    row, col = lax.axis_index("rows"), lax.axis_index("cols")
    meet(peers)

    def rates_early():
        rates.begin()
        rates.send(0)

    def rates_late():
        rates.forward(0)
        rates.send(2, 1)

    gather.run(rates_early, rates_late)

    for step in range(-3, 4):
        other = lax.rem(row + step + 32, 32)
        rows_there = gathered[
            other // 16, lax.rem(other // 4, 4), lax.rem(other, 4), 0, 0, ID_ROW : ID_ROW + 16
        ].astype(jnp.float32)[0:8]
        inside = jnp.logical_and(row + step >= 0, row + step < 32)
        ids[8 * (step + 3) : 8 * (step + 3) + 8, :] = jnp.where(inside, rows_there, -1.0)
    own_ids = ids[24:32, :]
    for number, offset in enumerate(OFFSETS):
        masks_ref[number] = jnp.where(ids[24 + offset : 32 + offset, :] == own_ids, 1.0, 0.0)
    masks_ref[len(OFFSETS)] = own_ids

    assemble(gathered, 0, staging, matrix, 0)
    for step in range(8):
        reduce_ref[256 * step : 256 * step + 256] = wide_rows(matrix, 256 * step, 256).astype(jnp.bfloat16)
    first = jnp.dot(x_ref[...], reduce_ref[...], preferred_element_type=jnp.float32)
    totals[0].start(
        jnp.concatenate(
            [jnp.sum(first, axis=0, keepdims=True), jnp.sum(first * first, axis=0, keepdims=True)], axis=0
        )
    )
    for step in range(5):
        spatial_ref[464 * step : 464 * step + 464] = wide_rows(matrix, 2048 + 464 * step, 464).astype(
            jnp.bfloat16
        )
    totals[0].middle()
    assemble(gathered, 16, staging, matrix, 0)
    for step in range(13):
        spatial_ref[2320 + 176 * step : 2320 + 176 * step + 176] = wide_rows(
            matrix, 176 * step, 176
        ).astype(jnp.bfloat16)
    for part in range(4):
        expand_ref[:, 512 * part : 512 * part + 512] = jnp.concatenate(
            [array[pl.ds(2288 + part, 512, stride=4), :] for array in matrix], axis=1
        ).astype(jnp.bfloat16)
    norms_ref[...] = wide_rows(matrix, 4336, 16)
    for store in stores[0:3]:
        store.start()

    def normal(total, values, gain, shift, kept):
        average = total[0:1] / 16384.0
        variance = total[1:2] / 16384.0 - average * average
        scale = lax.rsqrt(variance + EPSILON)
        centered = (values - average) * scale
        kept[0:128] = centered
        kept[128:136] = jnp.broadcast_to(scale, (8, scale.shape[1]))
        return centered * gain + shift

    def silu(values):
        return values * jax.nn.sigmoid(values)

    def stats(values):
        return jnp.concatenate(
            [jnp.sum(values, axis=0, keepdims=True), jnp.sum(values * values, axis=0, keepdims=True)], axis=0
        )

    normed = normal(totals[0].finish(), first, norms_ref[0:1], norms_ref[1:2], first_ref)
    act_map[...] = silu(normed).astype(jnp.bfloat16).reshape(8, 16, MID)
    halo.start()
    rates.forward(2, 1)
    rates.receive(0)
    rates.send(3, 4)
    halo.finish()
    widen_window(window_ref, wide)
    second = None
    for row_tap in range(3):
        part = None
        for col_tap in range(3):
            tap = 3 * row_tap + col_tap
            region = wide[4 * row_tap : 4 * row_tap + 8, 12 + 4 * col_tap : 28 + 4 * col_tap]
            product = jnp.dot(
                region.reshape(128, MID).astype(jnp.bfloat16),
                spatial_ref[512 * tap : 512 * tap + 512],
                preferred_element_type=jnp.float32,
            )
            part = product if part is None else part + product
        if row_tap != 1:
            part = part * across_lanes(pixel_mask(masks_ref[row_tap // 2]), MID)
        second = part if second is None else second + part
    totals[1].start(stats(second))
    assemble(gathered, 0, staging, head, 0)
    assemble(gathered, 16, staging, head, 16)
    totals[1].middle()
    for step in range(8):
        point_ref[256 * step : 256 * step + 256] = wide_rows(head, 256 * step, 256).astype(jnp.bfloat16)
        pool_ref[256 * step : 256 * step + 256] = wide_rows(head, 2048 + 256 * step, 256).astype(jnp.bfloat16)
    for step in range(5):
        project_ref[256 * step : 256 * step + 256] = wide_rows(head, 4097 + 256 * step, 256).astype(
            jnp.bfloat16
        )
    for store in stores[3:6]:
        store.start()
    misc_ref[0:8] = wide_rows(head, 4096, 8)
    misc_ref[8:72] = wide_rows(head, 5376, 64)
    normed = normal(totals[1].finish(), second, norms_ref[2:3], norms_ref[3:4], second_ref)
    rates.forward(3, 4)
    rates.receive(1)
    rates.send(5, 6)
    act_ref[...] = silu(normed).astype(jnp.bfloat16)
    third = jnp.dot(act_ref[...], expand_ref[...], preferred_element_type=jnp.float32)
    totals[2].start(stats(third))
    totals[2].middle()
    out_gain = jnp.concatenate([norms_ref[4 + part : 5 + part] for part in range(4)], axis=1)
    out_shift = jnp.concatenate([norms_ref[8 + part : 9 + part] for part in range(4)], axis=1)
    normed = normal(totals[2].finish(), third, out_gain, out_shift, third_ref)
    block_out = silu(normed + x_ref[...].astype(jnp.float32)).astype(jnp.bfloat16)
    out_ref[...] = block_out.reshape(8, 16, CIN)

    def slab_copy(step, sender):
        return remote(
            out_ref.at[:, :, pl.ds(pl.multiple_of(lax.rem(col + step, 4) * 512, 512), 512)],
            slab_ref.at[:, pl.ds(pl.multiple_of(sender * 16, 16), 16)],
            links.sends.at[slab_first + step - 1],
            links.recvs.at[slab_first + step - 1],
            device_of(row, lax.rem(col + step, 4)),
        )

    for step in (1, 2, 3):
        slab_copy(step, col).start()
    rates.forward(5, 6)
    rates.send(7, 8, 9)
    slab_ref[:, pl.ds(pl.multiple_of(col * 16, 16), 16)] = out_ref[
        :, :, pl.ds(pl.multiple_of(col * 512, 512), 512)
    ]
    for step in (1, 2, 3):
        copy = slab_copy(step, lax.rem(col + 4 - step, 4))
        copy.wait_recv()
        copy.wait_send()
    rates.forward(7, 8, 9)
    rates.receive(2, 3, 4, 5, 6, 7, 8, 9)
    rates.close()
    gather.close()
    for total in totals:
        total.close()
    for store in stores:
        store.wait()


def block_forward(arrays, collective):
    bf16, f32 = jnp.bfloat16, jnp.float32
    outs = [
        ((CIN, MID), bf16),
        ((9 * MID, MID), bf16),
        ((MID, CIN), bf16),
        ((CIN, ASPP), bf16),
        ((CIN, ASPP), bf16),
        ((5 * ASPP, ASPP), bf16),
        ((72, ASPP), f32),
        ((16, MID), f32),
        ((9, 8, 128), f32),
        ((136, MID), f32),
        ((136, MID), f32),
        ((136, CIN), f32),
        ((128, MID), bf16),
        ((16, 48, MID), bf16),
        ((8, 16, CIN), bf16),
        ((8, 64, CIN // 4), bf16),
        ((2, 4, 4, RATE_ROWS, CIN // 4), bf16),
    ]
    scratch = [pltpu.VMEM((2, 4, 4, 2, 2, PAYLOAD, 128), bf16)]
    scratch += [pltpu.VMEM((288, 128), f32)] * 4
    scratch += [pltpu.VMEM((4368, 128), f32)] * 4
    scratch += [pltpu.VMEM((5440, 128), f32)] * 2
    scratch += [
        pltpu.VMEM((56, 128), f32),
        pltpu.VMEM((16, 48, MID), f32),
        pltpu.VMEM((8, 16, MID), bf16),
        pltpu.VMEM((PAYLOAD, 128), f32),
        pltpu.VMEM((PAYLOAD, 128), bf16),
        pltpu.VMEM((RATE_ROWS, 512), bf16),
    ]
    scratch += [pltpu.VMEM(shape, dtype) for shape, dtype in outs[:6]]
    for rows, columns in ((2, MID), (2, MID), (2, CIN)):
        scratch += total_scratch(rows, columns)
    scratch += [pltpu.SemaphoreType.DMA((248,)), pltpu.SemaphoreType.DMA((248,))]
    return pl.pallas_call(
        block_forward_kernel,
        out_shape=[jax.ShapeDtypeStruct(shape, dtype) for shape, dtype in outs],
        in_specs=[VMEM, VMEM, VMEM, SMEM, VMEM],
        out_specs=[ANY] * 6 + [VMEM] * 10 + [ANY],
        scratch_shapes=scratch,
        compiler_params=pltpu.CompilerParams(
            collective_id=collective, has_side_effects=True, vmem_limit_bytes=60 * MEGABYTE
        ),
    )(*arrays)


class RatePieces:
    def __init__(self, links, units):
        self.links = links
        self.first = links.take(8 * units + 4)
        self.extra = self.first + 8 * units
        self.me = split_place()
        self.low_y = lax.rem(self.me["y"], 2)
        self.other = dict(self.me)
        self.other["y"] = self.me["y"] + 1 - 2 * self.low_y

    def rows(self, half):
        return pl.ds(half * (RATE_ROWS // 2), RATE_ROWS // 2)

    def piece(self, array, half, low_y, first_axis, second_axis):
        places = {RATE_ORDERS[half][0]: first_axis, RATE_ORDERS[half][1]: second_axis}
        return array.at[low_y, places["x"], places["z"], self.rows(half)]

    def remote(self, unit, half, slot, outgoing, incoming, axis, step):
        number = self.first + 8 * unit + 4 * half + slot
        return remote(
            outgoing,
            incoming,
            self.links.sends.at[number],
            self.links.recvs.at[number],
            device_at(moved(self.me, axis, step)),
        )

    def each(self):
        return [(half, step) for half in range(2) for step in (1, 2, 3)]


class RateFirst(RatePieces):
    def __init__(self, links, pieces, own, relays, parts, low_y):
        super().__init__(links, 4)
        self.pieces, self.own, self.relays, self.parts, self.from_y = pieces, own, relays, parts, low_y
        loads = links.take(6)
        self.loads = []
        for half in range(2):
            near, far = RATE_ORDERS[half]
            for slot, step in enumerate((0, 1, 3)):
                places = {near: slice(None), far: moved(self.me, far, step)[far]}
                self.loads.append(
                    pltpu.make_async_copy(
                        pieces.at[low_y, places["x"], places["z"], self.rows(half)],
                        own.at[half, slot],
                        links.recvs.at[loads + 3 * half + slot],
                    )
                )

    def part(self, step):
        return pl.ds(0, 64) if step == 1 else pl.ds(64, 48)

    def relay(self, unit, half, step):
        far = RATE_ORDERS[half][1]
        places = {RATE_ORDERS[half][0]: unit, far: moved(self.me, far, 2)[far]}
        rows = self.part(step)
        start = half * (RATE_ROWS // 2) + rows.start
        return self.remote(
            unit,
            half,
            step // 2 + 2,
            self.pieces.at[self.from_y, places["x"], places["z"], pl.ds(start, rows.size)],
            self.relays.at[half, unit, rows],
            far,
            step,
        )

    def copy(self, unit, half, step):
        far = RATE_ORDERS[half][1]
        slot = step // 2
        return self.remote(
            unit, half, slot, self.own.at[half, 1 + slot, unit], self.parts.at[half, unit, slot], far, step
        )

    def each(self):
        return [(half, step) for half in range(2) for step in (1, 3)]

    def send(self, *units):
        for unit in units:
            for half, step in self.each():
                self.relay(unit, half, step).start()

    def forward(self, *units):
        for unit in units:
            for half, step in self.each():
                self.relay(unit, half, step).wait_recv()
                rows = self.part(step)
                place = (half, 1 + step // 2, unit, rows)
                self.own[place] = self.own[place] + self.relays[half, unit, rows]
                self.copy(unit, half, step).start()

    def collect(self, *units):
        for unit in units:
            for half in range(2):
                total = self.own[half, 0, unit].astype(jnp.float32)
                for step in (1, 3):
                    self.copy(unit, half, step).wait_recv()
                    total = total + self.parts[half, unit, step // 2].astype(jnp.float32)
                self.own[half, 0, unit] = total.astype(jnp.bfloat16)
            for half, step in self.each():
                self.relay(unit, half, step).wait_send()
                self.copy(unit, half, step).wait_send()


class RateScatter(RatePieces):
    def __init__(self, links, sums, parts):
        super().__init__(links, 1)
        self.sums, self.parts = sums, parts

    def copy(self, half, step):
        near = RATE_ORDERS[half][0]
        outgoing = self.sums.at[half, moved(self.me, near, step)[near]]
        return self.remote(0, half, step - 1, outgoing, self.parts.at[half, step - 1], near, step)

    def pair(self, outgoing, incoming):
        return remote(
            outgoing,
            incoming,
            self.links.sends.at[self.extra],
            self.links.recvs.at[self.extra],
            device_at(self.other),
        )

    def send(self):
        for half, step in self.each():
            self.copy(half, step).start()

    def collect(self, target):
        for half in range(2):
            total = self.sums[half, self.me[RATE_ORDERS[half][0]]].astype(jnp.float32)
            for step in (1, 2, 3):
                self.copy(half, step).wait_recv()
                total = total + self.parts[half, step - 1].astype(jnp.float32)
            target[half] = total.astype(jnp.bfloat16)
        for half, step in self.each():
            self.copy(half, step).wait_send()


def disassemble(packed, first_row_group, staging, wide, stride):
    parts = len(wide)
    core = lax.rem(lax.axis_index("cols"), 2)
    count = BLOCK_ROWS if parts == 4 else HEAD_ROWS
    low_y = first_row_group // 16

    def step(group, carry):
        x, z = group // 4, lax.rem(group, 4)
        for column in range(4):
            area = staging[column]
            here = (lax.rem(column + core, 2), low_y, x, z, column // 2)
            if parts == 4:
                skip = 0
                area[272:288] = packed[here + (slice(272, 288),)].astype(jnp.float32)
            else:
                skip = 1
                area[80:112] = jnp.zeros((32, 128), jnp.float32)
            for part in range(parts):
                begin = (part - column * count) % parts
                number = (count - begin + parts - 1) // parts
                row = (column * count + begin - part) // parts
                origin = (4 * count // parts) * (group + stride) + row
                area[pl.ds(skip + begin, number, stride=parts), :] = wide[part][
                    pl.ds(origin, number), :
                ]
            if parts == 4:
                packed[here + (slice(0, 288),)] = area[0:288].astype(jnp.bfloat16)
            else:
                packed[here + (slice(272, 384),)] = area[0:112].astype(jnp.bfloat16)
        return carry

    lax.fori_loop(0, 16, step, 0)


def deal(wide, first, values):
    number = values.shape[0]
    for part, array in enumerate(wide):
        array[first : first + number, :] = values[:, 128 * part : 128 * part + 128]


def against_rows(left, right):
    return lax.dot_general(left, right, (((1,), (1,)), ((), ())), preferred_element_type=jnp.float32)


def over_pixels(left, right):
    return lax.dot_general(left, right, (((0,), (0,)), ((), ())), preferred_element_type=jnp.float32)


def block_backward_kernel(
    x_ref,
    grad_ref,
    norms_ref,
    masks_ref,
    first_ref,
    second_ref,
    third_ref,
    act_ref,
    window_ref,
    reduce_hbm,
    spatial_hbm,
    expand_hbm,
    point_ref,
    pool_ref,
    project_ref,
    misc_ref,
    pieces_ref,
    out_ref,
    held_ref,
    late_ref,
    pair_ref,
    s0,
    s1,
    s2,
    s3,
    w0,
    w1,
    w2,
    w3,
    wide,
    act_map,
    window,
    packed,
    twin_part,
    reduce_ref,
    spatial_ref,
    expand_ref,
    free_sem,
    *rest,
):
    staging, matrix, head = (s0, s1, s2, s3), (w0, w1, w2, w3), (w0, w1)
    links = Links(rest[-2], rest[-1])
    totals = [Total(links, *rest[4 * number : 4 * number + 4]) for number in range(3)]
    own, relays, first_parts, second_parts = rest[12:16]
    rates = [
        RateFirst(links, pieces_ref, own.at[low_y], relays.at[low_y], first_parts.at[low_y], low_y)
        for low_y in range(2)
    ]
    scatter = RateScatter(links, own.at[0, :, 0], second_parts)
    me = scatter.me
    twin = device_at(moved(me, "core", 1, 2))
    halo = Halo(links, act_map, window)
    load_first, twin_first, out_first = (links.take(number) for number in (3, 2, 2))
    loads = [
        pltpu.make_async_copy(source, target, links.recvs.at[load_first + number])
        for number, (source, target) in enumerate(
            ((expand_hbm, expand_ref), (spatial_hbm, spatial_ref), (reduce_hbm, reduce_ref))
        )
    ]
    for copy in loads + rates[0].loads + rates[1].loads:
        copy.start()

    def twin_copy(low_y):
        return remote(
            packed.at[1, low_y],
            twin_part,
            links.sends.at[twin_first + low_y],
            links.recvs.at[twin_first + low_y],
            twin,
        )

    def out_copy(low_y):
        return pltpu.make_async_copy(
            packed.at[0, low_y], held_ref.at[low_y], links.sends.at[out_first + low_y]
        )

    def join_twin(low_y):
        twin_copy(low_y).wait_recv()

        def add_block(index, carry):
            place = (index // 8, lax.rem(index // 2, 4), lax.rem(index, 2))
            packed[(0, low_y) + place] = packed[(0, low_y) + place] + twin_part[place]
            return carry

        lax.fori_loop(0, 32, add_block, 0)
        out_copy(low_y).start()

    peers = total_peers() + halo_peers()
    greet(peers)

    def slope(values):
        part = jax.nn.sigmoid(values)
        return part * (1.0 + values * (1.0 - part))

    def local_sums(grad, kept):
        return jnp.concatenate(
            [
                jnp.sum(grad, axis=0, keepdims=True),
                jnp.sum(grad * kept[0:128], axis=0, keepdims=True),
            ],
            axis=0,
        )

    def through_norm(total, grad, kept, gain):
        return (
            gain
            * kept[128:129]
            * (grad - total[0:1] / 16384.0 - kept[0:128] * (total[1:2] / 16384.0))
        ).astype(jnp.bfloat16)

    out_gain = jnp.concatenate([norms_ref[4 + part : 5 + part] for part in range(4)], axis=1)
    out_shift = jnp.concatenate([norms_ref[8 + part : 9 + part] for part in range(4)], axis=1)
    residual = third_ref[0:128] * out_gain + out_shift + x_ref[...].astype(jnp.float32)
    out_ref[...] = grad_ref[...] * slope(residual)
    third_sums = local_sums(out_ref[...], third_ref)
    meet(peers)
    rates[0].send(0, 1, 2, 3)
    totals[0].start(third_sums)
    for step in range(4):
        deal(head, 512 * step, point_ref[512 * step : 512 * step + 512].astype(jnp.float32))
    deal(head, 2048, pool_ref[0:672].astype(jnp.float32))
    disassemble(packed, 0, staging, head, 0)
    totals[0].middle()
    for step in range(4):
        deal(head, 344 * step, pool_ref[672 + 344 * step : 1016 + 344 * step].astype(jnp.float32))
    deal(head, 1376, misc_ref[0:1])
    for step in range(5):
        deal(head, 1377 + 256 * step, project_ref[256 * step : 256 * step + 256].astype(jnp.float32))
    deal(head, 2657, misc_ref[1:64])
    disassemble(packed, 16, staging, head, 0)
    third_grad = through_norm(totals[0].finish(), out_ref[...], third_ref, out_gain)
    for copy in rates[0].loads + rates[1].loads:
        copy.wait()
    rates[0].forward(0, 1)
    loads[0].wait()
    second_gain, second_shift = norms_ref[2:3], norms_ref[3:4]
    second_norm = second_ref[0:128] * second_gain + second_shift
    second_back = against_rows(third_grad, expand_ref[...]) * slope(second_norm)
    second_sums = local_sums(second_back, second_ref)
    totals[1].start(second_sums)
    for part in range(4):
        product = over_pixels(act_ref[...], third_grad[:, 512 * part : 512 * part + 512])
        for number, array in enumerate(matrix):
            array[pl.ds(2288 + part, 512, stride=4), :] = product[:, 128 * number : 128 * number + 128]
    totals[1].middle()
    widen_window(window_ref, wide)
    second_grad = through_norm(totals[1].finish(), second_back, second_ref, second_gain)
    act_map[...] = second_grad.reshape(8, 16, MID)
    halo.start()
    rates[0].forward(2, 3)
    rates[1].send(0, 1, 2, 3)

    def spatial_grad(tap):
        row_tap, col_tap = tap // 3, tap % 3
        region = wide[4 * row_tap : 4 * row_tap + 8, 12 + 4 * col_tap : 28 + 4 * col_tap].reshape(128, MID)
        if row_tap != 1:
            region = region * across_lanes(pixel_mask(masks_ref[row_tap // 2]), MID)
        return over_pixels(region.astype(jnp.bfloat16), second_grad)

    middle_tap = spatial_grad(4)
    deal(matrix, 0, middle_tap[272:512])
    for tap in range(5, 9):
        deal(matrix, 240 + 512 * (tap - 5), spatial_grad(tap))
    halo.finish()
    rates[0].collect(0, 1, 2, 3)
    scatter.send()
    widen_window(window, wide)
    loads[1].wait()
    first_back = None
    for row_tap in range(3):
        part = None
        for col_tap in range(3):
            tap = 3 * row_tap + col_tap
            region = wide[
                8 - 4 * row_tap : 16 - 4 * row_tap, 20 - 4 * col_tap : 36 - 4 * col_tap
            ]
            product = against_rows(
                region.reshape(128, MID).astype(jnp.bfloat16), spatial_ref[512 * tap : 512 * tap + 512]
            )
            part = product if part is None else part + product
        if row_tap != 1:
            part = part * across_lanes(pixel_mask(masks_ref[1 - row_tap // 2]), MID)
        first_back = part if first_back is None else first_back + part
    first_gain, first_shift = norms_ref[0:1], norms_ref[1:2]
    first_back = first_back * slope(first_ref[0:128] * first_gain + first_shift)
    first_sums = local_sums(first_back, first_ref)
    totals[2].start(first_sums)
    deal(matrix, 4336, first_sums[1:2])
    deal(matrix, 4337, first_sums[0:1])
    deal(matrix, 4338, second_sums[1:2])
    deal(matrix, 4339, second_sums[0:1])
    for part in range(4):
        deal(matrix, 4340 + part, third_sums[1:2, 512 * part : 512 * part + 512])
        deal(matrix, 4344 + part, third_sums[0:1, 512 * part : 512 * part + 512])
    deal(matrix, 4348, jnp.zeros((20, MID), jnp.float32))
    disassemble(packed, 16, staging, matrix, 0)
    twin_copy(1).start()
    totals[2].middle()
    widen_window(window_ref, wide)
    deal(matrix, 4096, middle_tap[0:272])
    for tap in range(4):
        deal(matrix, 2048 + 512 * tap, spatial_grad(tap))
    first_total = totals[2].finish()
    rates[1].forward(0, 1, 2, 3)
    join_twin(1)
    pl.semaphore_signal(free_sem, inc=1, device_id=twin, device_id_type=MESH)
    loads[2].wait()
    first_grad = through_norm(first_total, first_back, first_ref, first_gain)
    for part in range(4):
        rows = slice(512 * part, 512 * part + 512)
        deal(matrix, 512 * part, over_pixels(x_ref[:, rows], first_grad))
        out_ref[:, rows] = out_ref[:, rows] + against_rows(first_grad, reduce_ref[rows])
    disassemble(packed, 0, staging, matrix, 0)
    pl.semaphore_wait(free_sem, 1)
    twin_copy(0).start()
    rates[1].collect(0, 1, 2, 3)
    late_ref[...] = own[1, :, 0]
    scatter.collect(pair_ref)
    join_twin(0)
    for low_y in range(2):
        twin_copy(low_y).wait_send()
        out_copy(low_y).wait()
    for total in totals:
        total.close()


def block_backward(arrays, collective):
    bf16, f32 = jnp.bfloat16, jnp.float32
    half = RATE_ROWS // 2
    scratch = [pltpu.VMEM((384, 128), f32)] * 4
    scratch += [pltpu.VMEM((4368, 128), f32)] * 4
    scratch += [
        pltpu.VMEM((16, 48, MID), f32),
        pltpu.VMEM((8, 16, MID), bf16),
        pltpu.VMEM((16, 48, MID), bf16),
        pltpu.VMEM((2, 2, 4, 4, 2, PAYLOAD, 128), bf16),
        pltpu.VMEM((4, 4, 2, PAYLOAD, 128), bf16),
        pltpu.VMEM((CIN, MID), bf16),
        pltpu.VMEM((9 * MID, MID), bf16),
        pltpu.VMEM((MID, CIN), bf16),
        pltpu.SemaphoreType.REGULAR,
    ]
    for rows, columns in ((2, CIN), (2, MID), (2, MID)):
        scratch += total_scratch(rows, columns)
    scratch += [
        pltpu.VMEM((2, 2, 3, 4, half, 512), bf16),
        pltpu.VMEM((2, 2, 4, half, 512), bf16),
        pltpu.VMEM((2, 2, 4, 2, half, 512), bf16),
        pltpu.VMEM((2, 3, half, 512), bf16),
    ]
    scratch += [pltpu.SemaphoreType.DMA((232,)), pltpu.SemaphoreType.DMA((232,))]
    outs = [
        ((128, CIN), f32),
        ((2, 4, 4, 2, PAYLOAD, 128), bf16),
        ((2, 4, half, 512), bf16),
        ((2, half, 512), bf16),
    ]
    return pl.pallas_call(
        block_backward_kernel,
        out_shape=[jax.ShapeDtypeStruct(shape, dtype) for shape, dtype in outs],
        in_specs=[VMEM] * 9 + [ANY] * 3 + [VMEM] * (len(arrays) - 13) + [ANY],
        out_specs=[VMEM, ANY, VMEM, VMEM],
        scratch_shapes=scratch,
        compiler_params=pltpu.CompilerParams(
            collective_id=collective, has_side_effects=True, vmem_limit_bytes=62 * MEGABYTE
        ),
    )(*arrays)


def row_peers():
    row, col = lax.axis_index("rows"), lax.axis_index("cols")
    return [device_of(lax.rem(row + step + 32, 32), col) for step in (-3, -2, -1, 1, 2, 3)]


def row_moves():
    listed = []
    for branch, rate in enumerate(rate_list):
        for direction in range(2):
            for hop in range(4):
                lead = 8 * hop - rate if direction == 0 else rate - 8 * hop
                first, last = max(0, lead), min(8, lead + 8)
                if first < last:
                    sign = 1 if direction == 0 else -1
                    listed.append((branch, direction, sign * hop, first, first - lead, last - first))
    return listed


class RowShift:
    def __init__(self, links, sources, target):
        self.links, self.sources, self.target = links, sources, target
        self.moves = row_moves()
        self.first = links.take(len(self.moves))

    def copies(self, branch):
        row, col = lax.axis_index("rows"), lax.axis_index("cols")
        for number, (owner, direction, hop, first, top, size) in enumerate(self.moves):
            if owner == branch and hop:
                yield remote(
                    self.sources[branch][direction].at[pl.ds(first, size)],
                    self.target.at[branch, direction, pl.ds(top, size)],
                    self.links.sends.at[self.first + number],
                    self.links.recvs.at[self.first + number],
                    device_of(lax.rem(row + hop + 32, 32), col),
                )

    def start(self, branch):
        for copy in self.copies(branch):
            copy.start()
        for owner, direction, hop, first, top, size in self.moves:
            if owner == branch and hop == 0:
                self.target[branch, direction, top : top + size] = self.sources[branch][direction][
                    first : first + size
                ]

    def finish(self, branch):
        for copy in self.copies(branch):
            copy.wait_recv()
            copy.wait_send()


MARGIN = 24
SLOTS = (0, 2, 1)
SIDES, CENTER = (pl.ds(0, 2), pl.ds(2, 1))


def silu_value(values):
    return values * jax.nn.sigmoid(values)


def silu_grad(values):
    part = jax.nn.sigmoid(values)
    return part * (1.0 + values * (1.0 - part))


def two_sums(first, second):
    return jnp.concatenate(
        [jnp.sum(first, axis=0, keepdims=True), jnp.sum(second, axis=0, keepdims=True)], axis=0
    )


def centered_values(total, values):
    average = total[0:1] / 16384.0
    variance = total[1:2] / 16384.0 - average * average
    scale = lax.rsqrt(variance + EPSILON)
    return (values - average) * scale, scale


def norm_grad(total, grad, centered, scale, gain):
    return (
        gain * scale * (grad - total[0:1] / 16384.0 - centered * (total[1:2] / 16384.0))
    ).astype(jnp.bfloat16)


def pyramid_kernel(
    grid_ref,
    slab_ref,
    pieces_ref,
    point_hbm,
    pool_hbm,
    project_hbm,
    misc_ref,
    masks_ref,
    seg_ref,
    edge_ref,
    part_ref,
    weights_ref,
    loss_out,
    pooled_out,
    grad_out,
    point_out,
    pool_out,
    project_out,
    norms_out,
    pieces_hbm,
    kernels,
    padded,
    moved_maps,
    taps,
    core_part,
    high_out,
    high_part,
    tap_own,
    rows_out,
    rows_in,
    grads_own,
    grads_in,
    stack,
    grad_taps,
    back_out,
    back_in,
    pieces_out,
    point_ref,
    pool_ref,
    project_ref,
    heads_ref,
    *rest,
):
    bf16, f32 = jnp.bfloat16, jnp.float32
    links = Links(rest[-2], rest[-1])
    totals = [Total(links, *rest[4 * number : 4 * number + 4]) for number in range(5)]
    row, col = lax.axis_index("rows"), lax.axis_index("cols")
    core, high = lax.rem(col, 2), col // 2
    twin = device_of(row, col + 1 - 2 * core)
    far_twin = device_of(row, col + 2 - 4 * high)
    pieces_sem = links.take(4)
    tap_core, tap_high = links.take(6), links.take(6)
    stack_high, stack_core = links.take(6), links.take(6)
    back = links.take(3)
    forward_shift = RowShift(
        links, [[rows_out.at[branch, direction] for direction in range(2)] for branch in range(3)], rows_in
    )
    backward_shift = RowShift(
        links, [[grads_own.at[branch] for _ in range(2)] for branch in range(3)], grads_in
    )
    loads = [
        pltpu.make_async_copy(source, target, links.recvs.at[pieces_sem + number])
        for number, (source, target) in enumerate(
            (
                (pieces_ref, pieces_out),
                (point_hbm, point_ref),
                (pool_hbm, pool_ref),
                (project_hbm, project_ref),
            )
        )
    ]
    stores = [
        pltpu.make_async_copy(
            pieces_out.at[pl.ds(16 * part, 16)],
            pieces_hbm.at[pl.ds(16 * part, 16)],
            links.sends.at[pieces_sem + part],
        )
        for part in range(2)
    ]
    for load in loads:
        load.start()
    peers = total_peers() + row_peers()
    greet(peers)

    members_low = [jnp.where(masks_ref[8] == float(image), 1.0, 0.0) for image in range(4)]
    row_sums = jnp.sum(grid_ref[...].astype(f32), axis=1)
    pieces = []
    for image in range(4):
        chosen = members_low[image]
        pieces.append(
            jnp.concatenate(
                [
                    jnp.sum(row_sums * across_lanes(chosen, CIN), axis=0, keepdims=True),
                    jnp.sum(chosen, axis=0, keepdims=True),
                ],
                axis=1,
            )
        )
    pooled_here = jnp.concatenate(pieces, axis=0)

    def columns_of(place):
        return pl.ds(pl.multiple_of(place * 16, 16), 16)

    padded[:, 0:MARGIN] = jnp.zeros((8, MARGIN, 512), f32)
    padded[:, MARGIN + 64 :] = jnp.zeros((8, MARGIN, 512), f32)
    padded[:, MARGIN : MARGIN + 64] = slab_ref[...].astype(f32)
    for branch, rate in enumerate(rate_list):
        for side in range(2):
            start = MARGIN + (2 * side - 1) * rate
            moved_maps[2 * branch + side] = (
                padded[:, start : start + 64].reshape(512, 512).astype(bf16)
            )
    slab = slab_ref[...].reshape(512, 512)
    for load in loads:
        load.wait()

    def join(pair, carry):
        both = jnp.concatenate(
            [pieces_out[2 * pair, 0:216].astype(f32), pieces_out[2 * pair + 1, 0:216].astype(f32)], axis=0
        )
        kernels[pl.ds(pl.multiple_of(432 * pair, 16), 432)] = both.astype(bf16)
        return carry

    lax.fori_loop(0, 16, join, 0)
    meet(peers)
    totals[4].start(pooled_here)

    def tap_core_copy(branch, place):
        return remote(
            taps.at[pl.ds(3 * branch, 3), :, columns_of(2 * place + 1 - core)],
            core_part.at[branch, place],
            links.sends.at[tap_core + 2 * branch + place],
            links.recvs.at[tap_core + 2 * branch + place],
            twin,
        )

    def tap_high_copy(branch, slots):
        number = tap_high + 2 * branch + slots.start // 2
        return remote(
            high_out.at[branch, slots],
            high_part.at[branch, slots],
            links.sends.at[number],
            links.recvs.at[number],
            far_twin,
        )

    def tap_meet(branch):
        for place in range(2):
            tap_core_copy(branch, place).wait_recv()
        away = taps[pl.ds(3 * branch, 3), :, columns_of(2 * (1 - high) + core)].astype(f32)
        high_out[branch] = (away + core_part[branch, 1 - high].astype(f32)).astype(bf16)
        tap_high_copy(branch, SIDES).start()
        here = taps[pl.ds(3 * branch, 3), :, columns_of(col)].astype(f32)
        tap_own[branch] = here + core_part[branch, high].astype(f32)

    def tap_finish(branch):
        tap_high_copy(branch, SIDES).wait_recv()
        for direction in range(2):
            rows_out[branch, direction] = (
                tap_own[branch, direction] + high_part[branch, direction].astype(f32)
            ).astype(bf16)
        forward_shift.start(branch)

    for branch in range(3):
        result = None
        for col_tap in range(3):
            left = slab if col_tap == 1 else moved_maps[2 * branch + col_tap // 2]
            right = jnp.concatenate(
                [
                    kernels[(9 * branch + 3 * tap + col_tap) * 256 : (9 * branch + 3 * tap + col_tap + 1) * 256]
                    for tap in range(3)
                ],
                axis=0,
            )
            product = against_rows(left, right)
            result = product if result is None else result + product
        for slot, tap in enumerate(SLOTS):
            taps[3 * branch + slot] = result[:, 256 * tap : 256 * tap + 256].astype(bf16).reshape(8, 64, 256)
        for place in range(2):
            tap_core_copy(branch, place).start()
        if branch == 0:
            totals[4].middle()
        else:
            tap_meet(branch - 1)
    tap_meet(2)
    for branch in range(3):
        tap_high_copy(branch, CENTER).start()
    grid = grid_ref[...].reshape(128, CIN)
    branches = [jnp.dot(grid, point_ref[...], preferred_element_type=f32)]
    number = lax.broadcasted_iota(jnp.int32, (256, 256), 0) * HEADS
    lane_256 = lax.broadcasted_iota(jnp.int32, (256, 256), 1)
    number_32 = lax.broadcasted_iota(jnp.int32, (256, 32), 0) * HEADS
    lane_32 = lax.broadcasted_iota(jnp.int32, (256, 32), 1)
    lane_128 = lax.broadcasted_iota(jnp.int32, (256, 128), 1)

    def rows_of_head(head):
        return jnp.where(lane_32 == (number_32 + head) // 256, 1.0, 0.0).astype(bf16)

    def lanes_of_head(head):
        return lane_256 == lax.rem(number + head, 256)

    flat_heads = misc_ref[19:51].astype(bf16)
    heads = jnp.zeros((256, 128), f32)
    for head in range(HEADS):
        spread = jnp.dot(rows_of_head(head), flat_heads, preferred_element_type=f32)
        column = jnp.sum(jnp.where(lanes_of_head(head), spread, 0.0), axis=1, keepdims=True)
        heads = heads + jnp.where(lane_128 == head, column, 0.0)
    heads_ref[...] = heads.astype(bf16)
    bias = jnp.where(
        lax.broadcasted_iota(jnp.int32, (1, 128), 1) < HEADS, misc_ref[36:37, 0:128], 0.0
    )
    pooled_sums = totals[4].finish()
    area = jnp.concatenate([pooled_sums[:, CIN : CIN + 128]] * 16, axis=1) * 16.0
    pooled = pooled_sums[:, 0:CIN] / area
    pooled_out[...] = pooled
    pooled_low = jnp.concatenate([pooled, jnp.zeros((4, CIN), f32)], axis=0).astype(bf16)
    pool_pre = jnp.dot(pooled_low, pool_ref[...], preferred_element_type=f32)[0:4] + misc_ref[0:1]
    pool_act = silu_value(pool_pre)
    members = [across_lanes(pixel_mask(members_low[image]), ASPP) for image in range(4)]
    pool_map = members[0] * pool_act[0:1]
    for image in range(1, 4):
        pool_map = pool_map + members[image] * pool_act[image : image + 1]
    for branch in range(3):
        tap_finish(branch)
    for branch in range(3):
        tap_high_copy(branch, CENTER).wait_recv()
        forward_shift.finish(branch)
        value = (tap_own[branch, 2] + high_part[branch, 2].astype(f32)).reshape(128, 256)
        for direction in range(2):
            mask = across_lanes(pixel_mask(masks_ref[2 + 2 * branch + direction]), ASPP)
            value = value + rows_in[branch, direction].astype(f32).reshape(128, 256) * mask
        branches.append(value)
    before = jnp.concatenate(branches, axis=1)
    totals[0].start(two_sums(before, before * before))
    totals[0].middle()
    gains = jnp.concatenate([misc_ref[9 + 2 * branch : 10 + 2 * branch] for branch in range(4)], axis=1)
    shifts = jnp.concatenate([misc_ref[10 + 2 * branch : 11 + 2 * branch] for branch in range(4)], axis=1)
    centered, scale = centered_values(totals[0].finish(), before)
    normed = centered * gains + shifts
    joined = jnp.concatenate([silu_value(normed).astype(bf16), pool_map.astype(bf16)], axis=1)
    projected = jnp.dot(joined, project_ref[...], preferred_element_type=f32)
    totals[1].start(two_sums(projected, projected * projected))
    totals[1].middle()
    last_gain, last_shift = misc_ref[17:18], misc_ref[18:19]
    proj_centered, proj_scale = centered_values(totals[1].finish(), projected)
    proj_normed = proj_centered * last_gain + last_shift
    feature_map = silu_value(proj_normed).astype(bf16)
    logits = jnp.dot(feature_map, heads_ref[...], preferred_element_type=f32) + bias
    lane = lax.broadcasted_iota(jnp.int32, (128, 128), 1)

    def per_pixel(labels_ref):
        spread = jnp.broadcast_to(labels_ref[...].astype(f32)[:, None, :], (8, 16, 16))
        here = lax.broadcasted_iota(jnp.int32, (8, 16, 16), 1) == lax.broadcasted_iota(
            jnp.int32, (8, 16, 16), 2
        )
        return jnp.sum(jnp.where(here, spread, 0.0), axis=2, keepdims=True).reshape(128, 1)

    lane_value = lane.astype(f32)
    hot = (
        jnp.where(lane_value == per_pixel(seg_ref), 1.0, 0.0)
        + jnp.where(lane == SEG, per_pixel(edge_ref), 0.0)
        + jnp.where(lane_value == per_pixel(part_ref) + (SEG + 1.0), 1.0, 0.0)
    )

    def cross_entropy(inside):
        highest = jnp.max(jnp.where(inside, logits, -3.0e38), axis=1, keepdims=True)
        powers = jnp.where(inside, jnp.exp(jnp.where(inside, logits - highest, 0.0)), 0.0)
        total = jnp.sum(powers, axis=1, keepdims=True)
        picked = jnp.sum(jnp.where(inside, logits * hot, 0.0), axis=1, keepdims=True)
        return highest + jnp.log(total) - picked, powers / total

    seg_inside, part_inside = lane < SEG, jnp.logical_and(lane > SEG, lane < HEADS)
    seg_terms, seg_soft = cross_entropy(seg_inside)
    part_terms, part_soft = cross_entropy(part_inside)
    edge_inside = lane == SEG
    edge_all = (
        jnp.maximum(logits, 0.0) + jnp.log1p(jnp.exp(-jnp.abs(logits))) - hot * logits
    )
    edge_soft = jax.nn.sigmoid(logits)
    weights = [weights_ref[task].astype(f32) for task in range(3)]
    weight_total = weights[0] + weights[1] + weights[2]
    row_lane = lax.broadcasted_iota(jnp.int32, (1, 128), 1)
    shares = jnp.where(
        row_lane < SEG, weights[0], jnp.where(row_lane == SEG, weights[1], weights[2])
    ) / jnp.full((1, 128), weight_total)
    shares = jnp.where(row_lane < HEADS, shares, 0.0)
    terms = jnp.where(lane == 0, seg_terms, 0.0) + jnp.where(edge_inside, edge_all, 0.0)
    terms = (terms + jnp.where(lane == SEG + 1, part_terms, 0.0)) * shares
    loss_local = jnp.sum(jnp.sum(terms, axis=0, keepdims=True), axis=1, keepdims=True) / 16384.0
    soft = seg_soft + part_soft + jnp.where(edge_inside, edge_soft, 0.0)
    logit_grad = ((soft - hot) * shares / 16384.0).astype(bf16)
    feature_back = against_rows(logit_grad, heads_ref[...]) * silu_grad(proj_normed)
    proj_sums = two_sums(feature_back, feature_back * proj_centered)
    totals[2].start(
        jnp.concatenate([proj_sums, jnp.broadcast_to(loss_local, (1, ASPP))], axis=0)
    )
    heads_grad = over_pixels(feature_map, logit_grad)
    norms_out[11:64] = jnp.zeros((53, ASPP), f32)
    flat_grad = None
    for head in range(HEADS):
        column = jnp.broadcast_to(heads_grad[:, head : head + 1], (256, 256))
        spread = jnp.where(lanes_of_head(head), column, 0.0).astype(bf16)
        part = over_pixels(rows_of_head(head), spread)
        flat_grad = part if flat_grad is None else flat_grad + part
    norms_out[11:28] = flat_grad[0:17]
    norms_out[28:29, 0:128] = jnp.sum(logit_grad.astype(f32), axis=0, keepdims=True)
    totals[2].middle()
    total = totals[2].finish()
    loss_out[...] = total[2:3, 0:1]
    projected_grad = norm_grad(total, feature_back, proj_centered, proj_scale, last_gain)
    joined_grad = against_rows(projected_grad, project_ref[...])
    pool_map_grad = joined_grad[:, 4 * ASPP :]
    pool_local = jnp.concatenate(
        [jnp.sum(pool_map_grad * members[image], axis=0, keepdims=True) for image in range(4)], axis=0
    )
    branch_back = joined_grad[:, : 4 * ASPP] * silu_grad(normed)
    branch_sums = two_sums(branch_back, branch_back * centered)
    pool_row = jnp.concatenate([pool_local[image : image + 1] for image in range(4)], axis=1)
    totals[3].start(jnp.concatenate([branch_sums, pool_row], axis=0))
    project_out[...] = over_pixels(joined, projected_grad).astype(bf16)
    totals[3].middle()
    pool_slope = silu_grad(pool_pre)
    pool_pre_local = pool_local * pool_slope
    norms_out[0:1] = jnp.sum(pool_pre_local, axis=0, keepdims=True)
    for branch in range(4):
        lanes = slice(256 * branch, 256 * branch + 256)
        norms_out[1 + 2 * branch : 2 + 2 * branch] = branch_sums[1:2, lanes]
        norms_out[2 + 2 * branch : 3 + 2 * branch] = branch_sums[0:1, lanes]
    norms_out[9:10] = proj_sums[1:2]
    norms_out[10:11] = proj_sums[0:1]
    padding = jnp.zeros((4, ASPP), f32)
    pool_out[...] = over_pixels(
        pooled_low, jnp.concatenate([pool_pre_local, padding], axis=0).astype(bf16)
    ).astype(bf16)
    total = totals[3].finish()
    branch_grad = norm_grad(total, branch_back, centered, scale, gains)
    for branch in range(3):
        grads_own[branch] = branch_grad[:, 256 * branch + 256 : 256 * branch + 512].reshape(8, 16, 256)
        backward_shift.start(branch)

    def stack_high_copy(branch, slots, sender):
        view = stack.at[branch, slots, :, columns_of(sender)]
        number = stack_high + 2 * branch + slots.start // 2
        return remote(view, view, links.sends.at[number], links.recvs.at[number], far_twin)

    def stack_core_copy(branch, place, sender_core):
        view = stack.at[branch, :, :, columns_of(2 * place + sender_core)]
        number = stack_core + 2 * branch + place
        return remote(view, view, links.sends.at[number], links.recvs.at[number], twin)

    for branch in range(3):
        stack[branch, 2, :, columns_of(col)] = grads_own[branch]
        stack_high_copy(branch, CENTER, col).start()
    pool_grad = jnp.concatenate(
        [total[2:3, 256 * image : 256 * image + 256] for image in range(4)], axis=0
    )
    pooled_grad = against_rows(
        jnp.concatenate([pool_grad * pool_slope, padding], axis=0).astype(bf16), pool_ref[...]
    )[0:4] / area
    for branch in range(3):
        backward_shift.finish(branch)
        for slot, direction in ((0, 1), (1, 0)):
            mask = across_lanes(pixel_mask(masks_ref[2 + 2 * branch + direction]), ASPP)
            shifted = grads_in[branch, direction].astype(f32).reshape(128, 256) * mask
            stack[branch, slot, :, columns_of(col)] = shifted.astype(bf16).reshape(8, 16, 256)
        stack_high_copy(branch, SIDES, col).start()
    point_grad = branch_grad[:, 0:256]
    point_out[...] = over_pixels(grid, point_grad).astype(bf16)
    grad_out[...] = against_rows(point_grad, point_ref[...])
    for image in range(4):
        grad_out[...] = grad_out[...] + across_lanes(
            pixel_mask(members_low[image]), CIN
        ) * pooled_grad[image : image + 1]
    for branch in range(3):
        for slots in (SIDES, CENTER):
            stack_high_copy(branch, slots, col + 2 - 4 * high).wait_recv()
        for place in range(2):
            stack_core_copy(branch, place, core).start()
    def split(pair, carry):
        both = kernels[pl.ds(pl.multiple_of(432 * pair, 16), 432)].astype(f32)
        zeros = jnp.zeros((8, 512), f32)
        pieces_out[2 * pair] = jnp.concatenate([both[0:216], zeros], axis=0).astype(bf16)
        pieces_out[2 * pair + 1] = jnp.concatenate([both[216:432], zeros], axis=0).astype(bf16)
        return carry

    slab_grad = None
    for branch, rate in enumerate(rate_list):
        for place in range(2):
            stack_core_copy(branch, place, 1 - core).wait_recv()
        for slot, tap in enumerate(SLOTS):
            padded[:, MARGIN : MARGIN + 64, 0:256] = stack[branch, slot].astype(f32)
            for col_tap in range(3):
                start = MARGIN - (col_tap - 1) * rate
                lanes = slice(256 * (3 * tap + col_tap), 256 * (3 * tap + col_tap) + 256)
                grad_taps[:, lanes] = (
                    padded[:, start : start + 64, 0:256].reshape(512, 256).astype(bf16)
                )
        rows = slice(2304 * branch, 2304 * branch + 2304)
        product = jnp.dot(grad_taps[...], kernels[rows], preferred_element_type=f32)
        slab_grad = product if slab_grad is None else slab_grad + product
        kernels[rows] = over_pixels(grad_taps[...], slab).astype(bf16)
        if branch == 1:
            lax.fori_loop(0, 8, split, 0)
            stores[0].start()
    back_out[...] = slab_grad.astype(bf16).reshape(8, 64, 512)

    def back_copy(step, sender):
        return remote(
            back_out.at[:, columns_of(lax.rem(col + step, 4))],
            back_in.at[:, :, pl.ds(pl.multiple_of(sender * 512, 512), 512)],
            links.sends.at[back + step - 1],
            links.recvs.at[back + step - 1],
            device_of(row, lax.rem(col + step, 4)),
        )

    for step in (1, 2, 3):
        back_copy(step, col).start()
    back_in[:, :, pl.ds(pl.multiple_of(col * 512, 512), 512)] = back_out[:, columns_of(col)]

    lax.fori_loop(8, 16, split, 0)
    stores[1].start()
    for step in (1, 2, 3):
        copy = back_copy(step, lax.rem(col + 4 - step, 4))
        copy.wait_recv()
        copy.wait_send()
    grad_out[...] = grad_out[...] + back_in[...].reshape(128, CIN).astype(f32)
    for branch in range(3):
        for place in range(2):
            tap_core_copy(branch, place).wait_send()
            stack_core_copy(branch, place, core).wait_send()
        for slots in (SIDES, CENTER):
            tap_high_copy(branch, slots).wait_send()
            stack_high_copy(branch, slots, col).wait_send()
    for store in stores:
        store.wait()
    for total in totals:
        total.close()


def pyramid(arrays, collective):
    bf16, f32 = jnp.bfloat16, jnp.float32
    outs = [
        ((1, 1), f32),
        ((4, CIN), f32),
        ((128, CIN), f32),
        ((CIN, ASPP), bf16),
        ((CIN, ASPP), bf16),
        ((5 * ASPP, ASPP), bf16),
        ((64, ASPP), f32),
        ((32, RATE_ROWS, 512), bf16),
    ]
    scratch = [
        pltpu.VMEM((27 * ASPP, 512), bf16),
        pltpu.VMEM((8, 64 + 2 * MARGIN, 512), f32),
        pltpu.VMEM((6, 512, 512), bf16),
        pltpu.VMEM((9, 8, 64, ASPP), bf16),
        pltpu.VMEM((3, 2, 3, 8, 16, ASPP), bf16),
        pltpu.VMEM((3, 3, 8, 16, ASPP), bf16),
        pltpu.VMEM((3, 3, 8, 16, ASPP), bf16),
        pltpu.VMEM((3, 3, 8, 16, ASPP), f32),
        pltpu.VMEM((3, 2, 8, 16, ASPP), bf16),
        pltpu.VMEM((3, 2, 8, 16, ASPP), bf16),
        pltpu.VMEM((3, 8, 16, ASPP), bf16),
        pltpu.VMEM((3, 2, 8, 16, ASPP), bf16),
        pltpu.VMEM((3, 3, 8, 64, ASPP), bf16),
        pltpu.VMEM((512, 9 * ASPP), bf16),
        pltpu.VMEM((8, 64, 512), bf16),
        pltpu.VMEM((8, 16, CIN), bf16),
        pltpu.VMEM((32, RATE_ROWS, 512), bf16),
        pltpu.VMEM((CIN, ASPP), bf16),
        pltpu.VMEM((CIN, ASPP), bf16),
        pltpu.VMEM((5 * ASPP, ASPP), bf16),
        pltpu.VMEM((ASPP, 128), bf16),
    ]
    for rows, columns in ((2, 4 * ASPP), (2, ASPP), (3, ASPP), (3, 4 * ASPP), (4, CIN + 128)):
        scratch += total_scratch(rows, columns)
    scratch += [pltpu.SemaphoreType.DMA((184,)), pltpu.SemaphoreType.DMA((184,))]
    in_specs = [VMEM] * len(arrays)
    in_specs[2:6] = [ANY] * 4
    in_specs[-1] = SMEM
    return pl.pallas_call(
        pyramid_kernel,
        out_shape=[jax.ShapeDtypeStruct(shape, dtype) for shape, dtype in outs],
        in_specs=in_specs,
        out_specs=[VMEM] * (len(outs) - 1) + [ANY],
        scratch_shapes=scratch,
        compiler_params=pltpu.CompilerParams(
            collective_id=collective, has_side_effects=True, vmem_limit_bytes=62 * MEGABYTE
        ),
    )(*arrays)


def finish_kernel(
    loss_ref,
    pooled_ref,
    gradient_ref,
    flat_ref,
    rate_ref,
    block_ref,
    head_ref,
    rate_moment_ref,
    loss_out,
    pooled_out,
    gradient_out,
    block_out,
    head_out,
    rate_out,
):
    loss_out[...] = loss_ref[...]
    pooled_out[...] = pooled_ref[...]
    gradient_out[...] = gradient_ref[...]
    block_out[...] = MOMENTUM_KEEP * block_ref[...] + flat_ref[0:BLOCK_ROWS, :]
    head_out[...] = MOMENTUM_KEEP * head_ref[...] + flat_ref[BLOCK_ROWS : BLOCK_ROWS + HEAD_ROWS, :]
    rate_out[...] = MOMENTUM_KEEP * rate_moment_ref[...] + rate_ref[0:216]


def finish(loss, pooled, gradient, flat, rate, block_moment, head_moment, rate_moment):
    like = (loss, pooled, gradient, block_moment, head_moment, rate_moment)
    return pl.pallas_call(
        finish_kernel,
        out_shape=[jax.ShapeDtypeStruct(item.shape, jnp.float32) for item in like],
        in_specs=[VMEM] * 8,
        out_specs=[VMEM] * 6,
        compiler_params=pltpu.CompilerParams(vmem_limit_bytes=32 * MEGABYTE),
    )(loss, pooled, gradient, flat, rate, block_moment, head_moment, rate_moment)


def per_device(
    features,
    image_rows,
    seg_labels,
    edge_labels,
    part_labels,
    task_weights,
    block_params,
    block_moment,
    head_params,
    head_moment,
    rate_params,
    rate_moment,
):
    height, across, channels = features.shape
    pixels = height * across
    inputs = features.reshape(pixels, channels)
    (
        w_reduce,
        w_spatial,
        w_expand,
        w_point,
        w_pool,
        w_project,
        misc,
        norms,
        masks,
        first_kept,
        second_kept,
        third_kept,
        second_act,
        block_window,
        grid,
        slab_map,
        rates_all,
    ) = block_forward(
        (
            inputs,
            block_params.reshape(BLOCK_ROWS, 128),
            head_params.reshape(HEAD_ROWS, 128),
            image_rows,
            rate_params.T,
        ),
        1,
    )
    (
        loss_rows,
        pooled,
        out_grad,
        grad_point,
        grad_pool,
        grad_project,
        misc_grads,
        rate_pieces,
    ) = pyramid(
        (
            grid,
            slab_map,
            rates_all.reshape(32, RATE_ROWS, channels // 4),
            w_point,
            w_pool,
            w_project,
            misc,
            masks,
            seg_labels,
            edge_labels,
            part_labels,
            task_weights,
        ),
        2,
    )
    input_grad, *flat_sums = block_backward(
        (
            inputs,
            out_grad,
            norms,
            masks,
            first_kept,
            second_kept,
            third_kept,
            second_act,
            block_window,
            w_reduce,
            w_spatial,
            w_expand,
            grad_point,
            grad_pool,
            grad_project,
            misc_grads,
            rate_pieces.reshape(2, 4, 4, RATE_ROWS, channels // 4),
        ),
        16,
    )
    shares_all, rate_sum = scatter_params(flat_sums, 20)
    loss_out, pooled_out, gradient, block_next, head_next, rate_next = finish(
        loss_rows,
        pooled,
        input_grad,
        shares_all,
        rate_sum,
        block_moment.reshape(BLOCK_ROWS, 128),
        head_moment.reshape(HEAD_ROWS, 128),
        rate_moment.T,
    )
    return (
        loss_out.reshape(()),
        pooled_out,
        gradient.reshape(height, across, channels),
        block_next.reshape(-1),
        head_next.reshape(-1),
        rate_next.T,
    )


def solution(mesh):
    return jax.shard_map(
        per_device,
        mesh=mesh,
        in_specs=(
            P("rows", "cols", None),
            P("rows"),
            P("rows", "cols"),
            P("rows", "cols"),
            P("rows", "cols"),
            P(),
            P(("rows", "cols")),
            P(("rows", "cols")),
            P(("rows", "cols")),
            P(("rows", "cols")),
            P("cols", "rows"),
            P("cols", "rows"),
        ),
        out_specs=(
            P(),
            P(),
            P("rows", "cols", None),
            P(("rows", "cols")),
            P(("rows", "cols")),
            P("cols", "rows"),
        ),
        check_vma=False,
    )
```

```python
import functools
import math

import jax
import jax.numpy as jnp
from jax import lax
from jax.experimental import pallas as pl
from jax.experimental.pallas import tpu as pltpu
from jax.sharding import PartitionSpec as P

MESH = pl.DeviceIdType.MESH
ANY = pl.BlockSpec(memory_space=pl.ANY)
VMEM = pl.BlockSpec(memory_space=pltpu.VMEM)
SMEM = pl.BlockSpec(memory_space=pltpu.SMEM)
BLOCK_ROWS = 273
HEAD_ROWS = 85
PAYLOAD = 384

CIN = 2048
MID = 512
ASPP = 256
SEG = 13
PART = 3
HEADS = 17


EPSILON = 1e-05
MOMENTUM_KEEP = 0.5
rate_list = (6, 12, 18)
block_dilation = 4
widest_margin = 18


def device_of(row, col):
    return {"rows": row, "cols": col}


def split_place():
    row, col = lax.axis_index("rows"), lax.axis_index("cols")
    return {
        "y": (row // 16) + 2 * (col // 2),
        "x": lax.rem(row // 4, 4),
        "z": lax.rem(row, 4),
        "core": lax.rem(col, 2),
    }


def device_at(place):
    row = lax.rem(place["y"], 2) * 16 + place["x"] * 4 + place["z"]
    return device_of(row, (place["y"] // 2) * 2 + place["core"])


def moved(place, axis, step, extent=4):
    other = dict(place)
    other[axis] = lax.rem(place[axis] + step + extent, extent)
    return other


def greet(peers):
    barrier = pltpu.get_barrier_semaphore()
    for device in peers:
        pl.semaphore_signal(barrier, inc=1, device_id=device, device_id_type=MESH)


def meet(peers):
    pl.semaphore_wait(pltpu.get_barrier_semaphore(), len(peers))


def remote(source, target, send_sem, recv_sem, device):
    return pltpu.make_async_remote_copy(
        src_ref=source,
        dst_ref=target,
        send_sem=send_sem,
        recv_sem=recv_sem,
        device_id=device,
        device_id_type=MESH,
    )


GATHER_ORDERS = (("z", "x", "y"), ("x", "y", "z"), ("y", "z", "x"))


def axis_view(place, fixed):
    index = [slice(None)] * 4
    if "y" in fixed:
        index[0], index[3] = lax.rem(place["y"], 2), place["y"] // 2
    if "x" in fixed:
        index[1] = place["x"]
    if "z" in fixed:
        index[2] = place["z"]
    return tuple(index)


def scatter_kernel(p_ref, late_ref, pair_ref, o_ref, share_ref, held, rate_parts, rate_sums, rate_pair, *rest):
    relays = rest[0:3]
    parts = [rest[3 + 3 * third : 6 + 3 * third] for third in range(3)]
    sums = [rest[12 + 2 * third : 14 + 2 * third] for third in range(3)]
    links = Links(rest[-2], rest[-1])
    first, own_first = links.take(48), links.take(3)
    rates = RateScatter(links, late_ref, rate_parts)
    me = rates.me
    everywhere = (slice(None),) * 4
    own_copies = []
    for third in range(3):
        rows = pl.ds(third * 128, 128)
        own_copies.append(
            pltpu.make_async_copy(
                p_ref.at[everywhere + (rows,)],
                held.at[everywhere + (rows,)],
                links.sends.at[own_first + third],
            )
        )
        own_copies[third].start()
    partners = [moved(me, axis, step) for axis in "xyz" for step in (1, 2, 3)]
    peers = [device_at(place) for place in partners]
    greet(peers)
    meet(peers)
    rates.send()

    def view_of(third, phase, place, part=None):
        order = GATHER_ORDERS[third]
        axis = order[2 - phase]
        start, size = (0, 128) if part is None else (64 * part, 64)
        if phase == 0:
            return held.at[axis_view(place, [axis]) + (pl.ds(third * 128 + start, size),)]
        index = []
        for name, key in (("y", 0), ("x", 1), ("z", 2), ("y", 3)):
            if name not in order[: 3 - phase]:
                continue
            if name != axis:
                index.append(slice(None))
            elif name == "y":
                index.append(lax.rem(place["y"], 2) if key == 0 else place["y"] // 2)
            else:
                index.append(place[name])
        return sums[third][phase - 1].at[tuple(index) + (pl.ds(start, size),)]

    def link(third, phase, kind, step, outgoing, incoming):
        number = first + 16 * third + (6 + 5 * (phase - 1) if phase else 0) + kind
        return remote(
            outgoing,
            incoming,
            links.sends.at[number],
            links.recvs.at[number],
            device_at(moved(me, GATHER_ORDERS[third][2 - phase], step)),
        )

    def relay(third, step):
        axis = GATHER_ORDERS[third][2]
        outgoing = view_of(third, 0, moved(me, axis, 2), step // 2)
        return link(third, 0, 4 + step // 2, step, outgoing, relays[third].at[step // 2])

    def half_copy(third, step, part):
        axis = GATHER_ORDERS[third][2]
        outgoing = view_of(third, 0, moved(me, axis, step), part)
        target = parts[third][0]
        view = (step // 2,) + (slice(None),) * (len(target.shape) - 3) + (pl.ds(64 * part, 64),)
        return link(third, 0, step // 2 * 2 + part, step, outgoing, target.at[view])

    def copy(third, phase, step):
        axis = GATHER_ORDERS[third][2 - phase]
        outgoing = view_of(third, phase, moved(me, axis, step))
        return link(third, phase, step - 1, step, outgoing, parts[third][phase].at[step - 1])

    for third in range(3):
        own_copies[third].wait()
        for step in (1, 3):
            relay(third, step).start()
        for step in (1, 3):
            half_copy(third, step, 1 - step // 2).start()
    for third in range(3):
        axis = GATHER_ORDERS[third][2]
        for step in (1, 3):
            relay(third, step).wait_recv()
            view = view_of(third, 0, moved(me, axis, step), step // 2)
            view[...] = view[...] + relays[third][step // 2]
            half_copy(third, step, step // 2).start()
    rate_sums[0] = pair_ref[...]
    rates.collect(rate_sums.at[1])
    rate_exchange = rates.pair(rate_sums.at[1 - rates.low_y], rate_pair)
    rate_exchange.start()
    for phase in range(1, 4):
        for third in range(3):
            total = view_of(third, phase - 1, me)[...].astype(jnp.float32)
            for slot, step in enumerate((1, 2, 3) if phase > 1 else (1, 3)):
                if phase > 1:
                    copy(third, phase - 1, step).wait_recv()
                else:
                    for part in range(2):
                        half_copy(third, step, part).wait_recv()
                total = total + parts[third][phase - 1][slot].astype(jnp.float32)
            if phase == 3:
                o_ref[128 * third : 128 * third + 128] = total
            else:
                sums[third][phase - 1][...] = total.astype(jnp.bfloat16)
                for step in (1, 2, 3):
                    copy(third, phase, step).start()
    rate_exchange.wait()
    for half in range(2):
        rows = slice(half * (RATE_ROWS // 2), (half + 1) * (RATE_ROWS // 2))
        share_ref[rows] = rate_sums[rates.low_y, half].astype(jnp.float32) + rate_pair[half].astype(
            jnp.float32
        )
    for third in range(3):
        for step in (1, 3):
            relay(third, step).wait_send()
            for part in range(2):
                half_copy(third, step, part).wait_send()
        for phase in (1, 2):
            for step in (1, 2, 3):
                copy(third, phase, step).wait_send()


def scatter_params(arrays, collective):
    def shape_left(left, rows):
        shape = ()
        for name, number in (("y", 2), ("x", 4), ("z", 4), ("y", 2)):
            if name in left:
                shape += (number,)
        return shape + (rows, 128)

    relays = []
    parts = []
    sums = []
    for order in GATHER_ORDERS:
        relays.append(pltpu.VMEM((2,) + shape_left(order[:2], 64), jnp.bfloat16))
        for phase in range(3):
            number = 3 if phase else 2
            parts.append(pltpu.VMEM((number,) + shape_left(order[: 2 - phase], 128), jnp.bfloat16))
        for phase in range(2):
            sums.append(pltpu.VMEM(shape_left(order[: 2 - phase], 128), jnp.bfloat16))
    held = pltpu.VMEM((2, 4, 4, 2, PAYLOAD, 128), jnp.bfloat16)
    half = (2, RATE_ROWS // 2, 512)
    rates = [pltpu.VMEM(shape, jnp.bfloat16) for shape in ((2, 3) + half[1:], (2,) + half, half)]
    return pl.pallas_call(
        scatter_kernel,
        out_shape=[
            jax.ShapeDtypeStruct((PAYLOAD, 128), jnp.float32),
            jax.ShapeDtypeStruct((RATE_ROWS, 512), jnp.float32),
        ],
        in_specs=[ANY, VMEM, VMEM],
        out_specs=[VMEM, VMEM],
        scratch_shapes=[held]
        + rates
        + relays
        + parts
        + sums
        + [pltpu.SemaphoreType.DMA((72,)), pltpu.SemaphoreType.DMA((72,))],
        compiler_params=pltpu.CompilerParams(
            collective_id=collective, has_side_effects=True, vmem_limit_bytes=56 * MEGABYTE
        ),
    )(*arrays)


def neighbour(row, col, offset):
    return lax.rem(row + offset[0] + 32, 32), lax.rem(col + offset[1] + 4, 4)


MEGABYTE = 1024 * 1024
OFFSETS = (-4, 4, -6, 6, -12, 12, -18, 18)
ID_ROW = 368
RATE_ROWS = 224


class Links:
    def __init__(self, sends, recvs):
        self.sends, self.recvs = sends, recvs
        self.cursor = 0

    def take(self, number):
        first = self.cursor
        self.cursor = first + number
        return first


class Total:
    def __init__(self, links, near_value, far_value, near, far):
        self.links = links
        self.values, self.buffers = (near_value, far_value), (near, far)
        self.first = links.take(2)
        self.row, self.col = lax.axis_index("rows"), lax.axis_index("cols")
        self.me = ((self.row // 16) * 4 + self.col, lax.rem(self.row, 16))

    def device(self, far, index):
        if far:
            return device_of((self.row // 16) * 16 + index, self.col)
        return device_of((index // 4) * 16 + self.me[1], lax.rem(index, 4))

    def link(self, far, outgoing, incoming, index):
        return remote(
            outgoing,
            incoming,
            self.links.sends.at[self.first + far],
            self.links.recvs.at[self.first + far],
            self.device(far, index),
        )

    def send(self, far, value):
        buffer, me, size = self.buffers[far], self.me[far], self.buffers[far].shape[0]
        self.values[far][...] = value
        for step in range(1, size):
            self.link(far, self.values[far], buffer.at[me], lax.rem(me + step, size)).start()
        buffer[me] = value

    def others(self, far):
        buffer, me, size = self.buffers[far], self.me[far], self.buffers[far].shape[0]
        view = buffer.at[pl.ds(0, size - 1)]
        return self.link(far, view, view, lax.rem(me + 1, size))

    def collect(self, far):
        self.others(far).wait_recv()
        total = self.buffers[far][0]
        for index in range(1, self.buffers[far].shape[0]):
            total = total + self.buffers[far][index]
        return total

    def start(self, value):
        self.send(0, value)

    def middle(self):
        self.send(1, self.collect(0))

    def finish(self):
        return self.collect(1)

    def close(self):
        for far in range(2):
            self.others(far).wait_send()


def total_scratch(rows, columns):
    return [
        pltpu.VMEM((rows, columns), jnp.float32),
        pltpu.VMEM((rows, columns), jnp.float32),
        pltpu.VMEM((8, rows, columns), jnp.float32),
        pltpu.VMEM((16, rows, columns), jnp.float32),
    ]


def total_peers():
    row, col = lax.axis_index("rows"), lax.axis_index("cols")
    near_me, far_me = (row // 16) * 4 + col, lax.rem(row, 16)
    peers = []
    for step in range(1, 8):
        index = lax.rem(near_me + step, 8)
        peers.append(device_of((index // 4) * 16 + far_me, lax.rem(index, 4)))
    for step in range(1, 16):
        peers.append(device_of((row // 16) * 16 + lax.rem(far_me + step, 16), col))
    return peers


def halo_peers():
    row, col = lax.axis_index("rows"), lax.axis_index("cols")
    return [
        device_of(*neighbour(row, col, (row_step, col_step)))
        for row_step in (-1, 0, 1)
        for col_step in (-1, 0, 1)
        if (row_step, col_step) != (0, 0)
    ]


class Halo:
    def __init__(self, links, source, window):
        self.links, self.source, self.window = links, source, window
        self.first = links.take(9)

    def copies(self, own_side):
        row, col = lax.axis_index("rows"), lax.axis_index("cols")
        listed = []
        for row_step in (-1, 0, 1):
            for col_step in (-1, 0, 1):
                if (row_step, col_step) == (0, 0):
                    continue
                low, size, top = {-1: (0, 4, 12), 0: (0, 8, 4), 1: (4, 4, 0)}[row_step]
                left = {-1: 32, 0: 16, 1: 0}[col_step]
                number = self.first + 3 * (row_step + 1) + col_step + 1
                listed.append(
                    remote(
                        self.source.at[pl.ds(low, size)],
                        self.window.at[pl.ds(top, size), pl.ds(left, 16)],
                        self.links.sends.at[number],
                        self.links.recvs.at[number],
                        device_of(*neighbour(row, col, (row_step, col_step))),
                    )
                )
        return listed

    def start(self):
        for copy in self.copies(True):
            copy.start()
        self.window[4:12, 16:32] = self.source[...]

    def finish(self):
        for copy in self.copies(False):
            copy.wait_recv()
        for copy in self.copies(False):
            copy.wait_send()


def widen_window(window, wide):
    col = lax.axis_index("cols")
    left = jnp.where(col > 0, 1.0, 0.0)
    right = jnp.where(col < 3, 1.0, 0.0)
    wide[:, 0:16] = window[:, 0:16].astype(jnp.float32) * left
    wide[:, 16:32] = window[:, 16:32].astype(jnp.float32)
    wide[:, 32:48] = window[:, 32:48].astype(jnp.float32) * right


def pixel_mask(mask):
    return jnp.broadcast_to(mask[:, None, :], (8, 16, 128)).reshape(128, 128)


def across_lanes(mask, width):
    return jnp.concatenate([mask] * (width // 128), axis=1)


class Gather:
    def __init__(self, links, source, target):
        self.links, self.source, self.target = links, source, target
        self.first = links.take(48)
        self.core_first = links.take(12)
        self.me = split_place()
        self.twin = moved(self.me, "core", 1, 2)

    def block(self, place, third, free, part=None):
        fixed = [axis for axis in "xyz" if axis not in free]
        rows = pl.ds(third * 128, 128) if part is None else pl.ds(third * 128 + 64 * part, 64)
        return self.target.at[axis_view(place, fixed) + (place["core"], rows)]

    def link(self, third, phase, kind, step, outgoing, incoming):
        number = self.first + 16 * third + 5 * phase + kind
        return remote(
            outgoing,
            incoming,
            self.links.sends.at[number],
            self.links.recvs.at[number],
            device_at(moved(self.me, GATHER_ORDERS[third][phase], step)),
        )

    def copy(self, third, phase, step, sender):
        free = GATHER_ORDERS[third][:phase]
        if phase == 0:
            outgoing = self.source.at[pl.ds(third * 128, 128)]
        else:
            outgoing = self.block(self.me, third, free)
        return self.link(third, phase, step - 1, step, outgoing, self.block(sender, third, free))

    def half(self, third, step, part, sender):
        free = GATHER_ORDERS[third][:2]
        outgoing = self.block(self.me, third, free, part)
        return self.link(third, 2, step // 2 * 2 + part, step, outgoing, self.block(sender, third, free, part))

    def relay(self, third, step, sender):
        order = GATHER_ORDERS[third]
        view = self.block(moved(sender, order[2], 4 - step), third, order[:2], step // 2)
        return self.link(third, 2, 4 + step // 2, step, view, view)

    def core_copy(self, third, distance, sender):
        order = GATHER_ORDERS[third]
        view = self.block(moved(sender, order[2], distance), third, order[:2])
        number = self.core_first + 4 * third + distance
        return remote(
            view, view, self.links.sends.at[number], self.links.recvs.at[number], device_at(self.twin)
        )

    def behind(self, third, phase, step):
        return moved(self.me, GATHER_ORDERS[third][phase], 4 - step)

    def run(self, early, late):
        me = self.me
        for phase in range(2):
            for third in range(3):
                if phase > 0:
                    for step in (1, 2, 3):
                        self.copy(third, phase - 1, step, self.behind(third, phase - 1, step)).wait_recv()
                for step in (1, 2, 3):
                    self.copy(third, phase, step, me).start()
                if phase == 0:
                    self.block(me, third, ())[...] = self.source[pl.ds(third * 128, 128)]
            if phase == 0:
                early()
        for third in range(3):
            for step in (1, 2, 3):
                self.copy(third, 1, step, self.behind(third, 1, step)).wait_recv()
            for first in (0, 1):
                for step in (1, 3):
                    self.half(third, step, (step // 2 + first) % 2, me).start()
            self.core_copy(third, 0, me).start()
        for third in range(3):
            for step in (1, 3):
                self.half(third, step, step // 2, self.behind(third, 2, step)).wait_recv()
                self.relay(third, step, me).start()
        for third in range(3):
            for step in (1, 3):
                self.half(third, step, 1 - step // 2, self.behind(third, 2, step)).wait_recv()
                self.core_copy(third, 4 - step, me).start()
        late()
        for third in range(3):
            for step in (1, 3):
                self.relay(third, step, self.behind(third, 2, step)).wait_recv()
            self.core_copy(third, 2, me).start()
        for third in range(3):
            for distance in range(4):
                self.core_copy(third, distance, self.twin).wait_recv()

    def close(self):
        for third in range(3):
            for phase in range(2):
                for step in (1, 2, 3):
                    self.copy(third, phase, step, self.me).wait_send()
            for step in (1, 3):
                self.relay(third, step, self.me).wait_send()
                for part in range(2):
                    self.half(third, step, part, self.me).wait_send()
            for distance in range(4):
                self.core_copy(third, distance, self.me).wait_send()


RATE_ORDERS = (("x", "z"), ("z", "x"))


class RateGather:
    def __init__(self, links, source, target):
        self.links, self.source, self.target = links, source, target
        self.first = links.take(82)
        self.me = split_place()
        self.low_y = lax.rem(self.me["y"], 2)
        self.other = dict(self.me)
        self.other["y"] = self.me["y"] + 1 - 2 * self.low_y
        self.half = RATE_ROWS // 2

    def own(self):
        return pltpu.make_async_copy(
            self.source,
            self.target.at[self.low_y, self.me["x"], self.me["z"]],
            self.links.recvs.at[self.first + 81],
        )

    def pair(self, sender):
        return remote(
            self.source,
            self.target.at[lax.rem(sender["y"], 2), self.me["x"], self.me["z"]],
            self.links.sends.at[self.first + 80],
            self.links.recvs.at[self.first + 80],
            device_at(self.other),
        )

    def axis(self, half, unit):
        return RATE_ORDERS[half][0 if unit < 2 else 1]

    def piece(self, half, unit, place, part=None):
        near = RATE_ORDERS[half][0]
        low_y = lax.rem(self.low_y + (unit if unit < 2 else (unit - 2) // 4), 2)
        places = {"x": place["x"], "z": place["z"]}
        if unit >= 2:
            places[near] = lax.rem(places[near] + (unit - 2) % 4, 4)
        start, size = {None: (0, 112), 0: (0, 64), 1: (64, 48)}[part]
        return self.target.at[low_y, places["x"], places["z"], pl.ds(half * self.half + start, size)]

    def link(self, half, unit, kind, step, view):
        number = self.first + 8 * unit + 4 * half + 2 * kind + step // 2
        return remote(
            view,
            view,
            self.links.sends.at[number],
            self.links.recvs.at[number],
            device_at(moved(self.me, self.axis(half, unit), step)),
        )

    def copy(self, half, unit, step, sender):
        return self.link(half, unit, 0, step, self.piece(half, unit, sender))

    def relay(self, half, unit, step, sender):
        first = moved(sender, self.axis(half, unit), 4 - step)
        return self.link(half, unit, 1, step, self.piece(half, unit, first, step // 2))

    def behind(self, half, unit, step):
        return moved(self.me, self.axis(half, unit), 4 - step)

    def each(self):
        return [(half, step) for half in range(2) for step in (1, 3)]

    def begin(self):
        self.own().start()
        self.pair(self.me).start()

    def send(self, *units):
        for unit in units:
            if unit == 0:
                self.own().wait()
            if unit == 1:
                self.pair(self.other).wait_recv()
            for half, step in self.each():
                self.copy(half, unit, step, self.me).start()

    def forward(self, *units):
        for unit in units:
            for half, step in self.each():
                self.copy(half, unit, step, self.behind(half, unit, step)).wait_recv()
                self.relay(half, unit, step, self.me).start()

    def receive(self, *units):
        for unit in units:
            for half, step in self.each():
                self.relay(half, unit, step, self.behind(half, unit, step)).wait_recv()

    def close(self):
        self.pair(self.me).wait_send()
        for unit in range(10):
            for half, step in self.each():
                self.copy(half, unit, step, self.me).wait_send()
                self.relay(half, unit, step, self.me).wait_send()


def assemble(gathered, first_row_group, staging, wide, stride, begin_group=0, end_group=16):
    parts = len(wide)
    count, offset = (BLOCK_ROWS, 0) if parts == 4 else (HEAD_ROWS, BLOCK_ROWS)

    def step(group, carry):
        low_y, x, z = first_row_group // 16, group // 4, lax.rem(group, 4)
        for column in range(4):
            area = staging[column]
            if parts == 4:
                area[0:288] = gathered[low_y, x, z, column // 2, column % 2, 0:288].astype(jnp.float32)
            else:
                area[0:96] = gathered[low_y, x, z, column // 2, column % 2, 272:368].astype(jnp.float32)
            skip = offset - (0 if parts == 4 else 272)
            for part in range(parts):
                begin = (part - column * count) % parts
                number = (count - begin + parts - 1) // parts
                row = (column * count + begin - part) // parts
                group_rows = 4 * count // parts
                target = group_rows * (group + stride) + row
                wide[part][pl.ds(target, number), :] = area[
                    pl.ds(skip + begin, number, stride=parts), :
                ]
        return carry

    lax.fori_loop(begin_group, end_group, step, 0)


def wide_rows(wide, first, number):
    return jnp.concatenate([part[pl.ds(first, number), :] for part in wide], axis=1)


def block_forward_kernel(
    x_ref,
    block_ref,
    head_ref,
    image_ref,
    rate_params_ref,
    reduce_hbm,
    spatial_hbm,
    expand_hbm,
    point_hbm,
    pool_hbm,
    project_hbm,
    misc_ref,
    norms_ref,
    masks_ref,
    first_ref,
    second_ref,
    third_ref,
    act_ref,
    window_ref,
    out_ref,
    slab_ref,
    rates_ref,
    gathered,
    s0,
    s1,
    s2,
    s3,
    w0,
    w1,
    w2,
    w3,
    h0,
    h1,
    ids,
    wide,
    act_map,
    payload_wide,
    payload_ref,
    rate_ref,
    reduce_ref,
    spatial_ref,
    expand_ref,
    point_ref,
    pool_ref,
    project_ref,
    *rest,
):
    staging, matrix, head = (s0, s1, s2, s3), (w0, w1, w2, w3), (h0, h1)
    links = Links(rest[-2], rest[-1])
    totals = [Total(links, *rest[4 * number : 4 * number + 4]) for number in range(3)]
    peers = total_peers() + halo_peers()
    greet(peers)
    payload_wide[0:BLOCK_ROWS, :] = block_ref[...]
    payload_wide[BLOCK_ROWS : BLOCK_ROWS + HEAD_ROWS, :] = head_ref[...]
    payload_wide[BLOCK_ROWS + HEAD_ROWS : PAYLOAD, :] = jnp.zeros(
        (PAYLOAD - BLOCK_ROWS - HEAD_ROWS, 128), jnp.float32
    )
    for step in range(8):
        payload_wide[ID_ROW + step : ID_ROW + step + 1, :] = jnp.full(
            (1, 128), image_ref[step].astype(jnp.float32)
        )
    payload_ref[...] = payload_wide[...].astype(jnp.bfloat16)
    rate_ref[...] = jnp.concatenate(
        [rate_params_ref[...], jnp.zeros((RATE_ROWS - 216, 512), jnp.float32)], axis=0
    ).astype(jnp.bfloat16)
    gather = Gather(links, payload_ref, gathered)
    rates = RateGather(links, rate_ref, rates_ref)
    halo = Halo(links, act_map, window_ref)
    slab_first = links.take(3)
    out_first = links.take(6)
    stores = [
        pltpu.make_async_copy(source, target, links.sends.at[out_first + number])
        for number, (source, target) in enumerate(
            (
                (reduce_ref, reduce_hbm),
                (spatial_ref, spatial_hbm),
                (expand_ref, expand_hbm),
                (point_ref, point_hbm),
                (pool_ref, pool_hbm),
                (project_ref, project_hbm),
            )
        )
    ]
    row, col = lax.axis_index("rows"), lax.axis_index("cols")
    meet(peers)

    def rates_early():
        rates.begin()
        rates.send(0)

    def rates_late():
        rates.forward(0)
        rates.send(2, 1, 3, 5)

    gather.run(rates_early, rates_late)

    assemble(gathered, 0, staging, matrix, 0, 0, 8)
    for step in range(8):
        reduce_ref[256 * step : 256 * step + 256] = wide_rows(matrix, 256 * step, 256).astype(jnp.bfloat16)
    first = jnp.dot(x_ref[...], reduce_ref[...], preferred_element_type=jnp.float32)
    totals[0].start(
        jnp.concatenate(
            [jnp.sum(first, axis=0, keepdims=True), jnp.sum(first * first, axis=0, keepdims=True)], axis=0
        )
    )
    for step in range(-3, 4):
        other = lax.rem(row + step + 32, 32)
        rows_there = gathered[
            other // 16, lax.rem(other // 4, 4), lax.rem(other, 4), 0, 0, ID_ROW : ID_ROW + 16
        ].astype(jnp.float32)[0:8]
        inside = jnp.logical_and(row + step >= 0, row + step < 32)
        ids[8 * (step + 3) : 8 * (step + 3) + 8, :] = jnp.where(inside, rows_there, -1.0)
    own_ids = ids[24:32, :]
    for number, offset in enumerate(OFFSETS):
        masks_ref[number] = jnp.where(ids[24 + offset : 32 + offset, :] == own_ids, 1.0, 0.0)
    masks_ref[len(OFFSETS)] = own_ids
    assemble(gathered, 0, staging, matrix, 0, 8, 16)
    for step in range(5):
        spatial_ref[464 * step : 464 * step + 464] = wide_rows(matrix, 2048 + 464 * step, 464).astype(
            jnp.bfloat16
        )
    totals[0].middle()
    assemble(gathered, 16, staging, matrix, 0)
    for step in range(13):
        spatial_ref[2320 + 176 * step : 2320 + 176 * step + 176] = wide_rows(
            matrix, 176 * step, 176
        ).astype(jnp.bfloat16)
    for part in range(4):
        expand_ref[:, 512 * part : 512 * part + 512] = jnp.concatenate(
            [array[pl.ds(2288 + part, 512, stride=4), :] for array in matrix], axis=1
        ).astype(jnp.bfloat16)
    norms_ref[...] = wide_rows(matrix, 4336, 16)
    for store in stores[0:3]:
        store.start()

    def normal(total, values, gain, shift, kept):
        average = total[0:1] / 16384.0
        variance = total[1:2] / 16384.0 - average * average
        scale = lax.rsqrt(variance + EPSILON)
        centered = (values - average) * scale
        kept[0:128] = centered
        kept[128:136] = jnp.broadcast_to(scale, (8, scale.shape[1]))
        return centered * gain + shift

    def silu(values):
        return values * jax.nn.sigmoid(values)

    def stats(values):
        return jnp.concatenate(
            [jnp.sum(values, axis=0, keepdims=True), jnp.sum(values * values, axis=0, keepdims=True)], axis=0
        )

    normed = normal(totals[0].finish(), first, norms_ref[0:1], norms_ref[1:2], first_ref)
    act_map[...] = silu(normed).astype(jnp.bfloat16).reshape(8, 16, MID)
    halo.start()
    rates.forward(2, 1)
    rates.receive(0)
    rates.forward(3, 5)
    rates.send(4, 6)
    halo.finish()
    widen_window(window_ref, wide)
    second = None
    for row_tap in range(3):
        part = None
        for col_tap in range(3):
            tap = 3 * row_tap + col_tap
            region = wide[4 * row_tap : 4 * row_tap + 8, 12 + 4 * col_tap : 28 + 4 * col_tap]
            product = jnp.dot(
                region.reshape(128, MID).astype(jnp.bfloat16),
                spatial_ref[512 * tap : 512 * tap + 512],
                preferred_element_type=jnp.float32,
            )
            part = product if part is None else part + product
        if row_tap != 1:
            part = part * across_lanes(pixel_mask(masks_ref[row_tap // 2]), MID)
        second = part if second is None else second + part
    totals[1].start(stats(second))
    assemble(gathered, 0, staging, head, 0)
    assemble(gathered, 16, staging, head, 16)
    totals[1].middle()
    for step in range(8):
        point_ref[256 * step : 256 * step + 256] = wide_rows(head, 256 * step, 256).astype(jnp.bfloat16)
        pool_ref[256 * step : 256 * step + 256] = wide_rows(head, 2048 + 256 * step, 256).astype(jnp.bfloat16)
    for step in range(5):
        project_ref[256 * step : 256 * step + 256] = wide_rows(head, 4097 + 256 * step, 256).astype(
            jnp.bfloat16
        )
    for store in stores[3:6]:
        store.start()
    misc_ref[0:8] = wide_rows(head, 4096, 8)
    misc_ref[8:72] = wide_rows(head, 5376, 64)
    normed = normal(totals[1].finish(), second, norms_ref[2:3], norms_ref[3:4], second_ref)
    rates.forward(4, 6)
    rates.receive(1)
    rates.send(7, 8)
    act_ref[...] = silu(normed).astype(jnp.bfloat16)
    third = jnp.dot(act_ref[...], expand_ref[...], preferred_element_type=jnp.float32)
    totals[2].start(stats(third))
    totals[2].middle()
    out_gain = jnp.concatenate([norms_ref[4 + part : 5 + part] for part in range(4)], axis=1)
    out_shift = jnp.concatenate([norms_ref[8 + part : 9 + part] for part in range(4)], axis=1)
    normed = normal(totals[2].finish(), third, out_gain, out_shift, third_ref)
    block_out = silu(normed + x_ref[...].astype(jnp.float32)).astype(jnp.bfloat16)
    out_ref[...] = block_out.reshape(8, 16, CIN)

    def slab_copy(step, sender):
        return remote(
            out_ref.at[:, :, pl.ds(pl.multiple_of(lax.rem(col + step, 4) * 512, 512), 512)],
            slab_ref.at[:, pl.ds(pl.multiple_of(sender * 16, 16), 16)],
            links.sends.at[slab_first + step - 1],
            links.recvs.at[slab_first + step - 1],
            device_of(row, lax.rem(col + step, 4)),
        )

    for step in (1, 2, 3):
        slab_copy(step, col).start()
    rates.forward(7, 8)
    rates.send(9)
    slab_ref[:, pl.ds(pl.multiple_of(col * 16, 16), 16)] = out_ref[
        :, :, pl.ds(pl.multiple_of(col * 512, 512), 512)
    ]
    for step in (1, 2, 3):
        copy = slab_copy(step, lax.rem(col + 4 - step, 4))
        copy.wait_recv()
        copy.wait_send()
    rates.forward(9)
    rates.receive(2, 3, 4, 5, 6, 7, 8, 9)
    rates.close()
    gather.close()
    for total in totals:
        total.close()
    for store in stores:
        store.wait()


def block_forward(arrays, collective):
    bf16, f32 = jnp.bfloat16, jnp.float32
    outs = [
        ((CIN, MID), bf16),
        ((9 * MID, MID), bf16),
        ((MID, CIN), bf16),
        ((CIN, ASPP), bf16),
        ((CIN, ASPP), bf16),
        ((5 * ASPP, ASPP), bf16),
        ((72, ASPP), f32),
        ((16, MID), f32),
        ((9, 8, 128), f32),
        ((136, MID), f32),
        ((136, MID), f32),
        ((136, CIN), f32),
        ((128, MID), bf16),
        ((16, 48, MID), bf16),
        ((8, 16, CIN), bf16),
        ((8, 64, CIN // 4), bf16),
        ((2, 4, 4, RATE_ROWS, CIN // 4), bf16),
    ]
    scratch = [pltpu.VMEM((2, 4, 4, 2, 2, PAYLOAD, 128), bf16)]
    scratch += [pltpu.VMEM((288, 128), f32)] * 4
    scratch += [pltpu.VMEM((4368, 128), f32)] * 4
    scratch += [pltpu.VMEM((5440, 128), f32)] * 2
    scratch += [
        pltpu.VMEM((56, 128), f32),
        pltpu.VMEM((16, 48, MID), f32),
        pltpu.VMEM((8, 16, MID), bf16),
        pltpu.VMEM((PAYLOAD, 128), f32),
        pltpu.VMEM((PAYLOAD, 128), bf16),
        pltpu.VMEM((RATE_ROWS, 512), bf16),
    ]
    scratch += [pltpu.VMEM(shape, dtype) for shape, dtype in outs[:6]]
    for rows, columns in ((2, MID), (2, MID), (2, CIN)):
        scratch += total_scratch(rows, columns)
    scratch += [pltpu.SemaphoreType.DMA((256,)), pltpu.SemaphoreType.DMA((256,))]
    return pl.pallas_call(
        block_forward_kernel,
        out_shape=[jax.ShapeDtypeStruct(shape, dtype) for shape, dtype in outs],
        in_specs=[VMEM, VMEM, VMEM, SMEM, VMEM],
        out_specs=[ANY] * 6 + [VMEM] * 10 + [ANY],
        scratch_shapes=scratch,
        compiler_params=pltpu.CompilerParams(
            collective_id=collective, has_side_effects=True, vmem_limit_bytes=60 * MEGABYTE
        ),
    )(*arrays)


class RatePieces:
    def __init__(self, links, units):
        self.links = links
        self.first = links.take(8 * units + 4)
        self.extra = self.first + 8 * units
        self.me = split_place()
        self.low_y = lax.rem(self.me["y"], 2)
        self.other = dict(self.me)
        self.other["y"] = self.me["y"] + 1 - 2 * self.low_y

    def rows(self, half):
        return pl.ds(half * (RATE_ROWS // 2), RATE_ROWS // 2)

    def piece(self, array, half, low_y, first_axis, second_axis):
        places = {RATE_ORDERS[half][0]: first_axis, RATE_ORDERS[half][1]: second_axis}
        return array.at[low_y, places["x"], places["z"], self.rows(half)]

    def remote(self, unit, half, slot, outgoing, incoming, axis, step):
        number = self.first + 8 * unit + 4 * half + slot
        return remote(
            outgoing,
            incoming,
            self.links.sends.at[number],
            self.links.recvs.at[number],
            device_at(moved(self.me, axis, step)),
        )

    def each(self):
        return [(half, step) for half in range(2) for step in (1, 2, 3)]


class RateFirst(RatePieces):
    def __init__(self, links, pieces, own, relays, parts, low_y):
        super().__init__(links, 4)
        self.pieces, self.own, self.relays, self.parts, self.from_y = pieces, own, relays, parts, low_y
        loads = links.take(6)
        self.loads = []
        for half in range(2):
            near, far = RATE_ORDERS[half]
            for slot, step in enumerate((0, 1, 3)):
                places = {near: slice(None), far: moved(self.me, far, step)[far]}
                self.loads.append(
                    pltpu.make_async_copy(
                        pieces.at[low_y, places["x"], places["z"], self.rows(half)],
                        own.at[half, slot],
                        links.recvs.at[loads + 3 * half + slot],
                    )
                )

    def part(self, step):
        return pl.ds(0, 64) if step == 1 else pl.ds(64, 48)

    def relay(self, unit, half, step):
        far = RATE_ORDERS[half][1]
        places = {RATE_ORDERS[half][0]: unit, far: moved(self.me, far, 2)[far]}
        rows = self.part(step)
        start = half * (RATE_ROWS // 2) + rows.start
        return self.remote(
            unit,
            half,
            step // 2 + 2,
            self.pieces.at[self.from_y, places["x"], places["z"], pl.ds(start, rows.size)],
            self.relays.at[half, unit, rows],
            far,
            step,
        )

    def copy(self, unit, half, step):
        far = RATE_ORDERS[half][1]
        slot = step // 2
        return self.remote(
            unit, half, slot, self.own.at[half, 1 + slot, unit], self.parts.at[half, unit, slot], far, step
        )

    def each(self):
        return [(half, step) for half in range(2) for step in (1, 3)]

    def send(self, *units):
        for unit in units:
            for half, step in self.each():
                self.relay(unit, half, step).start()

    def forward(self, *units):
        for unit in units:
            for half, step in self.each():
                self.relay(unit, half, step).wait_recv()
                rows = self.part(step)
                place = (half, 1 + step // 2, unit, rows)
                self.own[place] = self.own[place] + self.relays[half, unit, rows]
                self.copy(unit, half, step).start()

    def collect(self, *units):
        for unit in units:
            for half in range(2):
                total = self.own[half, 0, unit].astype(jnp.float32)
                for step in (1, 3):
                    self.copy(unit, half, step).wait_recv()
                    total = total + self.parts[half, unit, step // 2].astype(jnp.float32)
                self.own[half, 0, unit] = total.astype(jnp.bfloat16)
            for half, step in self.each():
                self.relay(unit, half, step).wait_send()
                self.copy(unit, half, step).wait_send()


class RateScatter(RatePieces):
    def __init__(self, links, sums, parts):
        super().__init__(links, 1)
        self.sums, self.parts = sums, parts

    def copy(self, half, step):
        near = RATE_ORDERS[half][0]
        outgoing = self.sums.at[half, moved(self.me, near, step)[near]]
        return self.remote(0, half, step - 1, outgoing, self.parts.at[half, step - 1], near, step)

    def pair(self, outgoing, incoming):
        return remote(
            outgoing,
            incoming,
            self.links.sends.at[self.extra],
            self.links.recvs.at[self.extra],
            device_at(self.other),
        )

    def send(self):
        for half, step in self.each():
            self.copy(half, step).start()

    def collect(self, target):
        for half in range(2):
            total = self.sums[half, self.me[RATE_ORDERS[half][0]]].astype(jnp.float32)
            for step in (1, 2, 3):
                self.copy(half, step).wait_recv()
                total = total + self.parts[half, step - 1].astype(jnp.float32)
            target[half] = total.astype(jnp.bfloat16)
        for half, step in self.each():
            self.copy(half, step).wait_send()


def disassemble(packed, first_row_group, staging, wide, stride, begin_group=0, end_group=16):
    parts = len(wide)
    core = lax.rem(lax.axis_index("cols"), 2)
    count = BLOCK_ROWS if parts == 4 else HEAD_ROWS
    low_y = first_row_group // 16

    def step(group, carry):
        x, z = group // 4, lax.rem(group, 4)
        for column in range(4):
            area = staging[column]
            here = (lax.rem(column + core, 2), low_y, x, z, column // 2)
            if parts == 4:
                skip = 0
                area[272:288] = packed[here + (slice(272, 288),)].astype(jnp.float32)
            else:
                skip = 1
                area[80:112] = jnp.zeros((32, 128), jnp.float32)
            for part in range(parts):
                begin = (part - column * count) % parts
                number = (count - begin + parts - 1) // parts
                row = (column * count + begin - part) // parts
                origin = (4 * count // parts) * (group + stride) + row
                area[pl.ds(skip + begin, number, stride=parts), :] = wide[part][
                    pl.ds(origin, number), :
                ]
            if parts == 4:
                packed[here + (slice(0, 288),)] = area[0:288].astype(jnp.bfloat16)
            else:
                packed[here + (slice(272, 384),)] = area[0:112].astype(jnp.bfloat16)
        return carry

    lax.fori_loop(begin_group, end_group, step, 0)


def deal(wide, first, values):
    number = values.shape[0]
    for part, array in enumerate(wide):
        array[first : first + number, :] = values[:, 128 * part : 128 * part + 128]


def against_rows(left, right):
    return lax.dot_general(left, right, (((1,), (1,)), ((), ())), preferred_element_type=jnp.float32)


def over_pixels(left, right):
    return lax.dot_general(left, right, (((0,), (0,)), ((), ())), preferred_element_type=jnp.float32)


def block_backward_kernel(
    x_ref,
    grad_ref,
    norms_ref,
    masks_ref,
    first_ref,
    second_ref,
    third_ref,
    act_ref,
    window_ref,
    reduce_hbm,
    spatial_hbm,
    expand_hbm,
    point_ref,
    pool_ref,
    project_ref,
    misc_ref,
    pieces_ref,
    out_ref,
    held_ref,
    late_ref,
    pair_ref,
    s0,
    s1,
    s2,
    s3,
    w0,
    w1,
    w2,
    w3,
    wide,
    act_map,
    window,
    packed,
    twin_part,
    reduce_ref,
    spatial_ref,
    expand_ref,
    free_sem,
    *rest,
):
    staging, matrix, head = (s0, s1, s2, s3), (w0, w1, w2, w3), (w0, w1)
    links = Links(rest[-2], rest[-1])
    totals = [Total(links, *rest[4 * number : 4 * number + 4]) for number in range(3)]
    own, relays, first_parts, second_parts = rest[12:16]
    rates = [
        RateFirst(links, pieces_ref, own.at[low_y], relays.at[low_y], first_parts.at[low_y], low_y)
        for low_y in range(2)
    ]
    scatter = RateScatter(links, own.at[0, :, 0], second_parts)
    me = scatter.me
    twin = device_at(moved(me, "core", 1, 2))
    halo = Halo(links, act_map, window)
    load_first, twin_first, out_first = (links.take(number) for number in (3, 2, 2))
    loads = [
        pltpu.make_async_copy(source, target, links.recvs.at[load_first + number])
        for number, (source, target) in enumerate(
            ((expand_hbm, expand_ref), (spatial_hbm, spatial_ref), (reduce_hbm, reduce_ref))
        )
    ]
    for copy in loads + rates[0].loads + rates[1].loads:
        copy.start()

    def twin_copy(low_y):
        return remote(
            packed.at[1, low_y],
            twin_part,
            links.sends.at[twin_first + low_y],
            links.recvs.at[twin_first + low_y],
            twin,
        )

    def out_copy(low_y):
        return pltpu.make_async_copy(
            packed.at[0, low_y], held_ref.at[low_y], links.sends.at[out_first + low_y]
        )

    def join_twin(low_y):
        twin_copy(low_y).wait_recv()

        def add_block(index, carry):
            place = (index // 8, lax.rem(index // 2, 4), lax.rem(index, 2))
            packed[(0, low_y) + place] = packed[(0, low_y) + place] + twin_part[place]
            return carry

        lax.fori_loop(0, 32, add_block, 0)
        out_copy(low_y).start()

    peers = total_peers() + halo_peers()
    greet(peers)

    def slope(values):
        part = jax.nn.sigmoid(values)
        return part * (1.0 + values * (1.0 - part))

    def local_sums(grad, kept):
        return jnp.concatenate(
            [
                jnp.sum(grad, axis=0, keepdims=True),
                jnp.sum(grad * kept[0:128], axis=0, keepdims=True),
            ],
            axis=0,
        )

    def through_norm(total, grad, kept, gain):
        return (
            gain
            * kept[128:129]
            * (grad - total[0:1] / 16384.0 - kept[0:128] * (total[1:2] / 16384.0))
        ).astype(jnp.bfloat16)

    out_gain = jnp.concatenate([norms_ref[4 + part : 5 + part] for part in range(4)], axis=1)
    out_shift = jnp.concatenate([norms_ref[8 + part : 9 + part] for part in range(4)], axis=1)
    residual = third_ref[0:128] * out_gain + out_shift + x_ref[...].astype(jnp.float32)
    out_ref[...] = grad_ref[...] * slope(residual)
    third_sums = local_sums(out_ref[...], third_ref)
    meet(peers)
    rates[0].send(0, 1, 2, 3)
    totals[0].start(third_sums)
    for step in range(4):
        deal(head, 512 * step, point_ref[512 * step : 512 * step + 512].astype(jnp.float32))
    deal(head, 2048, pool_ref[0:672].astype(jnp.float32))
    disassemble(packed, 0, staging, head, 0)
    totals[0].middle()
    for step in range(4):
        deal(head, 344 * step, pool_ref[672 + 344 * step : 1016 + 344 * step].astype(jnp.float32))
    deal(head, 1376, misc_ref[0:1])
    for step in range(5):
        deal(head, 1377 + 256 * step, project_ref[256 * step : 256 * step + 256].astype(jnp.float32))
    deal(head, 2657, misc_ref[1:64])
    disassemble(packed, 16, staging, head, 0)
    third_grad = through_norm(totals[0].finish(), out_ref[...], third_ref, out_gain)
    for copy in rates[0].loads + rates[1].loads:
        copy.wait()
    rates[0].forward(0, 1)
    loads[0].wait()
    second_gain, second_shift = norms_ref[2:3], norms_ref[3:4]
    second_norm = second_ref[0:128] * second_gain + second_shift
    second_back = against_rows(third_grad, expand_ref[...]) * slope(second_norm)
    second_sums = local_sums(second_back, second_ref)
    totals[1].start(second_sums)
    for part in range(4):
        product = over_pixels(act_ref[...], third_grad[:, 512 * part : 512 * part + 512])
        for number, array in enumerate(matrix):
            array[pl.ds(2288 + part, 512, stride=4), :] = product[:, 128 * number : 128 * number + 128]
    totals[1].middle()
    widen_window(window_ref, wide)
    second_grad = through_norm(totals[1].finish(), second_back, second_ref, second_gain)
    act_map[...] = second_grad.reshape(8, 16, MID)
    halo.start()
    rates[0].forward(2, 3)
    rates[1].send(0, 1, 2, 3)

    def spatial_grad(tap):
        row_tap, col_tap = tap // 3, tap % 3
        region = wide[4 * row_tap : 4 * row_tap + 8, 12 + 4 * col_tap : 28 + 4 * col_tap].reshape(128, MID)
        if row_tap != 1:
            region = region * across_lanes(pixel_mask(masks_ref[row_tap // 2]), MID)
        return over_pixels(region.astype(jnp.bfloat16), second_grad)

    middle_tap = spatial_grad(4)
    deal(matrix, 0, middle_tap[272:512])
    for tap in range(5, 9):
        deal(matrix, 240 + 512 * (tap - 5), spatial_grad(tap))
    halo.finish()
    rates[0].collect(0, 1, 2, 3)
    scatter.send()
    widen_window(window, wide)
    loads[1].wait()
    first_back = None
    for row_tap in range(3):
        part = None
        for col_tap in range(3):
            tap = 3 * row_tap + col_tap
            region = wide[
                8 - 4 * row_tap : 16 - 4 * row_tap, 20 - 4 * col_tap : 36 - 4 * col_tap
            ]
            product = against_rows(
                region.reshape(128, MID).astype(jnp.bfloat16), spatial_ref[512 * tap : 512 * tap + 512]
            )
            part = product if part is None else part + product
        if row_tap != 1:
            part = part * across_lanes(pixel_mask(masks_ref[1 - row_tap // 2]), MID)
        first_back = part if first_back is None else first_back + part
    first_gain, first_shift = norms_ref[0:1], norms_ref[1:2]
    first_back = first_back * slope(first_ref[0:128] * first_gain + first_shift)
    first_sums = local_sums(first_back, first_ref)
    totals[2].start(first_sums)
    deal(matrix, 4336, first_sums[1:2])
    deal(matrix, 4337, first_sums[0:1])
    deal(matrix, 4338, second_sums[1:2])
    deal(matrix, 4339, second_sums[0:1])
    for part in range(4):
        deal(matrix, 4340 + part, third_sums[1:2, 512 * part : 512 * part + 512])
        deal(matrix, 4344 + part, third_sums[0:1, 512 * part : 512 * part + 512])
    deal(matrix, 4348, jnp.zeros((20, MID), jnp.float32))
    disassemble(packed, 16, staging, matrix, 0)
    twin_copy(1).start()
    totals[2].middle()
    widen_window(window_ref, wide)
    deal(matrix, 4096, middle_tap[0:272])
    for tap in range(4):
        deal(matrix, 2048 + 512 * tap, spatial_grad(tap))
    disassemble(packed, 0, staging, matrix, 0, 8, 16)
    first_total = totals[2].finish()
    rates[1].forward(0, 1, 2, 3)
    join_twin(1)
    pl.semaphore_signal(free_sem, inc=1, device_id=twin, device_id_type=MESH)
    loads[2].wait()
    first_grad = through_norm(first_total, first_back, first_ref, first_gain)
    for part in range(4):
        rows = slice(512 * part, 512 * part + 512)
        deal(matrix, 512 * part, over_pixels(x_ref[:, rows], first_grad))
        out_ref[:, rows] = out_ref[:, rows] + against_rows(first_grad, reduce_ref[rows])
    disassemble(packed, 0, staging, matrix, 0, 0, 8)
    pl.semaphore_wait(free_sem, 1)
    twin_copy(0).start()
    rates[1].collect(0, 1, 2, 3)
    late_ref[...] = own[1, :, 0]
    scatter.collect(pair_ref)
    join_twin(0)
    for low_y in range(2):
        twin_copy(low_y).wait_send()
        out_copy(low_y).wait()
    for total in totals:
        total.close()


def block_backward(arrays, collective):
    bf16, f32 = jnp.bfloat16, jnp.float32
    half = RATE_ROWS // 2
    scratch = [pltpu.VMEM((384, 128), f32)] * 4
    scratch += [pltpu.VMEM((4368, 128), f32)] * 4
    scratch += [
        pltpu.VMEM((16, 48, MID), f32),
        pltpu.VMEM((8, 16, MID), bf16),
        pltpu.VMEM((16, 48, MID), bf16),
        pltpu.VMEM((2, 2, 4, 4, 2, PAYLOAD, 128), bf16),
        pltpu.VMEM((4, 4, 2, PAYLOAD, 128), bf16),
        pltpu.VMEM((CIN, MID), bf16),
        pltpu.VMEM((9 * MID, MID), bf16),
        pltpu.VMEM((MID, CIN), bf16),
        pltpu.SemaphoreType.REGULAR,
    ]
    for rows, columns in ((2, CIN), (2, MID), (2, MID)):
        scratch += total_scratch(rows, columns)
    scratch += [
        pltpu.VMEM((2, 2, 3, 4, half, 512), bf16),
        pltpu.VMEM((2, 2, 4, half, 512), bf16),
        pltpu.VMEM((2, 2, 4, 2, half, 512), bf16),
        pltpu.VMEM((2, 3, half, 512), bf16),
    ]
    scratch += [pltpu.SemaphoreType.DMA((232,)), pltpu.SemaphoreType.DMA((232,))]
    outs = [
        ((128, CIN), f32),
        ((2, 4, 4, 2, PAYLOAD, 128), bf16),
        ((2, 4, half, 512), bf16),
        ((2, half, 512), bf16),
    ]
    return pl.pallas_call(
        block_backward_kernel,
        out_shape=[jax.ShapeDtypeStruct(shape, dtype) for shape, dtype in outs],
        in_specs=[VMEM] * 9 + [ANY] * 3 + [VMEM] * (len(arrays) - 13) + [ANY],
        out_specs=[VMEM, ANY, VMEM, VMEM],
        scratch_shapes=scratch,
        compiler_params=pltpu.CompilerParams(
            collective_id=collective, has_side_effects=True, vmem_limit_bytes=62 * MEGABYTE
        ),
    )(*arrays)


def row_peers():
    row, col = lax.axis_index("rows"), lax.axis_index("cols")
    return [device_of(lax.rem(row + step + 32, 32), col) for step in (-3, -2, -1, 1, 2, 3)]


def row_moves():
    listed = []
    for branch, rate in enumerate(rate_list):
        for direction in range(2):
            for hop in range(4):
                lead = 8 * hop - rate if direction == 0 else rate - 8 * hop
                first, last = max(0, lead), min(8, lead + 8)
                if first < last:
                    sign = 1 if direction == 0 else -1
                    listed.append((branch, direction, sign * hop, first, first - lead, last - first))
    return listed


class RowShift:
    def __init__(self, links, sources, target):
        self.links, self.sources, self.target = links, sources, target
        self.moves = row_moves()
        self.first = links.take(len(self.moves))

    def copies(self, branch):
        row, col = lax.axis_index("rows"), lax.axis_index("cols")
        for number, (owner, direction, hop, first, top, size) in enumerate(self.moves):
            if owner == branch and hop:
                yield remote(
                    self.sources[branch][direction].at[pl.ds(first, size)],
                    self.target.at[branch, direction, pl.ds(top, size)],
                    self.links.sends.at[self.first + number],
                    self.links.recvs.at[self.first + number],
                    device_of(lax.rem(row + hop + 32, 32), col),
                )

    def start(self, branch):
        for copy in self.copies(branch):
            copy.start()
        for owner, direction, hop, first, top, size in self.moves:
            if owner == branch and hop == 0:
                self.target[branch, direction, top : top + size] = self.sources[branch][direction][
                    first : first + size
                ]

    def finish(self, branch):
        for copy in self.copies(branch):
            copy.wait_recv()
            copy.wait_send()


MARGIN = 24
SLOTS = (0, 2, 1)
SIDES, CENTER = (pl.ds(0, 2), pl.ds(2, 1))


def silu_value(values):
    return values * jax.nn.sigmoid(values)


def silu_grad(values):
    part = jax.nn.sigmoid(values)
    return part * (1.0 + values * (1.0 - part))


def two_sums(first, second):
    return jnp.concatenate(
        [jnp.sum(first, axis=0, keepdims=True), jnp.sum(second, axis=0, keepdims=True)], axis=0
    )


def centered_values(total, values):
    average = total[0:1] / 16384.0
    variance = total[1:2] / 16384.0 - average * average
    scale = lax.rsqrt(variance + EPSILON)
    return (values - average) * scale, scale


def norm_grad(total, grad, centered, scale, gain):
    return (
        gain * scale * (grad - total[0:1] / 16384.0 - centered * (total[1:2] / 16384.0))
    ).astype(jnp.bfloat16)


def pyramid_kernel(
    grid_ref,
    slab_ref,
    pieces_ref,
    point_hbm,
    pool_hbm,
    project_hbm,
    misc_ref,
    masks_ref,
    seg_ref,
    edge_ref,
    part_ref,
    weights_ref,
    loss_out,
    pooled_out,
    grad_out,
    point_out,
    pool_out,
    project_out,
    norms_out,
    pieces_hbm,
    kernels,
    padded,
    moved_maps,
    taps,
    core_part,
    high_out,
    high_part,
    tap_own,
    rows_out,
    rows_in,
    grads_own,
    grads_in,
    stack,
    grad_taps,
    back_out,
    back_in,
    pieces_out,
    point_ref,
    pool_ref,
    project_ref,
    heads_ref,
    *rest,
):
    bf16, f32 = jnp.bfloat16, jnp.float32
    links = Links(rest[-2], rest[-1])
    totals = [Total(links, *rest[4 * number : 4 * number + 4]) for number in range(5)]
    row, col = lax.axis_index("rows"), lax.axis_index("cols")
    core, high = lax.rem(col, 2), col // 2
    twin = device_of(row, col + 1 - 2 * core)
    far_twin = device_of(row, col + 2 - 4 * high)
    pieces_sem = links.take(4)
    tap_core, tap_high = links.take(6), links.take(6)
    stack_high, stack_core = links.take(6), links.take(6)
    back = links.take(3)
    forward_shift = RowShift(
        links, [[rows_out.at[branch, direction] for direction in range(2)] for branch in range(3)], rows_in
    )
    backward_shift = RowShift(
        links, [[grads_own.at[branch] for _ in range(2)] for branch in range(3)], grads_in
    )
    loads = [
        pltpu.make_async_copy(source, target, links.recvs.at[pieces_sem + number])
        for number, (source, target) in enumerate(
            (
                (pieces_ref, pieces_out),
                (point_hbm, point_ref),
                (pool_hbm, pool_ref),
                (project_hbm, project_ref),
            )
        )
    ]
    stores = [
        pltpu.make_async_copy(
            pieces_out.at[pl.ds(16 * part, 16)],
            pieces_hbm.at[pl.ds(16 * part, 16)],
            links.sends.at[pieces_sem + part],
        )
        for part in range(2)
    ]
    for load in loads:
        load.start()
    peers = total_peers() + row_peers()
    greet(peers)

    members_low = [jnp.where(masks_ref[8] == float(image), 1.0, 0.0) for image in range(4)]
    row_sums = jnp.sum(grid_ref[...].astype(f32), axis=1)
    pieces = []
    for image in range(4):
        chosen = members_low[image]
        pieces.append(
            jnp.concatenate(
                [
                    jnp.sum(row_sums * across_lanes(chosen, CIN), axis=0, keepdims=True),
                    jnp.sum(chosen, axis=0, keepdims=True),
                ],
                axis=1,
            )
        )
    pooled_here = jnp.concatenate(pieces, axis=0)

    def columns_of(place):
        return pl.ds(pl.multiple_of(place * 16, 16), 16)

    padded[:, 0:MARGIN] = jnp.zeros((8, MARGIN, 512), f32)
    padded[:, MARGIN + 64 :] = jnp.zeros((8, MARGIN, 512), f32)
    padded[:, MARGIN : MARGIN + 64] = slab_ref[...].astype(f32)
    for branch, rate in enumerate(rate_list):
        for side in range(2):
            start = MARGIN + (2 * side - 1) * rate
            moved_maps[2 * branch + side] = (
                padded[:, start : start + 64].reshape(512, 512).astype(bf16)
            )
    slab = slab_ref[...].reshape(512, 512)
    for load in loads:
        load.wait()

    def join(pair, carry):
        both = jnp.concatenate(
            [pieces_out[2 * pair, 0:216].astype(f32), pieces_out[2 * pair + 1, 0:216].astype(f32)], axis=0
        )
        kernels[pl.ds(pl.multiple_of(432 * pair, 16), 432)] = both.astype(bf16)
        return carry

    lax.fori_loop(0, 16, join, 0)
    meet(peers)
    totals[4].start(pooled_here)

    def tap_core_copy(branch, place):
        return remote(
            taps.at[pl.ds(3 * branch, 3), :, columns_of(2 * place + 1 - core)],
            core_part.at[branch, place],
            links.sends.at[tap_core + 2 * branch + place],
            links.recvs.at[tap_core + 2 * branch + place],
            twin,
        )

    def tap_high_copy(branch, slots):
        number = tap_high + 2 * branch + slots.start // 2
        return remote(
            high_out.at[branch, slots],
            high_part.at[branch, slots],
            links.sends.at[number],
            links.recvs.at[number],
            far_twin,
        )

    def tap_meet(branch):
        for place in range(2):
            tap_core_copy(branch, place).wait_recv()
        away = taps[pl.ds(3 * branch, 3), :, columns_of(2 * (1 - high) + core)].astype(f32)
        high_out[branch] = (away + core_part[branch, 1 - high].astype(f32)).astype(bf16)
        tap_high_copy(branch, SIDES).start()
        here = taps[pl.ds(3 * branch, 3), :, columns_of(col)].astype(f32)
        tap_own[branch] = here + core_part[branch, high].astype(f32)

    def tap_finish(branch):
        tap_high_copy(branch, SIDES).wait_recv()
        for direction in range(2):
            rows_out[branch, direction] = (
                tap_own[branch, direction] + high_part[branch, direction].astype(f32)
            ).astype(bf16)
        forward_shift.start(branch)

    for branch in range(3):
        result = None
        for col_tap in range(3):
            left = slab if col_tap == 1 else moved_maps[2 * branch + col_tap // 2]
            right = jnp.concatenate(
                [
                    kernels[(9 * branch + 3 * tap + col_tap) * 256 : (9 * branch + 3 * tap + col_tap + 1) * 256]
                    for tap in range(3)
                ],
                axis=0,
            )
            product = against_rows(left, right)
            result = product if result is None else result + product
        for slot, tap in enumerate(SLOTS):
            taps[3 * branch + slot] = result[:, 256 * tap : 256 * tap + 256].astype(bf16).reshape(8, 64, 256)
        for place in range(2):
            tap_core_copy(branch, place).start()
        if branch == 0:
            totals[4].middle()
        else:
            tap_meet(branch - 1)
    tap_meet(2)
    for branch in range(3):
        tap_high_copy(branch, CENTER).start()
    grid = grid_ref[...].reshape(128, CIN)
    branches = [jnp.dot(grid, point_ref[...], preferred_element_type=f32)]
    number = lax.broadcasted_iota(jnp.int32, (256, 256), 0) * HEADS
    lane_256 = lax.broadcasted_iota(jnp.int32, (256, 256), 1)
    number_32 = lax.broadcasted_iota(jnp.int32, (256, 32), 0) * HEADS
    lane_32 = lax.broadcasted_iota(jnp.int32, (256, 32), 1)
    lane_128 = lax.broadcasted_iota(jnp.int32, (256, 128), 1)

    def rows_of_head(head):
        return jnp.where(lane_32 == (number_32 + head) // 256, 1.0, 0.0).astype(bf16)

    def lanes_of_head(head):
        return lane_256 == lax.rem(number + head, 256)

    flat_heads = misc_ref[19:51].astype(bf16)
    heads = jnp.zeros((256, 128), f32)
    for head in range(HEADS):
        spread = jnp.dot(rows_of_head(head), flat_heads, preferred_element_type=f32)
        column = jnp.sum(jnp.where(lanes_of_head(head), spread, 0.0), axis=1, keepdims=True)
        heads = heads + jnp.where(lane_128 == head, column, 0.0)
    heads_ref[...] = heads.astype(bf16)
    bias = jnp.where(
        lax.broadcasted_iota(jnp.int32, (1, 128), 1) < HEADS, misc_ref[36:37, 0:128], 0.0
    )
    pooled_sums = totals[4].finish()
    area = jnp.concatenate([pooled_sums[:, CIN : CIN + 128]] * 16, axis=1) * 16.0
    pooled = pooled_sums[:, 0:CIN] / area
    pooled_out[...] = pooled
    pooled_low = jnp.concatenate([pooled, jnp.zeros((4, CIN), f32)], axis=0).astype(bf16)
    pool_pre = jnp.dot(pooled_low, pool_ref[...], preferred_element_type=f32)[0:4] + misc_ref[0:1]
    pool_act = silu_value(pool_pre)
    members = [across_lanes(pixel_mask(members_low[image]), ASPP) for image in range(4)]
    pool_map = members[0] * pool_act[0:1]
    for image in range(1, 4):
        pool_map = pool_map + members[image] * pool_act[image : image + 1]
    for branch in range(3):
        tap_finish(branch)
    for branch in range(3):
        tap_high_copy(branch, CENTER).wait_recv()
        forward_shift.finish(branch)
        value = (tap_own[branch, 2] + high_part[branch, 2].astype(f32)).reshape(128, 256)
        for direction in range(2):
            mask = across_lanes(pixel_mask(masks_ref[2 + 2 * branch + direction]), ASPP)
            value = value + rows_in[branch, direction].astype(f32).reshape(128, 256) * mask
        branches.append(value)
    before = jnp.concatenate(branches, axis=1)
    totals[0].start(two_sums(before, before * before))
    totals[0].middle()
    gains = jnp.concatenate([misc_ref[9 + 2 * branch : 10 + 2 * branch] for branch in range(4)], axis=1)
    shifts = jnp.concatenate([misc_ref[10 + 2 * branch : 11 + 2 * branch] for branch in range(4)], axis=1)
    centered, scale = centered_values(totals[0].finish(), before)
    normed = centered * gains + shifts
    joined = jnp.concatenate([silu_value(normed).astype(bf16), pool_map.astype(bf16)], axis=1)
    projected = jnp.dot(joined, project_ref[...], preferred_element_type=f32)
    totals[1].start(two_sums(projected, projected * projected))
    totals[1].middle()
    last_gain, last_shift = misc_ref[17:18], misc_ref[18:19]
    proj_centered, proj_scale = centered_values(totals[1].finish(), projected)
    proj_normed = proj_centered * last_gain + last_shift
    feature_map = silu_value(proj_normed).astype(bf16)
    logits = jnp.dot(feature_map, heads_ref[...], preferred_element_type=f32) + bias
    lane = lax.broadcasted_iota(jnp.int32, (128, 128), 1)

    def per_pixel(labels_ref):
        spread = jnp.broadcast_to(labels_ref[...].astype(f32)[:, None, :], (8, 16, 16))
        here = lax.broadcasted_iota(jnp.int32, (8, 16, 16), 1) == lax.broadcasted_iota(
            jnp.int32, (8, 16, 16), 2
        )
        return jnp.sum(jnp.where(here, spread, 0.0), axis=2, keepdims=True).reshape(128, 1)

    lane_value = lane.astype(f32)
    hot = (
        jnp.where(lane_value == per_pixel(seg_ref), 1.0, 0.0)
        + jnp.where(lane == SEG, per_pixel(edge_ref), 0.0)
        + jnp.where(lane_value == per_pixel(part_ref) + (SEG + 1.0), 1.0, 0.0)
    )

    def cross_entropy(inside):
        highest = jnp.max(jnp.where(inside, logits, -3.0e38), axis=1, keepdims=True)
        powers = jnp.where(inside, jnp.exp(jnp.where(inside, logits - highest, 0.0)), 0.0)
        total = jnp.sum(powers, axis=1, keepdims=True)
        picked = jnp.sum(jnp.where(inside, logits * hot, 0.0), axis=1, keepdims=True)
        return highest + jnp.log(total) - picked, powers / total

    seg_inside, part_inside = lane < SEG, jnp.logical_and(lane > SEG, lane < HEADS)
    seg_terms, seg_soft = cross_entropy(seg_inside)
    part_terms, part_soft = cross_entropy(part_inside)
    edge_inside = lane == SEG
    edge_all = (
        jnp.maximum(logits, 0.0) + jnp.log1p(jnp.exp(-jnp.abs(logits))) - hot * logits
    )
    edge_soft = jax.nn.sigmoid(logits)
    weights = [weights_ref[task].astype(f32) for task in range(3)]
    weight_total = weights[0] + weights[1] + weights[2]
    row_lane = lax.broadcasted_iota(jnp.int32, (1, 128), 1)
    shares = jnp.where(
        row_lane < SEG, weights[0], jnp.where(row_lane == SEG, weights[1], weights[2])
    ) / jnp.full((1, 128), weight_total)
    shares = jnp.where(row_lane < HEADS, shares, 0.0)
    terms = jnp.where(lane == 0, seg_terms, 0.0) + jnp.where(edge_inside, edge_all, 0.0)
    terms = (terms + jnp.where(lane == SEG + 1, part_terms, 0.0)) * shares
    loss_local = jnp.sum(jnp.sum(terms, axis=0, keepdims=True), axis=1, keepdims=True) / 16384.0
    soft = seg_soft + part_soft + jnp.where(edge_inside, edge_soft, 0.0)
    logit_grad = ((soft - hot) * shares / 16384.0).astype(bf16)
    feature_back = against_rows(logit_grad, heads_ref[...]) * silu_grad(proj_normed)
    proj_sums = two_sums(feature_back, feature_back * proj_centered)
    totals[2].start(
        jnp.concatenate([proj_sums, jnp.broadcast_to(loss_local, (1, ASPP))], axis=0)
    )
    heads_grad = over_pixels(feature_map, logit_grad)
    norms_out[11:64] = jnp.zeros((53, ASPP), f32)
    flat_grad = None
    for head in range(HEADS):
        column = jnp.broadcast_to(heads_grad[:, head : head + 1], (256, 256))
        spread = jnp.where(lanes_of_head(head), column, 0.0).astype(bf16)
        part = over_pixels(rows_of_head(head), spread)
        flat_grad = part if flat_grad is None else flat_grad + part
    norms_out[11:28] = flat_grad[0:17]
    norms_out[28:29, 0:128] = jnp.sum(logit_grad.astype(f32), axis=0, keepdims=True)
    totals[2].middle()
    total = totals[2].finish()
    loss_out[...] = total[2:3, 0:1]
    projected_grad = norm_grad(total, feature_back, proj_centered, proj_scale, last_gain)
    joined_grad = against_rows(projected_grad, project_ref[...])
    pool_map_grad = joined_grad[:, 4 * ASPP :]
    pool_local = jnp.concatenate(
        [jnp.sum(pool_map_grad * members[image], axis=0, keepdims=True) for image in range(4)], axis=0
    )
    branch_back = joined_grad[:, : 4 * ASPP] * silu_grad(normed)
    branch_sums = two_sums(branch_back, branch_back * centered)
    pool_row = jnp.concatenate([pool_local[image : image + 1] for image in range(4)], axis=1)
    totals[3].start(jnp.concatenate([branch_sums, pool_row], axis=0))
    project_out[...] = over_pixels(joined, projected_grad).astype(bf16)
    totals[3].middle()
    pool_slope = silu_grad(pool_pre)
    pool_pre_local = pool_local * pool_slope
    norms_out[0:1] = jnp.sum(pool_pre_local, axis=0, keepdims=True)
    for branch in range(4):
        lanes = slice(256 * branch, 256 * branch + 256)
        norms_out[1 + 2 * branch : 2 + 2 * branch] = branch_sums[1:2, lanes]
        norms_out[2 + 2 * branch : 3 + 2 * branch] = branch_sums[0:1, lanes]
    norms_out[9:10] = proj_sums[1:2]
    norms_out[10:11] = proj_sums[0:1]
    padding = jnp.zeros((4, ASPP), f32)
    pool_out[...] = over_pixels(
        pooled_low, jnp.concatenate([pool_pre_local, padding], axis=0).astype(bf16)
    ).astype(bf16)
    total = totals[3].finish()
    branch_grad = norm_grad(total, branch_back, centered, scale, gains)
    for branch in range(3):
        grads_own[branch] = branch_grad[:, 256 * branch + 256 : 256 * branch + 512].reshape(8, 16, 256)
        backward_shift.start(branch)

    def stack_high_copy(branch, slots, sender):
        view = stack.at[branch, slots, :, columns_of(sender)]
        number = stack_high + 2 * branch + slots.start // 2
        return remote(view, view, links.sends.at[number], links.recvs.at[number], far_twin)

    def stack_core_copy(branch, place, sender_core):
        view = stack.at[branch, :, :, columns_of(2 * place + sender_core)]
        number = stack_core + 2 * branch + place
        return remote(view, view, links.sends.at[number], links.recvs.at[number], twin)

    for branch in range(3):
        stack[branch, 2, :, columns_of(col)] = grads_own[branch]
        stack_high_copy(branch, CENTER, col).start()
    pool_grad = jnp.concatenate(
        [total[2:3, 256 * image : 256 * image + 256] for image in range(4)], axis=0
    )
    pooled_grad = against_rows(
        jnp.concatenate([pool_grad * pool_slope, padding], axis=0).astype(bf16), pool_ref[...]
    )[0:4] / area
    for branch in range(3):
        backward_shift.finish(branch)
        for slot, direction in ((0, 1), (1, 0)):
            mask = across_lanes(pixel_mask(masks_ref[2 + 2 * branch + direction]), ASPP)
            shifted = grads_in[branch, direction].astype(f32).reshape(128, 256) * mask
            stack[branch, slot, :, columns_of(col)] = shifted.astype(bf16).reshape(8, 16, 256)
        stack_high_copy(branch, SIDES, col).start()
    point_grad = branch_grad[:, 0:256]
    point_out[...] = over_pixels(grid, point_grad).astype(bf16)
    grad_out[...] = against_rows(point_grad, point_ref[...])
    for image in range(4):
        grad_out[...] = grad_out[...] + across_lanes(
            pixel_mask(members_low[image]), CIN
        ) * pooled_grad[image : image + 1]
    for branch in range(3):
        for slots in (SIDES, CENTER):
            stack_high_copy(branch, slots, col + 2 - 4 * high).wait_recv()
        for place in range(2):
            stack_core_copy(branch, place, core).start()
    def split(pair, carry):
        both = kernels[pl.ds(pl.multiple_of(432 * pair, 16), 432)].astype(f32)
        zeros = jnp.zeros((8, 512), f32)
        pieces_out[2 * pair] = jnp.concatenate([both[0:216], zeros], axis=0).astype(bf16)
        pieces_out[2 * pair + 1] = jnp.concatenate([both[216:432], zeros], axis=0).astype(bf16)
        return carry

    slab_grad = None
    for branch, rate in enumerate(rate_list):
        for place in range(2):
            stack_core_copy(branch, place, 1 - core).wait_recv()
        for slot, tap in enumerate(SLOTS):
            padded[:, MARGIN : MARGIN + 64, 0:256] = stack[branch, slot].astype(f32)
            for col_tap in range(3):
                start = MARGIN - (col_tap - 1) * rate
                lanes = slice(256 * (3 * tap + col_tap), 256 * (3 * tap + col_tap) + 256)
                grad_taps[:, lanes] = (
                    padded[:, start : start + 64, 0:256].reshape(512, 256).astype(bf16)
                )
        rows = slice(2304 * branch, 2304 * branch + 2304)
        product = jnp.dot(grad_taps[...], kernels[rows], preferred_element_type=f32)
        slab_grad = product if slab_grad is None else slab_grad + product
        kernels[rows] = over_pixels(grad_taps[...], slab).astype(bf16)
        if branch == 1:
            lax.fori_loop(0, 8, split, 0)
            stores[0].start()
    back_out[...] = slab_grad.astype(bf16).reshape(8, 64, 512)

    def back_copy(step, sender):
        return remote(
            back_out.at[:, columns_of(lax.rem(col + step, 4))],
            back_in.at[:, :, pl.ds(pl.multiple_of(sender * 512, 512), 512)],
            links.sends.at[back + step - 1],
            links.recvs.at[back + step - 1],
            device_of(row, lax.rem(col + step, 4)),
        )

    for step in (1, 2, 3):
        back_copy(step, col).start()
    back_in[:, :, pl.ds(pl.multiple_of(col * 512, 512), 512)] = back_out[:, columns_of(col)]

    lax.fori_loop(8, 16, split, 0)
    stores[1].start()
    for step in (1, 2, 3):
        copy = back_copy(step, lax.rem(col + 4 - step, 4))
        copy.wait_recv()
        copy.wait_send()
    grad_out[...] = grad_out[...] + back_in[...].reshape(128, CIN).astype(f32)
    for branch in range(3):
        for place in range(2):
            tap_core_copy(branch, place).wait_send()
            stack_core_copy(branch, place, core).wait_send()
        for slots in (SIDES, CENTER):
            tap_high_copy(branch, slots).wait_send()
            stack_high_copy(branch, slots, col).wait_send()
    for store in stores:
        store.wait()
    for total in totals:
        total.close()


def pyramid(arrays, collective):
    bf16, f32 = jnp.bfloat16, jnp.float32
    outs = [
        ((1, 1), f32),
        ((4, CIN), f32),
        ((128, CIN), f32),
        ((CIN, ASPP), bf16),
        ((CIN, ASPP), bf16),
        ((5 * ASPP, ASPP), bf16),
        ((64, ASPP), f32),
        ((32, RATE_ROWS, 512), bf16),
    ]
    scratch = [
        pltpu.VMEM((27 * ASPP, 512), bf16),
        pltpu.VMEM((8, 64 + 2 * MARGIN, 512), f32),
        pltpu.VMEM((6, 512, 512), bf16),
        pltpu.VMEM((9, 8, 64, ASPP), bf16),
        pltpu.VMEM((3, 2, 3, 8, 16, ASPP), bf16),
        pltpu.VMEM((3, 3, 8, 16, ASPP), bf16),
        pltpu.VMEM((3, 3, 8, 16, ASPP), bf16),
        pltpu.VMEM((3, 3, 8, 16, ASPP), f32),
        pltpu.VMEM((3, 2, 8, 16, ASPP), bf16),
        pltpu.VMEM((3, 2, 8, 16, ASPP), bf16),
        pltpu.VMEM((3, 8, 16, ASPP), bf16),
        pltpu.VMEM((3, 2, 8, 16, ASPP), bf16),
        pltpu.VMEM((3, 3, 8, 64, ASPP), bf16),
        pltpu.VMEM((512, 9 * ASPP), bf16),
        pltpu.VMEM((8, 64, 512), bf16),
        pltpu.VMEM((8, 16, CIN), bf16),
        pltpu.VMEM((32, RATE_ROWS, 512), bf16),
        pltpu.VMEM((CIN, ASPP), bf16),
        pltpu.VMEM((CIN, ASPP), bf16),
        pltpu.VMEM((5 * ASPP, ASPP), bf16),
        pltpu.VMEM((ASPP, 128), bf16),
    ]
    for rows, columns in ((2, 4 * ASPP), (2, ASPP), (3, ASPP), (3, 4 * ASPP), (4, CIN + 128)):
        scratch += total_scratch(rows, columns)
    scratch += [pltpu.SemaphoreType.DMA((184,)), pltpu.SemaphoreType.DMA((184,))]
    in_specs = [VMEM] * len(arrays)
    in_specs[2:6] = [ANY] * 4
    in_specs[-1] = SMEM
    return pl.pallas_call(
        pyramid_kernel,
        out_shape=[jax.ShapeDtypeStruct(shape, dtype) for shape, dtype in outs],
        in_specs=in_specs,
        out_specs=[VMEM] * (len(outs) - 1) + [ANY],
        scratch_shapes=scratch,
        compiler_params=pltpu.CompilerParams(
            collective_id=collective, has_side_effects=True, vmem_limit_bytes=62 * MEGABYTE
        ),
    )(*arrays)


def finish_kernel(
    loss_ref,
    pooled_ref,
    gradient_ref,
    flat_ref,
    rate_ref,
    block_ref,
    head_ref,
    rate_moment_ref,
    loss_out,
    pooled_out,
    gradient_out,
    block_out,
    head_out,
    rate_out,
):
    loss_out[...] = loss_ref[...]
    pooled_out[...] = pooled_ref[...]
    gradient_out[...] = gradient_ref[...]
    block_out[...] = MOMENTUM_KEEP * block_ref[...] + flat_ref[0:BLOCK_ROWS, :]
    head_out[...] = MOMENTUM_KEEP * head_ref[...] + flat_ref[BLOCK_ROWS : BLOCK_ROWS + HEAD_ROWS, :]
    rate_out[...] = MOMENTUM_KEEP * rate_moment_ref[...] + rate_ref[0:216]


def finish(loss, pooled, gradient, flat, rate, block_moment, head_moment, rate_moment):
    like = (loss, pooled, gradient, block_moment, head_moment, rate_moment)
    return pl.pallas_call(
        finish_kernel,
        out_shape=[jax.ShapeDtypeStruct(item.shape, jnp.float32) for item in like],
        in_specs=[VMEM] * 8,
        out_specs=[VMEM] * 6,
        compiler_params=pltpu.CompilerParams(vmem_limit_bytes=32 * MEGABYTE),
    )(loss, pooled, gradient, flat, rate, block_moment, head_moment, rate_moment)


def per_device(
    features,
    image_rows,
    seg_labels,
    edge_labels,
    part_labels,
    task_weights,
    block_params,
    block_moment,
    head_params,
    head_moment,
    rate_params,
    rate_moment,
):
    height, across, channels = features.shape
    pixels = height * across
    inputs = features.reshape(pixels, channels)
    (
        w_reduce,
        w_spatial,
        w_expand,
        w_point,
        w_pool,
        w_project,
        misc,
        norms,
        masks,
        first_kept,
        second_kept,
        third_kept,
        second_act,
        block_window,
        grid,
        slab_map,
        rates_all,
    ) = block_forward(
        (
            inputs,
            block_params.reshape(BLOCK_ROWS, 128),
            head_params.reshape(HEAD_ROWS, 128),
            image_rows,
            rate_params.T,
        ),
        1,
    )
    (
        loss_rows,
        pooled,
        out_grad,
        grad_point,
        grad_pool,
        grad_project,
        misc_grads,
        rate_pieces,
    ) = pyramid(
        (
            grid,
            slab_map,
            rates_all.reshape(32, RATE_ROWS, channels // 4),
            w_point,
            w_pool,
            w_project,
            misc,
            masks,
            seg_labels,
            edge_labels,
            part_labels,
            task_weights,
        ),
        2,
    )
    input_grad, *flat_sums = block_backward(
        (
            inputs,
            out_grad,
            norms,
            masks,
            first_kept,
            second_kept,
            third_kept,
            second_act,
            block_window,
            w_reduce,
            w_spatial,
            w_expand,
            grad_point,
            grad_pool,
            grad_project,
            misc_grads,
            rate_pieces.reshape(2, 4, 4, RATE_ROWS, channels // 4),
        ),
        16,
    )
    shares_all, rate_sum = scatter_params(flat_sums, 20)
    loss_out, pooled_out, gradient, block_next, head_next, rate_next = finish(
        loss_rows,
        pooled,
        input_grad,
        shares_all,
        rate_sum,
        block_moment.reshape(BLOCK_ROWS, 128),
        head_moment.reshape(HEAD_ROWS, 128),
        rate_moment.T,
    )
    return (
        loss_out.reshape(()),
        pooled_out,
        gradient.reshape(height, across, channels),
        block_next.reshape(-1),
        head_next.reshape(-1),
        rate_next.T,
    )


def solution(mesh):
    return jax.shard_map(
        per_device,
        mesh=mesh,
        in_specs=(
            P("rows", "cols", None),
            P("rows"),
            P("rows", "cols"),
            P("rows", "cols"),
            P("rows", "cols"),
            P(),
            P(("rows", "cols")),
            P(("rows", "cols")),
            P(("rows", "cols")),
            P(("rows", "cols")),
            P("cols", "rows"),
            P("cols", "rows"),
        ),
        out_specs=(
            P(),
            P(),
            P("rows", "cols", None),
            P(("rows", "cols")),
            P(("rows", "cols")),
            P("cols", "rows"),
        ),
        check_vma=False,
    )
```

```python
import functools
import math

import jax
import jax.numpy as jnp
from jax import lax
from jax.experimental import pallas as pl
from jax.experimental.pallas import tpu as pltpu
from jax.sharding import PartitionSpec as P

MESH = pl.DeviceIdType.MESH
ANY = pl.BlockSpec(memory_space=pl.ANY)
VMEM = pl.BlockSpec(memory_space=pltpu.VMEM)
SMEM = pl.BlockSpec(memory_space=pltpu.SMEM)
BLOCK_ROWS = 273
HEAD_ROWS = 85
PAYLOAD = 384

CIN = 2048
MID = 512
ASPP = 256
SEG = 13
PART = 3
HEADS = 17


EPSILON = 1e-05
MOMENTUM_KEEP = 0.5
rate_list = (6, 12, 18)
block_dilation = 4
widest_margin = 18


def device_of(row, col):
    return {"rows": row, "cols": col}


def split_place():
    row, col = lax.axis_index("rows"), lax.axis_index("cols")
    return {
        "y": (row // 16) + 2 * (col // 2),
        "x": lax.rem(row // 4, 4),
        "z": lax.rem(row, 4),
        "core": lax.rem(col, 2),
    }


def device_at(place):
    row = lax.rem(place["y"], 2) * 16 + place["x"] * 4 + place["z"]
    return device_of(row, (place["y"] // 2) * 2 + place["core"])


def moved(place, axis, step, extent=4):
    other = dict(place)
    other[axis] = lax.rem(place[axis] + step + extent, extent)
    return other


def greet(peers):
    barrier = pltpu.get_barrier_semaphore()
    for device in peers:
        pl.semaphore_signal(barrier, inc=1, device_id=device, device_id_type=MESH)


def meet(peers):
    pl.semaphore_wait(pltpu.get_barrier_semaphore(), len(peers))


def remote(source, target, send_sem, recv_sem, device):
    return pltpu.make_async_remote_copy(
        src_ref=source,
        dst_ref=target,
        send_sem=send_sem,
        recv_sem=recv_sem,
        device_id=device,
        device_id_type=MESH,
    )


GATHER_ORDERS = (("z", "x", "y"), ("x", "y", "z"), ("y", "z", "x"))


def axis_view(place, fixed):
    index = [slice(None)] * 4
    if "y" in fixed:
        index[0], index[3] = lax.rem(place["y"], 2), place["y"] // 2
    if "x" in fixed:
        index[1] = place["x"]
    if "z" in fixed:
        index[2] = place["z"]
    return tuple(index)


def scatter_kernel(p_ref, late_ref, pair_ref, o_ref, share_ref, held, rate_parts, rate_sums, rate_pair, *rest):
    relays = rest[0:3]
    parts = [rest[3 + 3 * third : 6 + 3 * third] for third in range(3)]
    sums = [rest[12 + 2 * third : 14 + 2 * third] for third in range(3)]
    links = Links(rest[-2], rest[-1])
    first, own_first = links.take(48), links.take(3)
    rates = RateScatter(links, late_ref, rate_parts)
    me = rates.me
    everywhere = (slice(None),) * 4
    own_copies = []
    for third in range(3):
        rows = pl.ds(third * 128, 128)
        own_copies.append(
            pltpu.make_async_copy(
                p_ref.at[everywhere + (rows,)],
                held.at[everywhere + (rows,)],
                links.sends.at[own_first + third],
            )
        )
        own_copies[third].start()
    partners = [moved(me, axis, step) for axis in "xyz" for step in (1, 2, 3)]
    peers = [device_at(place) for place in partners]
    greet(peers)
    meet(peers)
    rates.send()

    def view_of(third, phase, place, part=None):
        order = GATHER_ORDERS[third]
        axis = order[2 - phase]
        start, size = (0, 128) if part is None else (64 * part, 64)
        if phase == 0:
            return held.at[axis_view(place, [axis]) + (pl.ds(third * 128 + start, size),)]
        index = []
        for name, key in (("y", 0), ("x", 1), ("z", 2), ("y", 3)):
            if name not in order[: 3 - phase]:
                continue
            if name != axis:
                index.append(slice(None))
            elif name == "y":
                index.append(lax.rem(place["y"], 2) if key == 0 else place["y"] // 2)
            else:
                index.append(place[name])
        return sums[third][phase - 1].at[tuple(index) + (pl.ds(start, size),)]

    def link(third, phase, kind, step, outgoing, incoming):
        number = first + 16 * third + (6 + 5 * (phase - 1) if phase else 0) + kind
        return remote(
            outgoing,
            incoming,
            links.sends.at[number],
            links.recvs.at[number],
            device_at(moved(me, GATHER_ORDERS[third][2 - phase], step)),
        )

    def relay(third, step):
        axis = GATHER_ORDERS[third][2]
        outgoing = view_of(third, 0, moved(me, axis, 2), step // 2)
        return link(third, 0, 4 + step // 2, step, outgoing, relays[third].at[step // 2])

    def half_copy(third, step, part):
        axis = GATHER_ORDERS[third][2]
        outgoing = view_of(third, 0, moved(me, axis, step), part)
        target = parts[third][0]
        view = (step // 2,) + (slice(None),) * (len(target.shape) - 3) + (pl.ds(64 * part, 64),)
        return link(third, 0, step // 2 * 2 + part, step, outgoing, target.at[view])

    def copy(third, phase, step):
        axis = GATHER_ORDERS[third][2 - phase]
        outgoing = view_of(third, phase, moved(me, axis, step))
        return link(third, phase, step - 1, step, outgoing, parts[third][phase].at[step - 1])

    for third in range(3):
        own_copies[third].wait()
        for step in (1, 3):
            relay(third, step).start()
        for step in (1, 3):
            half_copy(third, step, 1 - step // 2).start()
    for third in range(3):
        axis = GATHER_ORDERS[third][2]
        for step in (1, 3):
            relay(third, step).wait_recv()
            view = view_of(third, 0, moved(me, axis, step), step // 2)
            view[...] = view[...] + relays[third][step // 2]
            half_copy(third, step, step // 2).start()
    rate_sums[0] = pair_ref[...]
    rates.collect(rate_sums.at[1])
    rate_exchange = rates.pair(rate_sums.at[1 - rates.low_y], rate_pair)
    rate_exchange.start()
    for phase in range(1, 4):
        for third in range(3):
            total = view_of(third, phase - 1, me)[...].astype(jnp.float32)
            for slot, step in enumerate((1, 2, 3) if phase > 1 else (1, 3)):
                if phase > 1:
                    copy(third, phase - 1, step).wait_recv()
                else:
                    for part in range(2):
                        half_copy(third, step, part).wait_recv()
                total = total + parts[third][phase - 1][slot].astype(jnp.float32)
            if phase == 3:
                o_ref[128 * third : 128 * third + 128] = total
            else:
                sums[third][phase - 1][...] = total.astype(jnp.bfloat16)
                for step in (1, 2, 3):
                    copy(third, phase, step).start()
    rate_exchange.wait()
    for half in range(2):
        rows = slice(half * (RATE_ROWS // 2), (half + 1) * (RATE_ROWS // 2))
        share_ref[rows] = rate_sums[rates.low_y, half].astype(jnp.float32) + rate_pair[half].astype(
            jnp.float32
        )
    for third in range(3):
        for step in (1, 3):
            relay(third, step).wait_send()
            for part in range(2):
                half_copy(third, step, part).wait_send()
        for phase in (1, 2):
            for step in (1, 2, 3):
                copy(third, phase, step).wait_send()


def scatter_params(arrays, collective):
    def shape_left(left, rows):
        shape = ()
        for name, number in (("y", 2), ("x", 4), ("z", 4), ("y", 2)):
            if name in left:
                shape += (number,)
        return shape + (rows, 128)

    relays = []
    parts = []
    sums = []
    for order in GATHER_ORDERS:
        relays.append(pltpu.VMEM((2,) + shape_left(order[:2], 64), jnp.bfloat16))
        for phase in range(3):
            number = 3 if phase else 2
            parts.append(pltpu.VMEM((number,) + shape_left(order[: 2 - phase], 128), jnp.bfloat16))
        for phase in range(2):
            sums.append(pltpu.VMEM(shape_left(order[: 2 - phase], 128), jnp.bfloat16))
    held = pltpu.VMEM((2, 4, 4, 2, PAYLOAD, 128), jnp.bfloat16)
    half = (2, RATE_ROWS // 2, 512)
    rates = [pltpu.VMEM(shape, jnp.bfloat16) for shape in ((2, 3) + half[1:], (2,) + half, half)]
    return pl.pallas_call(
        scatter_kernel,
        out_shape=[
            jax.ShapeDtypeStruct((PAYLOAD, 128), jnp.float32),
            jax.ShapeDtypeStruct((RATE_ROWS, 512), jnp.float32),
        ],
        in_specs=[ANY, VMEM, VMEM],
        out_specs=[VMEM, VMEM],
        scratch_shapes=[held]
        + rates
        + relays
        + parts
        + sums
        + [pltpu.SemaphoreType.DMA((72,)), pltpu.SemaphoreType.DMA((72,))],
        compiler_params=pltpu.CompilerParams(
            collective_id=collective, has_side_effects=True, vmem_limit_bytes=56 * MEGABYTE
        ),
    )(*arrays)


def neighbour(row, col, offset):
    return lax.rem(row + offset[0] + 32, 32), lax.rem(col + offset[1] + 4, 4)


MEGABYTE = 1024 * 1024
OFFSETS = (-4, 4, -6, 6, -12, 12, -18, 18)
ID_ROW = 368
RATE_ROWS = 224


class Links:
    def __init__(self, sends, recvs):
        self.sends, self.recvs = sends, recvs
        self.cursor = 0

    def take(self, number):
        first = self.cursor
        self.cursor = first + number
        return first


class Total:
    def __init__(self, links, near_value, far_value, near, far):
        self.links = links
        self.values, self.buffers = (near_value, far_value), (near, far)
        self.first = links.take(2)
        self.row, self.col = lax.axis_index("rows"), lax.axis_index("cols")
        self.me = ((self.row // 16) * 4 + self.col, lax.rem(self.row, 16))

    def device(self, far, index):
        if far:
            return device_of((self.row // 16) * 16 + index, self.col)
        return device_of((index // 4) * 16 + self.me[1], lax.rem(index, 4))

    def link(self, far, outgoing, incoming, index):
        return remote(
            outgoing,
            incoming,
            self.links.sends.at[self.first + far],
            self.links.recvs.at[self.first + far],
            self.device(far, index),
        )

    def send(self, far, value):
        buffer, me, size = self.buffers[far], self.me[far], self.buffers[far].shape[0]
        self.values[far][...] = value
        for step in range(1, size):
            self.link(far, self.values[far], buffer.at[me], lax.rem(me + step, size)).start()
        buffer[me] = value

    def others(self, far):
        buffer, me, size = self.buffers[far], self.me[far], self.buffers[far].shape[0]
        view = buffer.at[pl.ds(0, size - 1)]
        return self.link(far, view, view, lax.rem(me + 1, size))

    def collect(self, far):
        self.others(far).wait_recv()
        total = self.buffers[far][0]
        for index in range(1, self.buffers[far].shape[0]):
            total = total + self.buffers[far][index]
        return total

    def start(self, value):
        self.send(0, value)

    def middle(self):
        self.send(1, self.collect(0))

    def finish(self):
        return self.collect(1)

    def close(self):
        for far in range(2):
            self.others(far).wait_send()


def total_scratch(rows, columns):
    return [
        pltpu.VMEM((rows, columns), jnp.float32),
        pltpu.VMEM((rows, columns), jnp.float32),
        pltpu.VMEM((8, rows, columns), jnp.float32),
        pltpu.VMEM((16, rows, columns), jnp.float32),
    ]


def total_peers():
    row, col = lax.axis_index("rows"), lax.axis_index("cols")
    near_me, far_me = (row // 16) * 4 + col, lax.rem(row, 16)
    peers = []
    for step in range(1, 8):
        index = lax.rem(near_me + step, 8)
        peers.append(device_of((index // 4) * 16 + far_me, lax.rem(index, 4)))
    for step in range(1, 16):
        peers.append(device_of((row // 16) * 16 + lax.rem(far_me + step, 16), col))
    return peers


def halo_peers():
    row, col = lax.axis_index("rows"), lax.axis_index("cols")
    return [
        device_of(*neighbour(row, col, (row_step, col_step)))
        for row_step in (-1, 0, 1)
        for col_step in (-1, 0, 1)
        if (row_step, col_step) != (0, 0)
    ]


class Halo:
    def __init__(self, links, source, window):
        self.links, self.source, self.window = links, source, window
        self.first = links.take(9)

    def copies(self, own_side):
        row, col = lax.axis_index("rows"), lax.axis_index("cols")
        listed = []
        for row_step in (-1, 0, 1):
            for col_step in (-1, 0, 1):
                if (row_step, col_step) == (0, 0):
                    continue
                low, size, top = {-1: (0, 4, 12), 0: (0, 8, 4), 1: (4, 4, 0)}[row_step]
                left = {-1: 32, 0: 16, 1: 0}[col_step]
                number = self.first + 3 * (row_step + 1) + col_step + 1
                listed.append(
                    remote(
                        self.source.at[pl.ds(low, size)],
                        self.window.at[pl.ds(top, size), pl.ds(left, 16)],
                        self.links.sends.at[number],
                        self.links.recvs.at[number],
                        device_of(*neighbour(row, col, (row_step, col_step))),
                    )
                )
        return listed

    def start(self):
        for copy in self.copies(True):
            copy.start()
        self.window[4:12, 16:32] = self.source[...]

    def finish(self):
        for copy in self.copies(False):
            copy.wait_recv()
        for copy in self.copies(False):
            copy.wait_send()


def widen_window(window, wide):
    col = lax.axis_index("cols")
    left = jnp.where(col > 0, 1.0, 0.0)
    right = jnp.where(col < 3, 1.0, 0.0)
    wide[:, 0:16] = window[:, 0:16].astype(jnp.float32) * left
    wide[:, 16:32] = window[:, 16:32].astype(jnp.float32)
    wide[:, 32:48] = window[:, 32:48].astype(jnp.float32) * right


def pixel_mask(mask):
    return jnp.broadcast_to(mask[:, None, :], (8, 16, 128)).reshape(128, 128)


def across_lanes(mask, width):
    return jnp.concatenate([mask] * (width // 128), axis=1)


class Gather:
    def __init__(self, links, source, target):
        self.links, self.source, self.target = links, source, target
        self.first = links.take(48)
        self.core_first = links.take(12)
        self.me = split_place()
        self.twin = moved(self.me, "core", 1, 2)

    def block(self, place, third, free, part=None):
        fixed = [axis for axis in "xyz" if axis not in free]
        rows = pl.ds(third * 128, 128) if part is None else pl.ds(third * 128 + 64 * part, 64)
        return self.target.at[axis_view(place, fixed) + (place["core"], rows)]

    def link(self, third, phase, kind, step, outgoing, incoming):
        number = self.first + 16 * third + 5 * phase + kind
        return remote(
            outgoing,
            incoming,
            self.links.sends.at[number],
            self.links.recvs.at[number],
            device_at(moved(self.me, GATHER_ORDERS[third][phase], step)),
        )

    def copy(self, third, phase, step, sender):
        free = GATHER_ORDERS[third][:phase]
        if phase == 0:
            outgoing = self.source.at[pl.ds(third * 128, 128)]
        else:
            outgoing = self.block(self.me, third, free)
        return self.link(third, phase, step - 1, step, outgoing, self.block(sender, third, free))

    def half(self, third, step, part, sender):
        free = GATHER_ORDERS[third][:2]
        outgoing = self.block(self.me, third, free, part)
        return self.link(third, 2, step // 2 * 2 + part, step, outgoing, self.block(sender, third, free, part))

    def relay(self, third, step, sender):
        order = GATHER_ORDERS[third]
        view = self.block(moved(sender, order[2], 4 - step), third, order[:2], step // 2)
        return self.link(third, 2, 4 + step // 2, step, view, view)

    def core_copy(self, third, distance, sender):
        order = GATHER_ORDERS[third]
        view = self.block(moved(sender, order[2], distance), third, order[:2])
        number = self.core_first + 4 * third + distance
        return remote(
            view, view, self.links.sends.at[number], self.links.recvs.at[number], device_at(self.twin)
        )

    def behind(self, third, phase, step):
        return moved(self.me, GATHER_ORDERS[third][phase], 4 - step)

    def run(self, early, late):
        me = self.me
        for phase in range(2):
            for third in range(3):
                if phase > 0:
                    for step in (1, 2, 3):
                        self.copy(third, phase - 1, step, self.behind(third, phase - 1, step)).wait_recv()
                for step in (1, 2, 3):
                    self.copy(third, phase, step, me).start()
                if phase == 0:
                    self.block(me, third, ())[...] = self.source[pl.ds(third * 128, 128)]
            if phase == 0:
                early()
        for third in range(3):
            for step in (1, 2, 3):
                self.copy(third, 1, step, self.behind(third, 1, step)).wait_recv()
            for first in (0, 1):
                for step in (1, 3):
                    self.half(third, step, (step // 2 + first) % 2, me).start()
            self.core_copy(third, 0, me).start()
        for third in range(3):
            for step in (1, 3):
                self.half(third, step, step // 2, self.behind(third, 2, step)).wait_recv()
                self.relay(third, step, me).start()
        for third in range(3):
            for step in (1, 3):
                self.half(third, step, 1 - step // 2, self.behind(third, 2, step)).wait_recv()
                self.core_copy(third, 4 - step, me).start()
        late()
        for third in range(3):
            for step in (1, 3):
                self.relay(third, step, self.behind(third, 2, step)).wait_recv()
            self.core_copy(third, 2, me).start()
        for third in range(3):
            for distance in range(4):
                self.core_copy(third, distance, self.twin).wait_recv()

    def close(self):
        for third in range(3):
            for phase in range(2):
                for step in (1, 2, 3):
                    self.copy(third, phase, step, self.me).wait_send()
            for step in (1, 3):
                self.relay(third, step, self.me).wait_send()
                for part in range(2):
                    self.half(third, step, part, self.me).wait_send()
            for distance in range(4):
                self.core_copy(third, distance, self.me).wait_send()


RATE_ORDERS = (("x", "z"), ("z", "x"))


class RateGather:
    def __init__(self, links, source, target):
        self.links, self.source, self.target = links, source, target
        self.first = links.take(82)
        self.me = split_place()
        self.low_y = lax.rem(self.me["y"], 2)
        self.other = dict(self.me)
        self.other["y"] = self.me["y"] + 1 - 2 * self.low_y
        self.half = RATE_ROWS // 2

    def own(self):
        return pltpu.make_async_copy(
            self.source,
            self.target.at[self.low_y, self.me["x"], self.me["z"]],
            self.links.recvs.at[self.first + 81],
        )

    def pair(self, sender):
        return remote(
            self.source,
            self.target.at[lax.rem(sender["y"], 2), self.me["x"], self.me["z"]],
            self.links.sends.at[self.first + 80],
            self.links.recvs.at[self.first + 80],
            device_at(self.other),
        )

    def axis(self, half, unit):
        return RATE_ORDERS[half][0 if unit < 2 else 1]

    def piece(self, half, unit, place, part=None):
        near = RATE_ORDERS[half][0]
        low_y = lax.rem(self.low_y + (unit if unit < 2 else (unit - 2) // 4), 2)
        places = {"x": place["x"], "z": place["z"]}
        if unit >= 2:
            places[near] = lax.rem(places[near] + (unit - 2) % 4, 4)
        start, size = {None: (0, 112), 0: (0, 64), 1: (64, 48)}[part]
        return self.target.at[low_y, places["x"], places["z"], pl.ds(half * self.half + start, size)]

    def link(self, half, unit, kind, step, view):
        number = self.first + 8 * unit + 4 * half + 2 * kind + step // 2
        return remote(
            view,
            view,
            self.links.sends.at[number],
            self.links.recvs.at[number],
            device_at(moved(self.me, self.axis(half, unit), step)),
        )

    def copy(self, half, unit, step, sender):
        return self.link(half, unit, 0, step, self.piece(half, unit, sender))

    def relay(self, half, unit, step, sender):
        first = moved(sender, self.axis(half, unit), 4 - step)
        return self.link(half, unit, 1, step, self.piece(half, unit, first, step // 2))

    def behind(self, half, unit, step):
        return moved(self.me, self.axis(half, unit), 4 - step)

    def each(self):
        return [(half, step) for half in range(2) for step in (1, 3)]

    def begin(self):
        self.own().start()
        self.pair(self.me).start()

    def send(self, *units):
        for unit in units:
            if unit == 0:
                self.own().wait()
            if unit == 1:
                self.pair(self.other).wait_recv()
            for half, step in self.each():
                self.copy(half, unit, step, self.me).start()

    def forward(self, *units):
        for unit in units:
            for half, step in self.each():
                self.copy(half, unit, step, self.behind(half, unit, step)).wait_recv()
                self.relay(half, unit, step, self.me).start()

    def receive(self, *units):
        for unit in units:
            for half, step in self.each():
                self.relay(half, unit, step, self.behind(half, unit, step)).wait_recv()

    def close(self):
        self.pair(self.me).wait_send()
        for unit in range(10):
            for half, step in self.each():
                self.copy(half, unit, step, self.me).wait_send()
                self.relay(half, unit, step, self.me).wait_send()


def assemble(gathered, first_row_group, staging, wide, stride, begin_group=0, end_group=16):
    parts = len(wide)
    count, offset = (BLOCK_ROWS, 0) if parts == 4 else (HEAD_ROWS, BLOCK_ROWS)

    def step(group, carry):
        low_y, x, z = first_row_group // 16, group // 4, lax.rem(group, 4)
        for column in range(4):
            area = staging[column]
            if parts == 4:
                area[0:288] = gathered[low_y, x, z, column // 2, column % 2, 0:288].astype(jnp.float32)
            else:
                area[0:96] = gathered[low_y, x, z, column // 2, column % 2, 272:368].astype(jnp.float32)
            skip = offset - (0 if parts == 4 else 272)
            for part in range(parts):
                begin = (part - column * count) % parts
                number = (count - begin + parts - 1) // parts
                row = (column * count + begin - part) // parts
                group_rows = 4 * count // parts
                target = group_rows * (group + stride) + row
                wide[part][pl.ds(target, number), :] = area[
                    pl.ds(skip + begin, number, stride=parts), :
                ]
        return carry

    lax.fori_loop(begin_group, end_group, step, 0)


def wide_rows(wide, first, number):
    return jnp.concatenate([part[pl.ds(first, number), :] for part in wide], axis=1)


def block_forward_kernel(
    x_ref,
    block_ref,
    head_ref,
    image_ref,
    rate_params_ref,
    reduce_hbm,
    spatial_hbm,
    expand_hbm,
    point_hbm,
    pool_hbm,
    project_hbm,
    misc_ref,
    norms_ref,
    masks_ref,
    first_ref,
    second_ref,
    third_ref,
    act_ref,
    window_ref,
    out_ref,
    slab_ref,
    rates_ref,
    gathered,
    s0,
    s1,
    s2,
    s3,
    w0,
    w1,
    w2,
    w3,
    h0,
    h1,
    ids,
    wide,
    act_map,
    payload_wide,
    payload_ref,
    rate_ref,
    reduce_ref,
    spatial_ref,
    expand_ref,
    point_ref,
    pool_ref,
    project_ref,
    *rest,
):
    staging, matrix, head = (s0, s1, s2, s3), (w0, w1, w2, w3), (h0, h1)
    links = Links(rest[-2], rest[-1])
    totals = [Total(links, *rest[4 * number : 4 * number + 4]) for number in range(3)]
    peers = total_peers() + halo_peers()
    greet(peers)
    payload_wide[0:BLOCK_ROWS, :] = block_ref[...]
    payload_wide[BLOCK_ROWS : BLOCK_ROWS + HEAD_ROWS, :] = head_ref[...]
    payload_wide[BLOCK_ROWS + HEAD_ROWS : PAYLOAD, :] = jnp.zeros(
        (PAYLOAD - BLOCK_ROWS - HEAD_ROWS, 128), jnp.float32
    )
    for step in range(8):
        payload_wide[ID_ROW + step : ID_ROW + step + 1, :] = jnp.full(
            (1, 128), image_ref[step].astype(jnp.float32)
        )
    payload_ref[...] = payload_wide[...].astype(jnp.bfloat16)
    rate_ref[...] = jnp.concatenate(
        [rate_params_ref[...], jnp.zeros((RATE_ROWS - 216, 512), jnp.float32)], axis=0
    ).astype(jnp.bfloat16)
    gather = Gather(links, payload_ref, gathered)
    rates = RateGather(links, rate_ref, rates_ref)
    halo = Halo(links, act_map, window_ref)
    slab_first = links.take(3)
    out_first = links.take(6)
    stores = [
        pltpu.make_async_copy(source, target, links.sends.at[out_first + number])
        for number, (source, target) in enumerate(
            (
                (reduce_ref, reduce_hbm),
                (spatial_ref, spatial_hbm),
                (expand_ref, expand_hbm),
                (point_ref, point_hbm),
                (pool_ref, pool_hbm),
                (project_ref, project_hbm),
            )
        )
    ]
    row, col = lax.axis_index("rows"), lax.axis_index("cols")
    meet(peers)

    def rates_early():
        rates.begin()
        rates.send(0)

    def rates_late():
        rates.forward(0)
        rates.send(2, 1, 3, 5)

    gather.run(rates_early, rates_late)

    assemble(gathered, 0, staging, matrix, 0, 0, 8)
    for step in range(8):
        reduce_ref[256 * step : 256 * step + 256] = wide_rows(matrix, 256 * step, 256).astype(jnp.bfloat16)
    first = jnp.dot(x_ref[...], reduce_ref[...], preferred_element_type=jnp.float32)
    totals[0].start(
        jnp.concatenate(
            [jnp.sum(first, axis=0, keepdims=True), jnp.sum(first * first, axis=0, keepdims=True)], axis=0
        )
    )
    for step in range(-3, 4):
        other = lax.rem(row + step + 32, 32)
        rows_there = gathered[
            other // 16, lax.rem(other // 4, 4), lax.rem(other, 4), 0, 0, ID_ROW : ID_ROW + 16
        ].astype(jnp.float32)[0:8]
        inside = jnp.logical_and(row + step >= 0, row + step < 32)
        ids[8 * (step + 3) : 8 * (step + 3) + 8, :] = jnp.where(inside, rows_there, -1.0)
    own_ids = ids[24:32, :]
    for number, offset in enumerate(OFFSETS):
        masks_ref[number] = jnp.where(ids[24 + offset : 32 + offset, :] == own_ids, 1.0, 0.0)
    masks_ref[len(OFFSETS)] = own_ids
    assemble(gathered, 0, staging, matrix, 0, 8, 16)
    for step in range(5):
        spatial_ref[464 * step : 464 * step + 464] = wide_rows(matrix, 2048 + 464 * step, 464).astype(
            jnp.bfloat16
        )
    totals[0].middle()
    assemble(gathered, 16, staging, matrix, 0)
    for step in range(13):
        spatial_ref[2320 + 176 * step : 2320 + 176 * step + 176] = wide_rows(
            matrix, 176 * step, 176
        ).astype(jnp.bfloat16)
    for part in range(4):
        expand_ref[:, 512 * part : 512 * part + 512] = jnp.concatenate(
            [array[pl.ds(2288 + part, 512, stride=4), :] for array in matrix], axis=1
        ).astype(jnp.bfloat16)
    norms_ref[...] = wide_rows(matrix, 4336, 16)
    for store in stores[0:3]:
        store.start()

    def normal(total, values, gain, shift, kept):
        average = total[0:1] / 16384.0
        variance = total[1:2] / 16384.0 - average * average
        scale = lax.rsqrt(variance + EPSILON)
        centered = (values - average) * scale
        kept[0:128] = centered
        kept[128:136] = jnp.broadcast_to(scale, (8, scale.shape[1]))
        return centered * gain + shift

    def silu(values):
        return values * jax.nn.sigmoid(values)

    def stats(values):
        return jnp.concatenate(
            [jnp.sum(values, axis=0, keepdims=True), jnp.sum(values * values, axis=0, keepdims=True)], axis=0
        )

    normed = normal(totals[0].finish(), first, norms_ref[0:1], norms_ref[1:2], first_ref)
    act_map[...] = silu(normed).astype(jnp.bfloat16).reshape(8, 16, MID)
    halo.start()
    rates.forward(2, 1)
    rates.receive(0)
    rates.forward(3, 5)
    rates.send(4, 6)
    halo.finish()
    widen_window(window_ref, wide)
    second = None
    for row_tap in range(3):
        part = None
        for col_tap in range(3):
            tap = 3 * row_tap + col_tap
            region = wide[4 * row_tap : 4 * row_tap + 8, 12 + 4 * col_tap : 28 + 4 * col_tap]
            product = jnp.dot(
                region.reshape(128, MID).astype(jnp.bfloat16),
                spatial_ref[512 * tap : 512 * tap + 512],
                preferred_element_type=jnp.float32,
            )
            part = product if part is None else part + product
        if row_tap != 1:
            part = part * across_lanes(pixel_mask(masks_ref[row_tap // 2]), MID)
        second = part if second is None else second + part
    totals[1].start(stats(second))
    assemble(gathered, 0, staging, head, 0)
    assemble(gathered, 16, staging, head, 16)
    totals[1].middle()
    for step in range(8):
        point_ref[256 * step : 256 * step + 256] = wide_rows(head, 256 * step, 256).astype(jnp.bfloat16)
        pool_ref[256 * step : 256 * step + 256] = wide_rows(head, 2048 + 256 * step, 256).astype(jnp.bfloat16)
    for step in range(5):
        project_ref[256 * step : 256 * step + 256] = wide_rows(head, 4097 + 256 * step, 256).astype(
            jnp.bfloat16
        )
    for store in stores[3:6]:
        store.start()
    misc_ref[0:8] = wide_rows(head, 4096, 8)
    misc_ref[8:72] = wide_rows(head, 5376, 64)
    normed = normal(totals[1].finish(), second, norms_ref[2:3], norms_ref[3:4], second_ref)
    rates.forward(4, 6)
    rates.receive(1)
    rates.send(7, 8)
    act_ref[...] = silu(normed).astype(jnp.bfloat16)
    third = jnp.dot(act_ref[...], expand_ref[...], preferred_element_type=jnp.float32)
    totals[2].start(stats(third))
    totals[2].middle()
    out_gain = jnp.concatenate([norms_ref[4 + part : 5 + part] for part in range(4)], axis=1)
    out_shift = jnp.concatenate([norms_ref[8 + part : 9 + part] for part in range(4)], axis=1)
    normed = normal(totals[2].finish(), third, out_gain, out_shift, third_ref)
    block_out = silu(normed + x_ref[...].astype(jnp.float32)).astype(jnp.bfloat16)
    out_ref[...] = block_out.reshape(8, 16, CIN)

    def slab_copy(step, sender):
        return remote(
            out_ref.at[:, :, pl.ds(pl.multiple_of(lax.rem(col + step, 4) * 512, 512), 512)],
            slab_ref.at[:, pl.ds(pl.multiple_of(sender * 16, 16), 16)],
            links.sends.at[slab_first + step - 1],
            links.recvs.at[slab_first + step - 1],
            device_of(row, lax.rem(col + step, 4)),
        )

    for step in (1, 2, 3):
        slab_copy(step, col).start()
    rates.forward(7, 8)
    rates.send(9)
    slab_ref[:, pl.ds(pl.multiple_of(col * 16, 16), 16)] = out_ref[
        :, :, pl.ds(pl.multiple_of(col * 512, 512), 512)
    ]
    for step in (1, 2, 3):
        copy = slab_copy(step, lax.rem(col + 4 - step, 4))
        copy.wait_recv()
        copy.wait_send()
    rates.forward(9)
    rates.receive(2, 3, 4, 5, 6, 7, 8, 9)
    rates.close()
    gather.close()
    for total in totals:
        total.close()
    for store in stores:
        store.wait()


def block_forward(arrays, collective):
    bf16, f32 = jnp.bfloat16, jnp.float32
    outs = [
        ((CIN, MID), bf16),
        ((9 * MID, MID), bf16),
        ((MID, CIN), bf16),
        ((CIN, ASPP), bf16),
        ((CIN, ASPP), bf16),
        ((5 * ASPP, ASPP), bf16),
        ((72, ASPP), f32),
        ((16, MID), f32),
        ((9, 8, 128), f32),
        ((136, MID), f32),
        ((136, MID), f32),
        ((136, CIN), f32),
        ((128, MID), bf16),
        ((16, 48, MID), bf16),
        ((8, 16, CIN), bf16),
        ((8, 64, CIN // 4), bf16),
        ((2, 4, 4, RATE_ROWS, CIN // 4), bf16),
    ]
    scratch = [pltpu.VMEM((2, 4, 4, 2, 2, PAYLOAD, 128), bf16)]
    scratch += [pltpu.VMEM((288, 128), f32)] * 4
    scratch += [pltpu.VMEM((4368, 128), f32)] * 4
    scratch += [pltpu.VMEM((5440, 128), f32)] * 2
    scratch += [
        pltpu.VMEM((56, 128), f32),
        pltpu.VMEM((16, 48, MID), f32),
        pltpu.VMEM((8, 16, MID), bf16),
        pltpu.VMEM((PAYLOAD, 128), f32),
        pltpu.VMEM((PAYLOAD, 128), bf16),
        pltpu.VMEM((RATE_ROWS, 512), bf16),
    ]
    scratch += [pltpu.VMEM(shape, dtype) for shape, dtype in outs[:6]]
    for rows, columns in ((2, MID), (2, MID), (2, CIN)):
        scratch += total_scratch(rows, columns)
    scratch += [pltpu.SemaphoreType.DMA((256,)), pltpu.SemaphoreType.DMA((256,))]
    return pl.pallas_call(
        block_forward_kernel,
        out_shape=[jax.ShapeDtypeStruct(shape, dtype) for shape, dtype in outs],
        in_specs=[VMEM, VMEM, VMEM, SMEM, VMEM],
        out_specs=[ANY] * 6 + [VMEM] * 10 + [ANY],
        scratch_shapes=scratch,
        compiler_params=pltpu.CompilerParams(
            collective_id=collective, has_side_effects=True, vmem_limit_bytes=60 * MEGABYTE
        ),
    )(*arrays)


class RatePieces:
    def __init__(self, links, units):
        self.links = links
        self.first = links.take(8 * units + 4)
        self.extra = self.first + 8 * units
        self.me = split_place()
        self.low_y = lax.rem(self.me["y"], 2)
        self.other = dict(self.me)
        self.other["y"] = self.me["y"] + 1 - 2 * self.low_y

    def rows(self, half):
        return pl.ds(half * (RATE_ROWS // 2), RATE_ROWS // 2)

    def piece(self, array, half, low_y, first_axis, second_axis):
        places = {RATE_ORDERS[half][0]: first_axis, RATE_ORDERS[half][1]: second_axis}
        return array.at[low_y, places["x"], places["z"], self.rows(half)]

    def remote(self, unit, half, slot, outgoing, incoming, axis, step):
        number = self.first + 8 * unit + 4 * half + slot
        return remote(
            outgoing,
            incoming,
            self.links.sends.at[number],
            self.links.recvs.at[number],
            device_at(moved(self.me, axis, step)),
        )

    def each(self):
        return [(half, step) for half in range(2) for step in (1, 2, 3)]


class RateFirst(RatePieces):
    def __init__(self, links, pieces, own, relays, parts, low_y):
        super().__init__(links, 4)
        self.pieces, self.own, self.relays, self.parts, self.from_y = pieces, own, relays, parts, low_y
        loads = links.take(6)
        self.loads = []
        for half in range(2):
            near, far = RATE_ORDERS[half]
            for slot, step in enumerate((0, 1, 3)):
                places = {near: slice(None), far: moved(self.me, far, step)[far]}
                self.loads.append(
                    pltpu.make_async_copy(
                        pieces.at[low_y, places["x"], places["z"], self.rows(half)],
                        own.at[half, slot],
                        links.recvs.at[loads + 3 * half + slot],
                    )
                )

    def part(self, step):
        return pl.ds(0, 64) if step == 1 else pl.ds(64, 48)

    def relay(self, unit, half, step):
        far = RATE_ORDERS[half][1]
        places = {RATE_ORDERS[half][0]: unit, far: moved(self.me, far, 2)[far]}
        rows = self.part(step)
        start = half * (RATE_ROWS // 2) + rows.start
        return self.remote(
            unit,
            half,
            step // 2 + 2,
            self.pieces.at[self.from_y, places["x"], places["z"], pl.ds(start, rows.size)],
            self.relays.at[half, unit, rows],
            far,
            step,
        )

    def copy(self, unit, half, step):
        far = RATE_ORDERS[half][1]
        slot = step // 2
        return self.remote(
            unit, half, slot, self.own.at[half, 1 + slot, unit], self.parts.at[half, unit, slot], far, step
        )

    def each(self):
        return [(half, step) for half in range(2) for step in (1, 3)]

    def send(self, *units):
        for unit in units:
            for half, step in self.each():
                self.relay(unit, half, step).start()

    def forward(self, *units):
        for unit in units:
            for half, step in self.each():
                self.relay(unit, half, step).wait_recv()
                rows = self.part(step)
                place = (half, 1 + step // 2, unit, rows)
                self.own[place] = self.own[place] + self.relays[half, unit, rows]
                self.copy(unit, half, step).start()

    def collect(self, *units):
        for unit in units:
            for half in range(2):
                total = self.own[half, 0, unit].astype(jnp.float32)
                for step in (1, 3):
                    self.copy(unit, half, step).wait_recv()
                    total = total + self.parts[half, unit, step // 2].astype(jnp.float32)
                self.own[half, 0, unit] = total.astype(jnp.bfloat16)
            for half, step in self.each():
                self.relay(unit, half, step).wait_send()
                self.copy(unit, half, step).wait_send()


class RateScatter(RatePieces):
    def __init__(self, links, sums, parts):
        super().__init__(links, 1)
        self.sums, self.parts = sums, parts

    def copy(self, half, step):
        near = RATE_ORDERS[half][0]
        outgoing = self.sums.at[half, moved(self.me, near, step)[near]]
        return self.remote(0, half, step - 1, outgoing, self.parts.at[half, step - 1], near, step)

    def pair(self, outgoing, incoming):
        return remote(
            outgoing,
            incoming,
            self.links.sends.at[self.extra],
            self.links.recvs.at[self.extra],
            device_at(self.other),
        )

    def send(self):
        for half, step in self.each():
            self.copy(half, step).start()

    def collect(self, target):
        for half in range(2):
            total = self.sums[half, self.me[RATE_ORDERS[half][0]]].astype(jnp.float32)
            for step in (1, 2, 3):
                self.copy(half, step).wait_recv()
                total = total + self.parts[half, step - 1].astype(jnp.float32)
            target[half] = total.astype(jnp.bfloat16)
        for half, step in self.each():
            self.copy(half, step).wait_send()


def disassemble(packed, first_row_group, staging, wide, stride, begin_group=0, end_group=16):
    parts = len(wide)
    core = lax.rem(lax.axis_index("cols"), 2)
    count = BLOCK_ROWS if parts == 4 else HEAD_ROWS
    low_y = first_row_group // 16

    def step(group, carry):
        x, z = group // 4, lax.rem(group, 4)
        for column in range(4):
            area = staging[column]
            here = (lax.rem(column + core, 2), low_y, x, z, column // 2)
            if parts == 4:
                skip = 0
                area[272:288] = packed[here + (slice(272, 288),)].astype(jnp.float32)
            else:
                skip = 1
                area[80:112] = jnp.zeros((32, 128), jnp.float32)
            for part in range(parts):
                begin = (part - column * count) % parts
                number = (count - begin + parts - 1) // parts
                row = (column * count + begin - part) // parts
                origin = (4 * count // parts) * (group + stride) + row
                area[pl.ds(skip + begin, number, stride=parts), :] = wide[part][
                    pl.ds(origin, number), :
                ]
            if parts == 4:
                packed[here + (slice(0, 288),)] = area[0:288].astype(jnp.bfloat16)
            else:
                packed[here + (slice(272, 384),)] = area[0:112].astype(jnp.bfloat16)
        return carry

    lax.fori_loop(begin_group, end_group, step, 0)


def deal(wide, first, values):
    number = values.shape[0]
    for part, array in enumerate(wide):
        array[first : first + number, :] = values[:, 128 * part : 128 * part + 128]


def against_rows(left, right):
    return lax.dot_general(left, right, (((1,), (1,)), ((), ())), preferred_element_type=jnp.float32)


def over_pixels(left, right):
    return lax.dot_general(left, right, (((0,), (0,)), ((), ())), preferred_element_type=jnp.float32)


def block_backward_kernel(
    x_ref,
    grad_ref,
    norms_ref,
    masks_ref,
    first_ref,
    second_ref,
    third_ref,
    act_ref,
    window_ref,
    reduce_hbm,
    spatial_hbm,
    expand_hbm,
    point_ref,
    pool_ref,
    project_ref,
    misc_ref,
    pieces_ref,
    out_ref,
    held_ref,
    late_ref,
    pair_ref,
    s0,
    s1,
    s2,
    s3,
    w0,
    w1,
    w2,
    w3,
    wide,
    act_map,
    window,
    packed,
    twin_part,
    reduce_ref,
    spatial_ref,
    expand_ref,
    free_sem,
    *rest,
):
    staging, matrix, head = (s0, s1, s2, s3), (w0, w1, w2, w3), (w0, w1)
    links = Links(rest[-2], rest[-1])
    totals = [Total(links, *rest[4 * number : 4 * number + 4]) for number in range(3)]
    own, relays, first_parts, second_parts = rest[12:16]
    rates = [
        RateFirst(links, pieces_ref, own.at[low_y], relays.at[low_y], first_parts.at[low_y], low_y)
        for low_y in range(2)
    ]
    scatter = RateScatter(links, own.at[0, :, 0], second_parts)
    me = scatter.me
    twin = device_at(moved(me, "core", 1, 2))
    halo = Halo(links, act_map, window)
    load_first, twin_first, out_first = (links.take(number) for number in (3, 2, 2))
    loads = [
        pltpu.make_async_copy(source, target, links.recvs.at[load_first + number])
        for number, (source, target) in enumerate(
            ((expand_hbm, expand_ref), (spatial_hbm, spatial_ref), (reduce_hbm, reduce_ref))
        )
    ]
    for copy in loads + rates[0].loads + rates[1].loads:
        copy.start()

    def twin_copy(low_y):
        return remote(
            packed.at[1, low_y],
            twin_part,
            links.sends.at[twin_first + low_y],
            links.recvs.at[twin_first + low_y],
            twin,
        )

    def out_copy(low_y):
        return pltpu.make_async_copy(
            packed.at[0, low_y], held_ref.at[low_y], links.sends.at[out_first + low_y]
        )

    def join_twin(low_y):
        twin_copy(low_y).wait_recv()

        def add_block(index, carry):
            place = (index // 8, lax.rem(index // 2, 4), lax.rem(index, 2))
            packed[(0, low_y) + place] = packed[(0, low_y) + place] + twin_part[place]
            return carry

        lax.fori_loop(0, 32, add_block, 0)
        out_copy(low_y).start()

    peers = total_peers() + halo_peers()
    greet(peers)

    def slope(values):
        part = jax.nn.sigmoid(values)
        return part * (1.0 + values * (1.0 - part))

    def local_sums(grad, kept):
        return jnp.concatenate(
            [
                jnp.sum(grad, axis=0, keepdims=True),
                jnp.sum(grad * kept[0:128], axis=0, keepdims=True),
            ],
            axis=0,
        )

    def through_norm(total, grad, kept, gain):
        return (
            gain
            * kept[128:129]
            * (grad - total[0:1] / 16384.0 - kept[0:128] * (total[1:2] / 16384.0))
        ).astype(jnp.bfloat16)

    out_gain = jnp.concatenate([norms_ref[4 + part : 5 + part] for part in range(4)], axis=1)
    out_shift = jnp.concatenate([norms_ref[8 + part : 9 + part] for part in range(4)], axis=1)
    residual = third_ref[0:128] * out_gain + out_shift + x_ref[...].astype(jnp.float32)
    out_ref[...] = grad_ref[...] * slope(residual)
    third_sums = local_sums(out_ref[...], third_ref)
    meet(peers)
    rates[0].send(0, 1, 2, 3)
    totals[0].start(third_sums)
    for step in range(4):
        deal(head, 512 * step, point_ref[512 * step : 512 * step + 512].astype(jnp.float32))
    deal(head, 2048, pool_ref[0:672].astype(jnp.float32))
    disassemble(packed, 0, staging, head, 0)
    totals[0].middle()
    for step in range(4):
        deal(head, 344 * step, pool_ref[672 + 344 * step : 1016 + 344 * step].astype(jnp.float32))
    deal(head, 1376, misc_ref[0:1])
    for step in range(5):
        deal(head, 1377 + 256 * step, project_ref[256 * step : 256 * step + 256].astype(jnp.float32))
    deal(head, 2657, misc_ref[1:64])
    disassemble(packed, 16, staging, head, 0)
    third_grad = through_norm(totals[0].finish(), out_ref[...], third_ref, out_gain)
    for copy in rates[0].loads + rates[1].loads:
        copy.wait()
    rates[0].forward(0, 1)
    loads[0].wait()
    second_gain, second_shift = norms_ref[2:3], norms_ref[3:4]
    second_norm = second_ref[0:128] * second_gain + second_shift
    second_back = against_rows(third_grad, expand_ref[...]) * slope(second_norm)
    second_sums = local_sums(second_back, second_ref)
    totals[1].start(second_sums)
    for part in range(4):
        product = over_pixels(act_ref[...], third_grad[:, 512 * part : 512 * part + 512])
        for number, array in enumerate(matrix):
            array[pl.ds(2288 + part, 512, stride=4), :] = product[:, 128 * number : 128 * number + 128]
    totals[1].middle()
    widen_window(window_ref, wide)
    second_grad = through_norm(totals[1].finish(), second_back, second_ref, second_gain)
    act_map[...] = second_grad.reshape(8, 16, MID)
    halo.start()
    rates[0].forward(2, 3)
    rates[1].send(0, 1, 2, 3)

    def spatial_grad(tap):
        row_tap, col_tap = tap // 3, tap % 3
        region = wide[4 * row_tap : 4 * row_tap + 8, 12 + 4 * col_tap : 28 + 4 * col_tap].reshape(128, MID)
        if row_tap != 1:
            region = region * across_lanes(pixel_mask(masks_ref[row_tap // 2]), MID)
        return over_pixels(region.astype(jnp.bfloat16), second_grad)

    middle_tap = spatial_grad(4)
    deal(matrix, 0, middle_tap[272:512])
    for tap in range(5, 9):
        deal(matrix, 240 + 512 * (tap - 5), spatial_grad(tap))
    halo.finish()
    rates[0].collect(0, 1, 2, 3)
    scatter.send()
    widen_window(window, wide)
    loads[1].wait()
    first_back = None
    for row_tap in range(3):
        part = None
        for col_tap in range(3):
            tap = 3 * row_tap + col_tap
            region = wide[
                8 - 4 * row_tap : 16 - 4 * row_tap, 20 - 4 * col_tap : 36 - 4 * col_tap
            ]
            product = against_rows(
                region.reshape(128, MID).astype(jnp.bfloat16), spatial_ref[512 * tap : 512 * tap + 512]
            )
            part = product if part is None else part + product
        if row_tap != 1:
            part = part * across_lanes(pixel_mask(masks_ref[1 - row_tap // 2]), MID)
        first_back = part if first_back is None else first_back + part
    first_gain, first_shift = norms_ref[0:1], norms_ref[1:2]
    first_back = first_back * slope(first_ref[0:128] * first_gain + first_shift)
    first_sums = local_sums(first_back, first_ref)
    totals[2].start(first_sums)
    deal(matrix, 4336, first_sums[1:2])
    deal(matrix, 4337, first_sums[0:1])
    deal(matrix, 4338, second_sums[1:2])
    deal(matrix, 4339, second_sums[0:1])
    for part in range(4):
        deal(matrix, 4340 + part, third_sums[1:2, 512 * part : 512 * part + 512])
        deal(matrix, 4344 + part, third_sums[0:1, 512 * part : 512 * part + 512])
    deal(matrix, 4348, jnp.zeros((20, MID), jnp.float32))
    disassemble(packed, 16, staging, matrix, 0)
    twin_copy(1).start()
    totals[2].middle()
    widen_window(window_ref, wide)
    deal(matrix, 4096, middle_tap[0:272])
    for tap in range(4):
        deal(matrix, 2048 + 512 * tap, spatial_grad(tap))
    disassemble(packed, 0, staging, matrix, 0, 8, 16)
    first_total = totals[2].finish()
    rates[1].forward(0, 1, 2, 3)
    join_twin(1)
    pl.semaphore_signal(free_sem, inc=1, device_id=twin, device_id_type=MESH)
    loads[2].wait()
    first_grad = through_norm(first_total, first_back, first_ref, first_gain)
    for part in range(4):
        rows = slice(512 * part, 512 * part + 512)
        deal(matrix, 512 * part, over_pixels(x_ref[:, rows], first_grad))
        out_ref[:, rows] = out_ref[:, rows] + against_rows(first_grad, reduce_ref[rows])
    disassemble(packed, 0, staging, matrix, 0, 0, 8)
    pl.semaphore_wait(free_sem, 1)
    twin_copy(0).start()
    rates[1].collect(0, 1, 2, 3)
    late_ref[...] = own[1, :, 0]
    scatter.collect(pair_ref)
    join_twin(0)
    for low_y in range(2):
        twin_copy(low_y).wait_send()
        out_copy(low_y).wait()
    for total in totals:
        total.close()


def block_backward(arrays, collective):
    bf16, f32 = jnp.bfloat16, jnp.float32
    half = RATE_ROWS // 2
    scratch = [pltpu.VMEM((384, 128), f32)] * 4
    scratch += [pltpu.VMEM((4368, 128), f32)] * 4
    scratch += [
        pltpu.VMEM((16, 48, MID), f32),
        pltpu.VMEM((8, 16, MID), bf16),
        pltpu.VMEM((16, 48, MID), bf16),
        pltpu.VMEM((2, 2, 4, 4, 2, PAYLOAD, 128), bf16),
        pltpu.VMEM((4, 4, 2, PAYLOAD, 128), bf16),
        pltpu.VMEM((CIN, MID), bf16),
        pltpu.VMEM((9 * MID, MID), bf16),
        pltpu.VMEM((MID, CIN), bf16),
        pltpu.SemaphoreType.REGULAR,
    ]
    for rows, columns in ((2, CIN), (2, MID), (2, MID)):
        scratch += total_scratch(rows, columns)
    scratch += [
        pltpu.VMEM((2, 2, 3, 4, half, 512), bf16),
        pltpu.VMEM((2, 2, 4, half, 512), bf16),
        pltpu.VMEM((2, 2, 4, 2, half, 512), bf16),
        pltpu.VMEM((2, 3, half, 512), bf16),
    ]
    scratch += [pltpu.SemaphoreType.DMA((232,)), pltpu.SemaphoreType.DMA((232,))]
    outs = [
        ((128, CIN), f32),
        ((2, 4, 4, 2, PAYLOAD, 128), bf16),
        ((2, 4, half, 512), bf16),
        ((2, half, 512), bf16),
    ]
    return pl.pallas_call(
        block_backward_kernel,
        out_shape=[jax.ShapeDtypeStruct(shape, dtype) for shape, dtype in outs],
        in_specs=[VMEM] * 9 + [ANY] * 3 + [VMEM] * (len(arrays) - 13) + [ANY],
        out_specs=[VMEM, ANY, VMEM, VMEM],
        scratch_shapes=scratch,
        compiler_params=pltpu.CompilerParams(
            collective_id=collective, has_side_effects=True, vmem_limit_bytes=62 * MEGABYTE
        ),
    )(*arrays)


def row_peers():
    row, col = lax.axis_index("rows"), lax.axis_index("cols")
    return [device_of(lax.rem(row + step + 32, 32), col) for step in (-3, -2, -1, 1, 2, 3)]


def row_moves():
    listed = []
    for branch, rate in enumerate(rate_list):
        for direction in range(2):
            for hop in range(4):
                lead = 8 * hop - rate if direction == 0 else rate - 8 * hop
                first, last = max(0, lead), min(8, lead + 8)
                if first < last:
                    sign = 1 if direction == 0 else -1
                    listed.append((branch, direction, sign * hop, first, first - lead, last - first))
    return listed


class RowShift:
    def __init__(self, links, sources, target):
        self.links, self.sources, self.target = links, sources, target
        self.moves = row_moves()
        self.first = links.take(len(self.moves))

    def copies(self, branch):
        row, col = lax.axis_index("rows"), lax.axis_index("cols")
        for number, (owner, direction, hop, first, top, size) in enumerate(self.moves):
            if owner == branch and hop:
                yield remote(
                    self.sources[branch][direction].at[pl.ds(first, size)],
                    self.target.at[branch, direction, pl.ds(top, size)],
                    self.links.sends.at[self.first + number],
                    self.links.recvs.at[self.first + number],
                    device_of(lax.rem(row + hop + 32, 32), col),
                )

    def start(self, branch):
        for copy in self.copies(branch):
            copy.start()
        for owner, direction, hop, first, top, size in self.moves:
            if owner == branch and hop == 0:
                self.target[branch, direction, top : top + size] = self.sources[branch][direction][
                    first : first + size
                ]

    def finish(self, branch):
        for copy in self.copies(branch):
            copy.wait_recv()
            copy.wait_send()


MARGIN = 24
SLOTS = (0, 2, 1)
SIDES, CENTER = (pl.ds(0, 2), pl.ds(2, 1))


def silu_value(values):
    return values * jax.nn.sigmoid(values)


def silu_grad(values):
    part = jax.nn.sigmoid(values)
    return part * (1.0 + values * (1.0 - part))


def two_sums(first, second):
    return jnp.concatenate(
        [jnp.sum(first, axis=0, keepdims=True), jnp.sum(second, axis=0, keepdims=True)], axis=0
    )


def centered_values(total, values):
    average = total[0:1] / 16384.0
    variance = total[1:2] / 16384.0 - average * average
    scale = lax.rsqrt(variance + EPSILON)
    return (values - average) * scale, scale


def norm_grad(total, grad, centered, scale, gain):
    return (
        gain * scale * (grad - total[0:1] / 16384.0 - centered * (total[1:2] / 16384.0))
    ).astype(jnp.bfloat16)


def pyramid_kernel(
    grid_ref,
    slab_ref,
    pieces_ref,
    point_hbm,
    pool_hbm,
    project_hbm,
    misc_ref,
    masks_ref,
    seg_ref,
    edge_ref,
    part_ref,
    weights_ref,
    loss_out,
    pooled_out,
    grad_out,
    point_out,
    pool_out,
    project_out,
    norms_out,
    pieces_hbm,
    kernels,
    padded,
    moved_maps,
    taps,
    core_part,
    high_out,
    high_part,
    tap_own,
    rows_out,
    rows_in,
    grads_own,
    grads_in,
    stack,
    grad_taps,
    back_out,
    back_in,
    pieces_out,
    point_ref,
    pool_ref,
    project_ref,
    heads_ref,
    *rest,
):
    bf16, f32 = jnp.bfloat16, jnp.float32
    links = Links(rest[-2], rest[-1])
    totals = [Total(links, *rest[4 * number : 4 * number + 4]) for number in range(5)]
    row, col = lax.axis_index("rows"), lax.axis_index("cols")
    core, high = lax.rem(col, 2), col // 2
    twin = device_of(row, col + 1 - 2 * core)
    far_twin = device_of(row, col + 2 - 4 * high)
    pieces_sem = links.take(4)
    tap_core, tap_high = links.take(6), links.take(6)
    stack_high, stack_core = links.take(6), links.take(6)
    back = links.take(3)
    forward_shift = RowShift(
        links, [[rows_out.at[branch, direction] for direction in range(2)] for branch in range(3)], rows_in
    )
    backward_shift = RowShift(
        links, [[grads_own.at[branch] for _ in range(2)] for branch in range(3)], grads_in
    )
    loads = [
        pltpu.make_async_copy(source, target, links.recvs.at[pieces_sem + number])
        for number, (source, target) in enumerate(
            (
                (pieces_ref, pieces_out),
                (point_hbm, point_ref),
                (pool_hbm, pool_ref),
                (project_hbm, project_ref),
            )
        )
    ]
    stores = [
        pltpu.make_async_copy(
            pieces_out.at[pl.ds(16 * part, 16)],
            pieces_hbm.at[pl.ds(16 * part, 16)],
            links.sends.at[pieces_sem + part],
        )
        for part in range(2)
    ]
    for load in loads:
        load.start()
    peers = total_peers() + row_peers()
    greet(peers)

    members_low = [jnp.where(masks_ref[8] == float(image), 1.0, 0.0) for image in range(4)]
    row_sums = jnp.sum(grid_ref[...].astype(f32), axis=1)
    pieces = []
    for image in range(4):
        chosen = members_low[image]
        pieces.append(
            jnp.concatenate(
                [
                    jnp.sum(row_sums * across_lanes(chosen, CIN), axis=0, keepdims=True),
                    jnp.sum(chosen, axis=0, keepdims=True),
                ],
                axis=1,
            )
        )
    pooled_here = jnp.concatenate(pieces, axis=0)

    def columns_of(place):
        return pl.ds(pl.multiple_of(place * 16, 16), 16)

    padded[:, 0:MARGIN] = jnp.zeros((8, MARGIN, 512), f32)
    padded[:, MARGIN + 64 :] = jnp.zeros((8, MARGIN, 512), f32)
    padded[:, MARGIN : MARGIN + 64] = slab_ref[...].astype(f32)

    def move_columns(branch):
        for side in range(2):
            start = MARGIN + (2 * side - 1) * rate_list[branch]
            moved_maps[2 * branch + side] = (
                padded[:, start : start + 64].reshape(512, 512).astype(bf16)
            )

    move_columns(0)
    slab = slab_ref[...].reshape(512, 512)
    for load in loads:
        load.wait()

    def join(pair, carry):
        both = jnp.concatenate(
            [pieces_out[2 * pair, 0:216].astype(f32), pieces_out[2 * pair + 1, 0:216].astype(f32)], axis=0
        )
        kernels[pl.ds(pl.multiple_of(432 * pair, 16), 432)] = both.astype(bf16)
        return carry

    lax.fori_loop(0, 6, join, 0)
    meet(peers)
    totals[4].start(pooled_here)

    def tap_core_copy(branch, place):
        return remote(
            taps.at[pl.ds(3 * branch, 3), :, columns_of(2 * place + 1 - core)],
            core_part.at[branch, place],
            links.sends.at[tap_core + 2 * branch + place],
            links.recvs.at[tap_core + 2 * branch + place],
            twin,
        )

    def tap_high_copy(branch, slots):
        number = tap_high + 2 * branch + slots.start // 2
        return remote(
            high_out.at[branch, slots],
            high_part.at[branch, slots],
            links.sends.at[number],
            links.recvs.at[number],
            far_twin,
        )

    def tap_meet(branch):
        for place in range(2):
            tap_core_copy(branch, place).wait_recv()
        away = taps[pl.ds(3 * branch, 3), :, columns_of(2 * (1 - high) + core)].astype(f32)
        high_out[branch] = (away + core_part[branch, 1 - high].astype(f32)).astype(bf16)
        tap_high_copy(branch, SIDES).start()
        here = taps[pl.ds(3 * branch, 3), :, columns_of(col)].astype(f32)
        tap_own[branch] = here + core_part[branch, high].astype(f32)

    def tap_finish(branch):
        tap_high_copy(branch, SIDES).wait_recv()
        for direction in range(2):
            rows_out[branch, direction] = (
                tap_own[branch, direction] + high_part[branch, direction].astype(f32)
            ).astype(bf16)
        forward_shift.start(branch)

    for branch in range(3):
        result = None
        for col_tap in range(3):
            left = slab if col_tap == 1 else moved_maps[2 * branch + col_tap // 2]
            right = jnp.concatenate(
                [
                    kernels[(9 * branch + 3 * tap + col_tap) * 256 : (9 * branch + 3 * tap + col_tap + 1) * 256]
                    for tap in range(3)
                ],
                axis=0,
            )
            product = against_rows(left, right)
            result = product if result is None else result + product
        for slot, tap in enumerate(SLOTS):
            taps[3 * branch + slot] = result[:, 256 * tap : 256 * tap + 256].astype(bf16).reshape(8, 64, 256)
        for place in range(2):
            tap_core_copy(branch, place).start()
        if branch == 0:
            lax.fori_loop(6, 16, join, 0)
            move_columns(1)
            totals[4].middle()
        else:
            if branch == 1:
                move_columns(2)
            tap_meet(branch - 1)
    tap_meet(2)
    for branch in range(3):
        tap_high_copy(branch, CENTER).start()
    grid = grid_ref[...].reshape(128, CIN)
    branches = [jnp.dot(grid, point_ref[...], preferred_element_type=f32)]
    number = lax.broadcasted_iota(jnp.int32, (256, 256), 0) * HEADS
    lane_256 = lax.broadcasted_iota(jnp.int32, (256, 256), 1)
    number_32 = lax.broadcasted_iota(jnp.int32, (256, 32), 0) * HEADS
    lane_32 = lax.broadcasted_iota(jnp.int32, (256, 32), 1)
    lane_128 = lax.broadcasted_iota(jnp.int32, (256, 128), 1)

    def rows_of_head(head):
        return jnp.where(lane_32 == (number_32 + head) // 256, 1.0, 0.0).astype(bf16)

    def lanes_of_head(head):
        return lane_256 == lax.rem(number + head, 256)

    flat_heads = misc_ref[19:51].astype(bf16)
    heads = jnp.zeros((256, 128), f32)
    for head in range(HEADS):
        spread = jnp.dot(rows_of_head(head), flat_heads, preferred_element_type=f32)
        column = jnp.sum(jnp.where(lanes_of_head(head), spread, 0.0), axis=1, keepdims=True)
        heads = heads + jnp.where(lane_128 == head, column, 0.0)
    heads_ref[...] = heads.astype(bf16)
    bias = jnp.where(
        lax.broadcasted_iota(jnp.int32, (1, 128), 1) < HEADS, misc_ref[36:37, 0:128], 0.0
    )
    pooled_sums = totals[4].finish()
    area = jnp.concatenate([pooled_sums[:, CIN : CIN + 128]] * 16, axis=1) * 16.0
    pooled = pooled_sums[:, 0:CIN] / area
    pooled_out[...] = pooled
    pooled_low = jnp.concatenate([pooled, jnp.zeros((4, CIN), f32)], axis=0).astype(bf16)
    pool_pre = jnp.dot(pooled_low, pool_ref[...], preferred_element_type=f32)[0:4] + misc_ref[0:1]
    pool_act = silu_value(pool_pre)
    members = [across_lanes(pixel_mask(members_low[image]), ASPP) for image in range(4)]
    pool_map = members[0] * pool_act[0:1]
    for image in range(1, 4):
        pool_map = pool_map + members[image] * pool_act[image : image + 1]
    for branch in range(3):
        tap_finish(branch)
    for branch in range(3):
        tap_high_copy(branch, CENTER).wait_recv()
        forward_shift.finish(branch)
        value = (tap_own[branch, 2] + high_part[branch, 2].astype(f32)).reshape(128, 256)
        for direction in range(2):
            mask = across_lanes(pixel_mask(masks_ref[2 + 2 * branch + direction]), ASPP)
            value = value + rows_in[branch, direction].astype(f32).reshape(128, 256) * mask
        branches.append(value)
    before = jnp.concatenate(branches, axis=1)
    totals[0].start(two_sums(before, before * before))
    totals[0].middle()
    gains = jnp.concatenate([misc_ref[9 + 2 * branch : 10 + 2 * branch] for branch in range(4)], axis=1)
    shifts = jnp.concatenate([misc_ref[10 + 2 * branch : 11 + 2 * branch] for branch in range(4)], axis=1)
    centered, scale = centered_values(totals[0].finish(), before)
    normed = centered * gains + shifts
    joined = jnp.concatenate([silu_value(normed).astype(bf16), pool_map.astype(bf16)], axis=1)
    projected = jnp.dot(joined, project_ref[...], preferred_element_type=f32)
    totals[1].start(two_sums(projected, projected * projected))
    totals[1].middle()
    last_gain, last_shift = misc_ref[17:18], misc_ref[18:19]
    proj_centered, proj_scale = centered_values(totals[1].finish(), projected)
    proj_normed = proj_centered * last_gain + last_shift
    feature_map = silu_value(proj_normed).astype(bf16)
    logits = jnp.dot(feature_map, heads_ref[...], preferred_element_type=f32) + bias
    lane = lax.broadcasted_iota(jnp.int32, (128, 128), 1)

    def per_pixel(labels_ref):
        spread = jnp.broadcast_to(labels_ref[...].astype(f32)[:, None, :], (8, 16, 16))
        here = lax.broadcasted_iota(jnp.int32, (8, 16, 16), 1) == lax.broadcasted_iota(
            jnp.int32, (8, 16, 16), 2
        )
        return jnp.sum(jnp.where(here, spread, 0.0), axis=2, keepdims=True).reshape(128, 1)

    lane_value = lane.astype(f32)
    hot = (
        jnp.where(lane_value == per_pixel(seg_ref), 1.0, 0.0)
        + jnp.where(lane == SEG, per_pixel(edge_ref), 0.0)
        + jnp.where(lane_value == per_pixel(part_ref) + (SEG + 1.0), 1.0, 0.0)
    )

    def cross_entropy(inside):
        highest = jnp.max(jnp.where(inside, logits, -3.0e38), axis=1, keepdims=True)
        powers = jnp.where(inside, jnp.exp(jnp.where(inside, logits - highest, 0.0)), 0.0)
        total = jnp.sum(powers, axis=1, keepdims=True)
        picked = jnp.sum(jnp.where(inside, logits * hot, 0.0), axis=1, keepdims=True)
        return highest + jnp.log(total) - picked, powers / total

    seg_inside, part_inside = lane < SEG, jnp.logical_and(lane > SEG, lane < HEADS)
    seg_terms, seg_soft = cross_entropy(seg_inside)
    part_terms, part_soft = cross_entropy(part_inside)
    edge_inside = lane == SEG
    edge_all = (
        jnp.maximum(logits, 0.0) + jnp.log1p(jnp.exp(-jnp.abs(logits))) - hot * logits
    )
    edge_soft = jax.nn.sigmoid(logits)
    weights = [weights_ref[task].astype(f32) for task in range(3)]
    weight_total = weights[0] + weights[1] + weights[2]
    row_lane = lax.broadcasted_iota(jnp.int32, (1, 128), 1)
    shares = jnp.where(
        row_lane < SEG, weights[0], jnp.where(row_lane == SEG, weights[1], weights[2])
    ) / jnp.full((1, 128), weight_total)
    shares = jnp.where(row_lane < HEADS, shares, 0.0)
    terms = jnp.where(lane == 0, seg_terms, 0.0) + jnp.where(edge_inside, edge_all, 0.0)
    terms = (terms + jnp.where(lane == SEG + 1, part_terms, 0.0)) * shares
    loss_local = jnp.sum(jnp.sum(terms, axis=0, keepdims=True), axis=1, keepdims=True) / 16384.0
    soft = seg_soft + part_soft + jnp.where(edge_inside, edge_soft, 0.0)
    logit_grad = ((soft - hot) * shares / 16384.0).astype(bf16)
    feature_back = against_rows(logit_grad, heads_ref[...]) * silu_grad(proj_normed)
    proj_sums = two_sums(feature_back, feature_back * proj_centered)
    totals[2].start(
        jnp.concatenate([proj_sums, jnp.broadcast_to(loss_local, (1, ASPP))], axis=0)
    )
    heads_grad = over_pixels(feature_map, logit_grad)
    norms_out[11:64] = jnp.zeros((53, ASPP), f32)
    flat_grad = None
    for head in range(HEADS):
        column = jnp.broadcast_to(heads_grad[:, head : head + 1], (256, 256))
        spread = jnp.where(lanes_of_head(head), column, 0.0).astype(bf16)
        part = over_pixels(rows_of_head(head), spread)
        flat_grad = part if flat_grad is None else flat_grad + part
    norms_out[11:28] = flat_grad[0:17]
    norms_out[28:29, 0:128] = jnp.sum(logit_grad.astype(f32), axis=0, keepdims=True)
    totals[2].middle()
    total = totals[2].finish()
    loss_out[...] = total[2:3, 0:1]
    projected_grad = norm_grad(total, feature_back, proj_centered, proj_scale, last_gain)
    joined_grad = against_rows(projected_grad, project_ref[...])
    pool_map_grad = joined_grad[:, 4 * ASPP :]
    pool_local = jnp.concatenate(
        [jnp.sum(pool_map_grad * members[image], axis=0, keepdims=True) for image in range(4)], axis=0
    )
    branch_back = joined_grad[:, : 4 * ASPP] * silu_grad(normed)
    branch_sums = two_sums(branch_back, branch_back * centered)
    pool_row = jnp.concatenate([pool_local[image : image + 1] for image in range(4)], axis=1)
    totals[3].start(jnp.concatenate([branch_sums, pool_row], axis=0))
    project_out[...] = over_pixels(joined, projected_grad).astype(bf16)
    totals[3].middle()
    pool_slope = silu_grad(pool_pre)
    pool_pre_local = pool_local * pool_slope
    norms_out[0:1] = jnp.sum(pool_pre_local, axis=0, keepdims=True)
    for branch in range(4):
        lanes = slice(256 * branch, 256 * branch + 256)
        norms_out[1 + 2 * branch : 2 + 2 * branch] = branch_sums[1:2, lanes]
        norms_out[2 + 2 * branch : 3 + 2 * branch] = branch_sums[0:1, lanes]
    norms_out[9:10] = proj_sums[1:2]
    norms_out[10:11] = proj_sums[0:1]
    padding = jnp.zeros((4, ASPP), f32)
    pool_out[...] = over_pixels(
        pooled_low, jnp.concatenate([pool_pre_local, padding], axis=0).astype(bf16)
    ).astype(bf16)
    total = totals[3].finish()
    branch_grad = norm_grad(total, branch_back, centered, scale, gains)
    for branch in range(3):
        grads_own[branch] = branch_grad[:, 256 * branch + 256 : 256 * branch + 512].reshape(8, 16, 256)
        backward_shift.start(branch)

    def stack_high_copy(branch, slots, sender):
        view = stack.at[branch, slots, :, columns_of(sender)]
        number = stack_high + 2 * branch + slots.start // 2
        return remote(view, view, links.sends.at[number], links.recvs.at[number], far_twin)

    def stack_core_copy(branch, place, sender_core):
        view = stack.at[branch, :, :, columns_of(2 * place + sender_core)]
        number = stack_core + 2 * branch + place
        return remote(view, view, links.sends.at[number], links.recvs.at[number], twin)

    for branch in range(3):
        stack[branch, 2, :, columns_of(col)] = grads_own[branch]
        stack_high_copy(branch, CENTER, col).start()
    pool_grad = jnp.concatenate(
        [total[2:3, 256 * image : 256 * image + 256] for image in range(4)], axis=0
    )
    pooled_grad = against_rows(
        jnp.concatenate([pool_grad * pool_slope, padding], axis=0).astype(bf16), pool_ref[...]
    )[0:4] / area
    for branch in range(3):
        backward_shift.finish(branch)
        for slot, direction in ((0, 1), (1, 0)):
            mask = across_lanes(pixel_mask(masks_ref[2 + 2 * branch + direction]), ASPP)
            shifted = grads_in[branch, direction].astype(f32).reshape(128, 256) * mask
            stack[branch, slot, :, columns_of(col)] = shifted.astype(bf16).reshape(8, 16, 256)
        stack_high_copy(branch, SIDES, col).start()
    point_grad = branch_grad[:, 0:256]
    point_out[...] = over_pixels(grid, point_grad).astype(bf16)
    grad_out[...] = against_rows(point_grad, point_ref[...])
    for image in range(4):
        grad_out[...] = grad_out[...] + across_lanes(
            pixel_mask(members_low[image]), CIN
        ) * pooled_grad[image : image + 1]
    for branch in range(3):
        for slots in (SIDES, CENTER):
            stack_high_copy(branch, slots, col + 2 - 4 * high).wait_recv()
        for place in range(2):
            stack_core_copy(branch, place, core).start()
    def split(pair, carry):
        both = kernels[pl.ds(pl.multiple_of(432 * pair, 16), 432)].astype(f32)
        zeros = jnp.zeros((8, 512), f32)
        pieces_out[2 * pair] = jnp.concatenate([both[0:216], zeros], axis=0).astype(bf16)
        pieces_out[2 * pair + 1] = jnp.concatenate([both[216:432], zeros], axis=0).astype(bf16)
        return carry

    slab_grad = None
    for branch, rate in enumerate(rate_list):
        for place in range(2):
            stack_core_copy(branch, place, 1 - core).wait_recv()
        for slot, tap in enumerate(SLOTS):
            padded[:, MARGIN : MARGIN + 64, 0:256] = stack[branch, slot].astype(f32)
            for col_tap in range(3):
                start = MARGIN - (col_tap - 1) * rate
                lanes = slice(256 * (3 * tap + col_tap), 256 * (3 * tap + col_tap) + 256)
                grad_taps[:, lanes] = (
                    padded[:, start : start + 64, 0:256].reshape(512, 256).astype(bf16)
                )
        rows = slice(2304 * branch, 2304 * branch + 2304)
        product = jnp.dot(grad_taps[...], kernels[rows], preferred_element_type=f32)
        slab_grad = product if slab_grad is None else slab_grad + product
        kernels[rows] = over_pixels(grad_taps[...], slab).astype(bf16)
        if branch == 1:
            lax.fori_loop(0, 8, split, 0)
            stores[0].start()
    back_out[...] = slab_grad.astype(bf16).reshape(8, 64, 512)

    def back_copy(step, sender):
        return remote(
            back_out.at[:, columns_of(lax.rem(col + step, 4))],
            back_in.at[:, :, pl.ds(pl.multiple_of(sender * 512, 512), 512)],
            links.sends.at[back + step - 1],
            links.recvs.at[back + step - 1],
            device_of(row, lax.rem(col + step, 4)),
        )

    for step in (1, 2, 3):
        back_copy(step, col).start()
    back_in[:, :, pl.ds(pl.multiple_of(col * 512, 512), 512)] = back_out[:, columns_of(col)]

    lax.fori_loop(8, 16, split, 0)
    stores[1].start()
    for step in (1, 2, 3):
        copy = back_copy(step, lax.rem(col + 4 - step, 4))
        copy.wait_recv()
        copy.wait_send()
    grad_out[...] = grad_out[...] + back_in[...].reshape(128, CIN).astype(f32)
    for branch in range(3):
        for place in range(2):
            tap_core_copy(branch, place).wait_send()
            stack_core_copy(branch, place, core).wait_send()
        for slots in (SIDES, CENTER):
            tap_high_copy(branch, slots).wait_send()
            stack_high_copy(branch, slots, col).wait_send()
    for store in stores:
        store.wait()
    for total in totals:
        total.close()


def pyramid(arrays, collective):
    bf16, f32 = jnp.bfloat16, jnp.float32
    outs = [
        ((1, 1), f32),
        ((4, CIN), f32),
        ((128, CIN), f32),
        ((CIN, ASPP), bf16),
        ((CIN, ASPP), bf16),
        ((5 * ASPP, ASPP), bf16),
        ((64, ASPP), f32),
        ((32, RATE_ROWS, 512), bf16),
    ]
    scratch = [
        pltpu.VMEM((27 * ASPP, 512), bf16),
        pltpu.VMEM((8, 64 + 2 * MARGIN, 512), f32),
        pltpu.VMEM((6, 512, 512), bf16),
        pltpu.VMEM((9, 8, 64, ASPP), bf16),
        pltpu.VMEM((3, 2, 3, 8, 16, ASPP), bf16),
        pltpu.VMEM((3, 3, 8, 16, ASPP), bf16),
        pltpu.VMEM((3, 3, 8, 16, ASPP), bf16),
        pltpu.VMEM((3, 3, 8, 16, ASPP), f32),
        pltpu.VMEM((3, 2, 8, 16, ASPP), bf16),
        pltpu.VMEM((3, 2, 8, 16, ASPP), bf16),
        pltpu.VMEM((3, 8, 16, ASPP), bf16),
        pltpu.VMEM((3, 2, 8, 16, ASPP), bf16),
        pltpu.VMEM((3, 3, 8, 64, ASPP), bf16),
        pltpu.VMEM((512, 9 * ASPP), bf16),
        pltpu.VMEM((8, 64, 512), bf16),
        pltpu.VMEM((8, 16, CIN), bf16),
        pltpu.VMEM((32, RATE_ROWS, 512), bf16),
        pltpu.VMEM((CIN, ASPP), bf16),
        pltpu.VMEM((CIN, ASPP), bf16),
        pltpu.VMEM((5 * ASPP, ASPP), bf16),
        pltpu.VMEM((ASPP, 128), bf16),
    ]
    for rows, columns in ((2, 4 * ASPP), (2, ASPP), (3, ASPP), (3, 4 * ASPP), (4, CIN + 128)):
        scratch += total_scratch(rows, columns)
    scratch += [pltpu.SemaphoreType.DMA((184,)), pltpu.SemaphoreType.DMA((184,))]
    in_specs = [VMEM] * len(arrays)
    in_specs[2:6] = [ANY] * 4
    in_specs[-1] = SMEM
    return pl.pallas_call(
        pyramid_kernel,
        out_shape=[jax.ShapeDtypeStruct(shape, dtype) for shape, dtype in outs],
        in_specs=in_specs,
        out_specs=[VMEM] * (len(outs) - 1) + [ANY],
        scratch_shapes=scratch,
        compiler_params=pltpu.CompilerParams(
            collective_id=collective, has_side_effects=True, vmem_limit_bytes=62 * MEGABYTE
        ),
    )(*arrays)


def finish_kernel(
    loss_ref,
    pooled_ref,
    gradient_ref,
    flat_ref,
    rate_ref,
    block_ref,
    head_ref,
    rate_moment_ref,
    loss_out,
    pooled_out,
    gradient_out,
    block_out,
    head_out,
    rate_out,
):
    loss_out[...] = loss_ref[...]
    pooled_out[...] = pooled_ref[...]
    gradient_out[...] = gradient_ref[...]
    block_out[...] = MOMENTUM_KEEP * block_ref[...] + flat_ref[0:BLOCK_ROWS, :]
    head_out[...] = MOMENTUM_KEEP * head_ref[...] + flat_ref[BLOCK_ROWS : BLOCK_ROWS + HEAD_ROWS, :]
    rate_out[...] = MOMENTUM_KEEP * rate_moment_ref[...] + rate_ref[0:216]


def finish(loss, pooled, gradient, flat, rate, block_moment, head_moment, rate_moment):
    like = (loss, pooled, gradient, block_moment, head_moment, rate_moment)
    return pl.pallas_call(
        finish_kernel,
        out_shape=[jax.ShapeDtypeStruct(item.shape, jnp.float32) for item in like],
        in_specs=[VMEM] * 8,
        out_specs=[VMEM] * 6,
        compiler_params=pltpu.CompilerParams(vmem_limit_bytes=32 * MEGABYTE),
    )(loss, pooled, gradient, flat, rate, block_moment, head_moment, rate_moment)


def per_device(
    features,
    image_rows,
    seg_labels,
    edge_labels,
    part_labels,
    task_weights,
    block_params,
    block_moment,
    head_params,
    head_moment,
    rate_params,
    rate_moment,
):
    height, across, channels = features.shape
    pixels = height * across
    inputs = features.reshape(pixels, channels)
    (
        w_reduce,
        w_spatial,
        w_expand,
        w_point,
        w_pool,
        w_project,
        misc,
        norms,
        masks,
        first_kept,
        second_kept,
        third_kept,
        second_act,
        block_window,
        grid,
        slab_map,
        rates_all,
    ) = block_forward(
        (
            inputs,
            block_params.reshape(BLOCK_ROWS, 128),
            head_params.reshape(HEAD_ROWS, 128),
            image_rows,
            rate_params.T,
        ),
        1,
    )
    (
        loss_rows,
        pooled,
        out_grad,
        grad_point,
        grad_pool,
        grad_project,
        misc_grads,
        rate_pieces,
    ) = pyramid(
        (
            grid,
            slab_map,
            rates_all.reshape(32, RATE_ROWS, channels // 4),
            w_point,
            w_pool,
            w_project,
            misc,
            masks,
            seg_labels,
            edge_labels,
            part_labels,
            task_weights,
        ),
        2,
    )
    input_grad, *flat_sums = block_backward(
        (
            inputs,
            out_grad,
            norms,
            masks,
            first_kept,
            second_kept,
            third_kept,
            second_act,
            block_window,
            w_reduce,
            w_spatial,
            w_expand,
            grad_point,
            grad_pool,
            grad_project,
            misc_grads,
            rate_pieces.reshape(2, 4, 4, RATE_ROWS, channels // 4),
        ),
        16,
    )
    shares_all, rate_sum = scatter_params(flat_sums, 20)
    loss_out, pooled_out, gradient, block_next, head_next, rate_next = finish(
        loss_rows,
        pooled,
        input_grad,
        shares_all,
        rate_sum,
        block_moment.reshape(BLOCK_ROWS, 128),
        head_moment.reshape(HEAD_ROWS, 128),
        rate_moment.T,
    )
    return (
        loss_out.reshape(()),
        pooled_out,
        gradient.reshape(height, across, channels),
        block_next.reshape(-1),
        head_next.reshape(-1),
        rate_next.T,
    )


def solution(mesh):
    return jax.shard_map(
        per_device,
        mesh=mesh,
        in_specs=(
            P("rows", "cols", None),
            P("rows"),
            P("rows", "cols"),
            P("rows", "cols"),
            P("rows", "cols"),
            P(),
            P(("rows", "cols")),
            P(("rows", "cols")),
            P(("rows", "cols")),
            P(("rows", "cols")),
            P("cols", "rows"),
            P("cols", "rows"),
        ),
        out_specs=(
            P(),
            P(),
            P("rows", "cols", None),
            P(("rows", "cols")),
            P(("rows", "cols")),
            P("cols", "rows"),
        ),
        check_vma=False,
    )
```
